32 devices in a mesh: dp: 8 (over z, y), tensor: 4 (over x, core).
Axes of the slice: x: 2, y: 2, z: 4, core: 2. Of those that a mesh axis runs over, the one named last changes fastest.
Arguments:
- states: bfloat16 [3072, 2048], P('dp'), may hold values from -6 to 6
- query_weight: bfloat16 [1, 2048, 1536], P(None, 'dp', 'tensor'), may hold values from -0.125 to 0.125
- keyvalue_matrix: bfloat16 [1, 2048, 768], P(None, 'dp'), may hold values from -0.125 to 0.125
- output_weight: bfloat16 [1, 2048, 1536], P(None, 'dp', 'tensor'), may hold values from -0.625 to 0.625
- gate_weight: bfloat16 [1, 2048, 4864], P(None, 'dp', 'tensor'), may hold values from -0.125 to 0.125
- up_weight: bfloat16 [1, 2048, 4864], P(None, 'dp', 'tensor'), may hold values from -0.125 to 0.125
- down_weight: bfloat16 [1, 2048, 4864], P(None, 'dp', 'tensor'), may hold values from -0.078125 to 0.078125
- norm_gains: bfloat16 [1, 2048, 2], P(None, 'dp'), may hold values from 0.099609375 to 1.8984375
- query_gain: float32 [1, 64], replicated, may hold values from 0.7 to 1.8
- key_gain: float32 [1, 64], replicated, may hold values from 0.7 to 1.8
- slot_sequence: int32 [24], replicated, may hold values from 0 to 1, as said below
- slot_offset: int32 [24], replicated, may hold values from 0 to 1408, as said below
- out_grad: bfloat16 [3072, 2048], P('dp'), may hold values from -6 to 6
Outputs:
- result: bfloat16 [3072, 2048], P('dp')
- states_grad: float32 [3072, 2048], P('dp')
- grad_query: float32 [1, 2048, 1536], P(None, 'dp', 'tensor')
- grad_keyvalue: float32 [1, 2048, 768], P(None, 'dp')
- grad_output: float32 [1, 2048, 1536], P(None, 'dp', 'tensor')
- grad_gate: float32 [1, 2048, 4864], P(None, 'dp', 'tensor')
- grad_up: float32 [1, 2048, 4864], P(None, 'dp', 'tensor')
- grad_down: float32 [1, 2048, 4864], P(None, 'dp', 'tensor')
- grad_norms: float32 [1, 2048, 2], P(None, 'dp')
- grad_querygain: float32 [1, 64], replicated
- grad_keygain: float32 [1, 64], replicated
The draws below stay inside these ranges and needn't reach their ends.
Inputs may be any that keep to these rules, and one draw needn't show every extreme that they name: Slot s (on index s // 3 of dp) holds 128 tokens of sequence slot_sequence[s]; every sequence has 8 to 32 blocks, and one has exactly 12, no fewer than any other. `slot_offset`: the blocks of one sequence have the offsets 0, 128, 256, ... each once.
All inputs are finite; a program needn't handle non-finite values.
Results may differ from the reference program's by a relative error of at most 0.015.
The reference program's roundings to bfloat16 on the way count: a program that leaves them out, or rounds other values in their place, can miss the bound.
Values may be sent and summed in bfloat16 or wider, within the bound.
A program may use at most 192 MiB of HBM per device.

```python
import math
import jax
import jax.numpy as jnp
from jax import lax

MODEL_WIDTH = 2048
QUERY_HEADS = 24
KEYVALUE_HEADS = 6
HEAD_WIDTH = 64
FF = 4864
LAYER_COUNT = 1
STRETCH = 128
SEQ_MIN = 8
SEQ_MAX = 32
STRETCHES = 24
TOKEN_TOTAL = 3072
SEQS = 2
FIRST_LEN = 12
N_TENSOR = 4


def deal_tables(key):
    picks_key, order_key, deal_key = jax.random.split(key, 3)
    spare_stretches = STRETCHES - FIRST_LEN - SEQ_MIN * (SEQS - 1)
    extra_room = SEQ_MAX - SEQ_MIN
    picked = (jax.random.permutation(picks_key, (SEQS - 1) * extra_room) < spare_stretches).astype(jnp.int32)
    lengths = jnp.concatenate([jnp.full((1,), FIRST_LEN, jnp.int32), SEQ_MIN + jnp.sum(picked.reshape(SEQS - 1, extra_room), axis=1).astype(jnp.int32)])
    lengths = lengths[jax.random.permutation(order_key, SEQS)]
    seq_ends = jnp.cumsum(lengths).astype(jnp.int32)
    seq_starts = seq_ends - lengths
    stretch_ids = jnp.arange(STRETCHES, dtype=jnp.int32)
    owner_seq = jnp.sum((stretch_ids[:, None] >= seq_ends[None, :]).astype(jnp.int32), axis=1)
    offset = (stretch_ids - seq_starts[owner_seq]) * STRETCH
    dealt_order = jax.random.permutation(deal_key, STRETCHES)
    return (owner_seq[dealt_order].astype(jnp.int32), offset[dealt_order].astype(jnp.int32))


def draw_slot_sequence(key, part):
    tables = deal_tables(key)
    return tables[0]


def draw_slot_offset(key, part):
    tables = deal_tables(key)
    return tables[1]


def levels(own_key, dims, cuts, smallest, high):
    def one(position, shards_of):
        draws = jax.random.uniform(jax.random.fold_in(jax.random.fold_in(own_key, 6), position), (shards_of,), jnp.float32, smallest / len(cuts), high / len(cuts))
        return jnp.repeat(jnp.exp(draws), dims[position] // shards_of).reshape((-1,) + (1,) * (len(dims) - position - 1))

    factor_of = one(*cuts[0])
    for cut in cuts[1:]:
        factor_of = factor_of * one(*cut)
    return factor_of


def bell_draw(rng, dims, deviation, reach, cuts=(), kind=jnp.bfloat16):
    entries = jax.random.normal(rng, dims, jnp.float32) * deviation
    if len(cuts) > 0:
        entries = levels(rng, dims, cuts, -0.22, 0.18) * entries
    return jnp.clip(entries, min=-reach, max=reach).astype(kind)


def setup_inputs(seed: int = 0) -> dict:
    key_of = jax.random.split(jax.random.key(seed), 14)
    return {
        "states": bell_draw(key_of[0], (TOKEN_TOTAL, MODEL_WIDTH), 1.0, 6.0, ((0, 8),)),
        "query_weight": bell_draw(key_of[1], (LAYER_COUNT, MODEL_WIDTH, QUERY_HEADS * HEAD_WIDTH), MODEL_WIDTH ** -0.5, 0.125, ((1, 8), (2, 4))),
        "keyvalue_matrix": bell_draw(key_of[2], (LAYER_COUNT, MODEL_WIDTH, 2 * KEYVALUE_HEADS * HEAD_WIDTH), MODEL_WIDTH ** -0.5, 0.125, ((1, 8),)),
        "output_weight": bell_draw(key_of[3], (LAYER_COUNT, MODEL_WIDTH, QUERY_HEADS * HEAD_WIDTH), (QUERY_HEADS * HEAD_WIDTH // 16) ** -0.5, 0.625, ((1, 8), (2, 4))),
        "gate_weight": bell_draw(key_of[4], (LAYER_COUNT, MODEL_WIDTH, FF), MODEL_WIDTH ** -0.5, 0.125, ((1, 8), (2, 4))),
        "up_weight": bell_draw(key_of[5], (LAYER_COUNT, MODEL_WIDTH, FF), MODEL_WIDTH ** -0.5, 0.125, ((1, 8), (2, 4))),
        "down_weight": bell_draw(key_of[6], (LAYER_COUNT, MODEL_WIDTH, FF), FF ** -0.5, 0.078125, ((1, 8), (2, 4))),
        "norm_gains": jnp.clip(1.0 + 0.18 * jax.random.normal(key_of[7], (LAYER_COUNT, MODEL_WIDTH, 2), jnp.float32), 0.099609375, 1.8984375).astype(jnp.bfloat16),
        "query_gain": jnp.clip(jnp.exp(jax.random.uniform(key_of[8], (LAYER_COUNT, HEAD_WIDTH), jnp.float32, math.log(0.7), math.log(1.8))), 0.7, 1.8),
        "key_gain": jnp.clip(jnp.exp(jax.random.uniform(key_of[9], (LAYER_COUNT, HEAD_WIDTH), jnp.float32, math.log(0.7), math.log(1.8))), 0.7, 1.8),
        "slot_sequence": draw_slot_sequence(jax.random.fold_in(key_of[13], 71), 0),
        "slot_offset": draw_slot_offset(jax.random.fold_in(key_of[13], 71), 0),
        "out_grad": bell_draw(key_of[12], (TOKEN_TOTAL, MODEL_WIDTH), 1.0, 6.0, ((0, 8),)),
    }


PRECISE = lax.Precision.HIGHEST
EPSILON = 1e-06
NEGATIVE = -1e+30

@jax.custom_vjp
def low(v):
    return lax.optimization_barrier(v.astype(jnp.bfloat16)).astype(jnp.float32)

@jax.custom_vjp
def low_back(v):
    return v

def low_keep(v):
    return (low(v), None)

def low_pass(kept, grad):
    return (grad,)

def back_keep(v):
    return (v, None)

def back_low(kept, grad):
    return (low(grad),)
low.defvjp(low_keep, low_pass)
low_back.defvjp(back_keep, back_low)

def normed(vector, gain_vector):
    return vector * lax.rsqrt(lax.optimization_barrier(jnp.mean(vector * vector, axis=-1, keepdims=True)) + EPSILON) * gain_vector

def angles(positions, head_size):
    frequency = 10000.0 ** (-jnp.arange(head_size // 2, dtype=jnp.float32) * 2.0 / head_size)
    phase_angle = positions.astype(jnp.float32)[:, None] * frequency[None, :]
    return (jnp.cos(phase_angle)[:, None, :], jnp.sin(phase_angle)[:, None, :])

def rotated(vector, cosines, sines):
    half_width = vector.shape[-1] // 2
    front = vector[..., :half_width]
    behind = vector[..., half_width:]
    return jnp.concatenate([front * cosines - behind * sines, behind * cosines + front * sines], axis=-1)

def matmul(left_side, right_side):
    return jnp.dot(left_side, right_side, precision=PRECISE)

def attention(queries, key_head_rows, value_head_rows, seq_sorted, pos_sorted):
    span = 4 * STRETCH
    window = min(span + SEQ_MAX * STRETCH, TOKEN_TOTAL)
    score_scale = HEAD_WIDTH ** (-0.5)

    def block(block_index):
        block_start = block_index * span
        key_start = jnp.maximum(block_start + span - window, 0).astype(jnp.int32)
        query_block = lax.dynamic_slice_in_dim(queries, block_start, span, 0)
        key_block = lax.dynamic_slice_in_dim(key_head_rows, key_start, window, 0)
        value_block = lax.dynamic_slice_in_dim(value_head_rows, key_start, window, 0)
        seq_query = lax.dynamic_slice_in_dim(seq_sorted, block_start, span, 0)
        pos_query = lax.dynamic_slice_in_dim(pos_sorted, block_start, span, 0)
        seq_key = lax.dynamic_slice_in_dim(seq_sorted, key_start, window, 0)
        pos_key = lax.dynamic_slice_in_dim(pos_sorted, key_start, window, 0)
        scores = low_back(jnp.einsum('qhd,khd->hqk', query_block, key_block, precision=PRECISE) * score_scale)
        visible = (seq_key[None, :] == seq_query[:, None]) & (pos_key[None, :] <= pos_query[:, None])
        scores = jnp.where(visible[None], scores, NEGATIVE)
        top_score = lax.optimization_barrier(jnp.max(scores, axis=-1, keepdims=True))
        weights = jnp.exp(scores - top_score)
        weights = weights / lax.optimization_barrier(jnp.sum(weights, axis=-1, keepdims=True))
        return jnp.einsum('hqk,khd->qhd', weights, value_block, precision=PRECISE)
    blocks = lax.map(jax.checkpoint(block), jnp.arange(TOKEN_TOTAL // span, dtype=jnp.int32))
    return blocks.reshape(TOKEN_TOTAL, QUERY_HEADS, HEAD_WIDTH)

def reference(states, query_weight, keyvalue_matrix, output_weight, gate_weight, up_weight, down_weight, norm_gains, query_gain, key_gain, slot_sequence, slot_offset, out_grad):
    seq_tokens = jnp.repeat(slot_sequence, STRETCH)
    pos_tokens = jnp.repeat(slot_offset, STRETCH) + jnp.tile(jnp.arange(STRETCH, dtype=jnp.int32), STRETCHES)
    order = jnp.argsort(seq_tokens * TOKEN_TOTAL + pos_tokens).astype(jnp.int32)
    inverse = jnp.argsort(order).astype(jnp.int32)
    seq_sorted = seq_tokens[order]
    pos_sorted = pos_tokens[order]
    cosines, sines = angles(pos_tokens, HEAD_WIDTH)
    heads_group = QUERY_HEADS // N_TENSOR
    sharing_count = QUERY_HEADS // KEYVALUE_HEADS

    def forward(states_f, query_w, keyvalue_w, output_w, gate_w, up_w, down_w, norm_w, query_g, key_g):
        hidden_state = states_f
        for layer_index in range(LAYER_COUNT):
            attn_in = low(normed(hidden_state, norm_w[layer_index, :, 0]))
            query_lin = low_back(matmul(attn_in, query_w[layer_index])).reshape(TOKEN_TOTAL, QUERY_HEADS, HEAD_WIDTH)
            queries = low(rotated(normed(query_lin, query_g[layer_index]), cosines, sines))
            keyvalue_linear = matmul(attn_in, keyvalue_w[layer_index])
            key_linear = keyvalue_linear[:, :KEYVALUE_HEADS * HEAD_WIDTH].reshape(TOKEN_TOTAL, KEYVALUE_HEADS, HEAD_WIDTH)
            value_linear = keyvalue_linear[:, KEYVALUE_HEADS * HEAD_WIDTH:].reshape(TOKEN_TOTAL, KEYVALUE_HEADS, HEAD_WIDTH)
            key_parts = []
            value_parts = []
            for group_index in range(N_TENSOR):
                group_keys = low(rotated(normed(low_back(key_linear), key_g[layer_index]), cosines, sines))
                group_values = low(low_back(value_linear))
                chosen = [(group_index * heads_group + head_index) // sharing_count for head_index in range(heads_group)]
                key_parts.append(group_keys[:, chosen])
                value_parts.append(group_values[:, chosen])
            all_keys = jnp.concatenate(key_parts, axis=1)
            all_values = jnp.concatenate(value_parts, axis=1)
            attended = attention(queries[order], all_keys[order], all_values[order], seq_sorted, pos_sorted)[inverse]
            attn_out = low(low_back(attended.reshape(TOKEN_TOTAL, QUERY_HEADS * HEAD_WIDTH)))
            hidden_state = hidden_state + low_back(matmul(attn_out, output_w[layer_index].T))
            ffn_in = low(normed(hidden_state, norm_w[layer_index, :, 1]))
            gate_pre = low_back(matmul(ffn_in, gate_w[layer_index]))
            up_pre = low_back(matmul(ffn_in, up_w[layer_index]))
            mixed = low(jax.nn.silu(gate_pre) * up_pre)
            hidden_state = hidden_state + low_back(matmul(mixed, down_w[layer_index].T))
        return hidden_state
    floats = [array.astype(jnp.float32) for array in (states, query_weight, keyvalue_matrix, output_weight, gate_weight, up_weight, down_weight, norm_gains, query_gain, key_gain)]
    output_state, pull_back = jax.vjp(forward, *floats)
    grads = pull_back(out_grad.astype(jnp.float32))
    return (output_state.astype(jnp.bfloat16), grads[0], grads[1], grads[2], grads[3], grads[4], grads[5], grads[6], grads[7], grads[8], grads[9])
```

```python
import functools

import jax
import jax.numpy as jnp
from jax import lax
from jax.experimental import pallas as pl
from jax.experimental.pallas import tpu as pltpu
from jax.sharding import PartitionSpec as P

QUERY_HEADS = 24
KEYVALUE_HEADS = 6
HEAD_WIDTH = 64
STRETCH = 128
EPSILON = 1e-06
PLANES = 4
PAIRS = 3
LOG2E = 1.4426950408889634
BF16 = jnp.bfloat16
F32 = jnp.float32


def product(left_side, right_side):
    return jnp.dot(left_side, right_side, preferred_element_type=F32)


def by_rows(left_side, right_side):
    return lax.dot_general(
        left_side, right_side, (((0,), (0,)), ((), ())), preferred_element_type=F32
    )


def by_cols(left_side, right_side):
    return lax.dot_general(
        left_side, right_side, (((1,), (1,)), ((), ())), preferred_element_type=F32
    )


def normed(vector, gain_vector):
    return (
        vector
        * lax.rsqrt(jnp.mean(vector * vector, axis=-1, keepdims=True) + EPSILON)
        * gain_vector
    )


def angles(positions, head_size):
    frequency = 10000.0 ** (-jnp.arange(head_size // 2, dtype=F32) * 2.0 / head_size)
    phase_angle = positions.astype(F32)[:, None] * frequency[None, :]
    return (jnp.cos(phase_angle)[:, None, :], jnp.sin(phase_angle)[:, None, :])


def rotated(vector, cosines, sines):
    half_width = vector.shape[-1] // 2
    front = vector[..., :half_width]
    behind = vector[..., half_width:]
    return jnp.concatenate(
        [front * cosines - behind * sines, behind * cosines + front * sines], axis=-1
    )


def visible_mask(shape, key_axis):
    keys = lax.broadcasted_iota(jnp.int32, shape, key_axis)
    queries = lax.rem(lax.broadcasted_iota(jnp.int32, shape, 1 - key_axis), STRETCH)
    return keys <= queries


def attend_kernel(count_ref, slots_ref, parity_ref, q_ref, kv_ref, out_ref, acc_ref):
    odd = parity_ref[0] == 1
    ones = jnp.ones((STRETCH, HEAD_WIDTH), BF16)

    def add_block(block, slot, last):
        tile = kv_ref[slot]
        keys = [tile[:, :64], tile[:, 64:128]]
        values = [
            jnp.concatenate([tile[:, 128:192], ones], axis=1),
            jnp.concatenate([tile[:, 192:256], ones], axis=1),
        ]
        middle_key = jnp.where(odd, keys[1], keys[0])
        middle_value = jnp.where(odd, values[1], values[0])
        for pair, key, value in (
            (0, keys[0], values[0]),
            (1, middle_key, middle_value),
            (2, keys[1], values[1]),
        ):
            scores = by_cols(q_ref[block, pair], key)
            weights = jnp.exp2(scores * (LOG2E * HEAD_WIDTH**-0.5))
            if last:
                weights = jnp.where(visible_mask(weights.shape, 1), weights, 0.0)
            acc_ref[pair] += product(weights.astype(BF16), value)

    def one_block(block, carry):
        acc_ref[...] = jnp.zeros_like(acc_ref)
        count = count_ref[block]

        def step(index, inner):
            add_block(block, slots_ref[block, index], False)
            return inner

        lax.fori_loop(0, count - 1, step, 0)
        add_block(block, slots_ref[block, count - 1], True)
        for pair in range(PAIRS):
            total = acc_ref[pair]
            denominator = total[:, HEAD_WIDTH:]
            out_ref[block, pair] = jnp.concatenate(
                [total[:, :HEAD_WIDTH] / denominator, jnp.log2(denominator)], axis=1
            )
        return carry

    lax.fori_loop(0, q_ref.shape[0], one_block, 0)


def attend(counts, slots, parity, queries, keyvalues):
    blocks = queries.shape[0]
    smem = pl.BlockSpec(memory_space=pltpu.SMEM)
    vmem = pl.BlockSpec(memory_space=pltpu.VMEM)
    return pl.pallas_call(
        attend_kernel,
        out_shape=jax.ShapeDtypeStruct((blocks, PAIRS, 2 * STRETCH, 128), F32),
        in_specs=[smem, smem, smem, vmem, vmem],
        out_specs=vmem,
        scratch_shapes=[pltpu.VMEM((PAIRS, 2 * STRETCH, 128), F32)],
        compiler_params=pltpu.CompilerParams(vmem_limit_bytes=40 << 20),
        cost_estimate=pl.CostEstimate(
            flops=4 * 20 * PAIRS * 256 * 128 * 64 * 4, bytes_accessed=8 << 20, transcendentals=0
        ),
        name="attend",
    )(counts, slots, parity, queries, keyvalues)


def attend_back_kernel(
    count_ref, slots_ref, parity_ref, q_ref, do_ref, log_ref, delta_ref, kv_ref, dq_ref, dkv_ref
):
    odd = parity_ref[0] == 1
    scale = HEAD_WIDTH**-0.5
    dq_ref[...] = jnp.zeros_like(dq_ref)
    dkv_ref[...] = jnp.zeros_like(dkv_ref)

    def add_block(block, slot, last):
        tile = kv_ref[slot]
        keys = [tile[:, :64], tile[:, 64:128]]
        values = [tile[:, 128:192], tile[:, 192:256]]
        middle_key = jnp.where(odd, keys[1], keys[0])
        middle_value = jnp.where(odd, values[1], values[0])
        d_keys, d_values = [], []
        for pair, key, value in (
            (0, keys[0], values[0]),
            (1, middle_key, middle_value),
            (2, keys[1], values[1]),
        ):
            query, d_out = q_ref[block, pair], do_ref[block, pair]
            scores = by_cols(key, query)
            weights = jnp.exp2(scores * (LOG2E * scale) - log_ref[block, pair])
            if last:
                weights = jnp.where(visible_mask(weights.shape, 0), weights, 0.0)
            d_weights = by_cols(value, d_out)
            d_scores = (weights * (d_weights - delta_ref[block, pair])).astype(BF16)
            d_values.append(product(weights.astype(BF16), d_out))
            d_keys.append(product(d_scores, query))
            dq_ref[block, pair] += by_rows(d_scores, key) * scale
        zero = jnp.zeros((STRETCH, HEAD_WIDTH), F32)
        parts = [
            (d_keys[0] + jnp.where(odd, zero, d_keys[1])) * scale,
            (d_keys[2] + jnp.where(odd, d_keys[1], zero)) * scale,
            d_values[0] + jnp.where(odd, zero, d_values[1]),
            d_values[2] + jnp.where(odd, d_values[1], zero),
        ]
        dkv_ref[slot] += jnp.concatenate(parts, axis=1)

    def one_block(block, carry):
        count = count_ref[block]

        def step(index, inner):
            add_block(block, slots_ref[block, index], False)
            return inner

        lax.fori_loop(0, count - 1, step, 0)
        add_block(block, slots_ref[block, count - 1], True)
        return carry

    lax.fori_loop(0, q_ref.shape[0], one_block, 0)


def attend_back(counts, slots, parity, queries, d_out, logs, delta, keyvalues):
    blocks = queries.shape[0]
    smem = pl.BlockSpec(memory_space=pltpu.SMEM)
    vmem = pl.BlockSpec(memory_space=pltpu.VMEM)
    return pl.pallas_call(
        attend_back_kernel,
        out_shape=(
            jax.ShapeDtypeStruct((blocks, PAIRS, 2 * STRETCH, HEAD_WIDTH), F32),
            jax.ShapeDtypeStruct(keyvalues.shape, F32),
        ),
        in_specs=[smem] * 3 + [vmem] * 5,
        out_specs=(vmem, vmem),
        compiler_params=pltpu.CompilerParams(vmem_limit_bytes=56 << 20),
        cost_estimate=pl.CostEstimate(
            flops=10 * 20 * PAIRS * 256 * 128 * 64 * 4, bytes_accessed=8 << 20, transcendentals=0
        ),
        name="attend_back",
    )(counts, slots, parity, queries, d_out, logs, delta, keyvalues)


def local(
    states,
    query_weight,
    keyvalue_matrix,
    output_weight,
    gate_weight,
    up_weight,
    down_weight,
    norm_gains,
    query_gain,
    key_gain,
    slot_sequence,
    slot_offset,
    out_grad,
):
    token_rows, width = states.shape
    dp_ranks = lax.axis_size("dp")
    tensor_ranks = lax.axis_size("tensor")
    lines = dp_ranks // PLANES
    rank, part = lax.axis_index("dp"), lax.axis_index("tensor")
    plane, line = rank // lines, rank % lines
    quarter = token_rows // tensor_ranks
    heads_here = QUERY_HEADS // tensor_ranks
    head_width = heads_here * HEAD_WIDTH
    sharing_count = QUERY_HEADS // KEYVALUE_HEADS
    blocks_here = token_rows // STRETCH
    slot_count = slot_sequence.shape[0]
    hidden = gate_weight.shape[2]
    slice_width = hidden // PLANES
    weight_rows = width // dp_ranks

    def send(value, kz=0, ky=0, kx=0, kc=0):
        move_rank, move_part = kz * lines + ky, kx * 2 + kc
        pairs = [
            (r * tensor_ranks + p, (r ^ move_rank) * tensor_ranks + (p ^ move_part))
            for r in range(dp_ranks)
            for p in range(tensor_ranks)
        ]
        return lax.ppermute(value, ("dp", "tensor"), pairs)

    def gather_planes(value):
        near = send(value, kz=1)
        far = send(value, kz=2)
        return [value, near, far, send(far, kz=1)]

    def gather_dp(value):
        whole = jnp.zeros((dp_ranks, *value.shape), value.dtype)
        for kz, piece in enumerate(gather_planes(value)):
            for ky in range(lines):
                got = send(piece, ky=ky) if ky else piece
                whole = lax.dynamic_update_index_in_dim(whole, got, rank ^ (kz * lines + ky), 0)
        return whole

    def rounded(value):
        return value.astype(BF16)

    def scatter_dp(whole):
        def piece(move):
            return lax.dynamic_index_in_dim(whole, rank ^ move, 0, keepdims=False)

        parts = []
        for kz in range(PLANES):
            total = piece(kz * lines).astype(F32)
            for ky in range(1, lines):
                total = total + send(rounded(piece(kz * lines + ky)), ky=ky).astype(F32)
            parts.append(total)
        return scatter_planes(parts)

    def scatter_planes(parts):
        near = parts[0] + send(rounded(parts[1]), kz=1).astype(F32)
        far = parts[2] + send(rounded(parts[3]), kz=1).astype(F32)
        return near + send(rounded(far), kz=2).astype(F32)

    def scatter_tensor(blocks):
        got = send(rounded(jnp.concatenate([blocks[1], blocks[3]], axis=0)), kc=1).astype(F32)
        rows = blocks[0].shape[0]
        here = blocks[0] + got[:rows]
        there = blocks[2] + got[rows:]
        return here + send(rounded(there), kx=1).astype(F32)

    def gather_tensor(block):
        both = jnp.concatenate([block, send(block, kx=1)], axis=0)
        return jnp.concatenate([both, send(both, kc=1)], axis=0)

    def in_order(blocks):
        whole = jnp.zeros_like(blocks)
        for index, move in enumerate((0, 2, 1, 3)):
            whole = lax.dynamic_update_slice_in_dim(
                whole,
                blocks[index * quarter : (index + 1) * quarter],
                (part ^ move) * quarter,
                0,
            )
        return whole

    def quarters(value):
        return [
            lax.dynamic_slice_in_dim(value, (part ^ move) * quarter, quarter, 0)
            for move in range(tensor_ranks)
        ]

    sequence_here = lax.dynamic_slice_in_dim(slot_sequence, rank * blocks_here, blocks_here)
    offset_here = lax.dynamic_slice_in_dim(slot_offset, rank * blocks_here, blocks_here)
    counts = offset_here // STRETCH + 1
    places = jnp.arange(slot_count, dtype=jnp.int32)
    same = (slot_sequence[None, None, :] == sequence_here[:, None, None]) & (
        slot_offset[None, None, :] == places[None, :, None] * STRETCH
    )
    slots = jnp.sum(jnp.where(same, places[None, None, :], 0), axis=2).astype(jnp.int32)
    parity = jnp.reshape(part % 2, (1,)).astype(jnp.int32)
    positions = (offset_here[:, None] + jnp.arange(STRETCH, dtype=jnp.int32)[None, :]).reshape(-1)
    cosines, sines = angles(positions, HEAD_WIDTH)

    first_key = (part * heads_here) // sharing_count * HEAD_WIDTH
    value_start = KEYVALUE_HEADS * HEAD_WIDTH
    kv_columns = [
        lax.dynamic_slice_in_dim(keyvalue_matrix[0], first_key, 2 * HEAD_WIDTH, 1),
        lax.dynamic_slice_in_dim(keyvalue_matrix[0], value_start + first_key, 2 * HEAD_WIDTH, 1),
    ]
    gains = gather_dp(norm_gains[0].T).transpose(1, 0, 2).reshape(2, width).astype(F32)
    w_attend = gather_dp(jnp.concatenate([query_weight[0], *kv_columns], axis=1)).reshape(width, -1)
    w_output = gather_dp(output_weight[0]).reshape(width, head_width)

    def sliced(weight):
        return weight[0].reshape(weight_rows, PLANES, slice_width).transpose(1, 0, 2)

    pad_first = -2 * slice_width % 128
    pad_second = -slice_width % 128
    packed = jnp.concatenate(
        [
            sliced(gate_weight),
            sliced(up_weight),
            jnp.zeros((PLANES, weight_rows, pad_first), BF16),
            sliced(down_weight),
            jnp.zeros((PLANES, weight_rows, pad_second), BF16),
        ],
        axis=2,
    )
    w_hidden = jnp.zeros((dp_ranks, weight_rows, packed.shape[2]), BF16)
    for kz in range(PLANES):
        piece = lax.dynamic_index_in_dim(packed, plane ^ kz, 0, keepdims=False)
        piece = send(piece, kz=kz) if kz else piece
        for ky in range(lines):
            got = send(piece, ky=ky) if ky else piece
            w_hidden = lax.dynamic_update_index_in_dim(w_hidden, got, rank ^ (kz * lines + ky), 0)
    w_hidden = w_hidden.reshape(width, -1)
    down_start = 2 * slice_width + pad_first
    w_gate_up = w_hidden[:, : 2 * slice_width]
    w_down = w_hidden[:, down_start : down_start + slice_width]

    def gather_group(block):
        return [gather_tensor(piece) for piece in gather_planes(block)]

    def quarter_of(value):
        return lax.dynamic_slice_in_dim(value, part * quarter, quarter, 0)

    query_g, key_g = query_gain[0], key_gain[0]
    attn_in = rounded(normed(states.astype(F32), gains[0]))
    lin = product(attn_in, w_attend)
    query_lin, keyvalue_lin = lin[:, :head_width], lin[:, head_width:]

    def query_side(linear, gain_vector):
        return rotated(
            normed(linear.reshape(token_rows, heads_here, HEAD_WIDTH), gain_vector), cosines, sines
        )

    def key_side(linear, gain_vector):
        keys = linear[:, : 2 * HEAD_WIDTH].reshape(token_rows, 2, HEAD_WIDTH)
        keys = rotated(normed(keys, gain_vector), cosines, sines)
        return jnp.concatenate(
            [keys.reshape(token_rows, 2 * HEAD_WIDTH), linear[:, 2 * HEAD_WIDTH :]], axis=1
        )

    def to_pairs(value):
        return (
            value.reshape(blocks_here, STRETCH, PAIRS, 2, -1)
            .transpose(0, 2, 3, 1, 4)
            .reshape(blocks_here, PAIRS, 2 * STRETCH, -1)
        )

    def from_pairs(value):
        return (
            value.reshape(blocks_here, PAIRS, 2, STRETCH, -1)
            .transpose(0, 3, 1, 2, 4)
            .reshape(token_rows, heads_here, -1)
        )

    queries = to_pairs(rounded(query_side(query_lin, query_g)))
    keyvalues = gather_dp(rounded(key_side(keyvalue_lin, key_g)))
    keyvalues = keyvalues.reshape(slot_count, STRETCH, 4 * HEAD_WIDTH)
    attended = attend(counts, slots, parity, queries, keyvalues)
    attn_out = rounded(from_pairs(attended[..., :HEAD_WIDTH]).reshape(token_rows, head_width))
    logs = attended[..., HEAD_WIDTH]

    branch = scatter_tensor(quarters(by_cols(attn_out, w_output)))
    states_quarter = quarter_of(states).astype(F32)
    middle = states_quarter + branch
    ffn_in = rounded(normed(middle, gains[1]))

    down_grads = gather_group(quarter_of(out_grad))
    ffn_ins = gather_group(ffn_in)
    mixed_chunks, d_chunks, back_parts, out_parts = [], [], [], []
    for down_grad, ffn_chunk in zip(down_grads, ffn_ins):
        gate_up = product(ffn_chunk, w_gate_up)
        gate_pre, up_pre = gate_up[:, :slice_width], gate_up[:, slice_width:]
        sigmoid_gate = jax.nn.sigmoid(gate_pre)
        mixed = rounded(gate_pre * sigmoid_gate * up_pre)
        d_mixed = product(down_grad, w_down)
        d_gate = d_mixed * up_pre * sigmoid_gate * (1.0 + gate_pre * (1.0 - sigmoid_gate))
        d_up = d_mixed * gate_pre * sigmoid_gate
        d_gate_up = jnp.concatenate([rounded(d_gate), rounded(d_up)], axis=1)
        mixed_chunks.append(mixed)
        d_chunks.append(d_gate_up)

        def reduced(value):
            blocks = value.reshape(4, quarter, width)
            return scatter_tensor([blocks[0], blocks[2], blocks[1], blocks[3]])

        back_parts.append(reduced(by_cols(d_gate_up, w_gate_up)))
        out_parts.append(reduced(by_cols(mixed, w_down)))
    d_ffn_in = scatter_planes(back_parts)

    def norm_back(vector, gain_vector, grad):
        inverse = lax.rsqrt(jnp.mean(vector * vector, axis=-1, keepdims=True) + EPSILON)
        unit = vector * inverse
        scaled = grad * gain_vector
        back = inverse * (scaled - unit * jnp.mean(scaled * unit, axis=-1, keepdims=True))
        return back, jnp.sum(grad * unit, axis=0)

    d_middle, d_gain_ffn = norm_back(middle, gains[1], d_ffn_in)
    grad_middle = quarter_of(out_grad).astype(F32) + d_middle
    output_grad = in_order(gather_tensor(rounded(grad_middle)))

    d_wout = by_rows(output_grad, attn_out)
    d_heads = rounded(product(output_grad, w_output)).reshape(token_rows, heads_here, HEAD_WIDTH)
    d_pairs = to_pairs(d_heads)
    delta = jnp.sum(d_pairs.astype(F32) * attended[..., :HEAD_WIDTH], axis=-1)
    d_query, d_keyvalue = attend_back(
        counts,
        slots,
        parity,
        queries,
        d_pairs,
        logs[:, :, None, :],
        delta[:, :, None, :],
        keyvalues,
    )
    d_keyvalue_here = scatter_dp(d_keyvalue.reshape(dp_ranks, token_rows, 4 * HEAD_WIDTH))
    _, query_pull = jax.vjp(query_side, query_lin, query_g)
    d_query_lin, d_querygain = query_pull(from_pairs(d_query))
    _, key_pull = jax.vjp(key_side, keyvalue_lin, key_g)
    d_keyvalue_lin, d_keygain = key_pull(d_keyvalue_here)
    d_lin = jnp.concatenate([rounded(d_query_lin), rounded(d_keyvalue_lin)], axis=1)
    d_attn_in = scatter_tensor(quarters(by_cols(d_lin, w_attend)))
    d_states, d_gain_attn = norm_back(states_quarter, gains[0], d_attn_in)
    states_grad = in_order(gather_tensor(rounded(grad_middle + d_states))).astype(F32)

    d_wattend = scatter_dp(by_rows(attn_in, d_lin).reshape(dp_ranks, weight_rows, -1))
    d_wout = scatter_dp(d_wout.reshape(dp_ranks, weight_rows, -1))
    ffn_all = jnp.concatenate(ffn_ins, axis=0)
    down_all = jnp.concatenate(down_grads, axis=0)
    grads_hidden = jnp.concatenate(
        [
            by_rows(ffn_all, jnp.concatenate(d_chunks, axis=0)),
            by_rows(down_all, jnp.concatenate(mixed_chunks, axis=0)),
        ],
        axis=1,
    ).reshape(dp_ranks, weight_rows, 3 * slice_width)
    collected = jnp.zeros((PLANES, weight_rows, 3 * slice_width), F32)
    for kz in range(PLANES):
        total = lax.dynamic_index_in_dim(grads_hidden, rank ^ (kz * lines), 0, keepdims=False)
        for ky in range(1, lines):
            piece = lax.dynamic_index_in_dim(
                grads_hidden, rank ^ (kz * lines + ky), 0, keepdims=False
            )
            total = total + send(rounded(piece), ky=ky).astype(F32)
        if kz:
            total = send(rounded(total), kz=kz).astype(F32)
        collected = lax.dynamic_update_index_in_dim(collected, total, plane ^ kz, 0)

    def unsliced(index):
        piece = collected[:, :, index * slice_width : (index + 1) * slice_width]
        return piece.transpose(1, 0, 2).reshape(1, weight_rows, hidden)

    kv_grad = d_wattend[:, head_width:]
    spread = jnp.zeros((weight_rows, 2 * value_start), F32)
    spread = lax.dynamic_update_slice_in_dim(spread, kv_grad[:, : 2 * HEAD_WIDTH], first_key, 1)
    spread = lax.dynamic_update_slice_in_dim(
        spread, kv_grad[:, 2 * HEAD_WIDTH :], value_start + first_key, 1
    )
    d_wkeyvalue = lax.psum(spread, "tensor")

    result_quarter = rounded(middle + scatter_planes(out_parts))
    result = in_order(gather_tensor(result_quarter))

    small = jnp.concatenate([d_gain_attn, d_gain_ffn, d_querygain, d_keygain])
    small = lax.psum(small, ("dp", "tensor"))
    d_gains = lax.dynamic_slice_in_dim(
        small[: 2 * width].reshape(2, width), rank * weight_rows, weight_rows, 1
    ).T
    return (
        result,
        states_grad,
        d_wattend[None, :, :head_width],
        d_wkeyvalue[None],
        d_wout[None],
        unsliced(0),
        unsliced(1),
        unsliced(2),
        d_gains[None],
        small[2 * width : 2 * width + HEAD_WIDTH][None],
        small[2 * width + HEAD_WIDTH :][None],
    )


def solution(mesh):
    return jax.shard_map(
        local,
        mesh=mesh,
        in_specs=(
            P("dp", None),
            P(None, "dp", "tensor"),
            P(None, "dp", None),
            P(None, "dp", "tensor"),
            P(None, "dp", "tensor"),
            P(None, "dp", "tensor"),
            P(None, "dp", "tensor"),
            P(None, "dp", None),
            P(),
            P(),
            P(),
            P(),
            P("dp", None),
        ),
        out_specs=(
            P("dp", None),
            P("dp", None),
            P(None, "dp", "tensor"),
            P(None, "dp", None),
            P(None, "dp", "tensor"),
            P(None, "dp", "tensor"),
            P(None, "dp", "tensor"),
            P(None, "dp", "tensor"),
            P(None, "dp", None),
            P(),
            P(),
        ),
        check_vma=False,
    )
```

```python
import functools

import jax
import jax.numpy as jnp
from jax import lax
from jax.experimental import pallas as pl
from jax.experimental.pallas import tpu as pltpu
from jax.sharding import PartitionSpec as P

QUERY_HEADS = 24
KEYVALUE_HEADS = 6
HEAD_WIDTH = 64
STRETCH = 128
EPSILON = 1e-06
PLANES = 4
PAIRS = 3
LOG2E = 1.4426950408889634
BF16 = jnp.bfloat16
F32 = jnp.float32


def product(left_side, right_side):
    return jnp.dot(left_side, right_side, preferred_element_type=F32)


def by_rows(left_side, right_side):
    return lax.dot_general(
        left_side, right_side, (((0,), (0,)), ((), ())), preferred_element_type=F32
    )


def by_cols(left_side, right_side):
    return lax.dot_general(
        left_side, right_side, (((1,), (1,)), ((), ())), preferred_element_type=F32
    )


def normed(vector, gain_vector):
    return (
        vector
        * lax.rsqrt(jnp.mean(vector * vector, axis=-1, keepdims=True) + EPSILON)
        * gain_vector
    )


def angles(positions, head_size):
    frequency = 10000.0 ** (-jnp.arange(head_size // 2, dtype=F32) * 2.0 / head_size)
    phase_angle = positions.astype(F32)[:, None] * frequency[None, :]
    return (jnp.cos(phase_angle)[:, None, :], jnp.sin(phase_angle)[:, None, :])


def rotated(vector, cosines, sines):
    half_width = vector.shape[-1] // 2
    front = vector[..., :half_width]
    behind = vector[..., half_width:]
    return jnp.concatenate(
        [front * cosines - behind * sines, behind * cosines + front * sines], axis=-1
    )


def visible_mask(shape, key_axis):
    keys = lax.broadcasted_iota(jnp.int32, shape, key_axis)
    queries = lax.rem(lax.broadcasted_iota(jnp.int32, shape, 1 - key_axis), STRETCH)
    return keys <= queries


def attend_kernel(count_ref, slots_ref, parity_ref, q_ref, kv_ref, out_ref, acc_ref):
    odd = parity_ref[0] == 1
    ones = jnp.ones((STRETCH, HEAD_WIDTH), BF16)

    def add_block(block, slot, last):
        tile = kv_ref[slot]
        keys = [tile[:, :64], tile[:, 64:128]]
        values = [
            jnp.concatenate([tile[:, 128:192], ones], axis=1),
            jnp.concatenate([tile[:, 192:256], ones], axis=1),
        ]
        middle_key = jnp.where(odd, keys[1], keys[0])
        middle_value = jnp.where(odd, values[1], values[0])
        for pair, key, value in (
            (0, keys[0], values[0]),
            (1, middle_key, middle_value),
            (2, keys[1], values[1]),
        ):
            scores = by_cols(q_ref[block, pair], key)
            weights = jnp.exp2(scores * (LOG2E * HEAD_WIDTH**-0.5))
            if last:
                weights = jnp.where(visible_mask(weights.shape, 1), weights, 0.0)
            acc_ref[pair] += product(weights.astype(BF16), value)

    def one_block(block, carry):
        acc_ref[...] = jnp.zeros_like(acc_ref)
        count = count_ref[block]

        def step(index, inner):
            add_block(block, slots_ref[block, index], False)
            return inner

        lax.fori_loop(0, count - 1, step, 0)
        add_block(block, slots_ref[block, count - 1], True)
        for pair in range(PAIRS):
            total = acc_ref[pair]
            denominator = total[:, HEAD_WIDTH:]
            out_ref[block, pair] = jnp.concatenate(
                [total[:, :HEAD_WIDTH] / denominator, jnp.log2(denominator)], axis=1
            )
        return carry

    lax.fori_loop(0, q_ref.shape[0], one_block, 0)


def attend(counts, slots, parity, queries, keyvalues):
    blocks = queries.shape[0]
    smem = pl.BlockSpec(memory_space=pltpu.SMEM)
    vmem = pl.BlockSpec(memory_space=pltpu.VMEM)
    return pl.pallas_call(
        attend_kernel,
        out_shape=jax.ShapeDtypeStruct((blocks, PAIRS, 2 * STRETCH, 128), F32),
        in_specs=[smem, smem, smem, vmem, vmem],
        out_specs=vmem,
        scratch_shapes=[pltpu.VMEM((PAIRS, 2 * STRETCH, 128), F32)],
        compiler_params=pltpu.CompilerParams(vmem_limit_bytes=40 << 20),
        cost_estimate=pl.CostEstimate(
            flops=4 * 20 * PAIRS * 256 * 128 * 64 * 4, bytes_accessed=8 << 20, transcendentals=0
        ),
        name="attend",
    )(counts, slots, parity, queries, keyvalues)


def attend_back_kernel(
    count_ref, slots_ref, parity_ref, q_ref, do_ref, log_ref, delta_ref, kv_ref, dq_ref, dkv_ref
):
    odd = parity_ref[0] == 1
    scale = HEAD_WIDTH**-0.5
    dq_ref[...] = jnp.zeros_like(dq_ref)
    dkv_ref[...] = jnp.zeros_like(dkv_ref)

    def add_block(block, slot, last):
        tile = kv_ref[slot]
        keys = [tile[:, :64], tile[:, 64:128]]
        values = [tile[:, 128:192], tile[:, 192:256]]
        middle_key = jnp.where(odd, keys[1], keys[0])
        middle_value = jnp.where(odd, values[1], values[0])
        d_keys, d_values = [], []
        for pair, key, value in (
            (0, keys[0], values[0]),
            (1, middle_key, middle_value),
            (2, keys[1], values[1]),
        ):
            query, d_out = q_ref[block, pair], do_ref[block, pair]
            scores = by_cols(key, query)
            weights = jnp.exp2(scores * (LOG2E * scale) - log_ref[block, pair])
            if last:
                weights = jnp.where(visible_mask(weights.shape, 0), weights, 0.0)
            d_weights = by_cols(value, d_out)
            d_scores = (weights * (d_weights - delta_ref[block, pair])).astype(BF16)
            d_values.append(product(weights.astype(BF16), d_out))
            d_keys.append(product(d_scores, query))
            dq_ref[block, pair] += by_rows(d_scores, key) * scale
        zero = jnp.zeros((STRETCH, HEAD_WIDTH), F32)
        parts = [
            (d_keys[0] + jnp.where(odd, zero, d_keys[1])) * scale,
            (d_keys[2] + jnp.where(odd, d_keys[1], zero)) * scale,
            d_values[0] + jnp.where(odd, zero, d_values[1]),
            d_values[2] + jnp.where(odd, d_values[1], zero),
        ]
        dkv_ref[slot] += jnp.concatenate(parts, axis=1)

    def one_block(block, carry):
        count = count_ref[block]

        def step(index, inner):
            add_block(block, slots_ref[block, index], False)
            return inner

        lax.fori_loop(0, count - 1, step, 0)
        add_block(block, slots_ref[block, count - 1], True)
        return carry

    lax.fori_loop(0, q_ref.shape[0], one_block, 0)


def attend_back(counts, slots, parity, queries, d_out, logs, delta, keyvalues):
    blocks = queries.shape[0]
    smem = pl.BlockSpec(memory_space=pltpu.SMEM)
    vmem = pl.BlockSpec(memory_space=pltpu.VMEM)
    return pl.pallas_call(
        attend_back_kernel,
        out_shape=(
            jax.ShapeDtypeStruct((blocks, PAIRS, 2 * STRETCH, HEAD_WIDTH), F32),
            jax.ShapeDtypeStruct(keyvalues.shape, F32),
        ),
        in_specs=[smem] * 3 + [vmem] * 5,
        out_specs=(vmem, vmem),
        compiler_params=pltpu.CompilerParams(vmem_limit_bytes=56 << 20),
        cost_estimate=pl.CostEstimate(
            flops=10 * 20 * PAIRS * 256 * 128 * 64 * 4, bytes_accessed=8 << 20, transcendentals=0
        ),
        name="attend_back",
    )(counts, slots, parity, queries, d_out, logs, delta, keyvalues)


class Place:
    def __init__(self, lines):
        rank, part = lax.axis_index("dp"), lax.axis_index("tensor")
        self.lines = lines
        self.z, self.y = rank // lines, lax.rem(rank, lines)
        self.x, self.c = part // 2, lax.rem(part, 2)
        self.quarter = self.c * 2 + self.x

    def plane(self, move):
        if move == 0:
            return self.z
        if move == 1:
            return self.z + 1 - 2 * lax.rem(self.z, 2)
        if move == 2:
            return self.z + 2 - 4 * (self.z // 2)
        return 3 - self.z

    def to(self, kz=0, ky=0, kx=0, kc=0):
        y = 1 - self.y if ky else self.y
        x = 1 - self.x if kx else self.x
        c = 1 - self.c if kc else self.c
        return (self.plane(kz) * self.lines + y, x * 2 + c)


class Links:
    def __init__(self, place, send_sems, recv_sems):
        self.place, self.send_sems, self.recv_sems = place, send_sems, recv_sems
        self.started = []

    def greet(self, moves):
        barrier = pltpu.get_barrier_semaphore()
        for move in moves:
            pl.semaphore_signal(
                barrier, inc=1, device_id=self.place.to(**move), device_id_type=pl.DeviceIdType.MESH
            )
        pl.semaphore_wait(barrier, len(moves))

    def send(self, source, target, **move):
        number = len(self.started)
        copy = pltpu.make_async_remote_copy(
            src_ref=source,
            dst_ref=target,
            send_sem=self.send_sems.at[number],
            recv_sem=self.recv_sems.at[number],
            device_id=self.place.to(**move),
            device_id_type=pl.DeviceIdType.MESH,
        )
        copy.start()
        self.started.append(copy)
        return copy

    def finish(self):
        for copy in self.started:
            copy.wait_send()


def rows_at(index, size):
    return pl.ds(pl.multiple_of(index * size, size), size)


MIDDLE_COPIES = 50


def middle_kernel(
    lines,
    slice_width,
    attn_ref,
    states_ref,
    grad_ref,
    gain_ref,
    w_output_any,
    w_hidden_any,
    down_any,
    middle_ref,
    back_ref,
    gain_out_ref,
    d_heads_ref,
    output_grad_ref,
    mixed_ref,
    collected_ref,
    w_output_ref,
    w_hidden_ref,
    down_ref,
    ffn_ref,
    d_hidden_ref,
    partial_ref,
    core_out,
    core_in,
    x_out,
    x_in,
    sums_ref,
    z_out,
    z_in,
    y_out,
    y_in,
    blocks_ref,
    g_out,
    local_sems,
    send_sems,
    recv_sems,
):
    here = Place(lines)
    links = Links(here, send_sems, recv_sems)
    quarter, width = middle_ref.shape
    half = 2 * quarter
    token_rows = 4 * quarter
    hidden = slice_width

    loads = [
        pltpu.make_async_copy(w_output_any, w_output_ref, local_sems.at[0]),
        pltpu.make_async_copy(w_hidden_any, w_hidden_ref, local_sems.at[1]),
        pltpu.make_async_copy(down_any, down_ref, local_sems.at[2]),
    ]
    for load in loads:
        load.start()
    links.greet([dict(kc=1), dict(kx=1), dict(ky=1), dict(kz=1), dict(kz=2), dict(kz=3)])
    mine = rows_at(here.quarter, quarter)
    my_half, other_half = rows_at(here.c, half), rows_at(1 - here.c, half)

    loads[0].wait()
    cut = 4
    piece = width // cut
    core_copies = []
    for part in range(cut):
        columns = slice(part * piece, (part + 1) * piece)
        weight = w_output_ref[columns, :]
        core_out[4, :, columns] = by_cols(attn_ref[other_half, :], weight).astype(BF16)
        core_copies.append(
            links.send(core_out.at[4, :, columns], core_in.at[4, :, columns], kc=1)
        )
        partial_ref[0, :half, columns] = by_cols(attn_ref[my_half, :], weight)
    x_copies = []
    x_mine, x_other = rows_at(here.x, quarter), rows_at(1 - here.x, quarter)
    for part in range(cut):
        columns = slice(part * piece, (part + 1) * piece)
        core_copies[part].wait_recv()
        x_out[4, :, columns] = (
            partial_ref[0, x_other, columns] + core_in[4, x_other, columns].astype(F32)
        ).astype(BF16)
        x_copies.append(links.send(x_out.at[4, :, columns], x_in.at[4, :, columns], kx=1))
        middle_ref[:, columns] = (
            states_ref[mine, columns].astype(F32)
            + partial_ref[0, x_mine, columns]
            + core_in[4, x_mine, columns].astype(F32)
        )
    for part in range(cut):
        columns = slice(part * piece, (part + 1) * piece)
        x_copies[part].wait_recv()
        middle_ref[:, columns] += x_in[4, :, columns].astype(F32)
    middle = middle_ref[...]
    inverse = lax.rsqrt(jnp.mean(middle * middle, axis=-1, keepdims=True) + EPSILON)
    ffn_ref[here.z, mine, :] = (middle * inverse * gain_ref[...]).astype(BF16)

    def block_of(move):
        return ffn_ref.at[here.plane(move), mine]

    far = links.send(block_of(0), block_of(0), kz=2)
    near = links.send(block_of(0), block_of(0), kz=1)
    across = {0: links.send(block_of(0), block_of(0), kx=1)}
    near.wait_recv()
    across[1] = links.send(block_of(1), block_of(1), kx=1)
    far.wait_recv()
    corner = links.send(block_of(2), block_of(2), kz=1)
    across[2] = links.send(block_of(2), block_of(2), kx=1)
    cores = {}

    def spread(move):
        across[move].wait_recv()
        both = ffn_ref.at[here.plane(move), my_half]
        cores[move] = links.send(both, both, kc=1)

    spread(0)
    loads[1].wait()
    loads[2].wait()
    core_copies, x_copies = [], []

    def add_cores(move):
        core_copies[move].wait_recv()
        total_rows = rows_at(here.c * 2 + 1 - here.x, quarter)
        x_out[move] = (
            partial_ref[move % 2, total_rows, :] + core_in[move, x_other, :].astype(F32)
        ).astype(BF16)
        x_copies.append(links.send(x_out.at[move], x_in.at[move], kx=1))
        sums_ref[move] = partial_ref[move % 2, mine, :] + core_in[move, x_mine, :].astype(F32)

    def add_x(move):
        x_copies[move].wait_recv()
        sums_ref[move] += x_in[move].astype(F32)

    order = (0, 1, 2, 3)
    for index, move in enumerate(order):
        if move < 3:
            if move == 2:
                corner.wait_recv()
                across[3] = links.send(block_of(3), block_of(3), kx=1)
        cores[move].wait_recv()
        plane = here.plane(move)
        chunk = ffn_ref[plane]
        gate_pre = by_cols(w_hidden_ref[:hidden, :], chunk)
        up_pre = by_cols(w_hidden_ref[hidden : 2 * hidden, :], chunk)
        sigmoid_gate = 1.0 / (1.0 + jnp.exp(-gate_pre))
        silu = gate_pre * sigmoid_gate
        columns = pl.ds(pl.multiple_of(plane * token_rows, token_rows), token_rows)
        mixed_ref[:, columns] = (silu * up_pre).astype(BF16)
        d_mixed = by_cols(w_hidden_ref[2 * hidden :, :], down_ref[plane])
        d_hidden_ref[:hidden, columns] = (
            d_mixed * up_pre * sigmoid_gate * (1.0 + gate_pre * (1.0 - sigmoid_gate))
        ).astype(BF16)
        d_hidden_ref[hidden:, columns] = (d_mixed * silu).astype(BF16)
        partial_ref[move % 2] = by_rows(d_hidden_ref[:, columns], w_hidden_ref[: 2 * hidden, :])
        core_out[move] = partial_ref[move % 2, other_half, :].astype(BF16)
        core_copies.append(links.send(core_out.at[move], core_in.at[move], kc=1))
        if index > 0:
            add_cores(order[index - 1])
        if move + 1 < 4:
            spread(move + 1)
    add_cores(3)

    weight_rows = width // (4 * lines)

    def gradient(move, line):
        rank = here.plane(move) * lines + line
        columns = pl.ds(pl.multiple_of(rank * weight_rows, weight_rows), weight_rows)
        first = jnp.zeros((2 * hidden, weight_rows), F32)
        second = jnp.zeros((hidden, weight_rows), F32)
        for plane in range(4):
            tokens = slice(plane * token_rows, (plane + 1) * token_rows)
            first += product(d_hidden_ref[:, tokens], ffn_ref[plane, :, columns])
            second += product(mixed_ref[:, tokens], down_ref[plane, :, columns])
        return first, second

    y_copies = {}
    for move in (3, 2, 1, 0):
        first, second = gradient(move, 1 - here.y)
        y_out[move, : 2 * hidden] = first.astype(BF16)
        y_out[move, 2 * hidden :] = second.astype(BF16)
        y_copies[move] = links.send(y_out.at[move], y_in.at[move], ky=1)

    add_x(0)
    add_x(1)
    z_out[0] = sums_ref[1].astype(BF16)
    z_copies = [links.send(z_out.at[0], z_in.at[0], kz=1)]
    add_x(2)
    add_x(3)
    z_out[1] = sums_ref[3].astype(BF16)
    z_copies.append(links.send(z_out.at[1], z_in.at[1], kz=1))
    first, second = gradient(3, here.y)
    blocks_ref[0, : 2 * hidden] = first
    blocks_ref[0, 2 * hidden :] = second
    z_copies[1].wait_recv()
    z_out[2] = (sums_ref[2] + z_in[1].astype(F32)).astype(BF16)
    z_copies.append(links.send(z_out.at[2], z_in.at[2], kz=2))
    for slot, move in enumerate((2, 1, 0)):
        first, second = gradient(move, here.y)
        blocks_ref[slot + 1, : 2 * hidden] = first
        blocks_ref[slot + 1, 2 * hidden :] = second
    z_copies[0].wait_recv()
    z_copies[2].wait_recv()
    d_normed = sums_ref[0] + z_in[0].astype(F32) + z_in[2].astype(F32)
    middle = middle_ref[...]
    inverse = lax.rsqrt(jnp.mean(middle * middle, axis=-1, keepdims=True) + EPSILON)
    unit = middle * inverse
    gain_out_ref[...] = jnp.sum(d_normed * unit, axis=0, keepdims=True)
    scaled = d_normed * gain_ref[...]
    back = inverse * (scaled - unit * jnp.mean(scaled * unit, axis=-1, keepdims=True))
    grad_middle = grad_ref[mine, :].astype(F32) + back
    back_ref[...] = grad_middle
    output_grad_ref[mine, :] = grad_middle.astype(BF16)
    block = output_grad_ref.at[mine]
    links.send(block, block, kx=1).wait_recv()
    both = output_grad_ref.at[my_half]
    core = links.send(both, both, kc=1)

    g_copies = []
    for slot, move in enumerate((3, 2, 1, 0)):
        y_copies[move].wait_recv()
        total = blocks_ref[slot] + y_in[move].astype(F32)
        if move:
            g_out[slot] = total.astype(BF16)
            g_copies.append(links.send(g_out.at[slot], collected_ref.at[here.z], kz=move))
        else:
            collected_ref[here.z] = total.astype(BF16)
    core.wait_recv()
    d_heads_ref[...] = product(output_grad_ref[...], w_output_ref[...]).astype(BF16)
    for copy in g_copies:
        copy.wait_recv()
    links.finish()


def middle(lines, slice_width, attn_out, states, out_grad, gain, w_output, w_hidden, down_grads):
    token_rows, width = states.shape
    quarter = token_rows // 4
    half = 2 * quarter
    hidden = slice_width
    weight_rows = width // (4 * lines)
    vmem = pl.BlockSpec(memory_space=pltpu.VMEM)
    hbm = pl.BlockSpec(memory_space=pl.ANY)
    shape = jax.ShapeDtypeStruct
    return pl.pallas_call(
        functools.partial(middle_kernel, lines, slice_width),
        out_shape=(
            shape((quarter, width), F32),
            shape((quarter, width), F32),
            shape((1, width), F32),
            shape(attn_out.shape, BF16),
            shape((token_rows, width), BF16),
            shape((hidden, 4 * token_rows), BF16),
            shape((4, 3 * hidden, weight_rows), BF16),
        ),
        in_specs=[vmem] * 4 + [hbm] * 3,
        out_specs=(vmem,) * 7,
        scratch_shapes=[
            pltpu.VMEM(w_output.shape, BF16),
            pltpu.VMEM(w_hidden.shape, BF16),
            pltpu.VMEM(down_grads.shape, BF16),
            pltpu.VMEM((4, token_rows, width), BF16),
            pltpu.VMEM((2 * hidden, 4 * token_rows), BF16),
            pltpu.VMEM((2, token_rows, width), F32),
            pltpu.VMEM((5, half, width), BF16),
            pltpu.VMEM((5, half, width), BF16),
            pltpu.VMEM((5, quarter, width), BF16),
            pltpu.VMEM((5, quarter, width), BF16),
            pltpu.VMEM((4, quarter, width), F32),
            pltpu.VMEM((3, quarter, width), BF16),
            pltpu.VMEM((3, quarter, width), BF16),
            pltpu.VMEM((4, 3 * hidden, weight_rows), BF16),
            pltpu.VMEM((4, 3 * hidden, weight_rows), BF16),
            pltpu.VMEM((4, 3 * hidden, weight_rows), F32),
            pltpu.VMEM((3, 3 * hidden, weight_rows), BF16),
            pltpu.SemaphoreType.DMA((3,)),
            pltpu.SemaphoreType.DMA((MIDDLE_COPIES,)),
            pltpu.SemaphoreType.DMA((MIDDLE_COPIES,)),
        ],
        compiler_params=pltpu.CompilerParams(
            collective_id=0, has_side_effects=True, vmem_limit_bytes=62 << 20
        ),
        name="middle",
    )(attn_out, states, out_grad, gain, w_output, w_hidden, down_grads)


def local(
    states,
    query_weight,
    keyvalue_matrix,
    output_weight,
    gate_weight,
    up_weight,
    down_weight,
    norm_gains,
    query_gain,
    key_gain,
    slot_sequence,
    slot_offset,
    out_grad,
):
    token_rows, width = states.shape
    dp_ranks = lax.axis_size("dp")
    tensor_ranks = lax.axis_size("tensor")
    lines = dp_ranks // PLANES
    rank, part = lax.axis_index("dp"), lax.axis_index("tensor")
    plane, line = rank // lines, rank % lines
    quarter = token_rows // tensor_ranks
    heads_here = QUERY_HEADS // tensor_ranks
    head_width = heads_here * HEAD_WIDTH
    sharing_count = QUERY_HEADS // KEYVALUE_HEADS
    blocks_here = token_rows // STRETCH
    slot_count = slot_sequence.shape[0]
    hidden = gate_weight.shape[2]
    slice_width = hidden // PLANES
    weight_rows = width // dp_ranks
    kernels = lines == 2 and weight_rows % 128 == 0 and tensor_ranks == 4

    def send(value, kz=0, ky=0, kx=0, kc=0):
        move_rank, move_part = kz * lines + ky, kx * 2 + kc
        pairs = [
            (r * tensor_ranks + p, (r ^ move_rank) * tensor_ranks + (p ^ move_part))
            for r in range(dp_ranks)
            for p in range(tensor_ranks)
        ]
        return lax.ppermute(value, ("dp", "tensor"), pairs)

    def gather_planes(value):
        near = send(value, kz=1)
        far = send(value, kz=2)
        return [value, near, far, send(far, kz=1)]

    def gather_dp(value):
        whole = jnp.zeros((dp_ranks, *value.shape), value.dtype)
        for kz, piece in enumerate(gather_planes(value)):
            for ky in range(lines):
                got = send(piece, ky=ky) if ky else piece
                whole = lax.dynamic_update_index_in_dim(whole, got, rank ^ (kz * lines + ky), 0)
        return whole

    def rounded(value):
        return value.astype(BF16)

    def scatter_dp(whole):
        def piece(move):
            return lax.dynamic_index_in_dim(whole, rank ^ move, 0, keepdims=False)

        parts = []
        for kz in range(PLANES):
            total = piece(kz * lines).astype(F32)
            for ky in range(1, lines):
                total = total + send(rounded(piece(kz * lines + ky)), ky=ky).astype(F32)
            parts.append(total)
        return scatter_planes(parts)

    def scatter_planes(parts):
        near = parts[0] + send(rounded(parts[1]), kz=1).astype(F32)
        far = parts[2] + send(rounded(parts[3]), kz=1).astype(F32)
        return near + send(rounded(far), kz=2).astype(F32)

    def scatter_tensor(blocks):
        got = send(rounded(jnp.concatenate([blocks[1], blocks[3]], axis=0)), kc=1).astype(F32)
        rows = blocks[0].shape[0]
        here = blocks[0] + got[:rows]
        there = blocks[2] + got[rows:]
        return here + send(rounded(there), kx=1).astype(F32)

    def gather_tensor(block):
        both = jnp.concatenate([block, send(block, kx=1)], axis=0)
        return jnp.concatenate([both, send(both, kc=1)], axis=0)

    def first_row(move):
        other = part ^ move
        return (other % 2 * 2 + other // 2) * quarter

    def in_order(blocks):
        whole = jnp.zeros_like(blocks)
        for index, move in enumerate((0, 2, 1, 3)):
            whole = lax.dynamic_update_slice_in_dim(
                whole, blocks[index * quarter : (index + 1) * quarter], first_row(move), 0
            )
        return whole

    def quarters(value):
        return [
            lax.dynamic_slice_in_dim(value, first_row(move), quarter, 0)
            for move in range(tensor_ranks)
        ]

    sequence_here = lax.dynamic_slice_in_dim(slot_sequence, rank * blocks_here, blocks_here)
    offset_here = lax.dynamic_slice_in_dim(slot_offset, rank * blocks_here, blocks_here)
    counts = offset_here // STRETCH + 1
    places = jnp.arange(slot_count, dtype=jnp.int32)
    same = (slot_sequence[None, None, :] == sequence_here[:, None, None]) & (
        slot_offset[None, None, :] == places[None, :, None] * STRETCH
    )
    slots = jnp.sum(jnp.where(same, places[None, None, :], 0), axis=2).astype(jnp.int32)
    parity = jnp.reshape(part % 2, (1,)).astype(jnp.int32)
    positions = (offset_here[:, None] + jnp.arange(STRETCH, dtype=jnp.int32)[None, :]).reshape(-1)
    cosines, sines = angles(positions, HEAD_WIDTH)

    first_key = (part * heads_here) // sharing_count * HEAD_WIDTH
    value_start = KEYVALUE_HEADS * HEAD_WIDTH
    kv_columns = [
        lax.dynamic_slice_in_dim(keyvalue_matrix[0], first_key, 2 * HEAD_WIDTH, 1),
        lax.dynamic_slice_in_dim(keyvalue_matrix[0], value_start + first_key, 2 * HEAD_WIDTH, 1),
    ]
    gains = gather_dp(norm_gains[0].T).transpose(1, 0, 2).reshape(2, width).astype(F32)
    w_attend = gather_dp(jnp.concatenate([query_weight[0], *kv_columns], axis=1)).reshape(width, -1)
    w_output = gather_dp(output_weight[0]).reshape(width, head_width)

    def turned(weight):
        pieces = weight[0].reshape(weight_rows, PLANES, slice_width)
        return pieces.transpose(1, 2, 0)

    def sliced(weight):
        return weight[0].reshape(weight_rows, PLANES, slice_width).transpose(1, 0, 2)

    pad_first = -2 * slice_width % 128
    pad_second = -slice_width % 128
    if kernels:
        packed = jnp.concatenate(
            [turned(gate_weight), turned(up_weight), turned(down_weight)], axis=1
        )
    else:
        packed = jnp.concatenate(
            [
                sliced(gate_weight),
                sliced(up_weight),
                jnp.zeros((PLANES, weight_rows, pad_first), BF16),
                sliced(down_weight),
                jnp.zeros((PLANES, weight_rows, pad_second), BF16),
            ],
            axis=2,
        )
    w_hidden = jnp.zeros((dp_ranks, *packed.shape[1:]), BF16)
    for kz in range(PLANES):
        piece = lax.dynamic_index_in_dim(packed, plane ^ kz, 0, keepdims=False)
        piece = send(piece, kz=kz) if kz else piece
        for ky in range(lines):
            got = send(piece, ky=ky) if ky else piece
            w_hidden = lax.dynamic_update_index_in_dim(w_hidden, got, rank ^ (kz * lines + ky), 0)
    if kernels:
        w_hidden = w_hidden.transpose(1, 0, 2).reshape(3 * slice_width, width)
    else:
        w_hidden = w_hidden.reshape(width, -1)
        down_start = 2 * slice_width + pad_first
        w_gate_up = w_hidden[:, : 2 * slice_width]
        w_down = w_hidden[:, down_start : down_start + slice_width]

    def gather_group(block):
        return [gather_tensor(piece) for piece in gather_planes(block)]

    def quarter_of(value):
        return lax.dynamic_slice_in_dim(value, first_row(0), quarter, 0)

    query_g, key_g = query_gain[0], key_gain[0]
    attn_in = rounded(normed(states.astype(F32), gains[0]))
    lin = product(attn_in, w_attend)
    query_lin, keyvalue_lin = lin[:, :head_width], lin[:, head_width:]

    def query_side(linear, gain_vector):
        return rotated(
            normed(linear.reshape(token_rows, heads_here, HEAD_WIDTH), gain_vector), cosines, sines
        )

    def key_side(linear, gain_vector):
        keys = linear[:, : 2 * HEAD_WIDTH].reshape(token_rows, 2, HEAD_WIDTH)
        keys = rotated(normed(keys, gain_vector), cosines, sines)
        return jnp.concatenate(
            [keys.reshape(token_rows, 2 * HEAD_WIDTH), linear[:, 2 * HEAD_WIDTH :]], axis=1
        )

    def to_pairs(value):
        return (
            value.reshape(blocks_here, STRETCH, PAIRS, 2, -1)
            .transpose(0, 2, 3, 1, 4)
            .reshape(blocks_here, PAIRS, 2 * STRETCH, -1)
        )

    def from_pairs(value):
        return (
            value.reshape(blocks_here, PAIRS, 2, STRETCH, -1)
            .transpose(0, 3, 1, 2, 4)
            .reshape(token_rows, heads_here, -1)
        )

    queries = to_pairs(rounded(query_side(query_lin, query_g)))
    keyvalues = gather_dp(rounded(key_side(keyvalue_lin, key_g)))
    keyvalues = keyvalues.reshape(slot_count, STRETCH, 4 * HEAD_WIDTH)
    attended = attend(counts, slots, parity, queries, keyvalues)
    attn_out = rounded(from_pairs(attended[..., :HEAD_WIDTH]).reshape(token_rows, head_width))
    logs = attended[..., HEAD_WIDTH]

    def norm_back(vector, gain_vector, grad):
        inverse = lax.rsqrt(jnp.mean(vector * vector, axis=-1, keepdims=True) + EPSILON)
        unit = vector * inverse
        scaled = grad * gain_vector
        back = inverse * (scaled - unit * jnp.mean(scaled * unit, axis=-1, keepdims=True))
        return back, jnp.sum(grad * unit, axis=0)


    def planes_in_order(chunks):
        whole = jnp.zeros((PLANES, *chunks[0].shape), chunks[0].dtype)
        for kz, chunk in enumerate(chunks):
            whole = lax.dynamic_update_index_in_dim(whole, chunk, plane ^ kz, 0)
        return whole

    states_quarter = quarter_of(states).astype(F32)
    down_grads = gather_group(quarter_of(out_grad))
    if kernels:
        down_all = planes_in_order([in_order(chunk) for chunk in down_grads])
        middle_rows, grad_middle, d_gain_ffn, d_heads, output_grad, mixed, collected = middle(
            lines, slice_width, attn_out, states, out_grad, gains[1:], w_output, w_hidden, down_all
        )
        d_gain_ffn = d_gain_ffn[0]
        d_wout = by_rows(output_grad, attn_out)
        out_parts = []
        for kz in range(PLANES):
            chunk = lax.dynamic_slice_in_dim(
                mixed, (plane ^ kz) * token_rows, token_rows, 1
            )
            out_parts.append(scatter_tensor(quarters(by_rows(chunk, w_hidden[2 * slice_width :]))))
    else:
        branch = scatter_tensor(quarters(by_cols(attn_out, w_output)))
        middle_rows = states_quarter + branch
        ffn_in = rounded(normed(middle_rows, gains[1]))

        ffn_ins = gather_group(ffn_in)
        mixed_chunks, d_chunks, back_parts, out_parts = [], [], [], []
        for down_grad, ffn_chunk in zip(down_grads, ffn_ins):
            gate_up = product(ffn_chunk, w_gate_up)
            gate_pre, up_pre = gate_up[:, :slice_width], gate_up[:, slice_width:]
            sigmoid_gate = jax.nn.sigmoid(gate_pre)
            mixed = rounded(gate_pre * sigmoid_gate * up_pre)
            d_mixed = product(down_grad, w_down)
            d_gate = d_mixed * up_pre * sigmoid_gate * (1.0 + gate_pre * (1.0 - sigmoid_gate))
            d_up = d_mixed * gate_pre * sigmoid_gate
            d_gate_up = jnp.concatenate([rounded(d_gate), rounded(d_up)], axis=1)
            mixed_chunks.append(mixed)
            d_chunks.append(d_gate_up)

            def reduced(value):
                blocks = value.reshape(4, quarter, width)
                return scatter_tensor([blocks[0], blocks[2], blocks[1], blocks[3]])

            back_parts.append(reduced(by_cols(d_gate_up, w_gate_up)))
            out_parts.append(reduced(by_cols(mixed, w_down)))
        d_ffn_in = scatter_planes(back_parts)

        d_middle, d_gain_ffn = norm_back(middle_rows, gains[1], d_ffn_in)
        grad_middle = quarter_of(out_grad).astype(F32) + d_middle
        output_grad = in_order(gather_tensor(rounded(grad_middle)))
        d_wout = by_rows(output_grad, attn_out)
        d_heads = rounded(product(output_grad, w_output))

    d_pairs = to_pairs(d_heads.reshape(token_rows, heads_here, HEAD_WIDTH))
    delta = jnp.sum(d_pairs.astype(F32) * attended[..., :HEAD_WIDTH], axis=-1)
    d_query, d_keyvalue = attend_back(
        counts,
        slots,
        parity,
        queries,
        d_pairs,
        logs[:, :, None, :],
        delta[:, :, None, :],
        keyvalues,
    )
    d_keyvalue_here = scatter_dp(d_keyvalue.reshape(dp_ranks, token_rows, 4 * HEAD_WIDTH))
    _, query_pull = jax.vjp(query_side, query_lin, query_g)
    d_query_lin, d_querygain = query_pull(from_pairs(d_query))
    _, key_pull = jax.vjp(key_side, keyvalue_lin, key_g)
    d_keyvalue_lin, d_keygain = key_pull(d_keyvalue_here)
    d_lin = jnp.concatenate([rounded(d_query_lin), rounded(d_keyvalue_lin)], axis=1)
    d_attn_in = scatter_tensor(quarters(by_cols(d_lin, w_attend)))
    d_states, d_gain_attn = norm_back(states_quarter, gains[0], d_attn_in)
    states_grad = in_order(gather_tensor(rounded(grad_middle + d_states))).astype(F32)

    d_wattend = scatter_dp(by_rows(attn_in, d_lin).reshape(dp_ranks, weight_rows, -1))
    d_wout = scatter_dp(d_wout.reshape(dp_ranks, weight_rows, -1))
    if not kernels:
        ffn_all = jnp.concatenate(ffn_ins, axis=0)
        down_all = jnp.concatenate(down_grads, axis=0)
        grads_hidden = jnp.concatenate(
            [
                by_rows(ffn_all, jnp.concatenate(d_chunks, axis=0)),
                by_rows(down_all, jnp.concatenate(mixed_chunks, axis=0)),
            ],
            axis=1,
        ).reshape(dp_ranks, weight_rows, 3 * slice_width)
        collected = jnp.zeros((PLANES, weight_rows, 3 * slice_width), F32)
        for kz in range(PLANES):
            total = lax.dynamic_index_in_dim(grads_hidden, rank ^ (kz * lines), 0, keepdims=False)
            for ky in range(1, lines):
                piece = lax.dynamic_index_in_dim(
                    grads_hidden, rank ^ (kz * lines + ky), 0, keepdims=False
                )
                total = total + send(rounded(piece), ky=ky).astype(F32)
            if kz:
                total = send(rounded(total), kz=kz).astype(F32)
            collected = lax.dynamic_update_index_in_dim(collected, total, plane ^ kz, 0)

    def unsliced(index):
        columns = slice(index * slice_width, (index + 1) * slice_width)
        if kernels:
            piece = collected[:, columns].transpose(2, 0, 1).astype(F32)
        else:
            piece = collected[:, :, columns].transpose(1, 0, 2)
        return piece.reshape(1, weight_rows, hidden)

    kv_grad = d_wattend[:, head_width:]
    spread = jnp.zeros((weight_rows, 2 * value_start), F32)
    spread = lax.dynamic_update_slice_in_dim(spread, kv_grad[:, : 2 * HEAD_WIDTH], first_key, 1)
    spread = lax.dynamic_update_slice_in_dim(
        spread, kv_grad[:, 2 * HEAD_WIDTH :], value_start + first_key, 1
    )
    d_wkeyvalue = lax.psum(spread, "tensor")

    result_quarter = rounded(middle_rows + scatter_planes(out_parts))
    result = in_order(gather_tensor(result_quarter))

    small = jnp.concatenate([d_gain_attn, d_gain_ffn, d_querygain, d_keygain])
    small = lax.psum(small, ("dp", "tensor"))
    d_gains = lax.dynamic_slice_in_dim(
        small[: 2 * width].reshape(2, width), rank * weight_rows, weight_rows, 1
    ).T
    return (
        result,
        states_grad,
        d_wattend[None, :, :head_width],
        d_wkeyvalue[None],
        d_wout[None],
        unsliced(0),
        unsliced(1),
        unsliced(2),
        d_gains[None],
        small[2 * width : 2 * width + HEAD_WIDTH][None],
        small[2 * width + HEAD_WIDTH :][None],
    )


def solution(mesh):
    return jax.shard_map(
        local,
        mesh=mesh,
        in_specs=(
            P("dp", None),
            P(None, "dp", "tensor"),
            P(None, "dp", None),
            P(None, "dp", "tensor"),
            P(None, "dp", "tensor"),
            P(None, "dp", "tensor"),
            P(None, "dp", "tensor"),
            P(None, "dp", None),
            P(),
            P(),
            P(),
            P(),
            P("dp", None),
        ),
        out_specs=(
            P("dp", None),
            P("dp", None),
            P(None, "dp", "tensor"),
            P(None, "dp", None),
            P(None, "dp", "tensor"),
            P(None, "dp", "tensor"),
            P(None, "dp", "tensor"),
            P(None, "dp", "tensor"),
            P(None, "dp", None),
            P(),
            P(),
        ),
        check_vma=False,
    )
```

```python
import functools

import jax
import jax.numpy as jnp
from jax import lax
from jax.experimental import pallas as pl
from jax.experimental.pallas import tpu as pltpu
from jax.sharding import PartitionSpec as P

QUERY_HEADS = 24
KEYVALUE_HEADS = 6
HEAD_WIDTH = 64
STRETCH = 128
EPSILON = 1e-06
PLANES = 4
PAIRS = 3
LOG2E = 1.4426950408889634
BF16 = jnp.bfloat16
F32 = jnp.float32


def product(left_side, right_side):
    return jnp.dot(left_side, right_side, preferred_element_type=F32)


def by_rows(left_side, right_side):
    return lax.dot_general(
        left_side, right_side, (((0,), (0,)), ((), ())), preferred_element_type=F32
    )


def by_cols(left_side, right_side):
    return lax.dot_general(
        left_side, right_side, (((1,), (1,)), ((), ())), preferred_element_type=F32
    )


def normed(vector, gain_vector):
    return (
        vector
        * lax.rsqrt(jnp.mean(vector * vector, axis=-1, keepdims=True) + EPSILON)
        * gain_vector
    )


def angles(positions, head_size):
    frequency = 10000.0 ** (-jnp.arange(head_size // 2, dtype=F32) * 2.0 / head_size)
    phase_angle = positions.astype(F32)[:, None] * frequency[None, :]
    return (jnp.cos(phase_angle)[:, None, :], jnp.sin(phase_angle)[:, None, :])


def rotated(vector, cosines, sines):
    half_width = vector.shape[-1] // 2
    front = vector[..., :half_width]
    behind = vector[..., half_width:]
    return jnp.concatenate(
        [front * cosines - behind * sines, behind * cosines + front * sines], axis=-1
    )


def visible_mask(shape, key_axis):
    keys = lax.broadcasted_iota(jnp.int32, shape, key_axis)
    queries = lax.rem(lax.broadcasted_iota(jnp.int32, shape, 1 - key_axis), STRETCH)
    return keys <= queries


def attend_kernel(count_ref, slots_ref, parity_ref, q_ref, kv_ref, out_ref, acc_ref):
    odd = parity_ref[0] == 1
    ones = jnp.ones((STRETCH, HEAD_WIDTH), BF16)

    def add_block(block, slot, last):
        tile = kv_ref[slot]
        keys = [tile[:, :64], tile[:, 64:128]]
        values = [
            jnp.concatenate([tile[:, 128:192], ones], axis=1),
            jnp.concatenate([tile[:, 192:256], ones], axis=1),
        ]
        middle_key = jnp.where(odd, keys[1], keys[0])
        middle_value = jnp.where(odd, values[1], values[0])
        for pair, key, value in (
            (0, keys[0], values[0]),
            (1, middle_key, middle_value),
            (2, keys[1], values[1]),
        ):
            scores = by_cols(q_ref[block, pair], key)
            weights = jnp.exp2(scores * (LOG2E * HEAD_WIDTH**-0.5))
            if last:
                weights = jnp.where(visible_mask(weights.shape, 1), weights, 0.0)
            acc_ref[pair] += product(weights.astype(BF16), value)

    def one_block(block, carry):
        acc_ref[...] = jnp.zeros_like(acc_ref)
        count = count_ref[block]

        def step(index, inner):
            add_block(block, slots_ref[block, index], False)
            return inner

        lax.fori_loop(0, count - 1, step, 0)
        add_block(block, slots_ref[block, count - 1], True)
        for pair in range(PAIRS):
            total = acc_ref[pair]
            denominator = total[:, HEAD_WIDTH:]
            out_ref[block, pair] = jnp.concatenate(
                [total[:, :HEAD_WIDTH] / denominator, jnp.log2(denominator)], axis=1
            )
        return carry

    lax.fori_loop(0, q_ref.shape[0], one_block, 0)


def attend(counts, slots, parity, queries, keyvalues):
    blocks = queries.shape[0]
    smem = pl.BlockSpec(memory_space=pltpu.SMEM)
    vmem = pl.BlockSpec(memory_space=pltpu.VMEM)
    return pl.pallas_call(
        attend_kernel,
        out_shape=jax.ShapeDtypeStruct((blocks, PAIRS, 2 * STRETCH, 128), F32),
        in_specs=[smem, smem, smem, vmem, vmem],
        out_specs=vmem,
        scratch_shapes=[pltpu.VMEM((PAIRS, 2 * STRETCH, 128), F32)],
        compiler_params=pltpu.CompilerParams(vmem_limit_bytes=40 << 20),
        cost_estimate=pl.CostEstimate(
            flops=4 * 20 * PAIRS * 256 * 128 * 64 * 4, bytes_accessed=8 << 20, transcendentals=0
        ),
        name="attend",
    )(counts, slots, parity, queries, keyvalues)


def attend_back_kernel(
    count_ref, slots_ref, parity_ref, q_ref, do_ref, log_ref, delta_ref, kv_ref, dq_ref, dkv_ref
):
    odd = parity_ref[0] == 1
    scale = HEAD_WIDTH**-0.5
    dq_ref[...] = jnp.zeros_like(dq_ref)
    dkv_ref[...] = jnp.zeros_like(dkv_ref)

    def add_block(block, slot, last):
        tile = kv_ref[slot]
        keys = [tile[:, :64], tile[:, 64:128]]
        values = [tile[:, 128:192], tile[:, 192:256]]
        middle_key = jnp.where(odd, keys[1], keys[0])
        middle_value = jnp.where(odd, values[1], values[0])
        d_keys, d_values = [], []
        for pair, key, value in (
            (0, keys[0], values[0]),
            (1, middle_key, middle_value),
            (2, keys[1], values[1]),
        ):
            query, d_out = q_ref[block, pair], do_ref[block, pair]
            scores = by_cols(key, query)
            weights = jnp.exp2(scores * (LOG2E * scale) - log_ref[block, pair])
            if last:
                weights = jnp.where(visible_mask(weights.shape, 0), weights, 0.0)
            d_weights = by_cols(value, d_out)
            d_scores = (weights * (d_weights - delta_ref[block, pair])).astype(BF16)
            d_values.append(product(weights.astype(BF16), d_out))
            d_keys.append(product(d_scores, query))
            dq_ref[block, pair] += by_rows(d_scores, key) * scale
        zero = jnp.zeros((STRETCH, HEAD_WIDTH), F32)
        parts = [
            (d_keys[0] + jnp.where(odd, zero, d_keys[1])) * scale,
            (d_keys[2] + jnp.where(odd, d_keys[1], zero)) * scale,
            d_values[0] + jnp.where(odd, zero, d_values[1]),
            d_values[2] + jnp.where(odd, d_values[1], zero),
        ]
        dkv_ref[slot] += jnp.concatenate(parts, axis=1)

    def one_block(block, carry):
        count = count_ref[block]

        def step(index, inner):
            add_block(block, slots_ref[block, index], False)
            return inner

        lax.fori_loop(0, count - 1, step, 0)
        add_block(block, slots_ref[block, count - 1], True)
        return carry

    lax.fori_loop(0, q_ref.shape[0], one_block, 0)


def attend_back(counts, slots, parity, queries, d_out, logs, delta, keyvalues):
    blocks = queries.shape[0]
    smem = pl.BlockSpec(memory_space=pltpu.SMEM)
    vmem = pl.BlockSpec(memory_space=pltpu.VMEM)
    return pl.pallas_call(
        attend_back_kernel,
        out_shape=(
            jax.ShapeDtypeStruct((blocks, PAIRS, 2 * STRETCH, HEAD_WIDTH), F32),
            jax.ShapeDtypeStruct(keyvalues.shape, F32),
        ),
        in_specs=[smem] * 3 + [vmem] * 5,
        out_specs=(vmem, vmem),
        compiler_params=pltpu.CompilerParams(vmem_limit_bytes=56 << 20),
        cost_estimate=pl.CostEstimate(
            flops=10 * 20 * PAIRS * 256 * 128 * 64 * 4, bytes_accessed=8 << 20, transcendentals=0
        ),
        name="attend_back",
    )(counts, slots, parity, queries, d_out, logs, delta, keyvalues)


class Place:
    def __init__(self, lines):
        rank, part = lax.axis_index("dp"), lax.axis_index("tensor")
        self.lines = lines
        self.z, self.y = rank // lines, lax.rem(rank, lines)
        self.x, self.c = part // 2, lax.rem(part, 2)
        self.quarter = self.c * 2 + self.x

    def plane(self, move):
        if move == 0:
            return self.z
        if move == 1:
            return self.z + 1 - 2 * lax.rem(self.z, 2)
        if move == 2:
            return self.z + 2 - 4 * (self.z // 2)
        return 3 - self.z

    def to(self, kz=0, ky=0, kx=0, kc=0):
        y = 1 - self.y if ky else self.y
        x = 1 - self.x if kx else self.x
        c = 1 - self.c if kc else self.c
        return (self.plane(kz) * self.lines + y, x * 2 + c)


class Links:
    def __init__(self, place, send_sems, recv_sems):
        self.place, self.send_sems, self.recv_sems = place, send_sems, recv_sems
        self.started = []

    def greet(self, moves):
        barrier = pltpu.get_barrier_semaphore()
        for move in moves:
            pl.semaphore_signal(
                barrier, inc=1, device_id=self.place.to(**move), device_id_type=pl.DeviceIdType.MESH
            )
        pl.semaphore_wait(barrier, len(moves))

    def send(self, source, target, **move):
        number = len(self.started)
        copy = pltpu.make_async_remote_copy(
            src_ref=source,
            dst_ref=target,
            send_sem=self.send_sems.at[number],
            recv_sem=self.recv_sems.at[number],
            device_id=self.place.to(**move),
            device_id_type=pl.DeviceIdType.MESH,
        )
        copy.start()
        self.started.append(copy)
        return copy

    def finish(self):
        for copy in self.started:
            copy.wait_send()


def rows_at(index, size):
    return pl.ds(pl.multiple_of(index * size, size), size)


MIDDLE_COPIES = 50


def middle_kernel(
    lines,
    slice_width,
    attn_ref,
    states_ref,
    grad_ref,
    gain_ref,
    w_output_any,
    w_hidden_any,
    down_any,
    middle_ref,
    back_ref,
    gain_out_ref,
    d_heads_ref,
    output_grad_ref,
    mixed_ref,
    collected_ref,
    w_output_ref,
    w_hidden_ref,
    down_ref,
    ffn_ref,
    d_hidden_ref,
    partial_ref,
    core_out,
    core_in,
    x_out,
    x_in,
    sums_ref,
    z_out,
    z_in,
    y_out,
    y_in,
    blocks_ref,
    g_out,
    local_sems,
    send_sems,
    recv_sems,
):
    here = Place(lines)
    links = Links(here, send_sems, recv_sems)
    quarter, width = middle_ref.shape
    half = 2 * quarter
    token_rows = 4 * quarter
    hidden = slice_width

    loads = [
        pltpu.make_async_copy(w_output_any, w_output_ref, local_sems.at[0]),
        pltpu.make_async_copy(w_hidden_any, w_hidden_ref, local_sems.at[1]),
        pltpu.make_async_copy(down_any, down_ref, local_sems.at[2]),
    ]
    for load in loads:
        load.start()
    links.greet([dict(kc=1), dict(kx=1), dict(ky=1), dict(kz=1), dict(kz=2), dict(kz=3)])
    mine = rows_at(here.quarter, quarter)
    my_half, other_half = rows_at(here.c, half), rows_at(1 - here.c, half)

    loads[0].wait()
    cut = 4
    piece = width // cut
    core_copies = []
    for part in range(cut):
        columns = slice(part * piece, (part + 1) * piece)
        weight = w_output_ref[columns, :]
        core_out[4, :, columns] = by_cols(attn_ref[other_half, :], weight).astype(BF16)
        core_copies.append(
            links.send(core_out.at[4, :, columns], core_in.at[4, :, columns], kc=1)
        )
        partial_ref[0, :half, columns] = by_cols(attn_ref[my_half, :], weight)
    x_copies = []
    x_mine, x_other = rows_at(here.x, quarter), rows_at(1 - here.x, quarter)
    for part in range(cut):
        columns = slice(part * piece, (part + 1) * piece)
        core_copies[part].wait_recv()
        x_out[4, :, columns] = (
            partial_ref[0, x_other, columns] + core_in[4, x_other, columns].astype(F32)
        ).astype(BF16)
        x_copies.append(links.send(x_out.at[4, :, columns], x_in.at[4, :, columns], kx=1))
        middle_ref[:, columns] = (
            states_ref[mine, columns].astype(F32)
            + partial_ref[0, x_mine, columns]
            + core_in[4, x_mine, columns].astype(F32)
        )
    for part in range(cut):
        columns = slice(part * piece, (part + 1) * piece)
        x_copies[part].wait_recv()
        middle_ref[:, columns] += x_in[4, :, columns].astype(F32)
    middle = middle_ref[...]
    inverse = lax.rsqrt(jnp.mean(middle * middle, axis=-1, keepdims=True) + EPSILON)
    ffn_ref[here.z, mine, :] = (middle * inverse * gain_ref[...]).astype(BF16)

    def block_of(move):
        return ffn_ref.at[here.plane(move), mine]

    far = links.send(block_of(0), block_of(0), kz=2)
    near = links.send(block_of(0), block_of(0), kz=1)
    across = {0: links.send(block_of(0), block_of(0), kx=1)}
    near.wait_recv()
    across[1] = links.send(block_of(1), block_of(1), kx=1)
    far.wait_recv()
    corner = links.send(block_of(2), block_of(2), kz=1)
    across[2] = links.send(block_of(2), block_of(2), kx=1)
    cores = {}

    def spread(move):
        across[move].wait_recv()
        both = ffn_ref.at[here.plane(move), my_half]
        cores[move] = links.send(both, both, kc=1)

    spread(0)
    loads[1].wait()
    loads[2].wait()
    core_copies, x_copies = [], []

    def add_cores(move):
        core_copies[move].wait_recv()
        total_rows = rows_at(here.c * 2 + 1 - here.x, quarter)
        x_out[move] = (
            partial_ref[move % 2, total_rows, :] + core_in[move, x_other, :].astype(F32)
        ).astype(BF16)
        x_copies.append(links.send(x_out.at[move], x_in.at[move], kx=1))
        sums_ref[move] = partial_ref[move % 2, mine, :] + core_in[move, x_mine, :].astype(F32)

    def add_x(move):
        x_copies[move].wait_recv()
        sums_ref[move] += x_in[move].astype(F32)

    order = (0, 1, 2, 3)
    for index, move in enumerate(order):
        if move < 3:
            if move == 2:
                corner.wait_recv()
                across[3] = links.send(block_of(3), block_of(3), kx=1)
        cores[move].wait_recv()
        plane = here.plane(move)
        chunk = ffn_ref[plane]
        gate_pre = by_cols(w_hidden_ref[:hidden, :], chunk)
        up_pre = by_cols(w_hidden_ref[hidden : 2 * hidden, :], chunk)
        sigmoid_gate = 1.0 / (1.0 + jnp.exp(-gate_pre))
        silu = gate_pre * sigmoid_gate
        columns = pl.ds(pl.multiple_of(plane * token_rows, token_rows), token_rows)
        mixed_ref[:, columns] = (silu * up_pre).astype(BF16)
        d_mixed = by_cols(w_hidden_ref[2 * hidden :, :], down_ref[plane])
        d_hidden_ref[:hidden, columns] = (
            d_mixed * up_pre * sigmoid_gate * (1.0 + gate_pre * (1.0 - sigmoid_gate))
        ).astype(BF16)
        d_hidden_ref[hidden:, columns] = (d_mixed * silu).astype(BF16)
        partial_ref[move % 2] = by_rows(d_hidden_ref[:, columns], w_hidden_ref[: 2 * hidden, :])
        core_out[move] = partial_ref[move % 2, other_half, :].astype(BF16)
        core_copies.append(links.send(core_out.at[move], core_in.at[move], kc=1))
        if index > 0:
            add_cores(order[index - 1])
        if move + 1 < 4:
            spread(move + 1)
    add_cores(3)

    weight_rows = width // (4 * lines)

    def gradient(move, line):
        rank = here.plane(move) * lines + line
        columns = pl.ds(pl.multiple_of(rank * weight_rows, weight_rows), weight_rows)
        first = jnp.zeros((2 * hidden, weight_rows), F32)
        second = jnp.zeros((hidden, weight_rows), F32)
        for plane in range(4):
            tokens = slice(plane * token_rows, (plane + 1) * token_rows)
            first += product(d_hidden_ref[:, tokens], ffn_ref[plane, :, columns])
            second += product(mixed_ref[:, tokens], down_ref[plane, :, columns])
        return first, second

    y_copies = {}
    for move in (3, 2, 1, 0):
        first, second = gradient(move, 1 - here.y)
        y_out[move, : 2 * hidden] = first.astype(BF16)
        y_out[move, 2 * hidden :] = second.astype(BF16)
        y_copies[move] = links.send(y_out.at[move], y_in.at[move], ky=1)

    add_x(0)
    add_x(1)
    z_out[0] = sums_ref[1].astype(BF16)
    z_copies = [links.send(z_out.at[0], z_in.at[0], kz=1)]
    add_x(2)
    add_x(3)
    z_out[1] = sums_ref[3].astype(BF16)
    z_copies.append(links.send(z_out.at[1], z_in.at[1], kz=1))
    first, second = gradient(3, here.y)
    blocks_ref[0, : 2 * hidden] = first
    blocks_ref[0, 2 * hidden :] = second
    z_copies[1].wait_recv()
    z_out[2] = (sums_ref[2] + z_in[1].astype(F32)).astype(BF16)
    z_copies.append(links.send(z_out.at[2], z_in.at[2], kz=2))
    for slot, move in enumerate((2, 1, 0)):
        first, second = gradient(move, here.y)
        blocks_ref[slot + 1, : 2 * hidden] = first
        blocks_ref[slot + 1, 2 * hidden :] = second
    z_copies[0].wait_recv()
    z_copies[2].wait_recv()
    d_normed = sums_ref[0] + z_in[0].astype(F32) + z_in[2].astype(F32)
    middle = middle_ref[...]
    inverse = lax.rsqrt(jnp.mean(middle * middle, axis=-1, keepdims=True) + EPSILON)
    unit = middle * inverse
    gain_out_ref[...] = jnp.sum(d_normed * unit, axis=0, keepdims=True)
    scaled = d_normed * gain_ref[...]
    back = inverse * (scaled - unit * jnp.mean(scaled * unit, axis=-1, keepdims=True))
    grad_middle = grad_ref[mine, :].astype(F32) + back
    back_ref[...] = grad_middle
    output_grad_ref[mine, :] = grad_middle.astype(BF16)
    block = output_grad_ref.at[mine]
    links.send(block, block, kx=1).wait_recv()
    both = output_grad_ref.at[my_half]
    core = links.send(both, both, kc=1)

    g_copies = []
    for slot, move in enumerate((3, 2, 1, 0)):
        y_copies[move].wait_recv()
        total = blocks_ref[slot] + y_in[move].astype(F32)
        if move:
            g_out[slot] = total.astype(BF16)
            g_copies.append(links.send(g_out.at[slot], collected_ref.at[here.z], kz=move))
        else:
            collected_ref[here.z] = total.astype(BF16)
    core.wait_recv()
    d_heads_ref[...] = product(output_grad_ref[...], w_output_ref[...]).astype(BF16)
    for copy in g_copies:
        copy.wait_recv()
    links.finish()


def middle(lines, slice_width, attn_out, states, out_grad, gain, w_output, w_hidden, down_grads):
    token_rows, width = states.shape
    quarter = token_rows // 4
    half = 2 * quarter
    hidden = slice_width
    weight_rows = width // (4 * lines)
    vmem = pl.BlockSpec(memory_space=pltpu.VMEM)
    hbm = pl.BlockSpec(memory_space=pl.ANY)
    shape = jax.ShapeDtypeStruct
    return pl.pallas_call(
        functools.partial(middle_kernel, lines, slice_width),
        out_shape=(
            shape((quarter, width), F32),
            shape((quarter, width), F32),
            shape((1, width), F32),
            shape(attn_out.shape, BF16),
            shape((token_rows, width), BF16),
            shape((hidden, 4 * token_rows), BF16),
            shape((4, 3 * hidden, weight_rows), BF16),
        ),
        in_specs=[vmem] * 4 + [hbm] * 3,
        out_specs=(vmem,) * 7,
        scratch_shapes=[
            pltpu.VMEM(w_output.shape, BF16),
            pltpu.VMEM(w_hidden.shape, BF16),
            pltpu.VMEM(down_grads.shape, BF16),
            pltpu.VMEM((4, token_rows, width), BF16),
            pltpu.VMEM((2 * hidden, 4 * token_rows), BF16),
            pltpu.VMEM((2, token_rows, width), F32),
            pltpu.VMEM((5, half, width), BF16),
            pltpu.VMEM((5, half, width), BF16),
            pltpu.VMEM((5, quarter, width), BF16),
            pltpu.VMEM((5, quarter, width), BF16),
            pltpu.VMEM((4, quarter, width), F32),
            pltpu.VMEM((3, quarter, width), BF16),
            pltpu.VMEM((3, quarter, width), BF16),
            pltpu.VMEM((4, 3 * hidden, weight_rows), BF16),
            pltpu.VMEM((4, 3 * hidden, weight_rows), BF16),
            pltpu.VMEM((4, 3 * hidden, weight_rows), F32),
            pltpu.VMEM((3, 3 * hidden, weight_rows), BF16),
            pltpu.SemaphoreType.DMA((3,)),
            pltpu.SemaphoreType.DMA((MIDDLE_COPIES,)),
            pltpu.SemaphoreType.DMA((MIDDLE_COPIES,)),
        ],
        compiler_params=pltpu.CompilerParams(
            collective_id=0, has_side_effects=True, vmem_limit_bytes=62 << 20
        ),
        name="middle",
    )(attn_out, states, out_grad, gain, w_output, w_hidden, down_grads)


class Gather:
    def __init__(self, links, block, own=None):
        self.links, self.block, self.y = links, block, links.place.y
        self.own = block(0, self.y) if own is None else own
        self.lines = []

    def over_lines(self, move):
        place = self.block(move, self.y)
        source = self.own if move == 0 else place
        self.lines.append(self.links.send(source, place, ky=1))

    def start(self):
        place = self.block(0, self.y)
        self.far = self.links.send(self.own, place, kz=2)
        self.near = self.links.send(self.own, place, kz=1)
        self.over_lines(0)

    def relay(self):
        self.near.wait_recv()
        self.over_lines(1)
        self.far.wait_recv()
        place = self.block(2, self.y)
        self.corner = self.links.send(place, place, kz=1)
        self.over_lines(2)

    def last(self):
        self.corner.wait_recv()
        self.over_lines(3)

    def finish(self):
        for copy in self.lines:
            copy.wait_recv()


def head_mean(value):
    row = lax.broadcasted_iota(jnp.int32, (128, 128), 0) // HEAD_WIDTH
    column = lax.broadcasted_iota(jnp.int32, (128, 128), 1) // HEAD_WIDTH
    average = jnp.where(row == column, 1.0 / HEAD_WIDTH, 0.0).astype(F32)
    return jnp.dot(
        value, average, preferred_element_type=F32, precision=lax.Precision.HIGHEST
    )


def halves_swapped(value):
    first = lax.rem(lax.broadcasted_iota(jnp.int32, value.shape, 1), HEAD_WIDTH) < HEAD_WIDTH // 2
    return jnp.where(
        first,
        pltpu.roll(value, 128 - HEAD_WIDTH // 2, 1),
        pltpu.roll(value, HEAD_WIDTH // 2, 1),
    )


FRONT_COPIES = 46


def front_kernel(
    lines,
    heads,
    states_ref,
    gains_in,
    w_attend_in,
    cosine_ref,
    sine_ref,
    head_gain_ref,
    w_output_in,
    w_hidden_in,
    grad_any,
    lin_ref,
    attn_in_ref,
    query_ref,
    kv_ref,
    gains_ref,
    w_attend_ref,
    w_output_ref,
    w_hidden_ref,
    down_ref,
    local_sems,
    send_sems,
    recv_sems,
):
    here = Place(lines)
    links = Links(here, send_sems, recv_sems)
    token_rows, width = states_ref.shape
    quarter = token_rows // 4
    half = 2 * quarter
    weight_rows = w_attend_in.shape[0]
    head_width = heads * HEAD_WIDTH
    mine, my_half = rows_at(here.quarter, quarter), rows_at(here.c, half)

    def rank(move, line):
        return here.plane(move) * lines + line

    def rows_of(ref):
        return lambda move, line: ref.at[rows_at(rank(move, line), weight_rows)]

    def columns_of(ref):
        return lambda move, line: ref.at[:, rows_at(rank(move, line), weight_rows)]

    loads = [
        pltpu.make_async_copy(w_output_in, rows_of(w_output_ref)(0, here.y), local_sems.at[0]),
        pltpu.make_async_copy(
            w_hidden_in.at[here.z], columns_of(w_hidden_ref)(0, here.y), local_sems.at[1]
        ),
        pltpu.make_async_copy(grad_any, down_ref.at[here.z], local_sems.at[2]),
    ]
    for load in loads:
        load.start()
    links.greet([dict(kc=1), dict(kx=1), dict(ky=1), dict(kz=1), dict(kz=2), dict(kz=3)])

    gains = Gather(links, columns_of(gains_ref), gains_in)
    gains.start()
    attend = Gather(links, rows_of(w_attend_ref), w_attend_in)
    attend.start()
    columns_of(gains_ref)(0, here.y)[...] = gains_in[...]
    rows_of(w_attend_ref)(0, here.y)[...] = w_attend_in[...]
    gains.relay()
    gains.last()
    gains.finish()
    states = states_ref[...].astype(F32)
    inverse = lax.rsqrt(jnp.mean(states * states, axis=-1, keepdims=True) + EPSILON)
    attn_in_ref[...] = (states * inverse * gains_ref[0:1, :]).astype(BF16)

    attend.relay()
    output = Gather(links, rows_of(w_output_ref), w_output_in)
    output.start()
    planes = [
        links.send(w_hidden_in.at[here.plane(move)], columns_of(w_hidden_ref)(0, here.y), kz=move)
        for move in (1, 2, 3)
    ]
    attend.last()
    attend.finish()
    lin = product(attn_in_ref[...], w_attend_ref[...])
    lin_ref[...] = lin
    blocks = token_rows // STRETCH
    own_rows = rows_at(rank(0, here.y), token_rows)

    def turned(group):
        columns = slice(group * 128, (group + 1) * 128)
        value = lin[:, columns]
        value = value * lax.rsqrt(head_mean(value * value) + EPSILON) * head_gain_ref[:, columns]
        return (value * cosine_ref[...] + halves_swapped(value) * sine_ref[...]).astype(BF16)

    keys = head_width // 128
    kv_ref[own_rows, :128] = turned(keys)
    kv_ref[own_rows, 128:] = lin[:, head_width + 128 :].astype(BF16)
    keyvalue = Gather(
        links, lambda move, line: kv_ref.at[rows_at(rank(move, line), token_rows)]
    )
    keyvalue.start()
    for pair in range(PAIRS):
        rotated_pair = turned(pair)
        for block in range(blocks):
            rows = rotated_pair[block * STRETCH : (block + 1) * STRETCH]
            query_ref[block, pair, :STRETCH] = rows[:, :HEAD_WIDTH]
            query_ref[block, pair, STRETCH:] = rows[:, HEAD_WIDTH:]
    keyvalue.relay()
    keyvalue.last()

    loads[2].wait()

    def block_of(move):
        return down_ref.at[here.plane(move), mine]

    far = links.send(block_of(0), block_of(0), kz=2)
    near = links.send(block_of(0), block_of(0), kz=1)
    loads[0].wait()
    loads[1].wait()
    output.relay()
    hidden_lines = []
    for move in range(4):
        if move:
            planes[move - 1].wait_recv()
        place = columns_of(w_hidden_ref)(move, here.y)
        hidden_lines.append(links.send(place, place, ky=1))
    near.wait_recv()
    across = [links.send(block_of(1), block_of(1), kx=1)]
    far.wait_recv()
    corner = links.send(block_of(2), block_of(2), kz=1)
    across.append(links.send(block_of(2), block_of(2), kx=1))
    output.last()
    corner.wait_recv()
    across.append(links.send(block_of(3), block_of(3), kx=1))
    cores = []
    for move in (1, 2, 3):
        across[move - 1].wait_recv()
        both = down_ref.at[here.plane(move), my_half]
        cores.append(links.send(both, both, kc=1))
    keyvalue.finish()
    output.finish()
    for copy in hidden_lines + cores:
        copy.wait_recv()
    links.finish()


def front(lines, heads, states, gains, w_attend, cosine, sine, head_gain, w_output, w_hidden, grad):
    token_rows, width = states.shape
    ranks = 4 * lines
    hidden = w_hidden.shape[1]
    blocks = token_rows // STRETCH
    vmem = pl.BlockSpec(memory_space=pltpu.VMEM)
    hbm = pl.BlockSpec(memory_space=pl.ANY)
    shape = jax.ShapeDtypeStruct
    return pl.pallas_call(
        functools.partial(front_kernel, lines, heads),
        out_shape=(
            shape((token_rows, w_attend.shape[1]), F32),
            shape((token_rows, width), BF16),
            shape((blocks, PAIRS, 2 * STRETCH, HEAD_WIDTH), BF16),
            shape((ranks * token_rows, 4 * HEAD_WIDTH), BF16),
            shape((gains.shape[0], width), F32),
            shape((width, w_attend.shape[1]), BF16),
            shape((width, w_output.shape[1]), BF16),
            shape((hidden, width), BF16),
            shape((4, token_rows, width), BF16),
        ),
        in_specs=[vmem] * 6 + [hbm] * 3,
        out_specs=(vmem,) * 6 + (hbm,) * 3,
        scratch_shapes=[
            pltpu.SemaphoreType.DMA((3,)),
            pltpu.SemaphoreType.DMA((FRONT_COPIES,)),
            pltpu.SemaphoreType.DMA((FRONT_COPIES,)),
        ],
        compiler_params=pltpu.CompilerParams(
            collective_id=1, has_side_effects=True, vmem_limit_bytes=56 << 20
        ),
        name="front",
    )(states, gains, w_attend, cosine, sine, head_gain, w_output, w_hidden, grad)


TAIL_COPIES = 50


class Scatter:
    ORDER = (3, 1, 2, 0)

    def __init__(self, links, y_out, y_in, z_out, z_in, sums):
        self.links = links
        self.y_out, self.y_in, self.z_out, self.z_in, self.sums = y_out, y_in, z_out, z_in, sums
        self.lines, self.planes = {}, {}

    def start(self, move, block):
        self.y_out[move] = block.astype(BF16)
        self.lines[move] = self.links.send(self.y_out.at[move], self.y_in.at[move], ky=1)

    def add(self, move, block):
        self.lines[move].wait_recv()
        total = block + self.y_in[move].astype(F32)
        if move in (3, 1):
            slot = 0 if move == 1 else 1
            self.z_out[slot] = total.astype(BF16)
            self.planes[slot] = self.links.send(self.z_out.at[slot], self.z_in.at[slot], kz=1)
        elif move == 2:
            self.planes[1].wait_recv()
            self.z_out[2] = (total + self.z_in[1].astype(F32)).astype(BF16)
            self.planes[2] = self.links.send(self.z_out.at[2], self.z_in.at[2], kz=2)
        else:
            self.sums[...] = total

    def finish(self):
        self.planes[0].wait_recv()
        self.planes[2].wait_recv()
        return self.sums[...] + self.z_in[0].astype(F32) + self.z_in[2].astype(F32)


def scatter_scratch(block):
    return [
        pltpu.VMEM((4, *block), BF16),
        pltpu.VMEM((4, *block), BF16),
        pltpu.VMEM((3, *block), BF16),
        pltpu.VMEM((3, *block), BF16),
        pltpu.VMEM(block, F32),
    ]


def tail_kernel(
    lines,
    heads,
    d_kv_ref,
    d_query_ref,
    lin_ref,
    attn_in_ref,
    output_grad_ref,
    attn_out_ref,
    w_attend_ref,
    back_ref,
    gains_ref,
    gain_ffn_ref,
    states_ref,
    middle_ref,
    mixed_ref,
    cosine_ref,
    sine_ref,
    head_gain_ref,
    w_hidden_any,
    result_ref,
    states_grad_ref,
    g_attend_ref,
    g_output_ref,
    g_kv_ref,
    small_ref,
    *scratch,
):
    here = Place(lines)
    (
        w_down_ref,
        d_lin_ref,
        partial_ref,
        core_out,
        core_in,
        x_out,
        x_in,
        sums_ref,
        z_out,
        z_in,
        small_out,
        small_in,
        local_sems,
        send_sems,
        recv_sems,
    ) = scratch[:15]
    links = Links(here, send_sems, recv_sems)
    kv_sum = Scatter(links, *scratch[15:20])
    output_sum = Scatter(links, *scratch[20:25])
    attend_sum = Scatter(links, *scratch[25:30])
    token_rows, width = states_ref.shape
    quarter = token_rows // 4
    half = 2 * quarter
    weight_rows = width // (4 * lines)
    head_width = heads * HEAD_WIDTH
    blocks = token_rows // STRETCH
    hidden = mixed_ref.shape[0]
    mine, other = rows_at(here.quarter, quarter), rows_at(here.c * 2 + 1 - here.x, quarter)
    my_half, other_half = rows_at(here.c, half), rows_at(1 - here.c, half)
    x_mine, x_other = rows_at(here.x, quarter), rows_at(1 - here.x, quarter)

    load = pltpu.make_async_copy(
        w_hidden_any.at[pl.ds(2 * hidden, hidden)], w_down_ref, local_sems.at[0]
    )
    load.start()
    links.greet([dict(kc=1), dict(kx=1), dict(ky=1), dict(kz=1), dict(kz=2)])

    def rank(move, line):
        return here.plane(move) * lines + line

    def kv_block(move, line):
        return d_kv_ref[rows_at(rank(move, line), token_rows), :]

    for move in Scatter.ORDER:
        kv_sum.start(move, kv_block(move, 1 - here.y))

    def columns(move, line):
        return rows_at(rank(move, line), weight_rows)

    def output_block(move, line):
        return by_rows(output_grad_ref[:, columns(move, line)], attn_out_ref[...])

    def attend_block(move, line):
        return by_rows(attn_in_ref[:, columns(move, line)], d_lin_ref[...])

    def group_back(group, grad):
        at = slice(group * 128, (group + 1) * 128)
        linear = lin_ref[:, at]
        inverse = lax.rsqrt(head_mean(linear * linear) + EPSILON)
        unit = linear * inverse
        grad = grad * cosine_ref[...] + halves_swapped(grad * sine_ref[...])
        gain = jnp.sum(grad * unit, axis=0, keepdims=True)
        scaled = grad * head_gain_ref[:, at]
        return inverse * (scaled - unit * head_mean(scaled * unit)), gain

    small_ref[...] = jnp.zeros_like(small_ref)
    small_ref[1:2, :] = gain_ffn_ref[...]
    for pair in range(PAIRS):
        grad = jnp.concatenate(
            [
                jnp.concatenate(
                    [d_query_ref[block, pair, :STRETCH], d_query_ref[block, pair, STRETCH:]], axis=1
                )
                for block in range(blocks)
            ],
            axis=0,
        )
        linear_grad, gain = group_back(pair, grad)
        d_lin_ref[:, pair * 128 : (pair + 1) * 128] = linear_grad.astype(BF16)
        small_ref[2:3, pair * 128 : (pair + 1) * 128] = gain

    for move in Scatter.ORDER[:2]:
        kv_sum.add(move, kv_block(move, here.y))

    core_copies, x_copies = {}, {}
    load.wait()

    def out_start(move, slot):
        at = pl.ds(pl.multiple_of(here.plane(move) * token_rows, token_rows), token_rows)
        partial_ref[slot] = by_rows(mixed_ref[:, at], w_down_ref[...])
        core_out[move] = partial_ref[slot, other_half, :].astype(BF16)
        core_copies[move] = links.send(core_out.at[move], core_in.at[move], kc=1)

    def add_cores(move, slot):
        core_copies[move].wait_recv()
        x_out[move] = (partial_ref[slot, other, :] + core_in[move, x_other, :].astype(F32)).astype(
            BF16
        )
        x_copies[move] = links.send(x_out.at[move], x_in.at[move], kx=1)
        sums_ref[move] = partial_ref[slot, mine, :] + core_in[move, x_mine, :].astype(F32)

    def add_x(move):
        x_copies[move].wait_recv()
        sums_ref[move] += x_in[move].astype(F32)

    out_start(3, 0)
    out_start(1, 1)
    for move in Scatter.ORDER[2:]:
        kv_sum.add(move, kv_block(move, here.y))
    add_cores(3, 0)
    out_start(2, 0)
    add_cores(1, 1)
    out_start(0, 1)
    for move in Scatter.ORDER:
        output_sum.start(move, output_block(move, 1 - here.y))

    d_kv = kv_sum.finish()
    linear_grad, gain = group_back(PAIRS, d_kv[:, :128])
    d_lin_ref[:, head_width : head_width + 128] = linear_grad.astype(BF16)
    d_lin_ref[:, head_width + 128 :] = d_kv[:, 128:].astype(BF16)
    small_ref[2:3, head_width : head_width + 128] = gain

    for move in Scatter.ORDER:
        attend_sum.start(move, attend_block(move, 1 - here.y))

    add_cores(2, 0)
    add_cores(0, 1)
    partial_ref[0] = by_cols(d_lin_ref[...], w_attend_ref[...])
    core_out[4] = partial_ref[0, other_half, :].astype(BF16)
    core_copies[4] = links.send(core_out.at[4], core_in.at[4], kc=1)
    add_cores(4, 0)
    for move in Scatter.ORDER[:2]:
        output_sum.add(move, output_block(move, here.y))
    for move in Scatter.ORDER[:2]:
        attend_sum.add(move, attend_block(move, here.y))
    add_x(4)
    states = states_ref[mine, :].astype(F32)
    inverse = lax.rsqrt(jnp.mean(states * states, axis=-1, keepdims=True) + EPSILON)
    unit = states * inverse
    grad = sums_ref[4]
    small_ref[0:1, :] = jnp.sum(grad * unit, axis=0, keepdims=True)
    scaled = grad * gains_ref[0:1, :]
    total = back_ref[...] + inverse * (
        scaled - unit * jnp.mean(scaled * unit, axis=-1, keepdims=True)
    )
    states_grad_ref[mine, :] = total.astype(BF16)
    block = states_grad_ref.at[mine]
    states_x = links.send(block, block, kx=1)

    def small_step(step, **move):
        small_out[step] = small_ref[...]
        return links.send(small_out.at[step], small_in.at[step], **move)

    small = small_step(0, kc=1)
    output_sum.add(2, output_block(2, here.y))
    attend_sum.add(2, attend_block(2, here.y))
    small.wait_recv()
    small_ref[...] += small_in[0]
    small = small_step(1, kx=1)
    states_x.wait_recv()
    both = states_grad_ref.at[my_half]
    states_core = links.send(both, both, kc=1)
    output_sum.add(0, output_block(0, here.y))
    attend_sum.add(0, attend_block(0, here.y))
    small.wait_recv()
    small_ref[...] += small_in[1]
    small = small_step(2, ky=1)

    add_x(3)
    add_x(1)
    z_out[1] = sums_ref[3].astype(BF16)
    z_out[0] = sums_ref[1].astype(BF16)
    z_copies = {1: links.send(z_out.at[1], z_in.at[1], kz=1)}
    z_copies[0] = links.send(z_out.at[0], z_in.at[0], kz=1)
    add_x(2)
    add_x(0)
    small.wait_recv()
    small_ref[...] += small_in[2]
    small = small_step(3, kz=1)
    z_copies[1].wait_recv()
    z_out[2] = (sums_ref[2] + z_in[1].astype(F32)).astype(BF16)
    z_copies[2] = links.send(z_out.at[2], z_in.at[2], kz=2)
    small.wait_recv()
    small_ref[...] += small_in[3]
    small = small_step(4, kz=2)

    total = attend_sum.finish()
    g_attend_ref[...] = total[:, :head_width]
    part = here.x * 2 + here.c
    g_kv_ref[part] = total[:, head_width:].astype(BF16)
    block = g_kv_ref.at[part]
    kv_core = links.send(block, block, kc=1)
    kv_x = links.send(block, block, kx=1)
    g_output_ref[...] = output_sum.finish()
    z_copies[0].wait_recv()
    z_copies[2].wait_recv()
    result_ref[mine, :] = (
        middle_ref[...] + sums_ref[0] + z_in[0].astype(F32) + z_in[2].astype(F32)
    ).astype(BF16)
    block = result_ref.at[mine]
    result_x = links.send(block, block, kx=1)
    kv_x.wait_recv()
    block = g_kv_ref.at[(1 - here.x) * 2 + here.c]
    kv_both = links.send(block, block, kc=1)
    small.wait_recv()
    small_ref[...] += small_in[4]
    result_x.wait_recv()
    both = result_ref.at[my_half]
    result_core = links.send(both, both, kc=1)
    for copy in (states_core, kv_core, kv_both, result_core):
        copy.wait_recv()
    links.finish()


def tail(lines, heads, *arguments):
    (d_kv, d_query, lin, attn_in, output_grad, attn_out, w_attend, *others) = arguments
    token_rows, width = attn_in.shape
    quarter = token_rows // 4
    half = 2 * quarter
    weight_rows = width // (4 * lines)
    head_width = heads * HEAD_WIDTH
    hidden = arguments[12].shape[0]
    vmem = pl.BlockSpec(memory_space=pltpu.VMEM)
    hbm = pl.BlockSpec(memory_space=pl.ANY)
    shape = jax.ShapeDtypeStruct
    return pl.pallas_call(
        functools.partial(tail_kernel, lines, heads),
        out_shape=(
            shape((token_rows, width), BF16),
            shape((token_rows, width), BF16),
            shape((weight_rows, head_width), F32),
            shape((weight_rows, head_width), F32),
            shape((4, weight_rows, 4 * HEAD_WIDTH), BF16),
            shape((8, width), F32),
        ),
        in_specs=[vmem] * 16 + [hbm],
        out_specs=(vmem,) * 6,
        scratch_shapes=[
            pltpu.VMEM((hidden, width), BF16),
            pltpu.VMEM(lin.shape, BF16),
            pltpu.VMEM((2, token_rows, width), F32),
            pltpu.VMEM((5, half, width), BF16),
            pltpu.VMEM((5, half, width), BF16),
            pltpu.VMEM((5, quarter, width), BF16),
            pltpu.VMEM((5, quarter, width), BF16),
            pltpu.VMEM((5, quarter, width), F32),
            pltpu.VMEM((3, quarter, width), BF16),
            pltpu.VMEM((3, quarter, width), BF16),
            pltpu.VMEM((5, 8, width), F32),
            pltpu.VMEM((5, 8, width), F32),
            pltpu.SemaphoreType.DMA((1,)),
            pltpu.SemaphoreType.DMA((TAIL_COPIES,)),
            pltpu.SemaphoreType.DMA((TAIL_COPIES,)),
            *scatter_scratch((token_rows, 4 * HEAD_WIDTH)),
            *scatter_scratch((weight_rows, head_width)),
            *scatter_scratch((weight_rows, lin.shape[1])),
        ],
        compiler_params=pltpu.CompilerParams(
            collective_id=2, has_side_effects=True, vmem_limit_bytes=62 << 20
        ),
        name="tail",
    )(*arguments)


def local_kernels(
    states,
    query_weight,
    keyvalue_matrix,
    output_weight,
    gate_weight,
    up_weight,
    down_weight,
    norm_gains,
    query_gain,
    key_gain,
    slot_sequence,
    slot_offset,
    out_grad,
):
    token_rows, width = states.shape
    dp_ranks = lax.axis_size("dp")
    tensor_ranks = lax.axis_size("tensor")
    lines = dp_ranks // PLANES
    rank, part = lax.axis_index("dp"), lax.axis_index("tensor")
    heads_here = QUERY_HEADS // tensor_ranks
    head_width = heads_here * HEAD_WIDTH
    sharing_count = QUERY_HEADS // KEYVALUE_HEADS
    blocks_here = token_rows // STRETCH
    slot_count = slot_sequence.shape[0]
    hidden = gate_weight.shape[2]
    slice_width = hidden // PLANES
    weight_rows = width // dp_ranks

    sequence_here = lax.dynamic_slice_in_dim(slot_sequence, rank * blocks_here, blocks_here)
    offset_here = lax.dynamic_slice_in_dim(slot_offset, rank * blocks_here, blocks_here)
    counts = offset_here // STRETCH + 1
    places = jnp.arange(slot_count, dtype=jnp.int32)
    same = (slot_sequence[None, None, :] == sequence_here[:, None, None]) & (
        slot_offset[None, None, :] == places[None, :, None] * STRETCH
    )
    slots = jnp.sum(jnp.where(same, places[None, None, :], 0), axis=2).astype(jnp.int32)
    parity = jnp.reshape(part % 2, (1,)).astype(jnp.int32)
    positions = (offset_here[:, None] + jnp.arange(STRETCH, dtype=jnp.int32)[None, :]).reshape(-1)
    columns = jnp.arange(2 * HEAD_WIDTH, dtype=jnp.int32)
    exponent = -(columns % (HEAD_WIDTH // 2)).astype(F32) * 2.0 / HEAD_WIDTH
    phase = positions.astype(F32)[:, None] * (10000.0**exponent)[None, :]
    cosine = jnp.cos(phase)
    sine = jnp.sin(phase) * jnp.where(columns % HEAD_WIDTH < HEAD_WIDTH // 2, -1.0, 1.0)[None, :]
    head_gain = jnp.concatenate([jnp.tile(query_gain[0], heads_here), jnp.tile(key_gain[0], 2)])

    first_key = (part * heads_here) // sharing_count * HEAD_WIDTH
    value_start = KEYVALUE_HEADS * HEAD_WIDTH
    w_attend = jnp.concatenate(
        [
            query_weight[0],
            lax.dynamic_slice_in_dim(keyvalue_matrix[0], first_key, 2 * HEAD_WIDTH, 1),
            lax.dynamic_slice_in_dim(
                keyvalue_matrix[0], value_start + first_key, 2 * HEAD_WIDTH, 1
            ),
        ],
        axis=1,
    )
    gains = jnp.pad(norm_gains[0].T.astype(F32), ((0, 6), (0, 0)))

    def turned(weight):
        return weight[0].reshape(weight_rows, PLANES, slice_width).transpose(1, 2, 0)

    packed = jnp.concatenate(
        [turned(gate_weight), turned(up_weight), turned(down_weight)], axis=1
    )
    lin, attn_in, queries, keyvalues, gains, w_attend, w_output, w_hidden, down_grads = front(
        lines,
        heads_here,
        states,
        gains,
        w_attend,
        cosine,
        sine,
        head_gain[None],
        output_weight[0],
        packed,
        out_grad,
    )
    keyvalues = keyvalues.reshape(slot_count, STRETCH, 4 * HEAD_WIDTH)
    attended = attend(counts, slots, parity, queries, keyvalues)

    def from_pairs(value):
        return (
            value.reshape(blocks_here, PAIRS, 2, STRETCH, HEAD_WIDTH)
            .transpose(0, 3, 1, 2, 4)
            .reshape(token_rows, head_width)
        )

    def to_pairs(value):
        return (
            value.reshape(blocks_here, STRETCH, PAIRS, 2, HEAD_WIDTH)
            .transpose(0, 2, 3, 1, 4)
            .reshape(blocks_here, PAIRS, 2 * STRETCH, HEAD_WIDTH)
        )

    attn_out = from_pairs(attended[..., :HEAD_WIDTH].astype(BF16))
    middle_rows, back, gain_ffn, d_heads, output_grad, mixed, collected = middle(
        lines, slice_width, attn_out, states, out_grad, gains[1:2], w_output, w_hidden, down_grads
    )
    d_pairs = to_pairs(d_heads)
    delta = jnp.sum(d_pairs.astype(F32) * attended[..., :HEAD_WIDTH], axis=-1)
    d_query, d_keyvalue = attend_back(
        counts,
        slots,
        parity,
        queries,
        d_pairs,
        attended[..., HEAD_WIDTH][:, :, None, :],
        delta[:, :, None, :],
        keyvalues,
    )
    result, states_grad, g_attend, g_output, g_kv, small = tail(
        lines,
        heads_here,
        d_keyvalue.reshape(dp_ranks * token_rows, 4 * HEAD_WIDTH),
        d_query,
        lin,
        attn_in,
        output_grad,
        attn_out,
        w_attend,
        back,
        gains,
        gain_ffn,
        states,
        middle_rows,
        mixed,
        cosine,
        sine,
        head_gain[None],
        w_hidden,
    )

    def hidden_grad(index):
        piece = collected[:, index * slice_width : (index + 1) * slice_width]
        return piece.transpose(2, 0, 1).astype(F32).reshape(1, weight_rows, hidden)

    d_keyvalue_matrix = jnp.zeros((weight_rows, 2 * value_start), F32)
    for other in range(tensor_ranks):
        start = (other * heads_here) // sharing_count * HEAD_WIDTH
        block = g_kv[other].astype(F32)
        for offset, piece in (
            (start, block[:, : 2 * HEAD_WIDTH]),
            (value_start + start, block[:, 2 * HEAD_WIDTH :]),
        ):
            after = 2 * value_start - offset - 2 * HEAD_WIDTH
            d_keyvalue_matrix += jnp.pad(piece, ((0, 0), (offset, after)))
    head_gains = small[2, : head_width + 2 * HEAD_WIDTH].reshape(-1, HEAD_WIDTH)
    d_gains = lax.dynamic_slice_in_dim(small[:2], rank * weight_rows, weight_rows, 1).T
    return (
        result,
        states_grad.astype(F32),
        g_attend[None],
        d_keyvalue_matrix[None],
        g_output[None],
        hidden_grad(0),
        hidden_grad(1),
        hidden_grad(2),
        d_gains[None],
        jnp.sum(head_gains[:heads_here], axis=0)[None],
        jnp.sum(head_gains[heads_here:], axis=0)[None],
    )


def local_permutes(
    states,
    query_weight,
    keyvalue_matrix,
    output_weight,
    gate_weight,
    up_weight,
    down_weight,
    norm_gains,
    query_gain,
    key_gain,
    slot_sequence,
    slot_offset,
    out_grad,
):
    token_rows, width = states.shape
    dp_ranks = lax.axis_size("dp")
    tensor_ranks = lax.axis_size("tensor")
    lines = dp_ranks // PLANES
    rank, part = lax.axis_index("dp"), lax.axis_index("tensor")
    plane, line = rank // lines, rank % lines
    quarter = token_rows // tensor_ranks
    heads_here = QUERY_HEADS // tensor_ranks
    head_width = heads_here * HEAD_WIDTH
    sharing_count = QUERY_HEADS // KEYVALUE_HEADS
    blocks_here = token_rows // STRETCH
    slot_count = slot_sequence.shape[0]
    hidden = gate_weight.shape[2]
    slice_width = hidden // PLANES
    weight_rows = width // dp_ranks

    def send(value, kz=0, ky=0, kx=0, kc=0):
        move_rank, move_part = kz * lines + ky, kx * 2 + kc
        pairs = [
            (r * tensor_ranks + p, (r ^ move_rank) * tensor_ranks + (p ^ move_part))
            for r in range(dp_ranks)
            for p in range(tensor_ranks)
        ]
        return lax.ppermute(value, ("dp", "tensor"), pairs)

    def gather_planes(value):
        near = send(value, kz=1)
        far = send(value, kz=2)
        return [value, near, far, send(far, kz=1)]

    def gather_dp(value):
        whole = jnp.zeros((dp_ranks, *value.shape), value.dtype)
        for kz, piece in enumerate(gather_planes(value)):
            for ky in range(lines):
                got = send(piece, ky=ky) if ky else piece
                whole = lax.dynamic_update_index_in_dim(whole, got, rank ^ (kz * lines + ky), 0)
        return whole

    def rounded(value):
        return value.astype(BF16)

    def scatter_dp(whole):
        def piece(move):
            return lax.dynamic_index_in_dim(whole, rank ^ move, 0, keepdims=False)

        parts = []
        for kz in range(PLANES):
            total = piece(kz * lines).astype(F32)
            for ky in range(1, lines):
                total = total + send(rounded(piece(kz * lines + ky)), ky=ky).astype(F32)
            parts.append(total)
        return scatter_planes(parts)

    def scatter_planes(parts):
        near = parts[0] + send(rounded(parts[1]), kz=1).astype(F32)
        far = parts[2] + send(rounded(parts[3]), kz=1).astype(F32)
        return near + send(rounded(far), kz=2).astype(F32)

    def scatter_tensor(blocks):
        got = send(rounded(jnp.concatenate([blocks[1], blocks[3]], axis=0)), kc=1).astype(F32)
        rows = blocks[0].shape[0]
        here = blocks[0] + got[:rows]
        there = blocks[2] + got[rows:]
        return here + send(rounded(there), kx=1).astype(F32)

    def gather_tensor(block):
        both = jnp.concatenate([block, send(block, kx=1)], axis=0)
        return jnp.concatenate([both, send(both, kc=1)], axis=0)

    def in_order(blocks):
        whole = jnp.zeros_like(blocks)
        for index, move in enumerate((0, 2, 1, 3)):
            whole = lax.dynamic_update_slice_in_dim(
                whole,
                blocks[index * quarter : (index + 1) * quarter],
                (part ^ move) * quarter,
                0,
            )
        return whole

    def quarters(value):
        return [
            lax.dynamic_slice_in_dim(value, (part ^ move) * quarter, quarter, 0)
            for move in range(tensor_ranks)
        ]

    sequence_here = lax.dynamic_slice_in_dim(slot_sequence, rank * blocks_here, blocks_here)
    offset_here = lax.dynamic_slice_in_dim(slot_offset, rank * blocks_here, blocks_here)
    counts = offset_here // STRETCH + 1
    places = jnp.arange(slot_count, dtype=jnp.int32)
    same = (slot_sequence[None, None, :] == sequence_here[:, None, None]) & (
        slot_offset[None, None, :] == places[None, :, None] * STRETCH
    )
    slots = jnp.sum(jnp.where(same, places[None, None, :], 0), axis=2).astype(jnp.int32)
    parity = jnp.reshape(part % 2, (1,)).astype(jnp.int32)
    positions = (offset_here[:, None] + jnp.arange(STRETCH, dtype=jnp.int32)[None, :]).reshape(-1)
    cosines, sines = angles(positions, HEAD_WIDTH)

    first_key = (part * heads_here) // sharing_count * HEAD_WIDTH
    value_start = KEYVALUE_HEADS * HEAD_WIDTH
    kv_columns = [
        lax.dynamic_slice_in_dim(keyvalue_matrix[0], first_key, 2 * HEAD_WIDTH, 1),
        lax.dynamic_slice_in_dim(keyvalue_matrix[0], value_start + first_key, 2 * HEAD_WIDTH, 1),
    ]
    gains = gather_dp(norm_gains[0].T).transpose(1, 0, 2).reshape(2, width).astype(F32)
    w_attend = gather_dp(jnp.concatenate([query_weight[0], *kv_columns], axis=1)).reshape(width, -1)
    w_output = gather_dp(output_weight[0]).reshape(width, head_width)

    def sliced(weight):
        return weight[0].reshape(weight_rows, PLANES, slice_width).transpose(1, 0, 2)

    pad_first = -2 * slice_width % 128
    pad_second = -slice_width % 128
    packed = jnp.concatenate(
        [
            sliced(gate_weight),
            sliced(up_weight),
            jnp.zeros((PLANES, weight_rows, pad_first), BF16),
            sliced(down_weight),
            jnp.zeros((PLANES, weight_rows, pad_second), BF16),
        ],
        axis=2,
    )
    w_hidden = jnp.zeros((dp_ranks, weight_rows, packed.shape[2]), BF16)
    for kz in range(PLANES):
        piece = lax.dynamic_index_in_dim(packed, plane ^ kz, 0, keepdims=False)
        piece = send(piece, kz=kz) if kz else piece
        for ky in range(lines):
            got = send(piece, ky=ky) if ky else piece
            w_hidden = lax.dynamic_update_index_in_dim(w_hidden, got, rank ^ (kz * lines + ky), 0)
    w_hidden = w_hidden.reshape(width, -1)
    down_start = 2 * slice_width + pad_first
    w_gate_up = w_hidden[:, : 2 * slice_width]
    w_down = w_hidden[:, down_start : down_start + slice_width]

    def gather_group(block):
        return [gather_tensor(piece) for piece in gather_planes(block)]

    def quarter_of(value):
        return lax.dynamic_slice_in_dim(value, part * quarter, quarter, 0)

    query_g, key_g = query_gain[0], key_gain[0]
    attn_in = rounded(normed(states.astype(F32), gains[0]))
    lin = product(attn_in, w_attend)
    query_lin, keyvalue_lin = lin[:, :head_width], lin[:, head_width:]

    def query_side(linear, gain_vector):
        return rotated(
            normed(linear.reshape(token_rows, heads_here, HEAD_WIDTH), gain_vector), cosines, sines
        )

    def key_side(linear, gain_vector):
        keys = linear[:, : 2 * HEAD_WIDTH].reshape(token_rows, 2, HEAD_WIDTH)
        keys = rotated(normed(keys, gain_vector), cosines, sines)
        return jnp.concatenate(
            [keys.reshape(token_rows, 2 * HEAD_WIDTH), linear[:, 2 * HEAD_WIDTH :]], axis=1
        )

    def to_pairs(value):
        return (
            value.reshape(blocks_here, STRETCH, PAIRS, 2, -1)
            .transpose(0, 2, 3, 1, 4)
            .reshape(blocks_here, PAIRS, 2 * STRETCH, -1)
        )

    def from_pairs(value):
        return (
            value.reshape(blocks_here, PAIRS, 2, STRETCH, -1)
            .transpose(0, 3, 1, 2, 4)
            .reshape(token_rows, heads_here, -1)
        )

    queries = to_pairs(rounded(query_side(query_lin, query_g)))
    keyvalues = gather_dp(rounded(key_side(keyvalue_lin, key_g)))
    keyvalues = keyvalues.reshape(slot_count, STRETCH, 4 * HEAD_WIDTH)
    attended = attend(counts, slots, parity, queries, keyvalues)
    attn_out = rounded(from_pairs(attended[..., :HEAD_WIDTH]).reshape(token_rows, head_width))
    logs = attended[..., HEAD_WIDTH]

    branch = scatter_tensor(quarters(by_cols(attn_out, w_output)))
    states_quarter = quarter_of(states).astype(F32)
    middle = states_quarter + branch
    ffn_in = rounded(normed(middle, gains[1]))

    down_grads = gather_group(quarter_of(out_grad))
    ffn_ins = gather_group(ffn_in)
    mixed_chunks, d_chunks, back_parts, out_parts = [], [], [], []
    for down_grad, ffn_chunk in zip(down_grads, ffn_ins):
        gate_up = product(ffn_chunk, w_gate_up)
        gate_pre, up_pre = gate_up[:, :slice_width], gate_up[:, slice_width:]
        sigmoid_gate = jax.nn.sigmoid(gate_pre)
        mixed = rounded(gate_pre * sigmoid_gate * up_pre)
        d_mixed = product(down_grad, w_down)
        d_gate = d_mixed * up_pre * sigmoid_gate * (1.0 + gate_pre * (1.0 - sigmoid_gate))
        d_up = d_mixed * gate_pre * sigmoid_gate
        d_gate_up = jnp.concatenate([rounded(d_gate), rounded(d_up)], axis=1)
        mixed_chunks.append(mixed)
        d_chunks.append(d_gate_up)

        def reduced(value):
            blocks = value.reshape(4, quarter, width)
            return scatter_tensor([blocks[0], blocks[2], blocks[1], blocks[3]])

        back_parts.append(reduced(by_cols(d_gate_up, w_gate_up)))
        out_parts.append(reduced(by_cols(mixed, w_down)))
    d_ffn_in = scatter_planes(back_parts)

    def norm_back(vector, gain_vector, grad):
        inverse = lax.rsqrt(jnp.mean(vector * vector, axis=-1, keepdims=True) + EPSILON)
        unit = vector * inverse
        scaled = grad * gain_vector
        back = inverse * (scaled - unit * jnp.mean(scaled * unit, axis=-1, keepdims=True))
        return back, jnp.sum(grad * unit, axis=0)

    d_middle, d_gain_ffn = norm_back(middle, gains[1], d_ffn_in)
    grad_middle = quarter_of(out_grad).astype(F32) + d_middle
    output_grad = in_order(gather_tensor(rounded(grad_middle)))

    d_wout = by_rows(output_grad, attn_out)
    d_heads = rounded(product(output_grad, w_output)).reshape(token_rows, heads_here, HEAD_WIDTH)
    d_pairs = to_pairs(d_heads)
    delta = jnp.sum(d_pairs.astype(F32) * attended[..., :HEAD_WIDTH], axis=-1)
    d_query, d_keyvalue = attend_back(
        counts,
        slots,
        parity,
        queries,
        d_pairs,
        logs[:, :, None, :],
        delta[:, :, None, :],
        keyvalues,
    )
    d_keyvalue_here = scatter_dp(d_keyvalue.reshape(dp_ranks, token_rows, 4 * HEAD_WIDTH))
    _, query_pull = jax.vjp(query_side, query_lin, query_g)
    d_query_lin, d_querygain = query_pull(from_pairs(d_query))
    _, key_pull = jax.vjp(key_side, keyvalue_lin, key_g)
    d_keyvalue_lin, d_keygain = key_pull(d_keyvalue_here)
    d_lin = jnp.concatenate([rounded(d_query_lin), rounded(d_keyvalue_lin)], axis=1)
    d_attn_in = scatter_tensor(quarters(by_cols(d_lin, w_attend)))
    d_states, d_gain_attn = norm_back(states_quarter, gains[0], d_attn_in)
    states_grad = in_order(gather_tensor(rounded(grad_middle + d_states))).astype(F32)

    d_wattend = scatter_dp(by_rows(attn_in, d_lin).reshape(dp_ranks, weight_rows, -1))
    d_wout = scatter_dp(d_wout.reshape(dp_ranks, weight_rows, -1))
    ffn_all = jnp.concatenate(ffn_ins, axis=0)
    down_all = jnp.concatenate(down_grads, axis=0)
    grads_hidden = jnp.concatenate(
        [
            by_rows(ffn_all, jnp.concatenate(d_chunks, axis=0)),
            by_rows(down_all, jnp.concatenate(mixed_chunks, axis=0)),
        ],
        axis=1,
    ).reshape(dp_ranks, weight_rows, 3 * slice_width)
    collected = jnp.zeros((PLANES, weight_rows, 3 * slice_width), F32)
    for kz in range(PLANES):
        total = lax.dynamic_index_in_dim(grads_hidden, rank ^ (kz * lines), 0, keepdims=False)
        for ky in range(1, lines):
            piece = lax.dynamic_index_in_dim(
                grads_hidden, rank ^ (kz * lines + ky), 0, keepdims=False
            )
            total = total + send(rounded(piece), ky=ky).astype(F32)
        if kz:
            total = send(rounded(total), kz=kz).astype(F32)
        collected = lax.dynamic_update_index_in_dim(collected, total, plane ^ kz, 0)

    def unsliced(index):
        piece = collected[:, :, index * slice_width : (index + 1) * slice_width]
        return piece.transpose(1, 0, 2).reshape(1, weight_rows, hidden)

    kv_grad = d_wattend[:, head_width:]
    spread = jnp.zeros((weight_rows, 2 * value_start), F32)
    spread = lax.dynamic_update_slice_in_dim(spread, kv_grad[:, : 2 * HEAD_WIDTH], first_key, 1)
    spread = lax.dynamic_update_slice_in_dim(
        spread, kv_grad[:, 2 * HEAD_WIDTH :], value_start + first_key, 1
    )
    d_wkeyvalue = lax.psum(spread, "tensor")

    result_quarter = rounded(middle + scatter_planes(out_parts))
    result = in_order(gather_tensor(result_quarter))

    small = jnp.concatenate([d_gain_attn, d_gain_ffn, d_querygain, d_keygain])
    small = lax.psum(small, ("dp", "tensor"))
    d_gains = lax.dynamic_slice_in_dim(
        small[: 2 * width].reshape(2, width), rank * weight_rows, weight_rows, 1
    ).T
    return (
        result,
        states_grad,
        d_wattend[None, :, :head_width],
        d_wkeyvalue[None],
        d_wout[None],
        unsliced(0),
        unsliced(1),
        unsliced(2),
        d_gains[None],
        small[2 * width : 2 * width + HEAD_WIDTH][None],
        small[2 * width + HEAD_WIDTH :][None],
    )


def local(*arguments):
    rows = arguments[0].shape[1] // lax.axis_size("dp")
    if lax.axis_size("dp") == 2 * PLANES and lax.axis_size("tensor") == 4 and rows % 128 == 0:
        return local_kernels(*arguments)
    return local_permutes(*arguments)


def solution(mesh):
    return jax.shard_map(
        local,
        mesh=mesh,
        in_specs=(
            P("dp", None),
            P(None, "dp", "tensor"),
            P(None, "dp", None),
            P(None, "dp", "tensor"),
            P(None, "dp", "tensor"),
            P(None, "dp", "tensor"),
            P(None, "dp", "tensor"),
            P(None, "dp", None),
            P(),
            P(),
            P(),
            P(),
            P("dp", None),
        ),
        out_specs=(
            P("dp", None),
            P("dp", None),
            P(None, "dp", "tensor"),
            P(None, "dp", None),
            P(None, "dp", "tensor"),
            P(None, "dp", "tensor"),
            P(None, "dp", "tensor"),
            P(None, "dp", "tensor"),
            P(None, "dp", None),
            P(),
            P(),
        ),
        check_vma=False,
    )
```

```python
import functools

import jax
import jax.numpy as jnp
from jax import lax
from jax.experimental import pallas as pl
from jax.experimental.pallas import tpu as pltpu
from jax.sharding import PartitionSpec as P

QUERY_HEADS = 24
KEYVALUE_HEADS = 6
HEAD_WIDTH = 64
STRETCH = 128
EPSILON = 1e-06
PLANES = 4
PAIRS = 3
LONGEST = 12
LOG2E = 1.4426950408889634
BF16 = jnp.bfloat16
F32 = jnp.float32


def product(left_side, right_side):
    return jnp.dot(left_side, right_side, preferred_element_type=F32)


def by_rows(left_side, right_side):
    return lax.dot_general(
        left_side, right_side, (((0,), (0,)), ((), ())), preferred_element_type=F32
    )


def by_cols(left_side, right_side):
    return lax.dot_general(
        left_side, right_side, (((1,), (1,)), ((), ())), preferred_element_type=F32
    )


def normed(vector, gain_vector):
    return (
        vector
        * lax.rsqrt(jnp.mean(vector * vector, axis=-1, keepdims=True) + EPSILON)
        * gain_vector
    )


def angles(positions, head_size):
    frequency = 10000.0 ** (-jnp.arange(head_size // 2, dtype=F32) * 2.0 / head_size)
    phase_angle = positions.astype(F32)[:, None] * frequency[None, :]
    return (jnp.cos(phase_angle)[:, None, :], jnp.sin(phase_angle)[:, None, :])


def rotated(vector, cosines, sines):
    half_width = vector.shape[-1] // 2
    front = vector[..., :half_width]
    behind = vector[..., half_width:]
    return jnp.concatenate(
        [front * cosines - behind * sines, behind * cosines + front * sines], axis=-1
    )


def visible_mask(shape, key_axis):
    keys = lax.broadcasted_iota(jnp.int32, shape, key_axis)
    queries = lax.rem(lax.broadcasted_iota(jnp.int32, shape, 1 - key_axis), STRETCH)
    return keys <= queries


def attend_kernel(count_ref, slots_ref, parity_ref, q_ref, kv_ref, out_ref, acc_ref):
    odd = parity_ref[0] == 1
    ones = jnp.ones((STRETCH, HEAD_WIDTH), BF16)

    def add_block(block, slot, last):
        tile = kv_ref[slot]
        keys = [tile[:, :64], tile[:, 64:128]]
        values = [
            jnp.concatenate([tile[:, 128:192], ones], axis=1),
            jnp.concatenate([tile[:, 192:256], ones], axis=1),
        ]
        middle_key = jnp.where(odd, keys[1], keys[0])
        middle_value = jnp.where(odd, values[1], values[0])
        for pair, key, value in (
            (0, keys[0], values[0]),
            (1, middle_key, middle_value),
            (2, keys[1], values[1]),
        ):
            scores = by_cols(q_ref[block, pair], key)
            weights = jnp.exp2(scores * (LOG2E * HEAD_WIDTH**-0.5))
            if last:
                weights = jnp.where(visible_mask(weights.shape, 1), weights, 0.0)
            acc_ref[pair] += product(weights.astype(BF16), value)

    def one_block(block, carry):
        acc_ref[...] = jnp.zeros_like(acc_ref)
        count = count_ref[block]

        def step(index, inner):
            add_block(block, slots_ref[block, index], False)
            return inner

        lax.fori_loop(0, count - 1, step, 0)
        add_block(block, slots_ref[block, count - 1], True)
        for pair in range(PAIRS):
            total = acc_ref[pair]
            denominator = total[:, HEAD_WIDTH:]
            out_ref[block, pair] = jnp.concatenate(
                [total[:, :HEAD_WIDTH] / denominator, jnp.log2(denominator)], axis=1
            )
        return carry

    lax.fori_loop(0, q_ref.shape[0], one_block, 0)


def attend(counts, slots, parity, queries, keyvalues):
    blocks = queries.shape[0]
    smem = pl.BlockSpec(memory_space=pltpu.SMEM)
    vmem = pl.BlockSpec(memory_space=pltpu.VMEM)
    return pl.pallas_call(
        attend_kernel,
        out_shape=jax.ShapeDtypeStruct((blocks, PAIRS, 2 * STRETCH, 128), F32),
        in_specs=[smem, smem, smem, vmem, vmem],
        out_specs=vmem,
        scratch_shapes=[pltpu.VMEM((PAIRS, 2 * STRETCH, 128), F32)],
        compiler_params=pltpu.CompilerParams(vmem_limit_bytes=40 << 20),
        cost_estimate=pl.CostEstimate(
            flops=4 * 20 * PAIRS * 256 * 128 * 64 * 4, bytes_accessed=8 << 20, transcendentals=0
        ),
        name="attend",
    )(counts, slots, parity, queries, keyvalues)


def attend_back_kernel(
    count_ref, slots_ref, parity_ref, q_ref, do_ref, log_ref, delta_ref, kv_ref, dq_ref, dkv_ref
):
    odd = parity_ref[0] == 1
    scale = HEAD_WIDTH**-0.5
    dq_ref[...] = jnp.zeros_like(dq_ref)
    dkv_ref[...] = jnp.zeros_like(dkv_ref)

    def add_block(block, slot, last):
        tile = kv_ref[slot]
        keys = [tile[:, :64], tile[:, 64:128]]
        values = [tile[:, 128:192], tile[:, 192:256]]
        middle_key = jnp.where(odd, keys[1], keys[0])
        middle_value = jnp.where(odd, values[1], values[0])
        d_keys, d_values = [], []
        for pair, key, value in (
            (0, keys[0], values[0]),
            (1, middle_key, middle_value),
            (2, keys[1], values[1]),
        ):
            query, d_out = q_ref[block, pair], do_ref[block, pair]
            scores = by_cols(key, query)
            weights = jnp.exp2(scores * (LOG2E * scale) - log_ref[block, pair])
            if last:
                weights = jnp.where(visible_mask(weights.shape, 0), weights, 0.0)
            d_weights = by_cols(value, d_out)
            d_scores = (weights * (d_weights - delta_ref[block, pair])).astype(BF16)
            d_values.append(product(weights.astype(BF16), d_out))
            d_keys.append(product(d_scores, query))
            dq_ref[block, pair] += by_rows(d_scores, key) * scale
        zero = jnp.zeros((STRETCH, HEAD_WIDTH), F32)
        parts = [
            (d_keys[0] + jnp.where(odd, zero, d_keys[1])) * scale,
            (d_keys[2] + jnp.where(odd, d_keys[1], zero)) * scale,
            d_values[0] + jnp.where(odd, zero, d_values[1]),
            d_values[2] + jnp.where(odd, d_values[1], zero),
        ]
        dkv_ref[slot] += jnp.concatenate(parts, axis=1)

    def one_block(block, carry):
        count = count_ref[block]

        def step(index, inner):
            add_block(block, slots_ref[block, index], False)
            return inner

        lax.fori_loop(0, count - 1, step, 0)
        add_block(block, slots_ref[block, count - 1], True)
        return carry

    lax.fori_loop(0, q_ref.shape[0], one_block, 0)


def attend_back(counts, slots, parity, queries, d_out, logs, delta, keyvalues):
    blocks = queries.shape[0]
    smem = pl.BlockSpec(memory_space=pltpu.SMEM)
    vmem = pl.BlockSpec(memory_space=pltpu.VMEM)
    return pl.pallas_call(
        attend_back_kernel,
        out_shape=(
            jax.ShapeDtypeStruct((blocks, PAIRS, 2 * STRETCH, HEAD_WIDTH), F32),
            jax.ShapeDtypeStruct(keyvalues.shape, F32),
        ),
        in_specs=[smem] * 3 + [vmem] * 5,
        out_specs=(vmem, vmem),
        compiler_params=pltpu.CompilerParams(vmem_limit_bytes=56 << 20),
        cost_estimate=pl.CostEstimate(
            flops=10 * 20 * PAIRS * 256 * 128 * 64 * 4, bytes_accessed=8 << 20, transcendentals=0
        ),
        name="attend_back",
    )(counts, slots, parity, queries, d_out, logs, delta, keyvalues)


class Place:
    def __init__(self, lines):
        rank, part = lax.axis_index("dp"), lax.axis_index("tensor")
        self.lines = lines
        self.z, self.y = rank // lines, lax.rem(rank, lines)
        self.x, self.c = part // 2, lax.rem(part, 2)
        self.quarter = self.c * 2 + self.x

    def plane(self, move):
        if move == 0:
            return self.z
        if move == 1:
            return self.z + 1 - 2 * lax.rem(self.z, 2)
        if move == 2:
            return self.z + 2 - 4 * (self.z // 2)
        return 3 - self.z

    def to(self, kz=0, ky=0, kx=0, kc=0):
        y = 1 - self.y if ky else self.y
        x = 1 - self.x if kx else self.x
        c = 1 - self.c if kc else self.c
        return (self.plane(kz) * self.lines + y, x * 2 + c)


class Links:
    def __init__(self, place, send_sems, recv_sems):
        self.place, self.send_sems, self.recv_sems = place, send_sems, recv_sems
        self.number, self.unsent = 0, []

    def greet(self, moves):
        barrier = pltpu.get_barrier_semaphore()
        for move in moves:
            pl.semaphore_signal(
                barrier, inc=1, device_id=self.place.to(**move), device_id_type=pl.DeviceIdType.MESH
            )
        pl.semaphore_wait(barrier, len(moves))

    def send(self, source, target, **move):
        number, self.number = self.number, self.number + 1
        copy = pltpu.make_async_remote_copy(
            src_ref=source,
            dst_ref=target,
            send_sem=self.send_sems.at[number],
            recv_sem=self.recv_sems.at[number],
            device_id=self.place.to(**move),
            device_id_type=pl.DeviceIdType.MESH,
        )
        copy.start()
        self.unsent.append(copy)
        return copy

    def sent(self, copy):
        copy.wait_send()
        self.unsent = [other for other in self.unsent if other is not copy]

    def finish(self):
        for copy in self.unsent:
            copy.wait_send()


def rows_at(index, size):
    return pl.ds(pl.multiple_of(index * size, size), size)


class Gather:
    def __init__(self, links, block, own=None):
        self.links, self.block, self.y = links, block, links.place.y
        self.own = block(0, self.y) if own is None else own
        self.lines = []

    def over_lines(self, move):
        place = self.block(move, self.y)
        source = self.own if move == 0 else place
        self.lines.append(self.links.send(source, place, ky=1))

    def start(self):
        place = self.block(0, self.y)
        self.far = self.links.send(self.own, place, kz=2)
        self.near = self.links.send(self.own, place, kz=1)
        self.over_lines(0)

    def relay(self):
        self.near.wait_recv()
        self.over_lines(1)
        self.far.wait_recv()
        place = self.block(2, self.y)
        self.corner = self.links.send(place, place, kz=1)
        self.over_lines(2)

    def last(self):
        self.corner.wait_recv()
        self.over_lines(3)

    def finish(self):
        for copy in self.lines:
            copy.wait_recv()


def head_mean(value):
    row = lax.broadcasted_iota(jnp.int32, (128, 128), 0) // HEAD_WIDTH
    column = lax.broadcasted_iota(jnp.int32, (128, 128), 1) // HEAD_WIDTH
    average = jnp.where(row == column, 1.0 / HEAD_WIDTH, 0.0).astype(F32)
    return jnp.dot(
        value, average, preferred_element_type=F32, precision=lax.Precision.HIGHEST
    )


def halves_swapped(value):
    first = lax.rem(lax.broadcasted_iota(jnp.int32, value.shape, 1), HEAD_WIDTH) < HEAD_WIDTH // 2
    return jnp.where(
        first,
        pltpu.roll(value, 128 - HEAD_WIDTH // 2, 1),
        pltpu.roll(value, HEAD_WIDTH // 2, 1),
    )


class Scatter:
    ORDER = (3, 1, 2, 0)

    def __init__(self, links, y_out, y_in, z_out, z_in, sums):
        self.links = links
        self.y_out, self.y_in, self.z_out, self.z_in, self.sums = y_out, y_in, z_out, z_in, sums
        self.lines, self.planes = {}, {}

    def start(self, move, block):
        self.y_out[move] = block.astype(BF16)
        self.lines[move] = self.links.send(self.y_out.at[move], self.y_in.at[move], ky=1)

    def add(self, move, block):
        self.lines[move].wait_recv()
        total = block + self.y_in[move].astype(F32)
        if move in (3, 1):
            slot = 0 if move == 1 else 1
            self.z_out[slot] = total.astype(BF16)
            self.planes[slot] = self.links.send(self.z_out.at[slot], self.z_in.at[slot], kz=1)
        elif move == 2:
            self.planes[1].wait_recv()
            self.z_out[2] = (total + self.z_in[1].astype(F32)).astype(BF16)
            self.planes[2] = self.links.send(self.z_out.at[2], self.z_in.at[2], kz=2)
        else:
            self.sums[...] = total

    def finish(self):
        self.planes[0].wait_recv()
        self.planes[2].wait_recv()
        return self.sums[...] + self.z_in[0].astype(F32) + self.z_in[2].astype(F32)


def scatter_scratch(block):
    return [
        pltpu.VMEM((4, *block), BF16),
        pltpu.VMEM((4, *block), BF16),
        pltpu.VMEM((3, *block), BF16),
        pltpu.VMEM((3, *block), BF16),
        pltpu.VMEM(block, F32),
    ]


FORWARD_COPIES = 100


def forward_kernel(
    lines,
    heads,
    slice_width,
    longest,
    sequence_ref,
    offset_ref,
    states_ref,
    gains_in,
    w_attend_in,
    cosine_ref,
    sine_ref,
    head_gain_ref,
    w_output_in,
    w_hidden_in,
    grad_any,
    lin_ref,
    attn_in_ref,
    query_ref,
    kv_ref,
    attended_ref,
    attn_out_ref,
    gains_ref,
    w_attend_ref,
    middle_ref,
    back_ref,
    gain_out_ref,
    d_heads_ref,
    output_grad_ref,
    mixed_ref,
    collected_ref,
    table_ref,
    w_down_any,
    acc_ref,
    w_output_ref,
    w_hidden_ref,
    down_ref,
    ffn_ref,
    d_hidden_ref,
    partial_ref,
    core_out,
    core_in,
    x_out,
    x_in,
    sums_ref,
    z_out,
    z_in,
    y_out,
    y_in,
    local_sems,
    send_sems,
    recv_sems,
):
    here = Place(lines)
    links = Links(here, send_sems, recv_sems)
    token_rows, width = states_ref.shape
    quarter = token_rows // 4
    half = 2 * quarter
    weight_rows = w_attend_in.shape[0]
    hidden = slice_width
    blocks = token_rows // STRETCH
    slot_count = offset_ref.shape[0]
    mine, my_half = rows_at(here.quarter, quarter), rows_at(here.c, half)
    other_half = rows_at(1 - here.c, half)
    x_mine, x_other = rows_at(here.x, quarter), rows_at(1 - here.x, quarter)
    odd = here.c == 1

    def rank(move, line):
        return here.plane(move) * lines + line

    def rows_of(ref, columns=slice(None)):
        return lambda move, line: ref.at[rows_at(rank(move, line), weight_rows), columns]

    def columns_of(ref):
        return lambda move, line: ref.at[:, rows_at(rank(move, line), weight_rows)]

    loads = [
        pltpu.make_async_copy(grad_any, down_ref.at[here.z], local_sems.at[0]),
        pltpu.make_async_copy(w_output_in, rows_of(w_output_ref)(0, here.y), local_sems.at[1]),
        pltpu.make_async_copy(
            w_hidden_in.at[here.z], columns_of(w_hidden_ref)(0, here.y), local_sems.at[2]
        ),
    ]
    for load in loads:
        load.start()
    links.greet([dict(kc=1), dict(kx=1), dict(ky=1), dict(kz=1), dict(kz=2), dict(kz=3)])

    kv_width = 4 * HEAD_WIDTH
    gains = Gather(links, columns_of(gains_ref), gains_in)
    gains.start()
    first, second = slice(0, kv_width), slice(kv_width, w_attend_in.shape[1])
    kv_weights = Gather(links, rows_of(w_attend_ref, first), w_attend_in.at[:, first])
    kv_weights.start()
    query_weights = Gather(links, rows_of(w_attend_ref, second), w_attend_in.at[:, second])
    query_weights.start()
    columns_of(gains_ref)(0, here.y)[...] = gains_in[...]
    rows_of(w_attend_ref)(0, here.y)[...] = w_attend_in[...]

    def fill(index, carry):
        block, place = index // longest, lax.rem(index, longest)
        sequence = sequence_ref[rank(0, here.y) * blocks + block]
        found = jnp.int32(0)
        for slot in range(slot_count):
            same = (sequence_ref[slot] == sequence) & (offset_ref[slot] == place * STRETCH)
            found = jnp.where(same, slot, found)
        table_ref[index] = found
        return carry

    lax.fori_loop(0, blocks * longest, fill, 0)
    gains.relay()
    gains.last()
    gains.finish()
    states = states_ref[...].astype(F32)
    inverse = lax.rsqrt(jnp.mean(states * states, axis=-1, keepdims=True) + EPSILON)
    attn_in_ref[...] = (states * inverse * gains_ref[0:1, :]).astype(BF16)

    def turned(value, group):
        value = (
            value
            * lax.rsqrt(head_mean(value * value) + EPSILON)
            * head_gain_ref[:, group * 128 : (group + 1) * 128]
        )
        return (value * cosine_ref[...] + halves_swapped(value) * sine_ref[...]).astype(BF16)

    kv_weights.relay()
    kv_weights.last()
    query_weights.relay()
    kv_weights.finish()
    lin = product(attn_in_ref[...], w_attend_ref[:, first])
    lin_ref[:, first] = lin
    own_blocks = pl.ds(rank(0, here.y) * blocks, blocks)
    kv_ref[own_blocks, :, :128] = turned(lin[:, :128], 0).reshape(blocks, STRETCH, 128)
    kv_ref[own_blocks, :, 128:] = lin[:, 128:].astype(BF16).reshape(blocks, STRETCH, 128)
    keyvalue = Gather(
        links, lambda move, line: kv_ref.at[pl.ds(rank(move, line) * blocks, blocks)]
    )
    keyvalue.start()
    query_weights.last()
    query_weights.finish()
    output = Gather(links, rows_of(w_output_ref), w_output_in)
    output.start()
    lin = product(attn_in_ref[...], w_attend_ref[:, second])
    lin_ref[:, second] = lin
    for pair in range(PAIRS):
        rotated_pair = turned(lin[:, pair * 128 : (pair + 1) * 128], pair + 1)
        for block in range(blocks):
            rows = rotated_pair[block * STRETCH : (block + 1) * STRETCH]
            query_ref[block, pair, :STRETCH] = rows[:, :HEAD_WIDTH]
            query_ref[block, pair, STRETCH:] = rows[:, HEAD_WIDTH:]
    keyvalue.relay()

    planes = [
        links.send(w_hidden_in.at[here.plane(move)], columns_of(w_hidden_ref)(0, here.y), kz=move)
        for move in (1, 2, 3)
    ]
    hidden_lines = []

    def hidden_line(move):
        if move:
            planes[move - 1].wait_recv()
        else:
            loads[2].wait()
        place = columns_of(w_hidden_ref)(move, here.y)
        hidden_lines.append(links.send(place, place, ky=1))

    def down_block(move):
        return down_ref.at[here.plane(move), mine]

    loads[0].wait()
    down_far = links.send(down_block(0), down_block(0), kz=2)
    down_near = links.send(down_block(0), down_block(0), kz=1)
    down_across, down_cores = {}, {}

    def down_x(move):
        down_across[move] = links.send(down_block(move), down_block(move), kx=1)

    def down_core(move):
        down_across[move].wait_recv()
        both = down_ref.at[here.plane(move), my_half]
        down_cores[move] = links.send(both, both, kc=1)

    keyvalue.last()
    hidden_line(0)
    keyvalue.finish()

    ones = jnp.ones((STRETCH, HEAD_WIDTH), BF16)

    def attend_block(block):
        acc_ref[...] = jnp.zeros_like(acc_ref)
        offset = offset_ref[rank(0, here.y) * blocks + block]
        shape = (2 * STRETCH, STRETCH)
        ahead = lax.broadcasted_iota(jnp.int32, shape, 1) - lax.rem(
            lax.broadcasted_iota(jnp.int32, shape, 0), STRETCH
        )

        def step(place, carry):
            slot = table_ref[block * longest + place]
            tile = kv_ref[slot]
            keys = [tile[:, :64], tile[:, 64:128]]
            values = [
                jnp.concatenate([tile[:, 128:192], ones], axis=1),
                jnp.concatenate([tile[:, 192:256], ones], axis=1),
            ]
            middle_key = jnp.where(odd, keys[1], keys[0])
            middle_value = jnp.where(odd, values[1], values[0])
            visible = ahead <= offset - place * STRETCH
            for pair, key, value in (
                (0, keys[0], values[0]),
                (1, middle_key, middle_value),
                (2, keys[1], values[1]),
            ):
                scores = by_cols(query_ref[block, pair], key)
                weights = jnp.exp2(scores * (LOG2E * HEAD_WIDTH**-0.5))
                weights = jnp.where(visible, weights, 0.0)
                acc_ref[pair] += product(weights.astype(BF16), value)
            return carry

        lax.fori_loop(0, longest, step, 0)
        for pair in range(PAIRS):
            total = acc_ref[pair]
            denominator = total[:, HEAD_WIDTH:]
            heads_out = total[:, :HEAD_WIDTH] / denominator
            attended_ref[block, pair] = jnp.concatenate(
                [heads_out, jnp.log2(denominator)], axis=1
            )
            attn_out_ref[
                block * STRETCH : (block + 1) * STRETCH, pair * 128 : (pair + 1) * 128
            ] = jnp.concatenate([heads_out[:STRETCH], heads_out[STRETCH:]], axis=1).astype(BF16)

    attend_block(0)
    output.relay()
    hidden_line(1)
    output.last()
    attend_block(1)
    down_near.wait_recv()
    down_x(1)
    hidden_line(2)
    attend_block(2)
    down_far.wait_recv()
    down_corner = links.send(down_block(2), down_block(2), kz=1)
    down_x(2)

    loads[1].wait()
    output.finish()
    cut = 4
    piece = width // cut
    core_copies = []
    for part in range(cut):
        columns = slice(part * piece, (part + 1) * piece)
        weight = w_output_ref[columns, :]
        core_out[4, :, columns] = by_cols(attn_out_ref[other_half, :], weight).astype(BF16)
        core_copies.append(
            links.send(core_out.at[4, :, columns], core_in.at[4, :, columns], kc=1)
        )
        partial_ref[0, :half, columns] = by_cols(attn_out_ref[my_half, :], weight)
    x_copies = []
    for part in range(cut):
        columns = slice(part * piece, (part + 1) * piece)
        core_copies[part].wait_recv()
        x_out[4, :, columns] = (
            partial_ref[0, x_other, columns] + core_in[4, x_other, columns].astype(F32)
        ).astype(BF16)
        x_copies.append(links.send(x_out.at[4, :, columns], x_in.at[4, :, columns], kx=1))
        middle_ref[:, columns] = (
            states_ref[mine, columns].astype(F32)
            + partial_ref[0, x_mine, columns]
            + core_in[4, x_mine, columns].astype(F32)
        )
    for part in range(cut):
        columns = slice(part * piece, (part + 1) * piece)
        x_copies[part].wait_recv()
        middle_ref[:, columns] += x_in[4, :, columns].astype(F32)
    middle = middle_ref[...]
    inverse = lax.rsqrt(jnp.mean(middle * middle, axis=-1, keepdims=True) + EPSILON)
    ffn_ref[here.z, mine, :] = (middle * inverse * gains_ref[1:2, :]).astype(BF16)

    def block_of(move):
        return ffn_ref.at[here.plane(move), mine]

    far = links.send(block_of(0), block_of(0), kz=2)
    near = links.send(block_of(0), block_of(0), kz=1)
    across = {0: links.send(block_of(0), block_of(0), kx=1)}
    down_core(1)
    hidden_line(3)
    down_corner.wait_recv()
    near.wait_recv()
    across[1] = links.send(block_of(1), block_of(1), kx=1)
    down_x(3)
    far.wait_recv()
    corner = links.send(block_of(2), block_of(2), kz=1)
    across[2] = links.send(block_of(2), block_of(2), kx=1)
    cores = {}

    def spread(move):
        across[move].wait_recv()
        both = ffn_ref.at[here.plane(move), my_half]
        cores[move] = links.send(both, both, kc=1)

    spread(0)
    down_core(2)
    for copy in hidden_lines:
        copy.wait_recv()

    core_copies, x_copies = [], []

    def add_cores(move):
        core_copies[move].wait_recv()
        total_rows = rows_at(here.c * 2 + 1 - here.x, quarter)
        x_out[move] = (
            partial_ref[move % 2, total_rows, :] + core_in[move, x_other, :].astype(F32)
        ).astype(BF16)
        x_copies.append(links.send(x_out.at[move], x_in.at[move], kx=1))
        sums_ref[move] = partial_ref[move % 2, mine, :] + core_in[move, x_mine, :].astype(F32)

    def add_x(move):
        x_copies[move].wait_recv()
        sums_ref[move] += x_in[move].astype(F32)

    for move in range(4):
        if move == 2:
            corner.wait_recv()
            across[3] = links.send(block_of(3), block_of(3), kx=1)
        cores[move].wait_recv()
        if move:
            down_cores[move].wait_recv()
        plane = here.plane(move)
        chunk = ffn_ref[plane]
        gate_pre = by_cols(w_hidden_ref[:hidden, :], chunk)
        up_pre = by_cols(w_hidden_ref[hidden : 2 * hidden, :], chunk)
        sigmoid_gate = 1.0 / (1.0 + jnp.exp(-gate_pre))
        silu = gate_pre * sigmoid_gate
        columns = pl.ds(pl.multiple_of(plane * token_rows, token_rows), token_rows)
        mixed_ref[:, columns] = (silu * up_pre).astype(BF16)
        d_mixed = by_cols(w_hidden_ref[2 * hidden :, :], down_ref[plane])
        d_hidden_ref[:hidden, columns] = (
            d_mixed * up_pre * sigmoid_gate * (1.0 + gate_pre * (1.0 - sigmoid_gate))
        ).astype(BF16)
        d_hidden_ref[hidden:, columns] = (d_mixed * silu).astype(BF16)
        partial_ref[move % 2] = by_rows(d_hidden_ref[:, columns], w_hidden_ref[: 2 * hidden, :])
        core_out[move] = partial_ref[move % 2, other_half, :].astype(BF16)
        core_copies.append(links.send(core_out.at[move], core_in.at[move], kc=1))
        if move == 0:
            down_core(3)
        if move > 0:
            add_cores(move - 1)
        if move + 1 < 4:
            spread(move + 1)
    add_cores(3)

    def gradient(move, line):
        columns = rows_at(rank(move, line), weight_rows)
        first = jnp.zeros((2 * hidden, weight_rows), F32)
        second = jnp.zeros((hidden, weight_rows), F32)
        for plane in range(4):
            tokens = slice(plane * token_rows, (plane + 1) * token_rows)
            first += product(d_hidden_ref[:, tokens], ffn_ref[plane, :, columns])
            second += product(mixed_ref[:, tokens], down_ref[plane, :, columns])
        return first, second

    y_copies = {}
    for move in (3, 2, 1, 0):
        first, second = gradient(move, 1 - here.y)
        y_out[move, : 2 * hidden] = first.astype(BF16)
        y_out[move, 2 * hidden :] = second.astype(BF16)
        y_copies[move] = links.send(y_out.at[move], y_in.at[move], ky=1)

    add_x(1)
    z_out[0] = sums_ref[1].astype(BF16)
    z_copies = [links.send(z_out.at[0], z_in.at[0], kz=1)]
    add_x(0)
    add_x(2)
    add_x(3)
    z_out[1] = sums_ref[3].astype(BF16)
    z_copies.append(links.send(z_out.at[1], z_in.at[1], kz=1))
    z_copies[1].wait_recv()
    z_out[2] = (sums_ref[2] + z_in[1].astype(F32)).astype(BF16)
    z_copies.append(links.send(z_out.at[2], z_in.at[2], kz=2))
    g_copies = []

    def send_gradient(move):
        first, second = gradient(move, here.y)
        y_copies[move].wait_recv()
        target = y_out.at[move] if move else collected_ref.at[here.z]
        if move:
            links.sent(y_copies[move])
        target[: 2 * hidden] = (first + y_in[move, : 2 * hidden].astype(F32)).astype(BF16)
        target[2 * hidden :] = (second + y_in[move, 2 * hidden :].astype(F32)).astype(BF16)
        if move:
            g_copies.append(links.send(target, collected_ref.at[here.z], kz=move))

    send_gradient(3)
    z_copies[0].wait_recv()
    z_copies[2].wait_recv()
    d_normed = sums_ref[0] + z_in[0].astype(F32) + z_in[2].astype(F32)
    middle = middle_ref[...]
    inverse = lax.rsqrt(jnp.mean(middle * middle, axis=-1, keepdims=True) + EPSILON)
    unit = middle * inverse
    gain_out_ref[...] = jnp.sum(d_normed * unit, axis=0, keepdims=True)
    scaled = d_normed * gains_ref[1:2, :]
    back = inverse * (scaled - unit * jnp.mean(scaled * unit, axis=-1, keepdims=True))
    grad_middle = down_ref[here.z, mine, :].astype(F32) + back
    back_ref[...] = grad_middle
    output_grad_ref[mine, :] = grad_middle.astype(BF16)
    block = output_grad_ref.at[mine]
    x_copy = links.send(block, block, kx=1)
    send_gradient(2)
    x_copy.wait_recv()
    both = output_grad_ref.at[my_half]
    core = links.send(both, both, kc=1)
    send_gradient(1)
    send_gradient(0)
    save = pltpu.make_async_copy(
        w_hidden_ref.at[pl.ds(2 * hidden, hidden)], w_down_any, local_sems.at[3]
    )
    save.start()
    core.wait_recv()
    d_heads_ref[...] = product(output_grad_ref[...], w_output_ref[...]).astype(BF16)
    for copy in g_copies:
        copy.wait_recv()
    save.wait()
    links.finish()


def forward(
    lines,
    heads,
    slice_width,
    longest,
    sequence,
    offset,
    states,
    gains,
    w_attend,
    cosine,
    sine,
    head_gain,
    w_output,
    w_hidden,
    grad,
):
    token_rows, width = states.shape
    ranks = 4 * lines
    quarter = token_rows // 4
    half = 2 * quarter
    hidden = slice_width
    head_width = heads * HEAD_WIDTH
    weight_rows = width // ranks
    blocks = token_rows // STRETCH
    vmem = pl.BlockSpec(memory_space=pltpu.VMEM)
    smem = pl.BlockSpec(memory_space=pltpu.SMEM)
    hbm = pl.BlockSpec(memory_space=pl.ANY)
    shape = jax.ShapeDtypeStruct
    return pl.pallas_call(
        functools.partial(forward_kernel, lines, heads, slice_width, longest),
        out_shape=(
            shape((token_rows, w_attend.shape[1]), F32),
            shape((token_rows, width), BF16),
            shape((blocks, PAIRS, 2 * STRETCH, HEAD_WIDTH), BF16),
            shape((ranks * blocks, STRETCH, 4 * HEAD_WIDTH), BF16),
            shape((blocks, PAIRS, 2 * STRETCH, 128), F32),
            shape((token_rows, head_width), BF16),
            shape((gains.shape[0], width), F32),
            shape((width, w_attend.shape[1]), BF16),
            shape((quarter, width), F32),
            shape((quarter, width), F32),
            shape((1, width), F32),
            shape((token_rows, head_width), BF16),
            shape((token_rows, width), BF16),
            shape((hidden, 4 * token_rows), BF16),
            shape((4, 3 * hidden, weight_rows), BF16),
            shape((blocks * longest,), jnp.int32),
            shape((hidden, width), BF16),
        ),
        in_specs=[smem] * 2 + [vmem] * 6 + [hbm] * 3,
        out_specs=(vmem,) * 15 + (smem, hbm),
        scratch_shapes=[
            pltpu.VMEM((PAIRS, 2 * STRETCH, 128), F32),
            pltpu.VMEM((width, head_width), BF16),
            pltpu.VMEM((3 * hidden, width), BF16),
            pltpu.VMEM((4, token_rows, width), BF16),
            pltpu.VMEM((4, token_rows, width), BF16),
            pltpu.VMEM((2 * hidden, 4 * token_rows), BF16),
            pltpu.VMEM((2, token_rows, width), F32),
            pltpu.VMEM((5, half, width), BF16),
            pltpu.VMEM((5, half, width), BF16),
            pltpu.VMEM((5, quarter, width), BF16),
            pltpu.VMEM((5, quarter, width), BF16),
            pltpu.VMEM((4, quarter, width), F32),
            pltpu.VMEM((3, quarter, width), BF16),
            pltpu.VMEM((3, quarter, width), BF16),
            pltpu.VMEM((4, 3 * hidden, weight_rows), BF16),
            pltpu.VMEM((4, 3 * hidden, weight_rows), BF16),
            pltpu.SemaphoreType.DMA((4,)),
            pltpu.SemaphoreType.DMA((FORWARD_COPIES,)),
            pltpu.SemaphoreType.DMA((FORWARD_COPIES,)),
        ],
        compiler_params=pltpu.CompilerParams(
            collective_id=0, has_side_effects=True, vmem_limit_bytes=64 << 20
        ),
        name="forward",
    )(
        sequence,
        offset,
        states,
        gains,
        w_attend,
        cosine,
        sine,
        head_gain,
        w_output,
        w_hidden,
        grad,
    )


BACKWARD_COPIES = 60


def backward_kernel(
    lines,
    heads,
    longest,
    sequence_ref,
    offset_ref,
    table_ref,
    query_ref,
    kv_ref,
    attended_ref,
    d_heads_ref,
    lin_ref,
    attn_in_ref,
    output_grad_ref,
    attn_out_ref,
    w_attend_ref,
    back_ref,
    gains_ref,
    gain_ffn_ref,
    states_ref,
    middle_ref,
    mixed_ref,
    cosine_ref,
    sine_ref,
    head_gain_ref,
    w_down_any,
    result_ref,
    states_grad_ref,
    g_attend_ref,
    g_output_ref,
    g_kv_ref,
    small_ref,
    *scratch,
):
    here = Place(lines)
    (
        w_down_ref,
        d_query_ref,
        d_kv_ref,
        d_lin_ref,
        partial_ref,
        core_out,
        core_in,
        x_out,
        x_in,
        sums_ref,
        z_out,
        z_in,
        small_out,
        small_in,
        local_sems,
        send_sems,
        recv_sems,
    ) = scratch[:17]
    links = Links(here, send_sems, recv_sems)
    kv_sum = Scatter(links, *scratch[17:22])
    output_sum = Scatter(links, *scratch[22:27])
    attend_sum = Scatter(links, *scratch[27:32])
    token_rows, width = states_ref.shape
    quarter = token_rows // 4
    half = 2 * quarter
    weight_rows = width // (4 * lines)
    kv_width = 4 * HEAD_WIDTH
    blocks = token_rows // STRETCH
    mine, other = rows_at(here.quarter, quarter), rows_at(here.c * 2 + 1 - here.x, quarter)
    my_half, other_half = rows_at(here.c, half), rows_at(1 - here.c, half)
    x_mine, x_other = rows_at(here.x, quarter), rows_at(1 - here.x, quarter)
    odd = here.c == 1
    scale = HEAD_WIDTH**-0.5

    load = pltpu.make_async_copy(w_down_any, w_down_ref, local_sems.at[0])
    load.start()
    links.greet([dict(kc=1), dict(kx=1), dict(ky=1), dict(kz=1), dict(kz=2)])

    def rank(move, line):
        return here.plane(move) * lines + line

    core_copies, x_copies = {}, {}
    load.wait()

    def out_start(move, slot):
        at = pl.ds(pl.multiple_of(here.plane(move) * token_rows, token_rows), token_rows)
        partial_ref[slot] = by_rows(mixed_ref[:, at], w_down_ref[...])
        core_out[move] = partial_ref[slot, other_half, :].astype(BF16)
        core_copies[move] = links.send(core_out.at[move], core_in.at[move], kc=1)

    def add_cores(move, slot):
        core_copies[move].wait_recv()
        x_out[move] = (partial_ref[slot, other, :] + core_in[move, x_other, :].astype(F32)).astype(
            BF16
        )
        x_copies[move] = links.send(x_out.at[move], x_in.at[move], kx=1)
        sums_ref[move] = partial_ref[slot, mine, :] + core_in[move, x_mine, :].astype(F32)

    def add_x(move):
        x_copies[move].wait_recv()
        sums_ref[move] += x_in[move].astype(F32)

    def columns(move, line):
        return rows_at(rank(move, line), weight_rows)

    def output_block(move, line):
        return by_rows(output_grad_ref[:, columns(move, line)], attn_out_ref[...])

    def attend_grad(move, line):
        return by_rows(attn_in_ref[:, columns(move, line)], d_lin_ref[...])

    out_start(3, 0)
    out_start(1, 1)
    add_cores(3, 0)
    out_start(2, 0)
    add_cores(1, 1)
    out_start(0, 1)
    for move in Scatter.ORDER:
        output_sum.start(move, output_block(move, 1 - here.y))
    add_cores(2, 0)
    add_cores(0, 1)

    one_row = jnp.ones((8, HEAD_WIDTH), F32)
    pick = jnp.where(
        lax.broadcasted_iota(jnp.int32, (8, HEAD_WIDTH), 1) == 0, 1.0, 0.0
    ).astype(F32)

    def as_row(weights, value):
        return lax.dot_general(
            weights,
            value,
            (((1,), (1,)), ((), ())),
            preferred_element_type=F32,
            precision=lax.Precision.HIGHEST,
        )[:1]

    def attend_block(block):
        offset = offset_ref[rank(0, here.y) * blocks + block]
        rows = slice(block * STRETCH, (block + 1) * STRETCH)
        shape = (STRETCH, 2 * STRETCH)
        ahead = lax.broadcasted_iota(jnp.int32, shape, 0) - lax.rem(
            lax.broadcasted_iota(jnp.int32, shape, 1), STRETCH
        )
        d_outs, deltas, logs = [], [], []
        for pair in range(PAIRS):
            both = d_heads_ref[rows, pair * 128 : (pair + 1) * 128]
            d_out = jnp.concatenate([both[:, :HEAD_WIDTH], both[:, HEAD_WIDTH:]], axis=0)
            kept = attended_ref[block, pair]
            d_outs.append(d_out)
            deltas.append(as_row(one_row, d_out.astype(F32) * kept[:, :HEAD_WIDTH]))
            logs.append(as_row(pick, kept[:, HEAD_WIDTH:]))
            d_query_ref[block, pair] = jnp.zeros((2 * STRETCH, HEAD_WIDTH), F32)

        def step(place, carry):
            slot = table_ref[block * longest + place]
            tile = kv_ref[slot]
            keys = [tile[:, :64], tile[:, 64:128]]
            values = [tile[:, 128:192], tile[:, 192:256]]
            middle_key = jnp.where(odd, keys[1], keys[0])
            middle_value = jnp.where(odd, values[1], values[0])
            visible = ahead <= offset - place * STRETCH
            d_keys, d_values = [], []
            for pair, key, value in (
                (0, keys[0], values[0]),
                (1, middle_key, middle_value),
                (2, keys[1], values[1]),
            ):
                query, d_out = query_ref[block, pair], d_outs[pair]
                scores = by_cols(key, query)
                weights = jnp.exp2(scores * (LOG2E * scale) - logs[pair])
                weights = jnp.where(visible, weights, 0.0)
                d_weights = by_cols(value, d_out)
                d_scores = (weights * (d_weights - deltas[pair])).astype(BF16)
                d_values.append(product(weights.astype(BF16), d_out))
                d_keys.append(product(d_scores, query))
                d_query_ref[block, pair] += by_rows(d_scores, key) * scale
            zero = jnp.zeros((STRETCH, HEAD_WIDTH), F32)
            parts = [
                (d_keys[0] + jnp.where(odd, zero, d_keys[1])) * scale,
                (d_keys[2] + jnp.where(odd, d_keys[1], zero)) * scale,
                d_values[0] + jnp.where(odd, zero, d_values[1]),
                d_values[2] + jnp.where(odd, d_values[1], zero),
            ]
            d_kv_ref[block * longest + place] = jnp.concatenate(parts, axis=1)
            return carry

        lax.fori_loop(0, longest, step, 0)

    attend_block(0)
    add_x(3)
    z_out[1] = sums_ref[3].astype(BF16)
    z_copies = {1: links.send(z_out.at[1], z_in.at[1], kz=1)}
    add_x(1)
    z_out[0] = sums_ref[1].astype(BF16)
    z_copies[0] = links.send(z_out.at[0], z_in.at[0], kz=1)
    for move in Scatter.ORDER[:2]:
        output_sum.add(move, output_block(move, here.y))
    attend_block(1)
    add_x(2)
    z_copies[1].wait_recv()
    z_out[2] = (sums_ref[2] + z_in[1].astype(F32)).astype(BF16)
    z_copies[2] = links.send(z_out.at[2], z_in.at[2], kz=2)
    add_x(0)
    for move in Scatter.ORDER[2:]:
        output_sum.add(move, output_block(move, here.y))
    attend_block(2)

    def kv_block(move, line):
        pieces = []
        for index in range(blocks):
            slot = rank(move, line) * blocks + index
            sequence = sequence_ref[slot]
            place = offset_ref[slot] // STRETCH
            total = jnp.zeros((STRETCH, kv_width), F32)
            for block in range(blocks):
                same = sequence_ref[rank(0, here.y) * blocks + block] == sequence
                total += jnp.where(same, d_kv_ref[block * longest + place], 0.0)
            pieces.append(total)
        return jnp.concatenate(pieces, axis=0)

    for move in Scatter.ORDER:
        kv_sum.start(move, kv_block(move, 1 - here.y))

    def group_back(group, at, grad):
        linear = lin_ref[:, at]
        inverse = lax.rsqrt(head_mean(linear * linear) + EPSILON)
        unit = linear * inverse
        grad = grad * cosine_ref[...] + halves_swapped(grad * sine_ref[...])
        gain = jnp.sum(grad * unit, axis=0, keepdims=True)
        scaled = grad * head_gain_ref[:, group * 128 : (group + 1) * 128]
        return inverse * (scaled - unit * head_mean(scaled * unit)), gain

    small_ref[...] = jnp.zeros_like(small_ref)
    small_ref[1:2, :] = gain_ffn_ref[...]
    for pair in range(PAIRS):
        grad = jnp.concatenate(
            [
                jnp.concatenate(
                    [d_query_ref[block, pair, :STRETCH], d_query_ref[block, pair, STRETCH:]], axis=1
                )
                for block in range(blocks)
            ],
            axis=0,
        )
        at = slice(kv_width + pair * 128, kv_width + (pair + 1) * 128)
        linear_grad, gain = group_back(pair + 1, at, grad)
        d_lin_ref[:, at] = linear_grad.astype(BF16)
        small_ref[2:3, (pair + 1) * 128 : (pair + 2) * 128] = gain
    for move in Scatter.ORDER:
        kv_sum.add(move, kv_block(move, here.y))
    d_kv = kv_sum.finish()
    linear_grad, gain = group_back(0, slice(0, 128), d_kv[:, :128])
    d_lin_ref[:, :128] = linear_grad.astype(BF16)
    d_lin_ref[:, 128:kv_width] = d_kv[:, 128:].astype(BF16)
    small_ref[2:3, :128] = gain

    for move in Scatter.ORDER:
        attend_sum.start(move, attend_grad(move, 1 - here.y))

    partial_ref[0] = by_cols(d_lin_ref[...], w_attend_ref[...])
    core_out[4] = partial_ref[0, other_half, :].astype(BF16)
    core_copies[4] = links.send(core_out.at[4], core_in.at[4], kc=1)
    add_cores(4, 0)
    attend_sum.add(3, attend_grad(3, here.y))
    attend_sum.add(1, attend_grad(1, here.y))
    add_x(4)
    states = states_ref[mine, :].astype(F32)
    inverse = lax.rsqrt(jnp.mean(states * states, axis=-1, keepdims=True) + EPSILON)
    unit = states * inverse
    grad = sums_ref[4]
    small_ref[0:1, :] = jnp.sum(grad * unit, axis=0, keepdims=True)
    scaled = grad * gains_ref[0:1, :]
    total = back_ref[...] + inverse * (
        scaled - unit * jnp.mean(scaled * unit, axis=-1, keepdims=True)
    )
    states_grad_ref[mine, :] = total.astype(BF16)
    block = states_grad_ref.at[mine]
    states_x = links.send(block, block, kx=1)

    def small_step(step, **move):
        small_out[step] = small_ref[...]
        return links.send(small_out.at[step], small_in.at[step], **move)

    small = small_step(0, kc=1)
    attend_sum.add(2, attend_grad(2, here.y))
    z_copies[0].wait_recv()
    z_copies[2].wait_recv()
    result_ref[mine, :] = (
        middle_ref[...] + sums_ref[0] + z_in[0].astype(F32) + z_in[2].astype(F32)
    ).astype(BF16)
    block = result_ref.at[mine]
    result_x = links.send(block, block, kx=1)
    small.wait_recv()
    small_ref[...] += small_in[0]
    small = small_step(1, kx=1)
    states_x.wait_recv()
    both = states_grad_ref.at[my_half]
    states_core = links.send(both, both, kc=1)
    small.wait_recv()
    small_ref[...] += small_in[1]
    small = small_step(2, ky=1)
    attend_sum.add(0, attend_grad(0, here.y))
    small.wait_recv()
    small_ref[...] += small_in[2]
    small = small_step(3, kz=1)
    g_output_ref[...] = output_sum.finish()
    result_x.wait_recv()
    both = result_ref.at[my_half]
    result_core = links.send(both, both, kc=1)
    small.wait_recv()
    small_ref[...] += small_in[3]
    small = small_step(4, kz=2)

    total = attend_sum.finish()
    part = here.x * 2 + here.c
    g_kv_ref[part] = total[:, :kv_width].astype(BF16)
    block = g_kv_ref.at[part]
    kv_x = links.send(block, block, kx=1)
    kv_core = links.send(block, block, kc=1)
    g_attend_ref[...] = total[:, kv_width:]
    kv_x.wait_recv()
    block = g_kv_ref.at[(1 - here.x) * 2 + here.c]
    kv_both = links.send(block, block, kc=1)
    small.wait_recv()
    small_ref[...] += small_in[4]
    for copy in (states_core, kv_core, kv_both, result_core):
        copy.wait_recv()
    links.finish()


def backward(lines, heads, longest, *arguments):
    kv, attn_in, lin, mixed = arguments[4], arguments[8], arguments[7], arguments[17]
    token_rows, width = attn_in.shape
    quarter = token_rows // 4
    half = 2 * quarter
    weight_rows = width // (4 * lines)
    head_width = heads * HEAD_WIDTH
    blocks = token_rows // STRETCH
    vmem = pl.BlockSpec(memory_space=pltpu.VMEM)
    smem = pl.BlockSpec(memory_space=pltpu.SMEM)
    hbm = pl.BlockSpec(memory_space=pl.ANY)
    shape = jax.ShapeDtypeStruct
    return pl.pallas_call(
        functools.partial(backward_kernel, lines, heads, longest),
        out_shape=(
            shape((token_rows, width), BF16),
            shape((token_rows, width), BF16),
            shape((weight_rows, head_width), F32),
            shape((weight_rows, head_width), F32),
            shape((4, weight_rows, 4 * HEAD_WIDTH), BF16),
            shape((8, width), F32),
        ),
        in_specs=[smem] * 3 + [vmem] * 18 + [hbm],
        out_specs=(vmem,) * 6,
        scratch_shapes=[
            pltpu.VMEM((mixed.shape[0], width), BF16),
            pltpu.VMEM((blocks, PAIRS, 2 * STRETCH, HEAD_WIDTH), F32),
            pltpu.VMEM((blocks * longest, STRETCH, 4 * HEAD_WIDTH), F32),
            pltpu.VMEM(lin.shape, BF16),
            pltpu.VMEM((2, token_rows, width), F32),
            pltpu.VMEM((5, half, width), BF16),
            pltpu.VMEM((5, half, width), BF16),
            pltpu.VMEM((5, quarter, width), BF16),
            pltpu.VMEM((5, quarter, width), BF16),
            pltpu.VMEM((5, quarter, width), F32),
            pltpu.VMEM((3, quarter, width), BF16),
            pltpu.VMEM((3, quarter, width), BF16),
            pltpu.VMEM((5, 8, width), F32),
            pltpu.VMEM((5, 8, width), F32),
            pltpu.SemaphoreType.DMA((1,)),
            pltpu.SemaphoreType.DMA((BACKWARD_COPIES,)),
            pltpu.SemaphoreType.DMA((BACKWARD_COPIES,)),
            *scatter_scratch((token_rows, 4 * HEAD_WIDTH)),
            *scatter_scratch((weight_rows, head_width)),
            *scatter_scratch((weight_rows, lin.shape[1])),
        ],
        compiler_params=pltpu.CompilerParams(
            collective_id=1, has_side_effects=True, vmem_limit_bytes=64 << 20
        ),
        name="backward",
    )(*arguments)


def local_kernels(
    states,
    query_weight,
    keyvalue_matrix,
    output_weight,
    gate_weight,
    up_weight,
    down_weight,
    norm_gains,
    query_gain,
    key_gain,
    slot_sequence,
    slot_offset,
    out_grad,
):
    token_rows, width = states.shape
    dp_ranks = lax.axis_size("dp")
    tensor_ranks = lax.axis_size("tensor")
    lines = dp_ranks // PLANES
    rank, part = lax.axis_index("dp"), lax.axis_index("tensor")
    heads_here = QUERY_HEADS // tensor_ranks
    head_width = heads_here * HEAD_WIDTH
    sharing_count = QUERY_HEADS // KEYVALUE_HEADS
    blocks_here = token_rows // STRETCH
    slot_count = slot_sequence.shape[0]
    hidden = gate_weight.shape[2]
    slice_width = hidden // PLANES
    weight_rows = width // dp_ranks

    offset_here = lax.dynamic_slice_in_dim(slot_offset, rank * blocks_here, blocks_here)
    positions = (offset_here[:, None] + jnp.arange(STRETCH, dtype=jnp.int32)[None, :]).reshape(-1)
    columns = jnp.arange(2 * HEAD_WIDTH, dtype=jnp.int32)
    exponent = -(columns % (HEAD_WIDTH // 2)).astype(F32) * 2.0 / HEAD_WIDTH
    phase = positions.astype(F32)[:, None] * (10000.0**exponent)[None, :]
    cosine = jnp.cos(phase)
    sine = jnp.sin(phase) * jnp.where(columns % HEAD_WIDTH < HEAD_WIDTH // 2, -1.0, 1.0)[None, :]
    head_gain = jnp.concatenate([jnp.tile(key_gain[0], 2), jnp.tile(query_gain[0], heads_here)])

    first_key = (part * heads_here) // sharing_count * HEAD_WIDTH
    value_start = KEYVALUE_HEADS * HEAD_WIDTH
    w_attend = jnp.concatenate(
        [
            lax.dynamic_slice_in_dim(keyvalue_matrix[0], first_key, 2 * HEAD_WIDTH, 1),
            lax.dynamic_slice_in_dim(
                keyvalue_matrix[0], value_start + first_key, 2 * HEAD_WIDTH, 1
            ),
            query_weight[0],
        ],
        axis=1,
    )
    gains = jnp.pad(norm_gains[0].T.astype(F32), ((0, 6), (0, 0)))

    def turned(weight):
        return weight[0].reshape(weight_rows, PLANES, slice_width).transpose(1, 2, 0)

    packed = jnp.concatenate(
        [turned(gate_weight), turned(up_weight), turned(down_weight)], axis=1
    )
    (
        lin,
        attn_in,
        queries,
        keyvalues,
        attended,
        attn_out,
        gains,
        w_attend,
        middle_rows,
        back,
        gain_ffn,
        d_heads,
        output_grad,
        mixed,
        collected,
        table,
        w_down,
    ) = forward(
        lines,
        heads_here,
        slice_width,
        LONGEST,
        slot_sequence,
        slot_offset,
        states,
        gains,
        w_attend,
        cosine,
        sine,
        head_gain[None],
        output_weight[0],
        packed,
        out_grad,
    )
    result, states_grad, g_attend, g_output, g_kv, small = backward(
        lines,
        heads_here,
        LONGEST,
        slot_sequence,
        slot_offset,
        table,
        queries,
        keyvalues,
        attended,
        d_heads,
        lin,
        attn_in,
        output_grad,
        attn_out,
        w_attend,
        back,
        gains,
        gain_ffn,
        states,
        middle_rows,
        mixed,
        cosine,
        sine,
        head_gain[None],
        w_down,
    )

    def hidden_grad(index):
        piece = collected[:, index * slice_width : (index + 1) * slice_width]
        return piece.transpose(2, 0, 1).astype(F32).reshape(1, weight_rows, hidden)

    d_keyvalue_matrix = jnp.zeros((weight_rows, 2 * value_start), F32)
    for other in range(tensor_ranks):
        start = (other * heads_here) // sharing_count * HEAD_WIDTH
        block = g_kv[other].astype(F32)
        for offset, piece in (
            (start, block[:, : 2 * HEAD_WIDTH]),
            (value_start + start, block[:, 2 * HEAD_WIDTH :]),
        ):
            after = 2 * value_start - offset - 2 * HEAD_WIDTH
            d_keyvalue_matrix += jnp.pad(piece, ((0, 0), (offset, after)))
    head_gains = small[2, : head_width + 2 * HEAD_WIDTH].reshape(-1, HEAD_WIDTH)
    d_gains = lax.dynamic_slice_in_dim(small[:2], rank * weight_rows, weight_rows, 1).T
    return (
        result,
        states_grad.astype(F32),
        g_attend[None],
        d_keyvalue_matrix[None],
        g_output[None],
        hidden_grad(0),
        hidden_grad(1),
        hidden_grad(2),
        d_gains[None],
        jnp.sum(head_gains[2:], axis=0)[None],
        jnp.sum(head_gains[:2], axis=0)[None],
    )


def local_permutes(
    states,
    query_weight,
    keyvalue_matrix,
    output_weight,
    gate_weight,
    up_weight,
    down_weight,
    norm_gains,
    query_gain,
    key_gain,
    slot_sequence,
    slot_offset,
    out_grad,
):
    token_rows, width = states.shape
    dp_ranks = lax.axis_size("dp")
    tensor_ranks = lax.axis_size("tensor")
    lines = dp_ranks // PLANES
    rank, part = lax.axis_index("dp"), lax.axis_index("tensor")
    plane, line = rank // lines, rank % lines
    quarter = token_rows // tensor_ranks
    heads_here = QUERY_HEADS // tensor_ranks
    head_width = heads_here * HEAD_WIDTH
    sharing_count = QUERY_HEADS // KEYVALUE_HEADS
    blocks_here = token_rows // STRETCH
    slot_count = slot_sequence.shape[0]
    hidden = gate_weight.shape[2]
    slice_width = hidden // PLANES
    weight_rows = width // dp_ranks

    def send(value, kz=0, ky=0, kx=0, kc=0):
        move_rank, move_part = kz * lines + ky, kx * 2 + kc
        pairs = [
            (r * tensor_ranks + p, (r ^ move_rank) * tensor_ranks + (p ^ move_part))
            for r in range(dp_ranks)
            for p in range(tensor_ranks)
        ]
        return lax.ppermute(value, ("dp", "tensor"), pairs)

    def gather_planes(value):
        near = send(value, kz=1)
        far = send(value, kz=2)
        return [value, near, far, send(far, kz=1)]

    def gather_dp(value):
        whole = jnp.zeros((dp_ranks, *value.shape), value.dtype)
        for kz, piece in enumerate(gather_planes(value)):
            for ky in range(lines):
                got = send(piece, ky=ky) if ky else piece
                whole = lax.dynamic_update_index_in_dim(whole, got, rank ^ (kz * lines + ky), 0)
        return whole

    def rounded(value):
        return value.astype(BF16)

    def scatter_dp(whole):
        def piece(move):
            return lax.dynamic_index_in_dim(whole, rank ^ move, 0, keepdims=False)

        parts = []
        for kz in range(PLANES):
            total = piece(kz * lines).astype(F32)
            for ky in range(1, lines):
                total = total + send(rounded(piece(kz * lines + ky)), ky=ky).astype(F32)
            parts.append(total)
        return scatter_planes(parts)

    def scatter_planes(parts):
        near = parts[0] + send(rounded(parts[1]), kz=1).astype(F32)
        far = parts[2] + send(rounded(parts[3]), kz=1).astype(F32)
        return near + send(rounded(far), kz=2).astype(F32)

    def scatter_tensor(blocks):
        got = send(rounded(jnp.concatenate([blocks[1], blocks[3]], axis=0)), kc=1).astype(F32)
        rows = blocks[0].shape[0]
        here = blocks[0] + got[:rows]
        there = blocks[2] + got[rows:]
        return here + send(rounded(there), kx=1).astype(F32)

    def gather_tensor(block):
        both = jnp.concatenate([block, send(block, kx=1)], axis=0)
        return jnp.concatenate([both, send(both, kc=1)], axis=0)

    def in_order(blocks):
        whole = jnp.zeros_like(blocks)
        for index, move in enumerate((0, 2, 1, 3)):
            whole = lax.dynamic_update_slice_in_dim(
                whole,
                blocks[index * quarter : (index + 1) * quarter],
                (part ^ move) * quarter,
                0,
            )
        return whole

    def quarters(value):
        return [
            lax.dynamic_slice_in_dim(value, (part ^ move) * quarter, quarter, 0)
            for move in range(tensor_ranks)
        ]

    sequence_here = lax.dynamic_slice_in_dim(slot_sequence, rank * blocks_here, blocks_here)
    offset_here = lax.dynamic_slice_in_dim(slot_offset, rank * blocks_here, blocks_here)
    counts = offset_here // STRETCH + 1
    places = jnp.arange(slot_count, dtype=jnp.int32)
    same = (slot_sequence[None, None, :] == sequence_here[:, None, None]) & (
        slot_offset[None, None, :] == places[None, :, None] * STRETCH
    )
    slots = jnp.sum(jnp.where(same, places[None, None, :], 0), axis=2).astype(jnp.int32)
    parity = jnp.reshape(part % 2, (1,)).astype(jnp.int32)
    positions = (offset_here[:, None] + jnp.arange(STRETCH, dtype=jnp.int32)[None, :]).reshape(-1)
    cosines, sines = angles(positions, HEAD_WIDTH)

    first_key = (part * heads_here) // sharing_count * HEAD_WIDTH
    value_start = KEYVALUE_HEADS * HEAD_WIDTH
    kv_columns = [
        lax.dynamic_slice_in_dim(keyvalue_matrix[0], first_key, 2 * HEAD_WIDTH, 1),
        lax.dynamic_slice_in_dim(keyvalue_matrix[0], value_start + first_key, 2 * HEAD_WIDTH, 1),
    ]
    gains = gather_dp(norm_gains[0].T).transpose(1, 0, 2).reshape(2, width).astype(F32)
    w_attend = gather_dp(jnp.concatenate([query_weight[0], *kv_columns], axis=1)).reshape(width, -1)
    w_output = gather_dp(output_weight[0]).reshape(width, head_width)

    def sliced(weight):
        return weight[0].reshape(weight_rows, PLANES, slice_width).transpose(1, 0, 2)

    pad_first = -2 * slice_width % 128
    pad_second = -slice_width % 128
    packed = jnp.concatenate(
        [
            sliced(gate_weight),
            sliced(up_weight),
            jnp.zeros((PLANES, weight_rows, pad_first), BF16),
            sliced(down_weight),
            jnp.zeros((PLANES, weight_rows, pad_second), BF16),
        ],
        axis=2,
    )
    w_hidden = jnp.zeros((dp_ranks, weight_rows, packed.shape[2]), BF16)
    for kz in range(PLANES):
        piece = lax.dynamic_index_in_dim(packed, plane ^ kz, 0, keepdims=False)
        piece = send(piece, kz=kz) if kz else piece
        for ky in range(lines):
            got = send(piece, ky=ky) if ky else piece
            w_hidden = lax.dynamic_update_index_in_dim(w_hidden, got, rank ^ (kz * lines + ky), 0)
    w_hidden = w_hidden.reshape(width, -1)
    down_start = 2 * slice_width + pad_first
    w_gate_up = w_hidden[:, : 2 * slice_width]
    w_down = w_hidden[:, down_start : down_start + slice_width]

    def gather_group(block):
        return [gather_tensor(piece) for piece in gather_planes(block)]

    def quarter_of(value):
        return lax.dynamic_slice_in_dim(value, part * quarter, quarter, 0)

    query_g, key_g = query_gain[0], key_gain[0]
    attn_in = rounded(normed(states.astype(F32), gains[0]))
    lin = product(attn_in, w_attend)
    query_lin, keyvalue_lin = lin[:, :head_width], lin[:, head_width:]

    def query_side(linear, gain_vector):
        return rotated(
            normed(linear.reshape(token_rows, heads_here, HEAD_WIDTH), gain_vector), cosines, sines
        )

    def key_side(linear, gain_vector):
        keys = linear[:, : 2 * HEAD_WIDTH].reshape(token_rows, 2, HEAD_WIDTH)
        keys = rotated(normed(keys, gain_vector), cosines, sines)
        return jnp.concatenate(
            [keys.reshape(token_rows, 2 * HEAD_WIDTH), linear[:, 2 * HEAD_WIDTH :]], axis=1
        )

    def to_pairs(value):
        return (
            value.reshape(blocks_here, STRETCH, PAIRS, 2, -1)
            .transpose(0, 2, 3, 1, 4)
            .reshape(blocks_here, PAIRS, 2 * STRETCH, -1)
        )

    def from_pairs(value):
        return (
            value.reshape(blocks_here, PAIRS, 2, STRETCH, -1)
            .transpose(0, 3, 1, 2, 4)
            .reshape(token_rows, heads_here, -1)
        )

    queries = to_pairs(rounded(query_side(query_lin, query_g)))
    keyvalues = gather_dp(rounded(key_side(keyvalue_lin, key_g)))
    keyvalues = keyvalues.reshape(slot_count, STRETCH, 4 * HEAD_WIDTH)
    attended = attend(counts, slots, parity, queries, keyvalues)
    attn_out = rounded(from_pairs(attended[..., :HEAD_WIDTH]).reshape(token_rows, head_width))
    logs = attended[..., HEAD_WIDTH]

    branch = scatter_tensor(quarters(by_cols(attn_out, w_output)))
    states_quarter = quarter_of(states).astype(F32)
    middle = states_quarter + branch
    ffn_in = rounded(normed(middle, gains[1]))

    down_grads = gather_group(quarter_of(out_grad))
    ffn_ins = gather_group(ffn_in)
    mixed_chunks, d_chunks, back_parts, out_parts = [], [], [], []
    for down_grad, ffn_chunk in zip(down_grads, ffn_ins):
        gate_up = product(ffn_chunk, w_gate_up)
        gate_pre, up_pre = gate_up[:, :slice_width], gate_up[:, slice_width:]
        sigmoid_gate = jax.nn.sigmoid(gate_pre)
        mixed = rounded(gate_pre * sigmoid_gate * up_pre)
        d_mixed = product(down_grad, w_down)
        d_gate = d_mixed * up_pre * sigmoid_gate * (1.0 + gate_pre * (1.0 - sigmoid_gate))
        d_up = d_mixed * gate_pre * sigmoid_gate
        d_gate_up = jnp.concatenate([rounded(d_gate), rounded(d_up)], axis=1)
        mixed_chunks.append(mixed)
        d_chunks.append(d_gate_up)

        def reduced(value):
            blocks = value.reshape(4, quarter, width)
            return scatter_tensor([blocks[0], blocks[2], blocks[1], blocks[3]])

        back_parts.append(reduced(by_cols(d_gate_up, w_gate_up)))
        out_parts.append(reduced(by_cols(mixed, w_down)))
    d_ffn_in = scatter_planes(back_parts)

    def norm_back(vector, gain_vector, grad):
        inverse = lax.rsqrt(jnp.mean(vector * vector, axis=-1, keepdims=True) + EPSILON)
        unit = vector * inverse
        scaled = grad * gain_vector
        back = inverse * (scaled - unit * jnp.mean(scaled * unit, axis=-1, keepdims=True))
        return back, jnp.sum(grad * unit, axis=0)

    d_middle, d_gain_ffn = norm_back(middle, gains[1], d_ffn_in)
    grad_middle = quarter_of(out_grad).astype(F32) + d_middle
    output_grad = in_order(gather_tensor(rounded(grad_middle)))

    d_wout = by_rows(output_grad, attn_out)
    d_heads = rounded(product(output_grad, w_output)).reshape(token_rows, heads_here, HEAD_WIDTH)
    d_pairs = to_pairs(d_heads)
    delta = jnp.sum(d_pairs.astype(F32) * attended[..., :HEAD_WIDTH], axis=-1)
    d_query, d_keyvalue = attend_back(
        counts,
        slots,
        parity,
        queries,
        d_pairs,
        logs[:, :, None, :],
        delta[:, :, None, :],
        keyvalues,
    )
    d_keyvalue_here = scatter_dp(d_keyvalue.reshape(dp_ranks, token_rows, 4 * HEAD_WIDTH))
    _, query_pull = jax.vjp(query_side, query_lin, query_g)
    d_query_lin, d_querygain = query_pull(from_pairs(d_query))
    _, key_pull = jax.vjp(key_side, keyvalue_lin, key_g)
    d_keyvalue_lin, d_keygain = key_pull(d_keyvalue_here)
    d_lin = jnp.concatenate([rounded(d_query_lin), rounded(d_keyvalue_lin)], axis=1)
    d_attn_in = scatter_tensor(quarters(by_cols(d_lin, w_attend)))
    d_states, d_gain_attn = norm_back(states_quarter, gains[0], d_attn_in)
    states_grad = in_order(gather_tensor(rounded(grad_middle + d_states))).astype(F32)

    d_wattend = scatter_dp(by_rows(attn_in, d_lin).reshape(dp_ranks, weight_rows, -1))
    d_wout = scatter_dp(d_wout.reshape(dp_ranks, weight_rows, -1))
    ffn_all = jnp.concatenate(ffn_ins, axis=0)
    down_all = jnp.concatenate(down_grads, axis=0)
    grads_hidden = jnp.concatenate(
        [
            by_rows(ffn_all, jnp.concatenate(d_chunks, axis=0)),
            by_rows(down_all, jnp.concatenate(mixed_chunks, axis=0)),
        ],
        axis=1,
    ).reshape(dp_ranks, weight_rows, 3 * slice_width)
    collected = jnp.zeros((PLANES, weight_rows, 3 * slice_width), F32)
    for kz in range(PLANES):
        total = lax.dynamic_index_in_dim(grads_hidden, rank ^ (kz * lines), 0, keepdims=False)
        for ky in range(1, lines):
            piece = lax.dynamic_index_in_dim(
                grads_hidden, rank ^ (kz * lines + ky), 0, keepdims=False
            )
            total = total + send(rounded(piece), ky=ky).astype(F32)
        if kz:
            total = send(rounded(total), kz=kz).astype(F32)
        collected = lax.dynamic_update_index_in_dim(collected, total, plane ^ kz, 0)

    def unsliced(index):
        piece = collected[:, :, index * slice_width : (index + 1) * slice_width]
        return piece.transpose(1, 0, 2).reshape(1, weight_rows, hidden)

    kv_grad = d_wattend[:, head_width:]
    spread = jnp.zeros((weight_rows, 2 * value_start), F32)
    spread = lax.dynamic_update_slice_in_dim(spread, kv_grad[:, : 2 * HEAD_WIDTH], first_key, 1)
    spread = lax.dynamic_update_slice_in_dim(
        spread, kv_grad[:, 2 * HEAD_WIDTH :], value_start + first_key, 1
    )
    d_wkeyvalue = lax.psum(spread, "tensor")

    result_quarter = rounded(middle + scatter_planes(out_parts))
    result = in_order(gather_tensor(result_quarter))

    small = jnp.concatenate([d_gain_attn, d_gain_ffn, d_querygain, d_keygain])
    small = lax.psum(small, ("dp", "tensor"))
    d_gains = lax.dynamic_slice_in_dim(
        small[: 2 * width].reshape(2, width), rank * weight_rows, weight_rows, 1
    ).T
    return (
        result,
        states_grad,
        d_wattend[None, :, :head_width],
        d_wkeyvalue[None],
        d_wout[None],
        unsliced(0),
        unsliced(1),
        unsliced(2),
        d_gains[None],
        small[2 * width : 2 * width + HEAD_WIDTH][None],
        small[2 * width + HEAD_WIDTH :][None],
    )


def local(*arguments):
    rows = arguments[0].shape[1] // lax.axis_size("dp")
    slots = arguments[10].shape[0]
    if lax.axis_size("dp") == 8 and lax.axis_size("tensor") == 4 and rows == 256 and slots == 24:
        return local_kernels(*arguments)
    return local_permutes(*arguments)


def solution(mesh):
    return jax.shard_map(
        local,
        mesh=mesh,
        in_specs=(
            P("dp", None),
            P(None, "dp", "tensor"),
            P(None, "dp", None),
            P(None, "dp", "tensor"),
            P(None, "dp", "tensor"),
            P(None, "dp", "tensor"),
            P(None, "dp", "tensor"),
            P(None, "dp", None),
            P(),
            P(),
            P(),
            P(),
            P("dp", None),
        ),
        out_specs=(
            P("dp", None),
            P("dp", None),
            P(None, "dp", "tensor"),
            P(None, "dp", None),
            P(None, "dp", "tensor"),
            P(None, "dp", "tensor"),
            P(None, "dp", "tensor"),
            P(None, "dp", "tensor"),
            P(None, "dp", None),
            P(),
            P(),
        ),
        check_vma=False,
    )
```

```python
import functools

import jax
import jax.numpy as jnp
from jax import lax
from jax.experimental import pallas as pl
from jax.experimental.pallas import tpu as pltpu
from jax.sharding import PartitionSpec as P

QUERY_HEADS = 24
KEYVALUE_HEADS = 6
HEAD_WIDTH = 64
STRETCH = 128
EPSILON = 1e-06
PLANES = 4
PAIRS = 3
LONGEST = 12
LOG2E = 1.4426950408889634
BF16 = jnp.bfloat16
F32 = jnp.float32


def product(left_side, right_side):
    return jnp.dot(left_side, right_side, preferred_element_type=F32)


def by_rows(left_side, right_side):
    return lax.dot_general(
        left_side, right_side, (((0,), (0,)), ((), ())), preferred_element_type=F32
    )


def by_cols(left_side, right_side):
    return lax.dot_general(
        left_side, right_side, (((1,), (1,)), ((), ())), preferred_element_type=F32
    )


def normed(vector, gain_vector):
    return (
        vector
        * lax.rsqrt(jnp.mean(vector * vector, axis=-1, keepdims=True) + EPSILON)
        * gain_vector
    )


def angles(positions, head_size):
    frequency = 10000.0 ** (-jnp.arange(head_size // 2, dtype=F32) * 2.0 / head_size)
    phase_angle = positions.astype(F32)[:, None] * frequency[None, :]
    return (jnp.cos(phase_angle)[:, None, :], jnp.sin(phase_angle)[:, None, :])


def rotated(vector, cosines, sines):
    half_width = vector.shape[-1] // 2
    front = vector[..., :half_width]
    behind = vector[..., half_width:]
    return jnp.concatenate(
        [front * cosines - behind * sines, behind * cosines + front * sines], axis=-1
    )


def visible_mask(shape, key_axis):
    keys = lax.broadcasted_iota(jnp.int32, shape, key_axis)
    queries = lax.rem(lax.broadcasted_iota(jnp.int32, shape, 1 - key_axis), STRETCH)
    return keys <= queries


def attend_kernel(count_ref, slots_ref, parity_ref, q_ref, kv_ref, out_ref, acc_ref):
    odd = parity_ref[0] == 1
    ones = jnp.ones((STRETCH, HEAD_WIDTH), BF16)

    def add_block(block, slot, last):
        tile = kv_ref[slot]
        keys = [tile[:, :64], tile[:, 64:128]]
        values = [
            jnp.concatenate([tile[:, 128:192], ones], axis=1),
            jnp.concatenate([tile[:, 192:256], ones], axis=1),
        ]
        middle_key = jnp.where(odd, keys[1], keys[0])
        middle_value = jnp.where(odd, values[1], values[0])
        for pair, key, value in (
            (0, keys[0], values[0]),
            (1, middle_key, middle_value),
            (2, keys[1], values[1]),
        ):
            scores = by_cols(q_ref[block, pair], key)
            weights = jnp.exp2(scores * (LOG2E * HEAD_WIDTH**-0.5))
            if last:
                weights = jnp.where(visible_mask(weights.shape, 1), weights, 0.0)
            acc_ref[pair] += product(weights.astype(BF16), value)

    def one_block(block, carry):
        acc_ref[...] = jnp.zeros_like(acc_ref)
        count = count_ref[block]

        def step(index, inner):
            add_block(block, slots_ref[block, index], False)
            return inner

        lax.fori_loop(0, count - 1, step, 0)
        add_block(block, slots_ref[block, count - 1], True)
        for pair in range(PAIRS):
            total = acc_ref[pair]
            denominator = total[:, HEAD_WIDTH:]
            out_ref[block, pair] = jnp.concatenate(
                [total[:, :HEAD_WIDTH] / denominator, jnp.log2(denominator)], axis=1
            )
        return carry

    lax.fori_loop(0, q_ref.shape[0], one_block, 0)


def attend(counts, slots, parity, queries, keyvalues):
    blocks = queries.shape[0]
    smem = pl.BlockSpec(memory_space=pltpu.SMEM)
    vmem = pl.BlockSpec(memory_space=pltpu.VMEM)
    return pl.pallas_call(
        attend_kernel,
        out_shape=jax.ShapeDtypeStruct((blocks, PAIRS, 2 * STRETCH, 128), F32),
        in_specs=[smem, smem, smem, vmem, vmem],
        out_specs=vmem,
        scratch_shapes=[pltpu.VMEM((PAIRS, 2 * STRETCH, 128), F32)],
        compiler_params=pltpu.CompilerParams(vmem_limit_bytes=40 << 20),
        cost_estimate=pl.CostEstimate(
            flops=4 * 20 * PAIRS * 256 * 128 * 64 * 4, bytes_accessed=8 << 20, transcendentals=0
        ),
        name="attend",
    )(counts, slots, parity, queries, keyvalues)


def attend_back_kernel(
    count_ref, slots_ref, parity_ref, q_ref, do_ref, log_ref, delta_ref, kv_ref, dq_ref, dkv_ref
):
    odd = parity_ref[0] == 1
    scale = HEAD_WIDTH**-0.5
    dq_ref[...] = jnp.zeros_like(dq_ref)
    dkv_ref[...] = jnp.zeros_like(dkv_ref)

    def add_block(block, slot, last):
        tile = kv_ref[slot]
        keys = [tile[:, :64], tile[:, 64:128]]
        values = [tile[:, 128:192], tile[:, 192:256]]
        middle_key = jnp.where(odd, keys[1], keys[0])
        middle_value = jnp.where(odd, values[1], values[0])
        d_keys, d_values = [], []
        for pair, key, value in (
            (0, keys[0], values[0]),
            (1, middle_key, middle_value),
            (2, keys[1], values[1]),
        ):
            query, d_out = q_ref[block, pair], do_ref[block, pair]
            scores = by_cols(key, query)
            weights = jnp.exp2(scores * (LOG2E * scale) - log_ref[block, pair])
            if last:
                weights = jnp.where(visible_mask(weights.shape, 0), weights, 0.0)
            d_weights = by_cols(value, d_out)
            d_scores = (weights * (d_weights - delta_ref[block, pair])).astype(BF16)
            d_values.append(product(weights.astype(BF16), d_out))
            d_keys.append(product(d_scores, query))
            dq_ref[block, pair] += by_rows(d_scores, key) * scale
        zero = jnp.zeros((STRETCH, HEAD_WIDTH), F32)
        parts = [
            (d_keys[0] + jnp.where(odd, zero, d_keys[1])) * scale,
            (d_keys[2] + jnp.where(odd, d_keys[1], zero)) * scale,
            d_values[0] + jnp.where(odd, zero, d_values[1]),
            d_values[2] + jnp.where(odd, d_values[1], zero),
        ]
        dkv_ref[slot] += jnp.concatenate(parts, axis=1)

    def one_block(block, carry):
        count = count_ref[block]

        def step(index, inner):
            add_block(block, slots_ref[block, index], False)
            return inner

        lax.fori_loop(0, count - 1, step, 0)
        add_block(block, slots_ref[block, count - 1], True)
        return carry

    lax.fori_loop(0, q_ref.shape[0], one_block, 0)


def attend_back(counts, slots, parity, queries, d_out, logs, delta, keyvalues):
    blocks = queries.shape[0]
    smem = pl.BlockSpec(memory_space=pltpu.SMEM)
    vmem = pl.BlockSpec(memory_space=pltpu.VMEM)
    return pl.pallas_call(
        attend_back_kernel,
        out_shape=(
            jax.ShapeDtypeStruct((blocks, PAIRS, 2 * STRETCH, HEAD_WIDTH), F32),
            jax.ShapeDtypeStruct(keyvalues.shape, F32),
        ),
        in_specs=[smem] * 3 + [vmem] * 5,
        out_specs=(vmem, vmem),
        compiler_params=pltpu.CompilerParams(vmem_limit_bytes=56 << 20),
        cost_estimate=pl.CostEstimate(
            flops=10 * 20 * PAIRS * 256 * 128 * 64 * 4, bytes_accessed=8 << 20, transcendentals=0
        ),
        name="attend_back",
    )(counts, slots, parity, queries, d_out, logs, delta, keyvalues)


class Place:
    def __init__(self, lines):
        rank, part = lax.axis_index("dp"), lax.axis_index("tensor")
        self.lines = lines
        self.z, self.y = rank // lines, lax.rem(rank, lines)
        self.x, self.c = part // 2, lax.rem(part, 2)
        self.quarter = self.c * 2 + self.x

    def plane(self, move):
        if move == 0:
            return self.z
        if move == 1:
            return self.z + 1 - 2 * lax.rem(self.z, 2)
        if move == 2:
            return self.z + 2 - 4 * (self.z // 2)
        return 3 - self.z

    def to(self, kz=0, ky=0, kx=0, kc=0):
        y = 1 - self.y if ky else self.y
        x = 1 - self.x if kx else self.x
        c = 1 - self.c if kc else self.c
        return (self.plane(kz) * self.lines + y, x * 2 + c)


class Links:
    def __init__(self, place, send_sems, recv_sems):
        self.place, self.send_sems, self.recv_sems = place, send_sems, recv_sems
        self.number, self.unsent = 0, []

    def greet(self, moves):
        barrier = pltpu.get_barrier_semaphore()
        for move in moves:
            pl.semaphore_signal(
                barrier, inc=1, device_id=self.place.to(**move), device_id_type=pl.DeviceIdType.MESH
            )
        pl.semaphore_wait(barrier, len(moves))

    def send(self, source, target, **move):
        number, self.number = self.number, self.number + 1
        copy = pltpu.make_async_remote_copy(
            src_ref=source,
            dst_ref=target,
            send_sem=self.send_sems.at[number],
            recv_sem=self.recv_sems.at[number],
            device_id=self.place.to(**move),
            device_id_type=pl.DeviceIdType.MESH,
        )
        copy.start()
        self.unsent.append(copy)
        return copy

    def sent(self, copy):
        copy.wait_send()
        self.unsent = [other for other in self.unsent if other is not copy]

    def finish(self):
        for copy in self.unsent:
            copy.wait_send()


def rows_at(index, size):
    return pl.ds(pl.multiple_of(index * size, size), size)


class Gather:
    def __init__(self, links, block, own=None):
        self.links, self.block, self.y = links, block, links.place.y
        self.own = block(0, self.y) if own is None else own
        self.lines = []

    def over_lines(self, move):
        place = self.block(move, self.y)
        source = self.own if move == 0 else place
        self.lines.append(self.links.send(source, place, ky=1))

    def start_planes(self):
        place = self.block(0, self.y)
        self.far = self.links.send(self.own, place, kz=2)
        self.near = self.links.send(self.own, place, kz=1)

    def start(self):
        self.start_planes()
        self.over_lines(0)

    def relay(self):
        self.near.wait_recv()
        self.over_lines(1)
        self.far.wait_recv()
        place = self.block(2, self.y)
        self.corner = self.links.send(place, place, kz=1)
        self.over_lines(2)

    def last(self):
        self.corner.wait_recv()
        self.over_lines(3)

    def finish(self):
        for copy in self.lines:
            copy.wait_recv()


def head_mean(value):
    row = lax.broadcasted_iota(jnp.int32, (128, 128), 0) // HEAD_WIDTH
    column = lax.broadcasted_iota(jnp.int32, (128, 128), 1) // HEAD_WIDTH
    average = jnp.where(row == column, 1.0 / HEAD_WIDTH, 0.0).astype(F32)
    return jnp.dot(
        value, average, preferred_element_type=F32, precision=lax.Precision.HIGHEST
    )


def halves_swapped(value):
    first = lax.rem(lax.broadcasted_iota(jnp.int32, value.shape, 1), HEAD_WIDTH) < HEAD_WIDTH // 2
    return jnp.where(
        first,
        pltpu.roll(value, 128 - HEAD_WIDTH // 2, 1),
        pltpu.roll(value, HEAD_WIDTH // 2, 1),
    )


class Scatter:
    ORDER = (3, 1, 2, 0)

    def __init__(self, links, y_out, y_in, z_out, z_in, sums):
        self.links = links
        self.y_out, self.y_in, self.z_out, self.z_in, self.sums = y_out, y_in, z_out, z_in, sums
        self.lines, self.planes = {}, {}

    def start(self, move, block):
        self.y_out[move] = block.astype(BF16)
        self.lines[move] = self.links.send(self.y_out.at[move], self.y_in.at[move], ky=1)

    def add(self, move, block):
        self.lines[move].wait_recv()
        total = block + self.y_in[move].astype(F32)
        if move in (3, 1):
            slot = 0 if move == 1 else 1
            self.z_out[slot] = total.astype(BF16)
            self.planes[slot] = self.links.send(self.z_out.at[slot], self.z_in.at[slot], kz=1)
        elif move == 2:
            self.planes[1].wait_recv()
            self.z_out[2] = (total + self.z_in[1].astype(F32)).astype(BF16)
            self.planes[2] = self.links.send(self.z_out.at[2], self.z_in.at[2], kz=2)
        else:
            self.sums[...] = total

    def finish(self):
        self.planes[0].wait_recv()
        self.planes[2].wait_recv()
        return self.sums[...] + self.z_in[0].astype(F32) + self.z_in[2].astype(F32)


def scatter_scratch(block):
    return [
        pltpu.VMEM((4, *block), BF16),
        pltpu.VMEM((4, *block), BF16),
        pltpu.VMEM((3, *block), BF16),
        pltpu.VMEM((3, *block), BF16),
        pltpu.VMEM(block, F32),
    ]


FORWARD_COPIES = 100


def forward_kernel(
    lines,
    heads,
    slice_width,
    longest,
    sequence_ref,
    offset_ref,
    states_ref,
    gains_in,
    w_attend_in,
    cosine_ref,
    sine_ref,
    head_gain_ref,
    w_output_in,
    w_hidden_in,
    grad_any,
    lin_any,
    attn_in_any,
    query_any,
    kv_any,
    attended_ref,
    attn_out_ref,
    gains_ref,
    w_attend_any,
    middle_ref,
    back_ref,
    gain_out_ref,
    d_heads_ref,
    output_grad_ref,
    mixed_ref,
    collected_ref,
    table_ref,
    w_down_any,
    lin_ref,
    attn_in_ref,
    query_ref,
    kv_ref,
    w_attend_ref,
    w_output_ref,
    w_hidden_ref,
    down_ref,
    ffn_ref,
    d_hidden_ref,
    partial_ref,
    core_out,
    core_in,
    x_out,
    x_in,
    sums_ref,
    z_out,
    z_in,
    y_out,
    y_in,
    local_sems,
    send_sems,
    recv_sems,
):
    here = Place(lines)
    links = Links(here, send_sems, recv_sems)
    token_rows, width = states_ref.shape
    quarter = token_rows // 4
    half = 2 * quarter
    weight_rows = w_attend_in.shape[0]
    hidden = slice_width
    blocks = token_rows // STRETCH
    slot_count = offset_ref.shape[0]
    mine, my_half = rows_at(here.quarter, quarter), rows_at(here.c, half)
    other_half = rows_at(1 - here.c, half)
    x_mine, x_other = rows_at(here.x, quarter), rows_at(1 - here.x, quarter)
    odd = here.c == 1

    def rank(move, line):
        return here.plane(move) * lines + line

    def rows_of(ref, columns=slice(None)):
        return lambda move, line: ref.at[rows_at(rank(move, line), weight_rows), columns]

    def columns_of(ref):
        return lambda move, line: ref.at[:, rows_at(rank(move, line), weight_rows)]

    loads = [
        pltpu.make_async_copy(grad_any, down_ref.at[here.z], local_sems.at[0]),
        pltpu.make_async_copy(w_output_in, rows_of(w_output_ref)(0, here.y), local_sems.at[1]),
        pltpu.make_async_copy(
            w_hidden_in.at[here.z], columns_of(w_hidden_ref)(0, here.y), local_sems.at[2]
        ),
    ]
    for load in loads:
        load.start()
    links.greet([dict(kc=1), dict(kx=1), dict(ky=1), dict(kz=1), dict(kz=2), dict(kz=3)])

    kv_width = 4 * HEAD_WIDTH
    gains = Gather(links, columns_of(gains_ref), gains_in)
    gains.start()
    first, second = slice(0, kv_width), slice(kv_width, w_attend_in.shape[1])
    kv_weights = Gather(links, rows_of(w_attend_ref, first), w_attend_in.at[:, first])
    kv_weights.start()
    query_weights = Gather(links, rows_of(w_attend_ref, second), w_attend_in.at[:, second])
    columns_of(gains_ref)(0, here.y)[...] = gains_in[...]
    rows_of(w_attend_ref)(0, here.y)[...] = w_attend_in[...]

    def fill(index, carry):
        block, place = index // longest, lax.rem(index, longest)
        sequence = sequence_ref[rank(0, here.y) * blocks + block]
        found = jnp.int32(0)
        for slot in range(slot_count):
            same = (sequence_ref[slot] == sequence) & (offset_ref[slot] == place * STRETCH)
            found = jnp.where(same, slot, found)
        table_ref[index] = found
        return carry

    lax.fori_loop(0, blocks * longest, fill, 0)
    kv_weights.relay()
    query_weights.start()
    gains.relay()
    gains.last()
    gains.finish()
    states = states_ref[...].astype(F32)
    inverse = lax.rsqrt(jnp.mean(states * states, axis=-1, keepdims=True) + EPSILON)
    attn_in_ref[...] = (states * inverse * gains_ref[0:1, :]).astype(BF16)

    def turned(value, group):
        value = (
            value
            * lax.rsqrt(head_mean(value * value) + EPSILON)
            * head_gain_ref[:, group * 128 : (group + 1) * 128]
        )
        return (value * cosine_ref[...] + halves_swapped(value) * sine_ref[...]).astype(BF16)

    kv_weights.last()
    kv_weights.finish()
    lin = product(attn_in_ref[...], w_attend_ref[:, first])
    lin_ref[:, first] = lin
    own_blocks = pl.ds(rank(0, here.y) * blocks, blocks)
    kv_ref[own_blocks, :, :128] = turned(lin[:, :128], 0).reshape(blocks, STRETCH, 128)
    kv_ref[own_blocks, :, 128:] = lin[:, 128:].astype(BF16).reshape(blocks, STRETCH, 128)
    keyvalue = Gather(
        links, lambda move, line: kv_ref.at[pl.ds(rank(move, line) * blocks, blocks)]
    )
    keyvalue.start()
    query_weights.relay()
    query_weights.last()
    keyvalue.relay()
    query_weights.finish()
    lin = product(attn_in_ref[...], w_attend_ref[:, second])
    lin_ref[:, second] = lin
    for pair in range(PAIRS):
        rotated_pair = turned(lin[:, pair * 128 : (pair + 1) * 128], pair + 1)
        for block in range(blocks):
            rows = rotated_pair[block * STRETCH : (block + 1) * STRETCH]
            query_ref[block, pair, :STRETCH] = rows[:, :HEAD_WIDTH]
            query_ref[block, pair, STRETCH:] = rows[:, HEAD_WIDTH:]
    keyvalue.last()

    output = Gather(links, rows_of(w_output_ref), w_output_in)
    output.start_planes()
    planes = {}

    def hidden_plane(move):
        planes[move] = links.send(
            w_hidden_in.at[here.plane(move)], columns_of(w_hidden_ref)(0, here.y), kz=move
        )

    hidden_lines = []

    def hidden_line(move):
        if move:
            planes[move].wait_recv()
        else:
            loads[2].wait()
        place = columns_of(w_hidden_ref)(move, here.y)
        hidden_lines.append(links.send(place, place, ky=1))

    def down_block(move):
        return down_ref.at[here.plane(move), mine]

    down_across, down_cores = {}, {}

    def down_x(move):
        down_across[move] = links.send(down_block(move), down_block(move), kx=1)

    def down_core(move):
        down_across[move].wait_recv()
        both = down_ref.at[here.plane(move), my_half]
        down_cores[move] = links.send(both, both, kc=1)

    saves = []

    def save(source, target):
        copy = pltpu.make_async_copy(source, target, local_sems.at[3 + len(saves)])
        copy.start()
        saves.append(copy)

    keyvalue.finish()
    output.over_lines(0)
    save(lin_ref, lin_any)
    save(attn_in_ref, attn_in_any)
    save(query_ref, query_any)
    save(kv_ref, kv_any)
    save(w_attend_ref, w_attend_any)

    span = longest * STRETCH
    ones = jnp.ones((span, HEAD_WIDTH), BF16)
    shape = (2 * STRETCH, span)
    ahead = lax.broadcasted_iota(jnp.int32, shape, 1) - lax.rem(
        lax.broadcasted_iota(jnp.int32, shape, 0), STRETCH
    )

    def attend_block(block):
        tiles = [kv_ref[table_ref[block * longest + place]] for place in range(longest)]
        tile = jnp.concatenate(tiles, axis=0)
        keys = [tile[:, :64], tile[:, 64:128]]
        values = [
            jnp.concatenate([tile[:, 128:192], ones], axis=1),
            jnp.concatenate([tile[:, 192:256], ones], axis=1),
        ]
        middle_key = jnp.where(odd, keys[1], keys[0])
        middle_value = jnp.where(odd, values[1], values[0])
        visible = ahead <= offset_ref[rank(0, here.y) * blocks + block]
        for pair, key, value in (
            (0, keys[0], values[0]),
            (1, middle_key, middle_value),
            (2, keys[1], values[1]),
        ):
            scores = by_cols(query_ref[block, pair], key)
            weights = jnp.exp2(scores * (LOG2E * HEAD_WIDTH**-0.5))
            weights = jnp.where(visible, weights, 0.0)
            total = product(weights.astype(BF16), value)
            denominator = total[:, HEAD_WIDTH:]
            heads_out = total[:, :HEAD_WIDTH] / denominator
            attended_ref[block, pair] = jnp.concatenate(
                [heads_out, jnp.log2(denominator)], axis=1
            )
            attn_out_ref[
                block * STRETCH : (block + 1) * STRETCH, pair * 128 : (pair + 1) * 128
            ] = jnp.concatenate([heads_out[:STRETCH], heads_out[STRETCH:]], axis=1).astype(BF16)

    attend_block(0)
    output.relay()
    loads[0].wait()
    down_far = links.send(down_block(0), down_block(0), kz=2)
    down_near = links.send(down_block(0), down_block(0), kz=1)
    attend_block(1)
    output.last()
    attend_block(2)
    down_near.wait_recv()
    down_x(1)
    output.finish()

    loads[1].wait()
    cut = 4
    piece = width // cut
    core_copies = []
    for part in range(cut):
        columns = slice(part * piece, (part + 1) * piece)
        weight = w_output_ref[columns, :]
        core_out[2, :, columns] = by_cols(attn_out_ref[other_half, :], weight).astype(BF16)
        core_copies.append(
            links.send(core_out.at[2, :, columns], core_in.at[4, :, columns], kc=1)
        )
        partial_ref[0, :half, columns] = by_cols(attn_out_ref[my_half, :], weight)
    x_copies = []
    down_far.wait_recv()
    down_corner = links.send(down_block(2), down_block(2), kz=1)
    down_x(2)
    for move in (1, 2, 3):
        hidden_plane(move)
    for part in range(cut):
        columns = slice(part * piece, (part + 1) * piece)
        core_copies[part].wait_recv()
        x_out[2, :, columns] = (
            partial_ref[0, x_other, columns] + core_in[4, x_other, columns].astype(F32)
        ).astype(BF16)
        x_copies.append(links.send(x_out.at[2, :, columns], x_in.at[4, :, columns], kx=1))
        middle_ref[:, columns] = (
            states_ref[mine, columns].astype(F32)
            + partial_ref[0, x_mine, columns]
            + core_in[4, x_mine, columns].astype(F32)
        )
    for part in range(cut):
        columns = slice(part * piece, (part + 1) * piece)
        x_copies[part].wait_recv()
        middle_ref[:, columns] += x_in[4, :, columns].astype(F32)
    middle = middle_ref[...]
    inverse = lax.rsqrt(jnp.mean(middle * middle, axis=-1, keepdims=True) + EPSILON)
    ffn_ref[here.z, mine, :] = (middle * inverse * gains_ref[1:2, :]).astype(BF16)

    def block_of(move):
        return ffn_ref.at[here.plane(move), mine]

    far = links.send(block_of(0), block_of(0), kz=2)
    near = links.send(block_of(0), block_of(0), kz=1)
    across = {0: links.send(block_of(0), block_of(0), kx=1)}
    cores = {}

    def spread(move):
        across[move].wait_recv()
        both = ffn_ref.at[here.plane(move), my_half]
        cores[move] = links.send(both, both, kc=1)

    hidden_line(0)
    down_corner.wait_recv()
    down_x(3)
    down_core(1)
    down_core(2)
    spread(0)
    hidden_line(1)
    near.wait_recv()
    across[1] = links.send(block_of(1), block_of(1), kx=1)
    hidden_line(2)
    hidden_line(3)
    far.wait_recv()
    corner = links.send(block_of(2), block_of(2), kz=1)
    across[2] = links.send(block_of(2), block_of(2), kx=1)
    for copy in hidden_lines:
        copy.wait_recv()

    core_copies, x_copies = [], []

    def add_cores(move):
        core_copies[move].wait_recv()
        total_rows = rows_at(here.c * 2 + 1 - here.x, quarter)
        if move > 1:
            links.sent(x_copies[move - 2])
        x_out[move % 2] = (
            partial_ref[move % 2, total_rows, :] + core_in[move, x_other, :].astype(F32)
        ).astype(BF16)
        x_copies.append(links.send(x_out.at[move % 2], x_in.at[move], kx=1))
        sums_ref[move] = partial_ref[move % 2, mine, :] + core_in[move, x_mine, :].astype(F32)

    z_copies = {}

    def add_x(move):
        x_copies[move].wait_recv()
        sums_ref[move] += x_in[move].astype(F32)
        if move:
            z_out[move - 1] = sums_ref[move].astype(BF16)
            z_copies[move] = links.send(z_out.at[move - 1], z_in.at[move - 1], kz=move)

    for move in range(4):
        if move == 1:
            corner.wait_recv()
            across[3] = links.send(block_of(3), block_of(3), kx=1)
            down_core(3)
        cores[move].wait_recv()
        if move:
            down_cores[move].wait_recv()
        plane = here.plane(move)
        chunk = ffn_ref[plane]
        gate_pre = by_cols(w_hidden_ref[:hidden, :], chunk)
        up_pre = by_cols(w_hidden_ref[hidden : 2 * hidden, :], chunk)
        sigmoid_gate = 1.0 / (1.0 + jnp.exp(-gate_pre))
        silu = gate_pre * sigmoid_gate
        columns = pl.ds(pl.multiple_of(plane * token_rows, token_rows), token_rows)
        mixed_ref[:, columns] = (silu * up_pre).astype(BF16)
        d_mixed = by_cols(w_hidden_ref[2 * hidden :, :], down_ref[plane])
        d_hidden_ref[:hidden, columns] = (
            d_mixed * up_pre * sigmoid_gate * (1.0 + gate_pre * (1.0 - sigmoid_gate))
        ).astype(BF16)
        d_hidden_ref[hidden:, columns] = (d_mixed * silu).astype(BF16)
        partial_ref[move % 2] = by_rows(d_hidden_ref[:, columns], w_hidden_ref[: 2 * hidden, :])
        if move > 1:
            links.sent(core_copies[move - 2])
        core_out[move % 2] = partial_ref[move % 2, other_half, :].astype(BF16)
        core_copies.append(links.send(core_out.at[move % 2], core_in.at[move], kc=1))
        if move > 0:
            add_cores(move - 1)
        if move + 1 < 4:
            spread(move + 1)
        if move > 1:
            add_x(move - 2)
    add_cores(3)

    def gradient(move, line):
        columns = rows_at(rank(move, line), weight_rows)
        first = jnp.zeros((2 * hidden, weight_rows), F32)
        second = jnp.zeros((hidden, weight_rows), F32)
        for plane in range(4):
            tokens = slice(plane * token_rows, (plane + 1) * token_rows)
            first += product(d_hidden_ref[:, tokens], ffn_ref[plane, :, columns])
            second += product(mixed_ref[:, tokens], down_ref[plane, :, columns])
        return first, second

    y_copies = {}
    for move in (3, 2, 1, 0):
        first, second = gradient(move, 1 - here.y)
        y_out[move, : 2 * hidden] = first.astype(BF16)
        y_out[move, 2 * hidden :] = second.astype(BF16)
        y_copies[move] = links.send(y_out.at[move], y_in.at[move], ky=1)

    add_x(2)
    add_x(3)
    g_copies = []

    def gradient_sum(move):
        first, second = gradient(move, here.y)
        y_copies[move].wait_recv()
        if move == 3:
            links.sent(y_copies[move])
        target = y_out.at[move] if move == 3 else collected_ref.at[here.plane(move)]
        target[: 2 * hidden] = (first + y_in[move, : 2 * hidden].astype(F32)).astype(BF16)
        target[2 * hidden :] = (second + y_in[move, 2 * hidden :].astype(F32)).astype(BF16)
        if move == 3:
            g_copies.append(links.send(target, collected_ref.at[here.z], kz=move))

    gradient_sum(3)
    for move in (1, 2, 3):
        z_copies[move].wait_recv()
    d_normed = sums_ref[0]
    for move in (1, 2, 3):
        d_normed += z_in[move - 1].astype(F32)
    middle = middle_ref[...]
    inverse = lax.rsqrt(jnp.mean(middle * middle, axis=-1, keepdims=True) + EPSILON)
    unit = middle * inverse
    gain_out_ref[...] = jnp.sum(d_normed * unit, axis=0, keepdims=True)
    scaled = d_normed * gains_ref[1:2, :]
    back = inverse * (scaled - unit * jnp.mean(scaled * unit, axis=-1, keepdims=True))
    grad_middle = down_ref[here.z, mine, :].astype(F32) + back
    back_ref[...] = grad_middle
    output_grad_ref[mine, :] = grad_middle.astype(BF16)
    block = output_grad_ref.at[mine]
    x_copy = links.send(block, block, kx=1)
    x_copy.wait_recv()
    both = output_grad_ref.at[my_half]
    core = links.send(both, both, kc=1)
    save(w_hidden_ref.at[pl.ds(2 * hidden, hidden)], w_down_any)
    for move in (2, 1, 0):
        gradient_sum(move)
    core.wait_recv()
    d_heads_ref[...] = product(output_grad_ref[...], w_output_ref[...]).astype(BF16)
    for copy in g_copies:
        copy.wait_recv()
    for copy in saves:
        copy.wait()
    links.finish()


def forward(
    lines,
    heads,
    slice_width,
    longest,
    sequence,
    offset,
    states,
    gains,
    w_attend,
    cosine,
    sine,
    head_gain,
    w_output,
    w_hidden,
    grad,
):
    token_rows, width = states.shape
    ranks = 4 * lines
    quarter = token_rows // 4
    half = 2 * quarter
    hidden = slice_width
    head_width = heads * HEAD_WIDTH
    weight_rows = width // ranks
    blocks = token_rows // STRETCH
    vmem = pl.BlockSpec(memory_space=pltpu.VMEM)
    smem = pl.BlockSpec(memory_space=pltpu.SMEM)
    hbm = pl.BlockSpec(memory_space=pl.ANY)
    shape = jax.ShapeDtypeStruct
    return pl.pallas_call(
        functools.partial(forward_kernel, lines, heads, slice_width, longest),
        out_shape=(
            shape((token_rows, w_attend.shape[1]), F32),
            shape((token_rows, width), BF16),
            shape((blocks, PAIRS, 2 * STRETCH, HEAD_WIDTH), BF16),
            shape((ranks * blocks, STRETCH, 4 * HEAD_WIDTH), BF16),
            shape((blocks, PAIRS, 2 * STRETCH, 128), F32),
            shape((token_rows, head_width), BF16),
            shape((gains.shape[0], width), F32),
            shape((width, w_attend.shape[1]), BF16),
            shape((quarter, width), F32),
            shape((quarter, width), F32),
            shape((1, width), F32),
            shape((token_rows, head_width), BF16),
            shape((token_rows, width), BF16),
            shape((hidden, 4 * token_rows), BF16),
            shape((4, 3 * hidden, weight_rows), BF16),
            shape((blocks * longest,), jnp.int32),
            shape((hidden, width), BF16),
        ),
        in_specs=[smem] * 2 + [vmem] * 6 + [hbm] * 3,
        out_specs=(hbm,) * 4 + (vmem,) * 3 + (hbm,) + (vmem,) * 7 + (smem, hbm),
        scratch_shapes=[
            pltpu.VMEM((token_rows, w_attend.shape[1]), F32),
            pltpu.VMEM((token_rows, width), BF16),
            pltpu.VMEM((blocks, PAIRS, 2 * STRETCH, HEAD_WIDTH), BF16),
            pltpu.VMEM((ranks * blocks, STRETCH, 4 * HEAD_WIDTH), BF16),
            pltpu.VMEM((width, w_attend.shape[1]), BF16),
            pltpu.VMEM((width, head_width), BF16),
            pltpu.VMEM((3 * hidden, width), BF16),
            pltpu.VMEM((4, token_rows, width), BF16),
            pltpu.VMEM((4, token_rows, width), BF16),
            pltpu.VMEM((2 * hidden, 4 * token_rows), BF16),
            pltpu.VMEM((2, token_rows, width), F32),
            pltpu.VMEM((3, half, width), BF16),
            pltpu.VMEM((5, half, width), BF16),
            pltpu.VMEM((3, quarter, width), BF16),
            pltpu.VMEM((5, quarter, width), BF16),
            pltpu.VMEM((4, quarter, width), F32),
            pltpu.VMEM((3, quarter, width), BF16),
            pltpu.VMEM((3, quarter, width), BF16),
            pltpu.VMEM((4, 3 * hidden, weight_rows), BF16),
            pltpu.VMEM((4, 3 * hidden, weight_rows), BF16),
            pltpu.SemaphoreType.DMA((10,)),
            pltpu.SemaphoreType.DMA((FORWARD_COPIES,)),
            pltpu.SemaphoreType.DMA((FORWARD_COPIES,)),
        ],
        compiler_params=pltpu.CompilerParams(
            collective_id=0, has_side_effects=True, vmem_limit_bytes=64 << 20
        ),
        name="forward",
    )(
        sequence,
        offset,
        states,
        gains,
        w_attend,
        cosine,
        sine,
        head_gain,
        w_output,
        w_hidden,
        grad,
    )


BACKWARD_COPIES = 60


def backward_kernel(
    lines,
    heads,
    longest,
    sequence_ref,
    offset_ref,
    table_ref,
    query_ref,
    kv_ref,
    attended_ref,
    d_heads_ref,
    attn_out_ref,
    gains_ref,
    gain_ffn_ref,
    cosine_ref,
    sine_ref,
    head_gain_ref,
    lin_any,
    attn_in_any,
    output_grad_any,
    w_attend_any,
    back_any,
    states_any,
    middle_any,
    mixed_any,
    w_down_any,
    collected_any,
    result_ref,
    states_grad_ref,
    g_attend_ref,
    g_output_ref,
    g_kv_ref,
    small_ref,
    hidden_grad_ref,
    *scratch,
):
    here = Place(lines)
    (
        lin_ref,
        attn_in_ref,
        output_grad_ref,
        w_attend_ref,
        back_ref,
        states_ref,
        middle_ref,
        mixed_ref,
        w_down_ref,
        d_query_ref,
        d_kv_ref,
        d_lin_ref,
        partial_ref,
        core_out,
        core_in,
        x_out,
        x_in,
        sums_ref,
        z_out,
        z_in,
        small_out,
        small_in,
        local_sems,
        send_sems,
        recv_sems,
    ) = scratch[:25]
    links = Links(here, send_sems, recv_sems)
    kv_sum = Scatter(links, *scratch[25:30])
    output_sum = Scatter(links, *scratch[30:35])
    attend_sum = Scatter(links, *scratch[35:40])
    token_rows, width = output_grad_ref.shape
    quarter = token_rows // 4
    half = 2 * quarter
    weight_rows = width // (4 * lines)
    kv_width = 4 * HEAD_WIDTH
    blocks = token_rows // STRETCH
    mine, other = rows_at(here.quarter, quarter), rows_at(here.c * 2 + 1 - here.x, quarter)
    my_half, other_half = rows_at(here.c, half), rows_at(1 - here.c, half)
    x_mine, x_other = rows_at(here.x, quarter), rows_at(1 - here.x, quarter)
    odd = here.c == 1
    scale = HEAD_WIDTH**-0.5

    loads = {}

    def load(number, source, target):
        copy = pltpu.make_async_copy(source, target, local_sems.at[number])
        copy.start()
        loads[number] = copy

    load(0, output_grad_any, output_grad_ref)
    load(1, w_down_any, w_down_ref)
    load(2, mixed_any, mixed_ref)
    load(3, lin_any, lin_ref)
    load(4, attn_in_any, attn_in_ref)
    load(5, w_attend_any, w_attend_ref)
    load(6, states_any.at[mine], states_ref)
    load(7, back_any, back_ref)
    load(8, middle_any, middle_ref)
    links.greet([dict(kc=1), dict(kx=1), dict(ky=1), dict(kz=1), dict(kz=2)])
    hidden_grads = {
        move: links.send(
            collected_any.at[here.plane(move)], hidden_grad_ref.at[move - 1], kz=move
        )
        for move in (2, 1)
    }

    def rank(move, line):
        return here.plane(move) * lines + line

    core_copies, x_copies = {}, {}

    def out_start(move, slot):
        at = pl.ds(pl.multiple_of(here.plane(move) * token_rows, token_rows), token_rows)
        partial_ref[slot] = by_rows(mixed_ref[:, at], w_down_ref[...])
        core_out[move] = partial_ref[slot, other_half, :].astype(BF16)
        core_copies[move] = links.send(core_out.at[move], core_in.at[move], kc=1)

    def add_cores(move, slot):
        core_copies[move].wait_recv()
        x_out[move] = (partial_ref[slot, other, :] + core_in[move, x_other, :].astype(F32)).astype(
            BF16
        )
        x_copies[move] = links.send(x_out.at[move], x_in.at[move], kx=1)
        sums_ref[move] = partial_ref[slot, mine, :] + core_in[move, x_mine, :].astype(F32)

    def add_x(move):
        x_copies[move].wait_recv()
        sums_ref[move] += x_in[move].astype(F32)

    def columns(move, line):
        return rows_at(rank(move, line), weight_rows)

    def output_block(move, line):
        return by_rows(output_grad_ref[:, columns(move, line)], attn_out_ref[...])

    def attend_grad(move, line):
        return by_rows(attn_in_ref[:, columns(move, line)], d_lin_ref[...])

    loads[0].wait()
    for move in Scatter.ORDER:
        output_sum.start(move, output_block(move, 1 - here.y))

    span = longest * STRETCH
    shape = (2 * STRETCH, span)
    ahead = lax.broadcasted_iota(jnp.int32, shape, 1) - lax.rem(
        lax.broadcasted_iota(jnp.int32, shape, 0), STRETCH
    )

    def attend_block(block):
        rows = slice(block * STRETCH, (block + 1) * STRETCH)
        tiles = [kv_ref[table_ref[block * longest + place]] for place in range(longest)]
        tile = jnp.concatenate(tiles, axis=0)
        keys = [tile[:, :64], tile[:, 64:128]]
        values = [tile[:, 128:192], tile[:, 192:256]]
        middle_key = jnp.where(odd, keys[1], keys[0])
        middle_value = jnp.where(odd, values[1], values[0])
        visible = ahead <= offset_ref[rank(0, here.y) * blocks + block]
        d_keys, d_values = [], []
        for pair, key, value in (
            (0, keys[0], values[0]),
            (1, middle_key, middle_value),
            (2, keys[1], values[1]),
        ):
            query = query_ref[block, pair]
            both = d_heads_ref[rows, pair * 128 : (pair + 1) * 128]
            d_out = jnp.concatenate([both[:, :HEAD_WIDTH], both[:, HEAD_WIDTH:]], axis=0)
            kept = attended_ref[block, pair]
            delta = jnp.sum(d_out.astype(F32) * kept[:, :HEAD_WIDTH], axis=-1, keepdims=True)
            scores = by_cols(query, key)
            weights = jnp.exp2(
                scores * (LOG2E * scale) - kept[:, HEAD_WIDTH : HEAD_WIDTH + 1]
            )
            weights = jnp.where(visible, weights, 0.0)
            d_weights = by_cols(d_out, value)
            d_scores = (weights * (d_weights - delta)).astype(BF16)
            d_values.append(by_rows(weights.astype(BF16), d_out))
            d_keys.append(by_rows(d_scores, query))
            d_query_ref[block, pair] = product(d_scores, key) * scale
        zero = jnp.zeros((span, HEAD_WIDTH), F32)
        parts = [
            (d_keys[0] + jnp.where(odd, zero, d_keys[1])) * scale,
            (d_keys[2] + jnp.where(odd, d_keys[1], zero)) * scale,
            d_values[0] + jnp.where(odd, zero, d_values[1]),
            d_values[2] + jnp.where(odd, d_values[1], zero),
        ]
        d_kv_ref[block * longest : (block + 1) * longest] = jnp.concatenate(
            parts, axis=1
        ).reshape(longest, STRETCH, kv_width)

    attend_block(0)
    loads[1].wait()
    loads[2].wait()
    out_start(3, 0)
    out_start(1, 1)
    attend_block(1)
    add_cores(3, 0)
    out_start(2, 0)
    add_cores(1, 1)
    out_start(0, 1)
    attend_block(2)

    def kv_block(move, line):
        pieces = []
        for index in range(blocks):
            slot = rank(move, line) * blocks + index
            sequence = sequence_ref[slot]
            place = offset_ref[slot] // STRETCH
            total = jnp.zeros((STRETCH, kv_width), F32)
            for block in range(blocks):
                same = sequence_ref[rank(0, here.y) * blocks + block] == sequence
                total += jnp.where(same, d_kv_ref[block * longest + place], 0.0)
            pieces.append(total)
        return jnp.concatenate(pieces, axis=0)

    for move in Scatter.ORDER:
        kv_sum.start(move, kv_block(move, 1 - here.y))

    def group_back(group, at, grad):
        linear = lin_ref[:, at]
        inverse = lax.rsqrt(head_mean(linear * linear) + EPSILON)
        unit = linear * inverse
        grad = grad * cosine_ref[...] + halves_swapped(grad * sine_ref[...])
        gain = jnp.sum(grad * unit, axis=0, keepdims=True)
        scaled = grad * head_gain_ref[:, group * 128 : (group + 1) * 128]
        return inverse * (scaled - unit * head_mean(scaled * unit)), gain

    loads[3].wait()
    add_cores(2, 0)
    add_cores(0, 1)
    for move in Scatter.ORDER[:2]:
        output_sum.add(move, output_block(move, here.y))
    small_ref[...] = jnp.zeros_like(small_ref)
    small_ref[1:2, :] = gain_ffn_ref[...]
    for pair in range(PAIRS):
        grad = jnp.concatenate(
            [
                jnp.concatenate(
                    [d_query_ref[block, pair, :STRETCH], d_query_ref[block, pair, STRETCH:]], axis=1
                )
                for block in range(blocks)
            ],
            axis=0,
        )
        at = slice(kv_width + pair * 128, kv_width + (pair + 1) * 128)
        linear_grad, gain = group_back(pair + 1, at, grad)
        d_lin_ref[:, at] = linear_grad.astype(BF16)
        small_ref[2:3, (pair + 1) * 128 : (pair + 2) * 128] = gain
    for move in Scatter.ORDER:
        kv_sum.add(move, kv_block(move, here.y))
    add_x(3)
    z_out[1] = sums_ref[3].astype(BF16)
    z_copies = {1: links.send(z_out.at[1], z_in.at[1], kz=1)}
    add_x(1)
    z_out[0] = sums_ref[1].astype(BF16)
    z_copies[0] = links.send(z_out.at[0], z_in.at[0], kz=1)
    d_kv = kv_sum.finish()
    for move in Scatter.ORDER[2:]:
        output_sum.add(move, output_block(move, here.y))
    linear_grad, gain = group_back(0, slice(0, 128), d_kv[:, :128])
    d_lin_ref[:, :128] = linear_grad.astype(BF16)
    d_lin_ref[:, 128:kv_width] = d_kv[:, 128:].astype(BF16)
    small_ref[2:3, :128] = gain

    loads[4].wait()
    for move in Scatter.ORDER:
        attend_sum.start(move, attend_grad(move, 1 - here.y))
    add_x(2)
    add_x(0)
    z_copies[1].wait_recv()
    z_out[2] = (sums_ref[2] + z_in[1].astype(F32)).astype(BF16)
    z_copies[2] = links.send(z_out.at[2], z_in.at[2], kz=2)

    loads[5].wait()
    partial_ref[0] = by_cols(d_lin_ref[...], w_attend_ref[...])
    core_out[4] = partial_ref[0, other_half, :].astype(BF16)
    core_copies[4] = links.send(core_out.at[4], core_in.at[4], kc=1)
    add_cores(4, 0)
    attend_sum.add(3, attend_grad(3, here.y))
    attend_sum.add(1, attend_grad(1, here.y))
    add_x(4)
    loads[6].wait()
    loads[7].wait()
    states = states_ref[...].astype(F32)
    inverse = lax.rsqrt(jnp.mean(states * states, axis=-1, keepdims=True) + EPSILON)
    unit = states * inverse
    grad = sums_ref[4]
    small_ref[0:1, :] = jnp.sum(grad * unit, axis=0, keepdims=True)
    scaled = grad * gains_ref[0:1, :]
    total = back_ref[...] + inverse * (
        scaled - unit * jnp.mean(scaled * unit, axis=-1, keepdims=True)
    )
    states_grad_ref[mine, :] = total.astype(BF16)
    block = states_grad_ref.at[mine]
    states_x = links.send(block, block, kx=1)

    def small_step(step, **move):
        small_out[step] = small_ref[...]
        return links.send(small_out.at[step], small_in.at[step], **move)

    small = small_step(0, kc=1)
    attend_sum.add(2, attend_grad(2, here.y))
    small.wait_recv()
    small_ref[...] += small_in[0]
    small = small_step(1, kx=1)
    states_x.wait_recv()
    both = states_grad_ref.at[my_half]
    states_core = links.send(both, both, kc=1)
    small.wait_recv()
    small_ref[...] += small_in[1]
    small = small_step(2, ky=1)
    attend_sum.add(0, attend_grad(0, here.y))
    small.wait_recv()
    small_ref[...] += small_in[2]
    small = small_step(3, kz=1)
    small.wait_recv()
    small_ref[...] += small_in[3]
    small = small_step(4, kz=2)

    total = attend_sum.finish()
    part = here.x * 2 + here.c
    g_kv_ref[part] = total[:, :kv_width].astype(BF16)
    block = g_kv_ref.at[part]
    kv_x = links.send(block, block, kx=1)
    kv_core = links.send(block, block, kc=1)
    g_attend_ref[...] = total[:, kv_width:]
    z_copies[0].wait_recv()
    z_copies[2].wait_recv()
    loads[8].wait()
    result_ref[mine, :] = (
        middle_ref[...] + sums_ref[0] + z_in[0].astype(F32) + z_in[2].astype(F32)
    ).astype(BF16)
    block = result_ref.at[mine]
    result_x = links.send(block, block, kx=1)
    kv_x.wait_recv()
    block = g_kv_ref.at[(1 - here.x) * 2 + here.c]
    kv_both = links.send(block, block, kc=1)
    g_output_ref[...] = output_sum.finish()
    small.wait_recv()
    small_ref[...] += small_in[4]
    result_x.wait_recv()
    both = result_ref.at[my_half]
    result_core = links.send(both, both, kc=1)
    for copy in (states_core, kv_core, kv_both, result_core, *hidden_grads.values()):
        copy.wait_recv()
    links.finish()


def backward(lines, heads, longest, *arguments):
    lin, attn_in, mixed, w_attend = arguments[13], arguments[14], arguments[20], arguments[16]
    token_rows, width = attn_in.shape
    quarter = token_rows // 4
    half = 2 * quarter
    weight_rows = width // (4 * lines)
    head_width = heads * HEAD_WIDTH
    blocks = token_rows // STRETCH
    vmem = pl.BlockSpec(memory_space=pltpu.VMEM)
    smem = pl.BlockSpec(memory_space=pltpu.SMEM)
    hbm = pl.BlockSpec(memory_space=pl.ANY)
    shape = jax.ShapeDtypeStruct
    return pl.pallas_call(
        functools.partial(backward_kernel, lines, heads, longest),
        out_shape=(
            shape((token_rows, width), BF16),
            shape((token_rows, width), BF16),
            shape((weight_rows, head_width), F32),
            shape((weight_rows, head_width), F32),
            shape((4, weight_rows, 4 * HEAD_WIDTH), BF16),
            shape((8, width), F32),
            shape((2, 3 * mixed.shape[0], weight_rows), BF16),
        ),
        in_specs=[smem] * 3 + [vmem] * 10 + [hbm] * 10,
        out_specs=(vmem,) * 6 + (hbm,),
        scratch_shapes=[
            pltpu.VMEM(lin.shape, F32),
            pltpu.VMEM(attn_in.shape, BF16),
            pltpu.VMEM((token_rows, width), BF16),
            pltpu.VMEM(w_attend.shape, BF16),
            pltpu.VMEM((quarter, width), F32),
            pltpu.VMEM((quarter, width), BF16),
            pltpu.VMEM((quarter, width), F32),
            pltpu.VMEM(mixed.shape, BF16),
            pltpu.VMEM((mixed.shape[0], width), BF16),
            pltpu.VMEM((blocks, PAIRS, 2 * STRETCH, HEAD_WIDTH), F32),
            pltpu.VMEM((blocks * longest, STRETCH, 4 * HEAD_WIDTH), F32),
            pltpu.VMEM(lin.shape, BF16),
            pltpu.VMEM((2, token_rows, width), F32),
            pltpu.VMEM((5, half, width), BF16),
            pltpu.VMEM((5, half, width), BF16),
            pltpu.VMEM((5, quarter, width), BF16),
            pltpu.VMEM((5, quarter, width), BF16),
            pltpu.VMEM((5, quarter, width), F32),
            pltpu.VMEM((3, quarter, width), BF16),
            pltpu.VMEM((3, quarter, width), BF16),
            pltpu.VMEM((5, 8, width), F32),
            pltpu.VMEM((5, 8, width), F32),
            pltpu.SemaphoreType.DMA((10,)),
            pltpu.SemaphoreType.DMA((BACKWARD_COPIES,)),
            pltpu.SemaphoreType.DMA((BACKWARD_COPIES,)),
            *scatter_scratch((token_rows, 4 * HEAD_WIDTH)),
            *scatter_scratch((weight_rows, head_width)),
            *scatter_scratch((weight_rows, lin.shape[1])),
        ],
        compiler_params=pltpu.CompilerParams(
            collective_id=1, has_side_effects=True, vmem_limit_bytes=64 << 20
        ),
        name="backward",
    )(*arguments)


def local_kernels(
    states,
    query_weight,
    keyvalue_matrix,
    output_weight,
    gate_weight,
    up_weight,
    down_weight,
    norm_gains,
    query_gain,
    key_gain,
    slot_sequence,
    slot_offset,
    out_grad,
):
    token_rows, width = states.shape
    dp_ranks = lax.axis_size("dp")
    tensor_ranks = lax.axis_size("tensor")
    lines = dp_ranks // PLANES
    rank, part = lax.axis_index("dp"), lax.axis_index("tensor")
    heads_here = QUERY_HEADS // tensor_ranks
    head_width = heads_here * HEAD_WIDTH
    sharing_count = QUERY_HEADS // KEYVALUE_HEADS
    blocks_here = token_rows // STRETCH
    slot_count = slot_sequence.shape[0]
    hidden = gate_weight.shape[2]
    slice_width = hidden // PLANES
    weight_rows = width // dp_ranks

    offset_here = lax.dynamic_slice_in_dim(slot_offset, rank * blocks_here, blocks_here)
    positions = (offset_here[:, None] + jnp.arange(STRETCH, dtype=jnp.int32)[None, :]).reshape(-1)
    columns = jnp.arange(2 * HEAD_WIDTH, dtype=jnp.int32)
    exponent = -(columns % (HEAD_WIDTH // 2)).astype(F32) * 2.0 / HEAD_WIDTH
    phase = positions.astype(F32)[:, None] * (10000.0**exponent)[None, :]
    cosine = jnp.cos(phase)
    sine = jnp.sin(phase) * jnp.where(columns % HEAD_WIDTH < HEAD_WIDTH // 2, -1.0, 1.0)[None, :]
    head_gain = jnp.concatenate([jnp.tile(key_gain[0], 2), jnp.tile(query_gain[0], heads_here)])

    first_key = (part * heads_here) // sharing_count * HEAD_WIDTH
    value_start = KEYVALUE_HEADS * HEAD_WIDTH
    w_attend = jnp.concatenate(
        [
            lax.dynamic_slice_in_dim(keyvalue_matrix[0], first_key, 2 * HEAD_WIDTH, 1),
            lax.dynamic_slice_in_dim(
                keyvalue_matrix[0], value_start + first_key, 2 * HEAD_WIDTH, 1
            ),
            query_weight[0],
        ],
        axis=1,
    )
    gains = jnp.pad(norm_gains[0].T.astype(F32), ((0, 6), (0, 0)))

    def turned(weight):
        return weight[0].reshape(weight_rows, PLANES, slice_width).transpose(1, 2, 0)

    packed = jnp.concatenate(
        [turned(gate_weight), turned(up_weight), turned(down_weight)], axis=1
    )
    (
        lin,
        attn_in,
        queries,
        keyvalues,
        attended,
        attn_out,
        gains,
        w_attend,
        middle_rows,
        back,
        gain_ffn,
        d_heads,
        output_grad,
        mixed,
        collected,
        table,
        w_down,
    ) = forward(
        lines,
        heads_here,
        slice_width,
        LONGEST,
        slot_sequence,
        slot_offset,
        states,
        gains,
        w_attend,
        cosine,
        sine,
        head_gain[None],
        output_weight[0],
        packed,
        out_grad,
    )
    result, states_grad, g_attend, g_output, g_kv, small, hidden_grads = backward(
        lines,
        heads_here,
        LONGEST,
        slot_sequence,
        slot_offset,
        table,
        queries,
        keyvalues,
        attended,
        d_heads,
        attn_out,
        gains,
        gain_ffn,
        cosine,
        sine,
        head_gain[None],
        lin,
        attn_in,
        output_grad,
        w_attend,
        back,
        states,
        middle_rows,
        mixed,
        w_down,
        collected,
    )
    plane = rank // lines
    for move in (1, 2):
        collected = lax.dynamic_update_index_in_dim(
            collected, hidden_grads[move - 1], plane ^ move, 0
        )

    def hidden_grad(index):
        piece = collected[:, index * slice_width : (index + 1) * slice_width]
        return piece.transpose(2, 0, 1).astype(F32).reshape(1, weight_rows, hidden)

    d_keyvalue_matrix = jnp.zeros((weight_rows, 2 * value_start), F32)
    for other in range(tensor_ranks):
        start = (other * heads_here) // sharing_count * HEAD_WIDTH
        block = g_kv[other].astype(F32)
        for offset, piece in (
            (start, block[:, : 2 * HEAD_WIDTH]),
            (value_start + start, block[:, 2 * HEAD_WIDTH :]),
        ):
            after = 2 * value_start - offset - 2 * HEAD_WIDTH
            d_keyvalue_matrix += jnp.pad(piece, ((0, 0), (offset, after)))
    head_gains = small[2, : head_width + 2 * HEAD_WIDTH].reshape(-1, HEAD_WIDTH)
    d_gains = lax.dynamic_slice_in_dim(small[:2], rank * weight_rows, weight_rows, 1).T
    return (
        result,
        states_grad.astype(F32),
        g_attend[None],
        d_keyvalue_matrix[None],
        g_output[None],
        hidden_grad(0),
        hidden_grad(1),
        hidden_grad(2),
        d_gains[None],
        jnp.sum(head_gains[2:], axis=0)[None],
        jnp.sum(head_gains[:2], axis=0)[None],
    )


def local_permutes(
    states,
    query_weight,
    keyvalue_matrix,
    output_weight,
    gate_weight,
    up_weight,
    down_weight,
    norm_gains,
    query_gain,
    key_gain,
    slot_sequence,
    slot_offset,
    out_grad,
):
    token_rows, width = states.shape
    dp_ranks = lax.axis_size("dp")
    tensor_ranks = lax.axis_size("tensor")
    lines = dp_ranks // PLANES
    rank, part = lax.axis_index("dp"), lax.axis_index("tensor")
    plane, line = rank // lines, rank % lines
    quarter = token_rows // tensor_ranks
    heads_here = QUERY_HEADS // tensor_ranks
    head_width = heads_here * HEAD_WIDTH
    sharing_count = QUERY_HEADS // KEYVALUE_HEADS
    blocks_here = token_rows // STRETCH
    slot_count = slot_sequence.shape[0]
    hidden = gate_weight.shape[2]
    slice_width = hidden // PLANES
    weight_rows = width // dp_ranks

    def send(value, kz=0, ky=0, kx=0, kc=0):
        move_rank, move_part = kz * lines + ky, kx * 2 + kc
        pairs = [
            (r * tensor_ranks + p, (r ^ move_rank) * tensor_ranks + (p ^ move_part))
            for r in range(dp_ranks)
            for p in range(tensor_ranks)
        ]
        return lax.ppermute(value, ("dp", "tensor"), pairs)

    def gather_planes(value):
        near = send(value, kz=1)
        far = send(value, kz=2)
        return [value, near, far, send(far, kz=1)]

    def gather_dp(value):
        whole = jnp.zeros((dp_ranks, *value.shape), value.dtype)
        for kz, piece in enumerate(gather_planes(value)):
            for ky in range(lines):
                got = send(piece, ky=ky) if ky else piece
                whole = lax.dynamic_update_index_in_dim(whole, got, rank ^ (kz * lines + ky), 0)
        return whole

    def rounded(value):
        return value.astype(BF16)

    def scatter_dp(whole):
        def piece(move):
            return lax.dynamic_index_in_dim(whole, rank ^ move, 0, keepdims=False)

        parts = []
        for kz in range(PLANES):
            total = piece(kz * lines).astype(F32)
            for ky in range(1, lines):
                total = total + send(rounded(piece(kz * lines + ky)), ky=ky).astype(F32)
            parts.append(total)
        return scatter_planes(parts)

    def scatter_planes(parts):
        near = parts[0] + send(rounded(parts[1]), kz=1).astype(F32)
        far = parts[2] + send(rounded(parts[3]), kz=1).astype(F32)
        return near + send(rounded(far), kz=2).astype(F32)

    def scatter_tensor(blocks):
        got = send(rounded(jnp.concatenate([blocks[1], blocks[3]], axis=0)), kc=1).astype(F32)
        rows = blocks[0].shape[0]
        here = blocks[0] + got[:rows]
        there = blocks[2] + got[rows:]
        return here + send(rounded(there), kx=1).astype(F32)

    def gather_tensor(block):
        both = jnp.concatenate([block, send(block, kx=1)], axis=0)
        return jnp.concatenate([both, send(both, kc=1)], axis=0)

    def in_order(blocks):
        whole = jnp.zeros_like(blocks)
        for index, move in enumerate((0, 2, 1, 3)):
            whole = lax.dynamic_update_slice_in_dim(
                whole,
                blocks[index * quarter : (index + 1) * quarter],
                (part ^ move) * quarter,
                0,
            )
        return whole

    def quarters(value):
        return [
            lax.dynamic_slice_in_dim(value, (part ^ move) * quarter, quarter, 0)
            for move in range(tensor_ranks)
        ]

    sequence_here = lax.dynamic_slice_in_dim(slot_sequence, rank * blocks_here, blocks_here)
    offset_here = lax.dynamic_slice_in_dim(slot_offset, rank * blocks_here, blocks_here)
    counts = offset_here // STRETCH + 1
    places = jnp.arange(slot_count, dtype=jnp.int32)
    same = (slot_sequence[None, None, :] == sequence_here[:, None, None]) & (
        slot_offset[None, None, :] == places[None, :, None] * STRETCH
    )
    slots = jnp.sum(jnp.where(same, places[None, None, :], 0), axis=2).astype(jnp.int32)
    parity = jnp.reshape(part % 2, (1,)).astype(jnp.int32)
    positions = (offset_here[:, None] + jnp.arange(STRETCH, dtype=jnp.int32)[None, :]).reshape(-1)
    cosines, sines = angles(positions, HEAD_WIDTH)

    first_key = (part * heads_here) // sharing_count * HEAD_WIDTH
    value_start = KEYVALUE_HEADS * HEAD_WIDTH
    kv_columns = [
        lax.dynamic_slice_in_dim(keyvalue_matrix[0], first_key, 2 * HEAD_WIDTH, 1),
        lax.dynamic_slice_in_dim(keyvalue_matrix[0], value_start + first_key, 2 * HEAD_WIDTH, 1),
    ]
    gains = gather_dp(norm_gains[0].T).transpose(1, 0, 2).reshape(2, width).astype(F32)
    w_attend = gather_dp(jnp.concatenate([query_weight[0], *kv_columns], axis=1)).reshape(width, -1)
    w_output = gather_dp(output_weight[0]).reshape(width, head_width)

    def sliced(weight):
        return weight[0].reshape(weight_rows, PLANES, slice_width).transpose(1, 0, 2)

    pad_first = -2 * slice_width % 128
    pad_second = -slice_width % 128
    packed = jnp.concatenate(
        [
            sliced(gate_weight),
            sliced(up_weight),
            jnp.zeros((PLANES, weight_rows, pad_first), BF16),
            sliced(down_weight),
            jnp.zeros((PLANES, weight_rows, pad_second), BF16),
        ],
        axis=2,
    )
    w_hidden = jnp.zeros((dp_ranks, weight_rows, packed.shape[2]), BF16)
    for kz in range(PLANES):
        piece = lax.dynamic_index_in_dim(packed, plane ^ kz, 0, keepdims=False)
        piece = send(piece, kz=kz) if kz else piece
        for ky in range(lines):
            got = send(piece, ky=ky) if ky else piece
            w_hidden = lax.dynamic_update_index_in_dim(w_hidden, got, rank ^ (kz * lines + ky), 0)
    w_hidden = w_hidden.reshape(width, -1)
    down_start = 2 * slice_width + pad_first
    w_gate_up = w_hidden[:, : 2 * slice_width]
    w_down = w_hidden[:, down_start : down_start + slice_width]

    def gather_group(block):
        return [gather_tensor(piece) for piece in gather_planes(block)]

    def quarter_of(value):
        return lax.dynamic_slice_in_dim(value, part * quarter, quarter, 0)

    query_g, key_g = query_gain[0], key_gain[0]
    attn_in = rounded(normed(states.astype(F32), gains[0]))
    lin = product(attn_in, w_attend)
    query_lin, keyvalue_lin = lin[:, :head_width], lin[:, head_width:]

    def query_side(linear, gain_vector):
        return rotated(
            normed(linear.reshape(token_rows, heads_here, HEAD_WIDTH), gain_vector), cosines, sines
        )

    def key_side(linear, gain_vector):
        keys = linear[:, : 2 * HEAD_WIDTH].reshape(token_rows, 2, HEAD_WIDTH)
        keys = rotated(normed(keys, gain_vector), cosines, sines)
        return jnp.concatenate(
            [keys.reshape(token_rows, 2 * HEAD_WIDTH), linear[:, 2 * HEAD_WIDTH :]], axis=1
        )

    def to_pairs(value):
        return (
            value.reshape(blocks_here, STRETCH, PAIRS, 2, -1)
            .transpose(0, 2, 3, 1, 4)
            .reshape(blocks_here, PAIRS, 2 * STRETCH, -1)
        )

    def from_pairs(value):
        return (
            value.reshape(blocks_here, PAIRS, 2, STRETCH, -1)
            .transpose(0, 3, 1, 2, 4)
            .reshape(token_rows, heads_here, -1)
        )

    queries = to_pairs(rounded(query_side(query_lin, query_g)))
    keyvalues = gather_dp(rounded(key_side(keyvalue_lin, key_g)))
    keyvalues = keyvalues.reshape(slot_count, STRETCH, 4 * HEAD_WIDTH)
    attended = attend(counts, slots, parity, queries, keyvalues)
    attn_out = rounded(from_pairs(attended[..., :HEAD_WIDTH]).reshape(token_rows, head_width))
    logs = attended[..., HEAD_WIDTH]

    branch = scatter_tensor(quarters(by_cols(attn_out, w_output)))
    states_quarter = quarter_of(states).astype(F32)
    middle = states_quarter + branch
    ffn_in = rounded(normed(middle, gains[1]))

    down_grads = gather_group(quarter_of(out_grad))
    ffn_ins = gather_group(ffn_in)
    mixed_chunks, d_chunks, back_parts, out_parts = [], [], [], []
    for down_grad, ffn_chunk in zip(down_grads, ffn_ins):
        gate_up = product(ffn_chunk, w_gate_up)
        gate_pre, up_pre = gate_up[:, :slice_width], gate_up[:, slice_width:]
        sigmoid_gate = jax.nn.sigmoid(gate_pre)
        mixed = rounded(gate_pre * sigmoid_gate * up_pre)
        d_mixed = product(down_grad, w_down)
        d_gate = d_mixed * up_pre * sigmoid_gate * (1.0 + gate_pre * (1.0 - sigmoid_gate))
        d_up = d_mixed * gate_pre * sigmoid_gate
        d_gate_up = jnp.concatenate([rounded(d_gate), rounded(d_up)], axis=1)
        mixed_chunks.append(mixed)
        d_chunks.append(d_gate_up)

        def reduced(value):
            blocks = value.reshape(4, quarter, width)
            return scatter_tensor([blocks[0], blocks[2], blocks[1], blocks[3]])

        back_parts.append(reduced(by_cols(d_gate_up, w_gate_up)))
        out_parts.append(reduced(by_cols(mixed, w_down)))
    d_ffn_in = scatter_planes(back_parts)

    def norm_back(vector, gain_vector, grad):
        inverse = lax.rsqrt(jnp.mean(vector * vector, axis=-1, keepdims=True) + EPSILON)
        unit = vector * inverse
        scaled = grad * gain_vector
        back = inverse * (scaled - unit * jnp.mean(scaled * unit, axis=-1, keepdims=True))
        return back, jnp.sum(grad * unit, axis=0)

    d_middle, d_gain_ffn = norm_back(middle, gains[1], d_ffn_in)
    grad_middle = quarter_of(out_grad).astype(F32) + d_middle
    output_grad = in_order(gather_tensor(rounded(grad_middle)))

    d_wout = by_rows(output_grad, attn_out)
    d_heads = rounded(product(output_grad, w_output)).reshape(token_rows, heads_here, HEAD_WIDTH)
    d_pairs = to_pairs(d_heads)
    delta = jnp.sum(d_pairs.astype(F32) * attended[..., :HEAD_WIDTH], axis=-1)
    d_query, d_keyvalue = attend_back(
        counts,
        slots,
        parity,
        queries,
        d_pairs,
        logs[:, :, None, :],
        delta[:, :, None, :],
        keyvalues,
    )
    d_keyvalue_here = scatter_dp(d_keyvalue.reshape(dp_ranks, token_rows, 4 * HEAD_WIDTH))
    _, query_pull = jax.vjp(query_side, query_lin, query_g)
    d_query_lin, d_querygain = query_pull(from_pairs(d_query))
    _, key_pull = jax.vjp(key_side, keyvalue_lin, key_g)
    d_keyvalue_lin, d_keygain = key_pull(d_keyvalue_here)
    d_lin = jnp.concatenate([rounded(d_query_lin), rounded(d_keyvalue_lin)], axis=1)
    d_attn_in = scatter_tensor(quarters(by_cols(d_lin, w_attend)))
    d_states, d_gain_attn = norm_back(states_quarter, gains[0], d_attn_in)
    states_grad = in_order(gather_tensor(rounded(grad_middle + d_states))).astype(F32)

    d_wattend = scatter_dp(by_rows(attn_in, d_lin).reshape(dp_ranks, weight_rows, -1))
    d_wout = scatter_dp(d_wout.reshape(dp_ranks, weight_rows, -1))
    ffn_all = jnp.concatenate(ffn_ins, axis=0)
    down_all = jnp.concatenate(down_grads, axis=0)
    grads_hidden = jnp.concatenate(
        [
            by_rows(ffn_all, jnp.concatenate(d_chunks, axis=0)),
            by_rows(down_all, jnp.concatenate(mixed_chunks, axis=0)),
        ],
        axis=1,
    ).reshape(dp_ranks, weight_rows, 3 * slice_width)
    collected = jnp.zeros((PLANES, weight_rows, 3 * slice_width), F32)
    for kz in range(PLANES):
        total = lax.dynamic_index_in_dim(grads_hidden, rank ^ (kz * lines), 0, keepdims=False)
        for ky in range(1, lines):
            piece = lax.dynamic_index_in_dim(
                grads_hidden, rank ^ (kz * lines + ky), 0, keepdims=False
            )
            total = total + send(rounded(piece), ky=ky).astype(F32)
        if kz:
            total = send(rounded(total), kz=kz).astype(F32)
        collected = lax.dynamic_update_index_in_dim(collected, total, plane ^ kz, 0)

    def unsliced(index):
        piece = collected[:, :, index * slice_width : (index + 1) * slice_width]
        return piece.transpose(1, 0, 2).reshape(1, weight_rows, hidden)

    kv_grad = d_wattend[:, head_width:]
    spread = jnp.zeros((weight_rows, 2 * value_start), F32)
    spread = lax.dynamic_update_slice_in_dim(spread, kv_grad[:, : 2 * HEAD_WIDTH], first_key, 1)
    spread = lax.dynamic_update_slice_in_dim(
        spread, kv_grad[:, 2 * HEAD_WIDTH :], value_start + first_key, 1
    )
    d_wkeyvalue = lax.psum(spread, "tensor")

    result_quarter = rounded(middle + scatter_planes(out_parts))
    result = in_order(gather_tensor(result_quarter))

    small = jnp.concatenate([d_gain_attn, d_gain_ffn, d_querygain, d_keygain])
    small = lax.psum(small, ("dp", "tensor"))
    d_gains = lax.dynamic_slice_in_dim(
        small[: 2 * width].reshape(2, width), rank * weight_rows, weight_rows, 1
    ).T
    return (
        result,
        states_grad,
        d_wattend[None, :, :head_width],
        d_wkeyvalue[None],
        d_wout[None],
        unsliced(0),
        unsliced(1),
        unsliced(2),
        d_gains[None],
        small[2 * width : 2 * width + HEAD_WIDTH][None],
        small[2 * width + HEAD_WIDTH :][None],
    )


def local(*arguments):
    rows = arguments[0].shape[1] // lax.axis_size("dp")
    slots = arguments[10].shape[0]
    if lax.axis_size("dp") == 8 and lax.axis_size("tensor") == 4 and rows == 256 and slots == 24:
        return local_kernels(*arguments)
    return local_permutes(*arguments)


def solution(mesh):
    return jax.shard_map(
        local,
        mesh=mesh,
        in_specs=(
            P("dp", None),
            P(None, "dp", "tensor"),
            P(None, "dp", None),
            P(None, "dp", "tensor"),
            P(None, "dp", "tensor"),
            P(None, "dp", "tensor"),
            P(None, "dp", "tensor"),
            P(None, "dp", None),
            P(),
            P(),
            P(),
            P(),
            P("dp", None),
        ),
        out_specs=(
            P("dp", None),
            P("dp", None),
            P(None, "dp", "tensor"),
            P(None, "dp", None),
            P(None, "dp", "tensor"),
            P(None, "dp", "tensor"),
            P(None, "dp", "tensor"),
            P(None, "dp", "tensor"),
            P(None, "dp", None),
            P(),
            P(),
        ),
        check_vma=False,
    )
```

```python
import functools

import jax
import jax.numpy as jnp
from jax import lax
from jax.experimental import pallas as pl
from jax.experimental.pallas import tpu as pltpu
from jax.sharding import PartitionSpec as P

QUERY_HEADS = 24
KEYVALUE_HEADS = 6
HEAD_WIDTH = 64
STRETCH = 128
EPSILON = 1e-06
PLANES = 4
PAIRS = 3
LONGEST = 12
LOG2E = 1.4426950408889634
BF16 = jnp.bfloat16
F32 = jnp.float32


def product(left_side, right_side):
    return jnp.dot(left_side, right_side, preferred_element_type=F32)


def by_rows(left_side, right_side):
    return lax.dot_general(
        left_side, right_side, (((0,), (0,)), ((), ())), preferred_element_type=F32
    )


def by_cols(left_side, right_side):
    return lax.dot_general(
        left_side, right_side, (((1,), (1,)), ((), ())), preferred_element_type=F32
    )


def normed(vector, gain_vector):
    return (
        vector
        * lax.rsqrt(jnp.mean(vector * vector, axis=-1, keepdims=True) + EPSILON)
        * gain_vector
    )


def angles(positions, head_size):
    frequency = 10000.0 ** (-jnp.arange(head_size // 2, dtype=F32) * 2.0 / head_size)
    phase_angle = positions.astype(F32)[:, None] * frequency[None, :]
    return (jnp.cos(phase_angle)[:, None, :], jnp.sin(phase_angle)[:, None, :])


def rotated(vector, cosines, sines):
    half_width = vector.shape[-1] // 2
    front = vector[..., :half_width]
    behind = vector[..., half_width:]
    return jnp.concatenate(
        [front * cosines - behind * sines, behind * cosines + front * sines], axis=-1
    )


def visible_mask(shape, key_axis):
    keys = lax.broadcasted_iota(jnp.int32, shape, key_axis)
    queries = lax.rem(lax.broadcasted_iota(jnp.int32, shape, 1 - key_axis), STRETCH)
    return keys <= queries


def attend_kernel(count_ref, slots_ref, parity_ref, q_ref, kv_ref, out_ref, acc_ref):
    odd = parity_ref[0] == 1
    ones = jnp.ones((STRETCH, HEAD_WIDTH), BF16)

    def add_block(block, slot, last):
        tile = kv_ref[slot]
        keys = [tile[:, :64], tile[:, 64:128]]
        values = [
            jnp.concatenate([tile[:, 128:192], ones], axis=1),
            jnp.concatenate([tile[:, 192:256], ones], axis=1),
        ]
        middle_key = jnp.where(odd, keys[1], keys[0])
        middle_value = jnp.where(odd, values[1], values[0])
        for pair, key, value in (
            (0, keys[0], values[0]),
            (1, middle_key, middle_value),
            (2, keys[1], values[1]),
        ):
            scores = by_cols(q_ref[block, pair], key)
            weights = jnp.exp2(scores * (LOG2E * HEAD_WIDTH**-0.5))
            if last:
                weights = jnp.where(visible_mask(weights.shape, 1), weights, 0.0)
            acc_ref[pair] += product(weights.astype(BF16), value)

    def one_block(block, carry):
        acc_ref[...] = jnp.zeros_like(acc_ref)
        count = count_ref[block]

        def step(index, inner):
            add_block(block, slots_ref[block, index], False)
            return inner

        lax.fori_loop(0, count - 1, step, 0)
        add_block(block, slots_ref[block, count - 1], True)
        for pair in range(PAIRS):
            total = acc_ref[pair]
            denominator = total[:, HEAD_WIDTH:]
            out_ref[block, pair] = jnp.concatenate(
                [total[:, :HEAD_WIDTH] / denominator, jnp.log2(denominator)], axis=1
            )
        return carry

    lax.fori_loop(0, q_ref.shape[0], one_block, 0)


def attend(counts, slots, parity, queries, keyvalues):
    blocks = queries.shape[0]
    smem = pl.BlockSpec(memory_space=pltpu.SMEM)
    vmem = pl.BlockSpec(memory_space=pltpu.VMEM)
    return pl.pallas_call(
        attend_kernel,
        out_shape=jax.ShapeDtypeStruct((blocks, PAIRS, 2 * STRETCH, 128), F32),
        in_specs=[smem, smem, smem, vmem, vmem],
        out_specs=vmem,
        scratch_shapes=[pltpu.VMEM((PAIRS, 2 * STRETCH, 128), F32)],
        compiler_params=pltpu.CompilerParams(vmem_limit_bytes=40 << 20),
        cost_estimate=pl.CostEstimate(
            flops=4 * 20 * PAIRS * 256 * 128 * 64 * 4, bytes_accessed=8 << 20, transcendentals=0
        ),
        name="attend",
    )(counts, slots, parity, queries, keyvalues)


def attend_back_kernel(
    count_ref, slots_ref, parity_ref, q_ref, do_ref, log_ref, delta_ref, kv_ref, dq_ref, dkv_ref
):
    odd = parity_ref[0] == 1
    scale = HEAD_WIDTH**-0.5
    dq_ref[...] = jnp.zeros_like(dq_ref)
    dkv_ref[...] = jnp.zeros_like(dkv_ref)

    def add_block(block, slot, last):
        tile = kv_ref[slot]
        keys = [tile[:, :64], tile[:, 64:128]]
        values = [tile[:, 128:192], tile[:, 192:256]]
        middle_key = jnp.where(odd, keys[1], keys[0])
        middle_value = jnp.where(odd, values[1], values[0])
        d_keys, d_values = [], []
        for pair, key, value in (
            (0, keys[0], values[0]),
            (1, middle_key, middle_value),
            (2, keys[1], values[1]),
        ):
            query, d_out = q_ref[block, pair], do_ref[block, pair]
            scores = by_cols(key, query)
            weights = jnp.exp2(scores * (LOG2E * scale) - log_ref[block, pair])
            if last:
                weights = jnp.where(visible_mask(weights.shape, 0), weights, 0.0)
            d_weights = by_cols(value, d_out)
            d_scores = (weights * (d_weights - delta_ref[block, pair])).astype(BF16)
            d_values.append(product(weights.astype(BF16), d_out))
            d_keys.append(product(d_scores, query))
            dq_ref[block, pair] += by_rows(d_scores, key) * scale
        zero = jnp.zeros((STRETCH, HEAD_WIDTH), F32)
        parts = [
            (d_keys[0] + jnp.where(odd, zero, d_keys[1])) * scale,
            (d_keys[2] + jnp.where(odd, d_keys[1], zero)) * scale,
            d_values[0] + jnp.where(odd, zero, d_values[1]),
            d_values[2] + jnp.where(odd, d_values[1], zero),
        ]
        dkv_ref[slot] += jnp.concatenate(parts, axis=1)

    def one_block(block, carry):
        count = count_ref[block]

        def step(index, inner):
            add_block(block, slots_ref[block, index], False)
            return inner

        lax.fori_loop(0, count - 1, step, 0)
        add_block(block, slots_ref[block, count - 1], True)
        return carry

    lax.fori_loop(0, q_ref.shape[0], one_block, 0)


def attend_back(counts, slots, parity, queries, d_out, logs, delta, keyvalues):
    blocks = queries.shape[0]
    smem = pl.BlockSpec(memory_space=pltpu.SMEM)
    vmem = pl.BlockSpec(memory_space=pltpu.VMEM)
    return pl.pallas_call(
        attend_back_kernel,
        out_shape=(
            jax.ShapeDtypeStruct((blocks, PAIRS, 2 * STRETCH, HEAD_WIDTH), F32),
            jax.ShapeDtypeStruct(keyvalues.shape, F32),
        ),
        in_specs=[smem] * 3 + [vmem] * 5,
        out_specs=(vmem, vmem),
        compiler_params=pltpu.CompilerParams(vmem_limit_bytes=56 << 20),
        cost_estimate=pl.CostEstimate(
            flops=10 * 20 * PAIRS * 256 * 128 * 64 * 4, bytes_accessed=8 << 20, transcendentals=0
        ),
        name="attend_back",
    )(counts, slots, parity, queries, d_out, logs, delta, keyvalues)


class Place:
    def __init__(self, lines):
        rank, part = lax.axis_index("dp"), lax.axis_index("tensor")
        self.lines = lines
        self.z, self.y = rank // lines, lax.rem(rank, lines)
        self.x, self.c = part // 2, lax.rem(part, 2)
        self.quarter = self.c * 2 + self.x

    def plane(self, move):
        if move == 0:
            return self.z
        if move == 1:
            return self.z + 1 - 2 * lax.rem(self.z, 2)
        if move == 2:
            return self.z + 2 - 4 * (self.z // 2)
        return 3 - self.z

    def to(self, kz=0, ky=0, kx=0, kc=0):
        y = 1 - self.y if ky else self.y
        x = 1 - self.x if kx else self.x
        c = 1 - self.c if kc else self.c
        return (self.plane(kz) * self.lines + y, x * 2 + c)


class Links:
    def __init__(self, place, send_sems, recv_sems):
        self.place, self.send_sems, self.recv_sems = place, send_sems, recv_sems
        self.number, self.unsent = 0, []

    def greet(self, moves):
        barrier = pltpu.get_barrier_semaphore()
        for move in moves:
            pl.semaphore_signal(
                barrier, inc=1, device_id=self.place.to(**move), device_id_type=pl.DeviceIdType.MESH
            )
        pl.semaphore_wait(barrier, len(moves))

    def send(self, source, target, **move):
        number, self.number = self.number, self.number + 1
        copy = pltpu.make_async_remote_copy(
            src_ref=source,
            dst_ref=target,
            send_sem=self.send_sems.at[number],
            recv_sem=self.recv_sems.at[number],
            device_id=self.place.to(**move),
            device_id_type=pl.DeviceIdType.MESH,
        )
        copy.start()
        self.unsent.append(copy)
        return copy

    def sent(self, copy):
        copy.wait_send()
        self.unsent = [other for other in self.unsent if other is not copy]

    def finish(self):
        for copy in self.unsent:
            copy.wait_send()


def rows_at(index, size):
    return pl.ds(pl.multiple_of(index * size, size), size)


class Gather:
    def __init__(self, links, block, own=None):
        self.links, self.block, self.y = links, block, links.place.y
        self.own = block(0, self.y) if own is None else own
        self.lines = []

    def over_lines(self, move):
        place = self.block(move, self.y)
        source = self.own if move == 0 else place
        self.lines.append(self.links.send(source, place, ky=1))

    def start_planes(self):
        place = self.block(0, self.y)
        self.far = self.links.send(self.own, place, kz=2)
        self.near = self.links.send(self.own, place, kz=1)

    def start(self):
        self.start_planes()
        self.over_lines(0)

    def relay(self):
        self.near.wait_recv()
        self.over_lines(1)
        self.far.wait_recv()
        place = self.block(2, self.y)
        self.corner = self.links.send(place, place, kz=1)
        self.over_lines(2)

    def last(self):
        self.corner.wait_recv()
        self.over_lines(3)

    def finish(self):
        for copy in self.lines:
            copy.wait_recv()


def head_mean(value):
    row = lax.broadcasted_iota(jnp.int32, (128, 128), 0) // HEAD_WIDTH
    column = lax.broadcasted_iota(jnp.int32, (128, 128), 1) // HEAD_WIDTH
    average = jnp.where(row == column, 1.0 / HEAD_WIDTH, 0.0).astype(F32)
    return jnp.dot(
        value, average, preferred_element_type=F32, precision=lax.Precision.HIGHEST
    )


def halves_swapped(value):
    first = lax.rem(lax.broadcasted_iota(jnp.int32, value.shape, 1), HEAD_WIDTH) < HEAD_WIDTH // 2
    return jnp.where(
        first,
        pltpu.roll(value, 128 - HEAD_WIDTH // 2, 1),
        pltpu.roll(value, HEAD_WIDTH // 2, 1),
    )


class Scatter:
    ORDER = (3, 1, 2, 0)

    def __init__(self, links, y_out, y_in, z_out, z_in, sums):
        self.links = links
        self.y_out, self.y_in, self.z_out, self.z_in, self.sums = y_out, y_in, z_out, z_in, sums
        self.lines, self.planes = {}, {}

    def start(self, move, block):
        self.y_out[move] = block.astype(BF16)
        self.lines[move] = self.links.send(self.y_out.at[move], self.y_in.at[move], ky=1)

    def add(self, move, block):
        self.lines[move].wait_recv()
        total = block + self.y_in[move].astype(F32)
        if move in (3, 1):
            slot = 0 if move == 1 else 1
            self.z_out[slot] = total.astype(BF16)
            self.planes[slot] = self.links.send(self.z_out.at[slot], self.z_in.at[slot], kz=1)
        elif move == 2:
            self.planes[1].wait_recv()
            self.z_out[2] = (total + self.z_in[1].astype(F32)).astype(BF16)
            self.planes[2] = self.links.send(self.z_out.at[2], self.z_in.at[2], kz=2)
        else:
            self.sums[...] = total

    def finish(self):
        self.planes[0].wait_recv()
        self.planes[2].wait_recv()
        return self.sums[...] + self.z_in[0].astype(F32) + self.z_in[2].astype(F32)


def scatter_scratch(block):
    return [
        pltpu.VMEM((4, *block), BF16),
        pltpu.VMEM((4, *block), BF16),
        pltpu.VMEM((3, *block), BF16),
        pltpu.VMEM((3, *block), BF16),
        pltpu.VMEM(block, F32),
    ]


FORWARD_COPIES = 100


def forward_kernel(
    lines,
    heads,
    slice_width,
    longest,
    sequence_ref,
    offset_ref,
    states_ref,
    gains_in,
    w_attend_in,
    cosine_ref,
    sine_ref,
    head_gain_ref,
    w_output_in,
    w_hidden_in,
    grad_any,
    lin_any,
    attn_in_any,
    query_any,
    kv_any,
    attended_ref,
    attn_out_ref,
    gains_ref,
    w_attend_any,
    middle_ref,
    back_ref,
    gain_out_ref,
    d_heads_ref,
    output_grad_ref,
    mixed_ref,
    table_ref,
    collected_any,
    staged_any,
    w_down_any,
    lin_ref,
    attn_in_ref,
    query_ref,
    kv_ref,
    w_attend_ref,
    w_output_ref,
    w_hidden_ref,
    down_ref,
    ffn_ref,
    d_hidden_ref,
    partial_ref,
    core_out,
    core_in,
    x_out,
    x_in,
    sums_ref,
    z_out,
    z_in,
    y_out,
    y_in,
    local_sems,
    send_sems,
    recv_sems,
):
    here = Place(lines)
    links = Links(here, send_sems, recv_sems)
    token_rows, width = states_ref.shape
    quarter = token_rows // 4
    half = 2 * quarter
    weight_rows = w_attend_in.shape[0]
    hidden = slice_width
    blocks = token_rows // STRETCH
    slot_count = offset_ref.shape[0]
    mine, my_half = rows_at(here.quarter, quarter), rows_at(here.c, half)
    other_half = rows_at(1 - here.c, half)
    x_mine, x_other = rows_at(here.x, quarter), rows_at(1 - here.x, quarter)
    odd = here.c == 1

    def rank(move, line):
        return here.plane(move) * lines + line

    def rows_of(ref, columns=slice(None)):
        return lambda move, line: ref.at[rows_at(rank(move, line), weight_rows), columns]

    def columns_of(ref):
        return lambda move, line: ref.at[:, rows_at(rank(move, line), weight_rows)]

    loads = [
        pltpu.make_async_copy(grad_any, down_ref.at[here.z], local_sems.at[0]),
        pltpu.make_async_copy(w_output_in, rows_of(w_output_ref)(0, here.y), local_sems.at[1]),
        pltpu.make_async_copy(
            w_hidden_in.at[here.z], columns_of(w_hidden_ref)(0, here.y), local_sems.at[2]
        ),
    ]
    for load in loads:
        load.start()
    links.greet([dict(kc=1), dict(kx=1), dict(ky=1), dict(kz=1), dict(kz=2), dict(kz=3)])

    kv_width = 4 * HEAD_WIDTH
    gains = Gather(links, columns_of(gains_ref), gains_in)
    gains.start()
    first, second = slice(0, kv_width), slice(kv_width, w_attend_in.shape[1])
    kv_weights = Gather(links, rows_of(w_attend_ref, first), w_attend_in.at[:, first])
    kv_weights.start()
    query_weights = Gather(links, rows_of(w_attend_ref, second), w_attend_in.at[:, second])
    columns_of(gains_ref)(0, here.y)[...] = gains_in[...]
    rows_of(w_attend_ref)(0, here.y)[...] = w_attend_in[...]

    def fill(index, carry):
        block, place = index // longest, lax.rem(index, longest)
        sequence = sequence_ref[rank(0, here.y) * blocks + block]
        found = jnp.int32(0)
        for slot in range(slot_count):
            same = (sequence_ref[slot] == sequence) & (offset_ref[slot] == place * STRETCH)
            found = jnp.where(same, slot, found)
        table_ref[index] = found
        return carry

    lax.fori_loop(0, blocks * longest, fill, 0)
    kv_weights.relay()
    query_weights.start()
    gains.relay()
    gains.last()
    gains.finish()
    states = states_ref[...].astype(F32)
    inverse = lax.rsqrt(jnp.mean(states * states, axis=-1, keepdims=True) + EPSILON)
    attn_in_ref[...] = (states * inverse * gains_ref[0:1, :]).astype(BF16)

    def turned(value, group):
        value = (
            value
            * lax.rsqrt(head_mean(value * value) + EPSILON)
            * head_gain_ref[:, group * 128 : (group + 1) * 128]
        )
        return (value * cosine_ref[...] + halves_swapped(value) * sine_ref[...]).astype(BF16)

    kv_weights.last()
    kv_weights.finish()
    lin = product(attn_in_ref[...], w_attend_ref[:, first])
    lin_ref[:, first] = lin
    own_blocks = pl.ds(rank(0, here.y) * blocks, blocks)
    kv_ref[own_blocks, :, :128] = turned(lin[:, :128], 0).reshape(blocks, STRETCH, 128)
    kv_ref[own_blocks, :, 128:] = lin[:, 128:].astype(BF16).reshape(blocks, STRETCH, 128)
    keyvalue = Gather(
        links, lambda move, line: kv_ref.at[pl.ds(rank(move, line) * blocks, blocks)]
    )
    keyvalue.start()
    query_weights.relay()
    query_weights.last()
    keyvalue.relay()
    query_weights.finish()
    lin = product(attn_in_ref[...], w_attend_ref[:, second])
    lin_ref[:, second] = lin
    for pair in range(PAIRS):
        rotated_pair = turned(lin[:, pair * 128 : (pair + 1) * 128], pair + 1)
        for block in range(blocks):
            rows = rotated_pair[block * STRETCH : (block + 1) * STRETCH]
            query_ref[block, pair, :STRETCH] = rows[:, :HEAD_WIDTH]
            query_ref[block, pair, STRETCH:] = rows[:, HEAD_WIDTH:]
    keyvalue.last()

    output = Gather(links, rows_of(w_output_ref), w_output_in)
    output.start_planes()
    planes = {}

    def hidden_plane(move):
        planes[move] = links.send(
            w_hidden_in.at[here.plane(move)], columns_of(w_hidden_ref)(0, here.y), kz=move
        )

    hidden_lines = []

    def hidden_line(move):
        if move:
            planes[move].wait_recv()
        else:
            loads[2].wait()
        place = columns_of(w_hidden_ref)(move, here.y)
        hidden_lines.append(links.send(place, place, ky=1))

    def down_block(move):
        return down_ref.at[here.plane(move), mine]

    down_across, down_cores = {}, {}

    def down_x(move):
        down_across[move] = links.send(down_block(move), down_block(move), kx=1)

    def down_core(move):
        down_across[move].wait_recv()
        both = down_ref.at[here.plane(move), my_half]
        down_cores[move] = links.send(both, both, kc=1)

    saves = []

    def save(source, target):
        copy = pltpu.make_async_copy(source, target, local_sems.at[3 + len(saves)])
        copy.start()
        saves.append(copy)

    keyvalue.finish()
    output.over_lines(0)
    save(lin_ref, lin_any)
    save(attn_in_ref, attn_in_any)
    save(query_ref, query_any)
    save(kv_ref, kv_any)
    save(w_attend_ref, w_attend_any)

    span = longest * STRETCH
    ones = jnp.ones((span, HEAD_WIDTH), BF16)
    shape = (2 * STRETCH, span)
    ahead = lax.broadcasted_iota(jnp.int32, shape, 1) - lax.rem(
        lax.broadcasted_iota(jnp.int32, shape, 0), STRETCH
    )

    def attend_block(block):
        tiles = [kv_ref[table_ref[block * longest + place]] for place in range(longest)]
        tile = jnp.concatenate(tiles, axis=0)
        keys = [tile[:, :64], tile[:, 64:128]]
        values = [
            jnp.concatenate([tile[:, 128:192], ones], axis=1),
            jnp.concatenate([tile[:, 192:256], ones], axis=1),
        ]
        middle_key = jnp.where(odd, keys[1], keys[0])
        middle_value = jnp.where(odd, values[1], values[0])
        visible = ahead <= offset_ref[rank(0, here.y) * blocks + block]
        for pair, key, value in (
            (0, keys[0], values[0]),
            (1, middle_key, middle_value),
            (2, keys[1], values[1]),
        ):
            scores = by_cols(query_ref[block, pair], key)
            weights = jnp.exp2(scores * (LOG2E * HEAD_WIDTH**-0.5))
            weights = jnp.where(visible, weights, 0.0)
            total = product(weights.astype(BF16), value)
            denominator = total[:, HEAD_WIDTH:]
            heads_out = total[:, :HEAD_WIDTH] / denominator
            attended_ref[block, pair] = jnp.concatenate(
                [heads_out, jnp.log2(denominator)], axis=1
            )
            attn_out_ref[
                block * STRETCH : (block + 1) * STRETCH, pair * 128 : (pair + 1) * 128
            ] = jnp.concatenate([heads_out[:STRETCH], heads_out[STRETCH:]], axis=1).astype(BF16)

    attend_block(0)
    output.relay()
    loads[0].wait()
    down_far = links.send(down_block(0), down_block(0), kz=2)
    down_near = links.send(down_block(0), down_block(0), kz=1)
    attend_block(1)
    output.last()
    attend_block(2)
    for move in (1, 2, 3):
        hidden_plane(move)
    hidden_line(0)
    down_near.wait_recv()
    down_x(1)
    output.finish()

    loads[1].wait()
    cut = 4
    piece = width // cut
    core_copies = []
    for part in range(cut):
        columns = slice(part * piece, (part + 1) * piece)
        weight = w_output_ref[columns, :]
        core_out[2, :, columns] = by_cols(attn_out_ref[other_half, :], weight).astype(BF16)
        core_copies.append(
            links.send(core_out.at[2, :, columns], core_in.at[4, :, columns], kc=1)
        )
        partial_ref[0, :half, columns] = by_cols(attn_out_ref[my_half, :], weight)
    x_copies = []
    down_far.wait_recv()
    down_corner = links.send(down_block(2), down_block(2), kz=1)
    down_x(2)
    for part in range(cut):
        columns = slice(part * piece, (part + 1) * piece)
        core_copies[part].wait_recv()
        x_out[2, :, columns] = (
            partial_ref[0, x_other, columns] + core_in[4, x_other, columns].astype(F32)
        ).astype(BF16)
        x_copies.append(links.send(x_out.at[2, :, columns], x_in.at[4, :, columns], kx=1))
        middle_ref[:, columns] = (
            states_ref[mine, columns].astype(F32)
            + partial_ref[0, x_mine, columns]
            + core_in[4, x_mine, columns].astype(F32)
        )
    for part in range(cut):
        columns = slice(part * piece, (part + 1) * piece)
        x_copies[part].wait_recv()
        middle_ref[:, columns] += x_in[4, :, columns].astype(F32)
    middle = middle_ref[...]
    inverse = lax.rsqrt(jnp.mean(middle * middle, axis=-1, keepdims=True) + EPSILON)
    ffn_ref[here.z, mine, :] = (middle * inverse * gains_ref[1:2, :]).astype(BF16)

    def block_of(move):
        return ffn_ref.at[here.plane(move), mine]

    far = links.send(block_of(0), block_of(0), kz=2)
    near = links.send(block_of(0), block_of(0), kz=1)
    across = {0: links.send(block_of(0), block_of(0), kx=1)}
    cores = {}

    def spread(move):
        across[move].wait_recv()
        both = ffn_ref.at[here.plane(move), my_half]
        cores[move] = links.send(both, both, kc=1)

    down_corner.wait_recv()
    down_x(3)
    down_core(1)
    down_core(2)
    hidden_line(1)
    far.wait_recv()
    corner = links.send(block_of(2), block_of(2), kz=1)
    across[2] = links.send(block_of(2), block_of(2), kx=1)
    near.wait_recv()
    across[1] = links.send(block_of(1), block_of(1), kx=1)
    hidden_line(2)
    hidden_line(3)
    spread(0)
    spread(2)
    corner.wait_recv()
    across[3] = links.send(block_of(3), block_of(3), kx=1)
    spread(1)
    down_core(3)
    for copy in hidden_lines:
        copy.wait_recv()

    core_copies, x_copies, z_copies = {}, {}, {}
    order = (2, 3, 1, 0)

    def add_cores(index):
        move, slot = order[index], index % 2
        core_copies[move].wait_recv()
        total_rows = rows_at(here.c * 2 + 1 - here.x, quarter)
        if index > 1:
            links.sent(x_copies[order[index - 2]])
        x_out[slot] = (
            partial_ref[slot, total_rows, :] + core_in[move, x_other, :].astype(F32)
        ).astype(BF16)
        x_copies[move] = links.send(x_out.at[slot], x_in.at[move], kx=1)
        sums_ref[move] = partial_ref[slot, mine, :] + core_in[move, x_mine, :].astype(F32)

    def add_x(move):
        x_copies[move].wait_recv()
        sums_ref[move] += x_in[move].astype(F32)
        if move:
            z_out[move - 1] = sums_ref[move].astype(BF16)
            z_copies[move] = links.send(z_out.at[move - 1], z_in.at[move - 1], kz=move)

    for index, move in enumerate(order):
        slot = index % 2
        cores[move].wait_recv()
        if move:
            down_cores[move].wait_recv()
        plane = here.plane(move)
        chunk = ffn_ref[plane]
        gate_pre = by_cols(w_hidden_ref[:hidden, :], chunk)
        up_pre = by_cols(w_hidden_ref[hidden : 2 * hidden, :], chunk)
        sigmoid_gate = 1.0 / (1.0 + jnp.exp(-gate_pre))
        silu = gate_pre * sigmoid_gate
        columns = pl.ds(pl.multiple_of(plane * token_rows, token_rows), token_rows)
        mixed_ref[:, columns] = (silu * up_pre).astype(BF16)
        d_mixed = by_cols(w_hidden_ref[2 * hidden :, :], down_ref[plane])
        d_hidden_ref[:hidden, columns] = (
            d_mixed * up_pre * sigmoid_gate * (1.0 + gate_pre * (1.0 - sigmoid_gate))
        ).astype(BF16)
        d_hidden_ref[hidden:, columns] = (d_mixed * silu).astype(BF16)
        partial_ref[slot] = by_rows(d_hidden_ref[:, columns], w_hidden_ref[: 2 * hidden, :])
        if index > 1:
            links.sent(core_copies[order[index - 2]])
        core_out[slot] = partial_ref[slot, other_half, :].astype(BF16)
        core_copies[move] = links.send(core_out.at[slot], core_in.at[move], kc=1)
        if index == 0:
            spread(3)
        if index > 0:
            add_cores(index - 1)
        if index > 1:
            add_x(order[index - 2])
    add_cores(3)

    def gradient(move, line):
        columns = rows_at(rank(move, line), weight_rows)
        first = jnp.zeros((2 * hidden, weight_rows), F32)
        second = jnp.zeros((hidden, weight_rows), F32)
        for plane in range(4):
            tokens = slice(plane * token_rows, (plane + 1) * token_rows)
            first += product(d_hidden_ref[:, tokens], ffn_ref[plane, :, columns])
            second += product(mixed_ref[:, tokens], down_ref[plane, :, columns])
        return first, second

    def keep(target, pieces):
        target[: 2 * hidden] = pieces[0].astype(BF16)
        target[2 * hidden :] = pieces[1].astype(BF16)

    y_copies = {}
    for move in (3, 2, 1, 0):
        keep(y_out.at[move], gradient(move, 1 - here.y))
        y_copies[move] = links.send(y_out.at[move], y_in.at[move], ky=1)
        if move == 3:
            add_x(1)
    add_x(0)

    def gradient_sum(move):
        first, second = gradient(move, here.y)
        y_copies[move].wait_recv()
        links.sent(y_copies[move])
        first += y_in[move, : 2 * hidden].astype(F32)
        second += y_in[move, 2 * hidden :].astype(F32)
        keep(y_out.at[move], (first, second))

    for move in (1, 2, 3):
        z_copies[move].wait_recv()
    d_normed = sums_ref[0]
    for move in (1, 2, 3):
        d_normed += z_in[move - 1].astype(F32)
    middle = middle_ref[...]
    inverse = lax.rsqrt(jnp.mean(middle * middle, axis=-1, keepdims=True) + EPSILON)
    unit = middle * inverse
    gain_out_ref[...] = jnp.sum(d_normed * unit, axis=0, keepdims=True)
    scaled = d_normed * gains_ref[1:2, :]
    back = inverse * (scaled - unit * jnp.mean(scaled * unit, axis=-1, keepdims=True))
    grad_middle = down_ref[here.z, mine, :].astype(F32) + back
    back_ref[...] = grad_middle
    output_grad_ref[mine, :] = grad_middle.astype(BF16)
    block = output_grad_ref.at[mine]
    x_copy = links.send(block, block, kx=1)
    gradient_sum(3)
    last = links.send(y_out.at[3], collected_any.at[here.z], kz=3)
    x_copy.wait_recv()
    both = output_grad_ref.at[my_half]
    core = links.send(both, both, kc=1)
    save(w_hidden_ref.at[pl.ds(2 * hidden, hidden)], w_down_any)
    gradient_sum(2)
    save(y_out.at[2], staged_any.at[1])
    core.wait_recv()
    d_heads_ref[...] = product(output_grad_ref[...], w_output_ref[...]).astype(BF16)
    gradient_sum(1)
    save(y_out.at[1], staged_any.at[0])
    gradient_sum(0)
    save(y_out.at[0], collected_any.at[here.z])
    last.wait_recv()
    for copy in saves:
        copy.wait()
    links.finish()


def forward(
    lines,
    heads,
    slice_width,
    longest,
    sequence,
    offset,
    states,
    gains,
    w_attend,
    cosine,
    sine,
    head_gain,
    w_output,
    w_hidden,
    grad,
):
    token_rows, width = states.shape
    ranks = 4 * lines
    quarter = token_rows // 4
    half = 2 * quarter
    hidden = slice_width
    head_width = heads * HEAD_WIDTH
    weight_rows = width // ranks
    blocks = token_rows // STRETCH
    vmem = pl.BlockSpec(memory_space=pltpu.VMEM)
    smem = pl.BlockSpec(memory_space=pltpu.SMEM)
    hbm = pl.BlockSpec(memory_space=pl.ANY)
    shape = jax.ShapeDtypeStruct
    return pl.pallas_call(
        functools.partial(forward_kernel, lines, heads, slice_width, longest),
        out_shape=(
            shape((token_rows, w_attend.shape[1]), F32),
            shape((token_rows, width), BF16),
            shape((blocks, PAIRS, 2 * STRETCH, HEAD_WIDTH), BF16),
            shape((ranks * blocks, STRETCH, 4 * HEAD_WIDTH), BF16),
            shape((blocks, PAIRS, 2 * STRETCH, 128), F32),
            shape((token_rows, head_width), BF16),
            shape((gains.shape[0], width), F32),
            shape((width, w_attend.shape[1]), BF16),
            shape((quarter, width), F32),
            shape((quarter, width), F32),
            shape((1, width), F32),
            shape((token_rows, head_width), BF16),
            shape((token_rows, width), BF16),
            shape((hidden, 4 * token_rows), BF16),
            shape((blocks * longest,), jnp.int32),
            shape((4, 3 * hidden, weight_rows), BF16),
            shape((2, 3 * hidden, weight_rows), BF16),
            shape((hidden, width), BF16),
        ),
        in_specs=[smem] * 2 + [vmem] * 6 + [hbm] * 3,
        out_specs=(hbm,) * 4 + (vmem,) * 3 + (hbm,) + (vmem,) * 6 + (smem,) + (hbm,) * 3,
        scratch_shapes=[
            pltpu.VMEM((token_rows, w_attend.shape[1]), F32),
            pltpu.VMEM((token_rows, width), BF16),
            pltpu.VMEM((blocks, PAIRS, 2 * STRETCH, HEAD_WIDTH), BF16),
            pltpu.VMEM((ranks * blocks, STRETCH, 4 * HEAD_WIDTH), BF16),
            pltpu.VMEM((width, w_attend.shape[1]), BF16),
            pltpu.VMEM((width, head_width), BF16),
            pltpu.VMEM((3 * hidden, width), BF16),
            pltpu.VMEM((4, token_rows, width), BF16),
            pltpu.VMEM((4, token_rows, width), BF16),
            pltpu.VMEM((2 * hidden, 4 * token_rows), BF16),
            pltpu.VMEM((2, token_rows, width), F32),
            pltpu.VMEM((3, half, width), BF16),
            pltpu.VMEM((5, half, width), BF16),
            pltpu.VMEM((3, quarter, width), BF16),
            pltpu.VMEM((5, quarter, width), BF16),
            pltpu.VMEM((4, quarter, width), F32),
            pltpu.VMEM((3, quarter, width), BF16),
            pltpu.VMEM((3, quarter, width), BF16),
            pltpu.VMEM((4, 3 * hidden, weight_rows), BF16),
            pltpu.VMEM((4, 3 * hidden, weight_rows), BF16),
            pltpu.SemaphoreType.DMA((16,)),
            pltpu.SemaphoreType.DMA((FORWARD_COPIES,)),
            pltpu.SemaphoreType.DMA((FORWARD_COPIES,)),
        ],
        compiler_params=pltpu.CompilerParams(
            collective_id=0, has_side_effects=True, vmem_limit_bytes=64 << 20
        ),
        name="forward",
    )(
        sequence,
        offset,
        states,
        gains,
        w_attend,
        cosine,
        sine,
        head_gain,
        w_output,
        w_hidden,
        grad,
    )


BACKWARD_COPIES = 60


def backward_kernel(
    lines,
    heads,
    longest,
    sequence_ref,
    offset_ref,
    table_ref,
    query_ref,
    kv_ref,
    attended_ref,
    d_heads_ref,
    attn_out_ref,
    gains_ref,
    gain_ffn_ref,
    cosine_ref,
    sine_ref,
    head_gain_ref,
    lin_any,
    attn_in_any,
    output_grad_any,
    w_attend_any,
    back_any,
    states_any,
    middle_any,
    mixed_any,
    w_down_any,
    staged_any,
    collected_in,
    result_ref,
    states_grad_ref,
    g_attend_ref,
    g_output_ref,
    g_kv_ref,
    small_ref,
    collected_any,
    *scratch,
):
    here = Place(lines)
    del collected_in
    (
        lin_ref,
        attn_in_ref,
        output_grad_ref,
        w_attend_ref,
        back_ref,
        states_ref,
        middle_ref,
        mixed_ref,
        w_down_ref,
        d_query_ref,
        d_kv_ref,
        d_lin_ref,
        partial_ref,
        core_out,
        core_in,
        x_out,
        x_in,
        sums_ref,
        z_out,
        z_in,
        small_out,
        small_in,
        local_sems,
        send_sems,
        recv_sems,
    ) = scratch[:25]
    links = Links(here, send_sems, recv_sems)
    kv_sum = Scatter(links, *scratch[25:30])
    output_sum = Scatter(links, *scratch[30:35])
    attend_sum = Scatter(links, *scratch[35:40])
    token_rows, width = output_grad_ref.shape
    quarter = token_rows // 4
    half = 2 * quarter
    weight_rows = width // (4 * lines)
    kv_width = 4 * HEAD_WIDTH
    blocks = token_rows // STRETCH
    mine, other = rows_at(here.quarter, quarter), rows_at(here.c * 2 + 1 - here.x, quarter)
    my_half, other_half = rows_at(here.c, half), rows_at(1 - here.c, half)
    x_mine, x_other = rows_at(here.x, quarter), rows_at(1 - here.x, quarter)
    odd = here.c == 1
    scale = HEAD_WIDTH**-0.5

    loads = {}

    def load(number, source, target):
        copy = pltpu.make_async_copy(source, target, local_sems.at[number])
        copy.start()
        loads[number] = copy

    load(0, output_grad_any, output_grad_ref)
    load(1, w_down_any, w_down_ref)
    load(2, mixed_any, mixed_ref)
    load(3, lin_any, lin_ref)
    load(4, attn_in_any, attn_in_ref)
    load(5, w_attend_any, w_attend_ref)
    load(6, states_any.at[mine], states_ref)
    load(7, back_any, back_ref)
    load(8, middle_any, middle_ref)
    links.greet([dict(kc=1), dict(kx=1), dict(ky=1), dict(kz=1), dict(kz=2)])
    hidden_pushes = [
        links.send(staged_any.at[move - 1], collected_any.at[here.z], kz=move) for move in (2, 1)
    ]

    def rank(move, line):
        return here.plane(move) * lines + line

    core_copies, x_copies = {}, {}

    def out_start(move, slot):
        at = pl.ds(pl.multiple_of(here.plane(move) * token_rows, token_rows), token_rows)
        partial_ref[slot] = by_rows(mixed_ref[:, at], w_down_ref[...])
        core_out[move] = partial_ref[slot, other_half, :].astype(BF16)
        core_copies[move] = links.send(core_out.at[move], core_in.at[move], kc=1)

    def add_cores(move, slot):
        core_copies[move].wait_recv()
        x_out[move] = (partial_ref[slot, other, :] + core_in[move, x_other, :].astype(F32)).astype(
            BF16
        )
        x_copies[move] = links.send(x_out.at[move], x_in.at[move], kx=1)
        sums_ref[move] = partial_ref[slot, mine, :] + core_in[move, x_mine, :].astype(F32)

    def add_x(move):
        x_copies[move].wait_recv()
        sums_ref[move] += x_in[move].astype(F32)

    def columns(move, line):
        return rows_at(rank(move, line), weight_rows)

    def output_block(move, line):
        return by_rows(output_grad_ref[:, columns(move, line)], attn_out_ref[...])

    def attend_grad(move, line):
        return by_rows(attn_in_ref[:, columns(move, line)], d_lin_ref[...])

    loads[0].wait()
    for move in Scatter.ORDER:
        output_sum.start(move, output_block(move, 1 - here.y))

    span = longest * STRETCH
    shape = (2 * STRETCH, span)
    ahead = lax.broadcasted_iota(jnp.int32, shape, 1) - lax.rem(
        lax.broadcasted_iota(jnp.int32, shape, 0), STRETCH
    )

    def attend_block(block):
        rows = slice(block * STRETCH, (block + 1) * STRETCH)
        tiles = [kv_ref[table_ref[block * longest + place]] for place in range(longest)]
        tile = jnp.concatenate(tiles, axis=0)
        keys = [tile[:, :64], tile[:, 64:128]]
        values = [tile[:, 128:192], tile[:, 192:256]]
        middle_key = jnp.where(odd, keys[1], keys[0])
        middle_value = jnp.where(odd, values[1], values[0])
        visible = ahead <= offset_ref[rank(0, here.y) * blocks + block]
        d_keys, d_values = [], []
        for pair, key, value in (
            (0, keys[0], values[0]),
            (1, middle_key, middle_value),
            (2, keys[1], values[1]),
        ):
            query = query_ref[block, pair]
            both = d_heads_ref[rows, pair * 128 : (pair + 1) * 128]
            d_out = jnp.concatenate([both[:, :HEAD_WIDTH], both[:, HEAD_WIDTH:]], axis=0)
            kept = attended_ref[block, pair]
            delta = jnp.sum(d_out.astype(F32) * kept[:, :HEAD_WIDTH], axis=-1, keepdims=True)
            scores = by_cols(query, key)
            weights = jnp.exp2(
                scores * (LOG2E * scale) - kept[:, HEAD_WIDTH : HEAD_WIDTH + 1]
            )
            weights = jnp.where(visible, weights, 0.0)
            d_weights = by_cols(d_out, value)
            d_scores = (weights * (d_weights - delta)).astype(BF16)
            d_values.append(by_rows(weights.astype(BF16), d_out))
            d_keys.append(by_rows(d_scores, query))
            d_query_ref[block, pair] = product(d_scores, key) * scale
        zero = jnp.zeros((span, HEAD_WIDTH), F32)
        parts = [
            (d_keys[0] + jnp.where(odd, zero, d_keys[1])) * scale,
            (d_keys[2] + jnp.where(odd, d_keys[1], zero)) * scale,
            d_values[0] + jnp.where(odd, zero, d_values[1]),
            d_values[2] + jnp.where(odd, d_values[1], zero),
        ]
        d_kv_ref[block * longest : (block + 1) * longest] = jnp.concatenate(
            parts, axis=1
        ).reshape(longest, STRETCH, kv_width)

    attend_block(0)
    loads[1].wait()
    loads[2].wait()
    out_start(3, 0)
    out_start(1, 1)
    attend_block(1)
    add_cores(3, 0)
    out_start(2, 0)
    add_cores(1, 1)
    out_start(0, 1)
    attend_block(2)

    def kv_block(move, line):
        pieces = []
        for index in range(blocks):
            slot = rank(move, line) * blocks + index
            sequence = sequence_ref[slot]
            place = offset_ref[slot] // STRETCH
            total = jnp.zeros((STRETCH, kv_width), F32)
            for block in range(blocks):
                same = sequence_ref[rank(0, here.y) * blocks + block] == sequence
                total += jnp.where(same, d_kv_ref[block * longest + place], 0.0)
            pieces.append(total)
        return jnp.concatenate(pieces, axis=0)

    for move in Scatter.ORDER:
        kv_sum.start(move, kv_block(move, 1 - here.y))

    def group_back(group, at, grad):
        linear = lin_ref[:, at]
        inverse = lax.rsqrt(head_mean(linear * linear) + EPSILON)
        unit = linear * inverse
        grad = grad * cosine_ref[...] + halves_swapped(grad * sine_ref[...])
        gain = jnp.sum(grad * unit, axis=0, keepdims=True)
        scaled = grad * head_gain_ref[:, group * 128 : (group + 1) * 128]
        return inverse * (scaled - unit * head_mean(scaled * unit)), gain

    loads[3].wait()
    add_cores(2, 0)
    add_cores(0, 1)
    for move in Scatter.ORDER[:2]:
        output_sum.add(move, output_block(move, here.y))
    small_ref[...] = jnp.zeros_like(small_ref)
    small_ref[1:2, :] = gain_ffn_ref[...]
    for pair in range(PAIRS):
        grad = jnp.concatenate(
            [
                jnp.concatenate(
                    [d_query_ref[block, pair, :STRETCH], d_query_ref[block, pair, STRETCH:]], axis=1
                )
                for block in range(blocks)
            ],
            axis=0,
        )
        at = slice(kv_width + pair * 128, kv_width + (pair + 1) * 128)
        linear_grad, gain = group_back(pair + 1, at, grad)
        d_lin_ref[:, at] = linear_grad.astype(BF16)
        small_ref[2:3, (pair + 1) * 128 : (pair + 2) * 128] = gain
    for move in Scatter.ORDER:
        kv_sum.add(move, kv_block(move, here.y))
    add_x(3)
    z_out[1] = sums_ref[3].astype(BF16)
    z_copies = {1: links.send(z_out.at[1], z_in.at[1], kz=1)}
    add_x(1)
    z_out[0] = sums_ref[1].astype(BF16)
    z_copies[0] = links.send(z_out.at[0], z_in.at[0], kz=1)
    d_kv = kv_sum.finish()
    for move in Scatter.ORDER[2:]:
        output_sum.add(move, output_block(move, here.y))
    linear_grad, gain = group_back(0, slice(0, 128), d_kv[:, :128])
    d_lin_ref[:, :128] = linear_grad.astype(BF16)
    d_lin_ref[:, 128:kv_width] = d_kv[:, 128:].astype(BF16)
    small_ref[2:3, :128] = gain

    loads[4].wait()
    for move in Scatter.ORDER:
        attend_sum.start(move, attend_grad(move, 1 - here.y))
    add_x(2)
    add_x(0)
    z_copies[1].wait_recv()
    z_out[2] = (sums_ref[2] + z_in[1].astype(F32)).astype(BF16)
    z_copies[2] = links.send(z_out.at[2], z_in.at[2], kz=2)

    loads[5].wait()
    partial_ref[0] = by_cols(d_lin_ref[...], w_attend_ref[...])
    core_out[4] = partial_ref[0, other_half, :].astype(BF16)
    core_copies[4] = links.send(core_out.at[4], core_in.at[4], kc=1)
    add_cores(4, 0)
    attend_sum.add(3, attend_grad(3, here.y))
    attend_sum.add(1, attend_grad(1, here.y))
    add_x(4)
    loads[6].wait()
    loads[7].wait()
    states = states_ref[...].astype(F32)
    inverse = lax.rsqrt(jnp.mean(states * states, axis=-1, keepdims=True) + EPSILON)
    unit = states * inverse
    grad = sums_ref[4]
    small_ref[0:1, :] = jnp.sum(grad * unit, axis=0, keepdims=True)
    scaled = grad * gains_ref[0:1, :]
    total = back_ref[...] + inverse * (
        scaled - unit * jnp.mean(scaled * unit, axis=-1, keepdims=True)
    )
    states_grad_ref[mine, :] = total.astype(BF16)
    block = states_grad_ref.at[mine]
    states_x = links.send(block, block, kx=1)

    def small_step(step, **move):
        small_out[step] = small_ref[...]
        return links.send(small_out.at[step], small_in.at[step], **move)

    small = small_step(0, kc=1)
    attend_sum.add(2, attend_grad(2, here.y))
    small.wait_recv()
    small_ref[...] += small_in[0]
    small = small_step(1, kx=1)
    states_x.wait_recv()
    both = states_grad_ref.at[my_half]
    states_core = links.send(both, both, kc=1)
    small.wait_recv()
    small_ref[...] += small_in[1]
    small = small_step(2, ky=1)
    attend_sum.add(0, attend_grad(0, here.y))
    small.wait_recv()
    small_ref[...] += small_in[2]
    small = small_step(3, kz=1)
    small.wait_recv()
    small_ref[...] += small_in[3]
    small = small_step(4, kz=2)

    total = attend_sum.finish()
    part = here.x * 2 + here.c
    g_kv_ref[part] = total[:, :kv_width].astype(BF16)
    block = g_kv_ref.at[part]
    kv_x = links.send(block, block, kx=1)
    kv_core = links.send(block, block, kc=1)
    g_attend_ref[...] = total[:, kv_width:]
    z_copies[0].wait_recv()
    z_copies[2].wait_recv()
    loads[8].wait()
    result_ref[mine, :] = (
        middle_ref[...] + sums_ref[0] + z_in[0].astype(F32) + z_in[2].astype(F32)
    ).astype(BF16)
    block = result_ref.at[mine]
    result_x = links.send(block, block, kx=1)
    kv_x.wait_recv()
    block = g_kv_ref.at[(1 - here.x) * 2 + here.c]
    kv_both = links.send(block, block, kc=1)
    g_output_ref[...] = output_sum.finish()
    small.wait_recv()
    small_ref[...] += small_in[4]
    result_x.wait_recv()
    both = result_ref.at[my_half]
    result_core = links.send(both, both, kc=1)
    for copy in (states_core, kv_core, kv_both, result_core, *hidden_pushes):
        copy.wait_recv()
    links.finish()


def backward(lines, heads, longest, *arguments):
    lin, attn_in, mixed, w_attend = arguments[13], arguments[14], arguments[20], arguments[16]
    token_rows, width = attn_in.shape
    quarter = token_rows // 4
    half = 2 * quarter
    weight_rows = width // (4 * lines)
    head_width = heads * HEAD_WIDTH
    blocks = token_rows // STRETCH
    vmem = pl.BlockSpec(memory_space=pltpu.VMEM)
    smem = pl.BlockSpec(memory_space=pltpu.SMEM)
    hbm = pl.BlockSpec(memory_space=pl.ANY)
    shape = jax.ShapeDtypeStruct
    return pl.pallas_call(
        functools.partial(backward_kernel, lines, heads, longest),
        out_shape=(
            shape((token_rows, width), BF16),
            shape((token_rows, width), BF16),
            shape((weight_rows, head_width), F32),
            shape((weight_rows, head_width), F32),
            shape((4, weight_rows, 4 * HEAD_WIDTH), BF16),
            shape((8, width), F32),
            shape(arguments[-1].shape, BF16),
        ),
        in_specs=[smem] * 3 + [vmem] * 10 + [hbm] * 11,
        out_specs=(vmem,) * 6 + (hbm,),
        scratch_shapes=[
            pltpu.VMEM(lin.shape, F32),
            pltpu.VMEM(attn_in.shape, BF16),
            pltpu.VMEM((token_rows, width), BF16),
            pltpu.VMEM(w_attend.shape, BF16),
            pltpu.VMEM((quarter, width), F32),
            pltpu.VMEM((quarter, width), BF16),
            pltpu.VMEM((quarter, width), F32),
            pltpu.VMEM(mixed.shape, BF16),
            pltpu.VMEM((mixed.shape[0], width), BF16),
            pltpu.VMEM((blocks, PAIRS, 2 * STRETCH, HEAD_WIDTH), F32),
            pltpu.VMEM((blocks * longest, STRETCH, 4 * HEAD_WIDTH), F32),
            pltpu.VMEM(lin.shape, BF16),
            pltpu.VMEM((2, token_rows, width), F32),
            pltpu.VMEM((5, half, width), BF16),
            pltpu.VMEM((5, half, width), BF16),
            pltpu.VMEM((5, quarter, width), BF16),
            pltpu.VMEM((5, quarter, width), BF16),
            pltpu.VMEM((5, quarter, width), F32),
            pltpu.VMEM((3, quarter, width), BF16),
            pltpu.VMEM((3, quarter, width), BF16),
            pltpu.VMEM((5, 8, width), F32),
            pltpu.VMEM((5, 8, width), F32),
            pltpu.SemaphoreType.DMA((10,)),
            pltpu.SemaphoreType.DMA((BACKWARD_COPIES,)),
            pltpu.SemaphoreType.DMA((BACKWARD_COPIES,)),
            *scatter_scratch((token_rows, 4 * HEAD_WIDTH)),
            *scatter_scratch((weight_rows, head_width)),
            *scatter_scratch((weight_rows, lin.shape[1])),
        ],
        compiler_params=pltpu.CompilerParams(
            collective_id=1, has_side_effects=True, vmem_limit_bytes=64 << 20
        ),
        input_output_aliases={len(arguments) - 1: 6},
        name="backward",
    )(*arguments)


def local_kernels(
    states,
    query_weight,
    keyvalue_matrix,
    output_weight,
    gate_weight,
    up_weight,
    down_weight,
    norm_gains,
    query_gain,
    key_gain,
    slot_sequence,
    slot_offset,
    out_grad,
):
    token_rows, width = states.shape
    dp_ranks = lax.axis_size("dp")
    tensor_ranks = lax.axis_size("tensor")
    lines = dp_ranks // PLANES
    rank, part = lax.axis_index("dp"), lax.axis_index("tensor")
    heads_here = QUERY_HEADS // tensor_ranks
    head_width = heads_here * HEAD_WIDTH
    sharing_count = QUERY_HEADS // KEYVALUE_HEADS
    blocks_here = token_rows // STRETCH
    slot_count = slot_sequence.shape[0]
    hidden = gate_weight.shape[2]
    slice_width = hidden // PLANES
    weight_rows = width // dp_ranks

    offset_here = lax.dynamic_slice_in_dim(slot_offset, rank * blocks_here, blocks_here)
    positions = (offset_here[:, None] + jnp.arange(STRETCH, dtype=jnp.int32)[None, :]).reshape(-1)
    columns = jnp.arange(2 * HEAD_WIDTH, dtype=jnp.int32)
    exponent = -(columns % (HEAD_WIDTH // 2)).astype(F32) * 2.0 / HEAD_WIDTH
    phase = positions.astype(F32)[:, None] * (10000.0**exponent)[None, :]
    cosine = jnp.cos(phase)
    sine = jnp.sin(phase) * jnp.where(columns % HEAD_WIDTH < HEAD_WIDTH // 2, -1.0, 1.0)[None, :]
    head_gain = jnp.concatenate([jnp.tile(key_gain[0], 2), jnp.tile(query_gain[0], heads_here)])

    first_key = (part * heads_here) // sharing_count * HEAD_WIDTH
    value_start = KEYVALUE_HEADS * HEAD_WIDTH
    w_attend = jnp.concatenate(
        [
            lax.dynamic_slice_in_dim(keyvalue_matrix[0], first_key, 2 * HEAD_WIDTH, 1),
            lax.dynamic_slice_in_dim(
                keyvalue_matrix[0], value_start + first_key, 2 * HEAD_WIDTH, 1
            ),
            query_weight[0],
        ],
        axis=1,
    )
    gains = jnp.pad(norm_gains[0].T.astype(F32), ((0, 6), (0, 0)))

    def turned(weight):
        return weight[0].reshape(weight_rows, PLANES, slice_width).transpose(1, 2, 0)

    packed = jnp.concatenate(
        [turned(gate_weight), turned(up_weight), turned(down_weight)], axis=1
    )
    (
        lin,
        attn_in,
        queries,
        keyvalues,
        attended,
        attn_out,
        gains,
        w_attend,
        middle_rows,
        back,
        gain_ffn,
        d_heads,
        output_grad,
        mixed,
        table,
        collected,
        staged,
        w_down,
    ) = forward(
        lines,
        heads_here,
        slice_width,
        LONGEST,
        slot_sequence,
        slot_offset,
        states,
        gains,
        w_attend,
        cosine,
        sine,
        head_gain[None],
        output_weight[0],
        packed,
        out_grad,
    )
    result, states_grad, g_attend, g_output, g_kv, small, collected = backward(
        lines,
        heads_here,
        LONGEST,
        slot_sequence,
        slot_offset,
        table,
        queries,
        keyvalues,
        attended,
        d_heads,
        attn_out,
        gains,
        gain_ffn,
        cosine,
        sine,
        head_gain[None],
        lin,
        attn_in,
        output_grad,
        w_attend,
        back,
        states,
        middle_rows,
        mixed,
        w_down,
        staged,
        collected,
    )

    def hidden_grad(index):
        piece = collected[:, index * slice_width : (index + 1) * slice_width]
        return piece.transpose(2, 0, 1).astype(F32).reshape(1, weight_rows, hidden)

    d_keyvalue_matrix = jnp.zeros((weight_rows, 2 * value_start), F32)
    for other in range(tensor_ranks):
        start = (other * heads_here) // sharing_count * HEAD_WIDTH
        block = g_kv[other].astype(F32)
        for offset, piece in (
            (start, block[:, : 2 * HEAD_WIDTH]),
            (value_start + start, block[:, 2 * HEAD_WIDTH :]),
        ):
            after = 2 * value_start - offset - 2 * HEAD_WIDTH
            d_keyvalue_matrix += jnp.pad(piece, ((0, 0), (offset, after)))
    head_gains = small[2, : head_width + 2 * HEAD_WIDTH].reshape(-1, HEAD_WIDTH)
    d_gains = lax.dynamic_slice_in_dim(small[:2], rank * weight_rows, weight_rows, 1).T
    return (
        result,
        states_grad.astype(F32),
        g_attend[None],
        d_keyvalue_matrix[None],
        g_output[None],
        hidden_grad(0),
        hidden_grad(1),
        hidden_grad(2),
        d_gains[None],
        jnp.sum(head_gains[2:], axis=0)[None],
        jnp.sum(head_gains[:2], axis=0)[None],
    )


def local_permutes(
    states,
    query_weight,
    keyvalue_matrix,
    output_weight,
    gate_weight,
    up_weight,
    down_weight,
    norm_gains,
    query_gain,
    key_gain,
    slot_sequence,
    slot_offset,
    out_grad,
):
    token_rows, width = states.shape
    dp_ranks = lax.axis_size("dp")
    tensor_ranks = lax.axis_size("tensor")
    lines = dp_ranks // PLANES
    rank, part = lax.axis_index("dp"), lax.axis_index("tensor")
    plane, line = rank // lines, rank % lines
    quarter = token_rows // tensor_ranks
    heads_here = QUERY_HEADS // tensor_ranks
    head_width = heads_here * HEAD_WIDTH
    sharing_count = QUERY_HEADS // KEYVALUE_HEADS
    blocks_here = token_rows // STRETCH
    slot_count = slot_sequence.shape[0]
    hidden = gate_weight.shape[2]
    slice_width = hidden // PLANES
    weight_rows = width // dp_ranks

    def send(value, kz=0, ky=0, kx=0, kc=0):
        move_rank, move_part = kz * lines + ky, kx * 2 + kc
        pairs = [
            (r * tensor_ranks + p, (r ^ move_rank) * tensor_ranks + (p ^ move_part))
            for r in range(dp_ranks)
            for p in range(tensor_ranks)
        ]
        return lax.ppermute(value, ("dp", "tensor"), pairs)

    def gather_planes(value):
        near = send(value, kz=1)
        far = send(value, kz=2)
        return [value, near, far, send(far, kz=1)]

    def gather_dp(value):
        whole = jnp.zeros((dp_ranks, *value.shape), value.dtype)
        for kz, piece in enumerate(gather_planes(value)):
            for ky in range(lines):
                got = send(piece, ky=ky) if ky else piece
                whole = lax.dynamic_update_index_in_dim(whole, got, rank ^ (kz * lines + ky), 0)
        return whole

    def rounded(value):
        return value.astype(BF16)

    def scatter_dp(whole):
        def piece(move):
            return lax.dynamic_index_in_dim(whole, rank ^ move, 0, keepdims=False)

        parts = []
        for kz in range(PLANES):
            total = piece(kz * lines).astype(F32)
            for ky in range(1, lines):
                total = total + send(rounded(piece(kz * lines + ky)), ky=ky).astype(F32)
            parts.append(total)
        return scatter_planes(parts)

    def scatter_planes(parts):
        near = parts[0] + send(rounded(parts[1]), kz=1).astype(F32)
        far = parts[2] + send(rounded(parts[3]), kz=1).astype(F32)
        return near + send(rounded(far), kz=2).astype(F32)

    def scatter_tensor(blocks):
        got = send(rounded(jnp.concatenate([blocks[1], blocks[3]], axis=0)), kc=1).astype(F32)
        rows = blocks[0].shape[0]
        here = blocks[0] + got[:rows]
        there = blocks[2] + got[rows:]
        return here + send(rounded(there), kx=1).astype(F32)

    def gather_tensor(block):
        both = jnp.concatenate([block, send(block, kx=1)], axis=0)
        return jnp.concatenate([both, send(both, kc=1)], axis=0)

    def in_order(blocks):
        whole = jnp.zeros_like(blocks)
        for index, move in enumerate((0, 2, 1, 3)):
            whole = lax.dynamic_update_slice_in_dim(
                whole,
                blocks[index * quarter : (index + 1) * quarter],
                (part ^ move) * quarter,
                0,
            )
        return whole

    def quarters(value):
        return [
            lax.dynamic_slice_in_dim(value, (part ^ move) * quarter, quarter, 0)
            for move in range(tensor_ranks)
        ]

    sequence_here = lax.dynamic_slice_in_dim(slot_sequence, rank * blocks_here, blocks_here)
    offset_here = lax.dynamic_slice_in_dim(slot_offset, rank * blocks_here, blocks_here)
    counts = offset_here // STRETCH + 1
    places = jnp.arange(slot_count, dtype=jnp.int32)
    same = (slot_sequence[None, None, :] == sequence_here[:, None, None]) & (
        slot_offset[None, None, :] == places[None, :, None] * STRETCH
    )
    slots = jnp.sum(jnp.where(same, places[None, None, :], 0), axis=2).astype(jnp.int32)
    parity = jnp.reshape(part % 2, (1,)).astype(jnp.int32)
    positions = (offset_here[:, None] + jnp.arange(STRETCH, dtype=jnp.int32)[None, :]).reshape(-1)
    cosines, sines = angles(positions, HEAD_WIDTH)

    first_key = (part * heads_here) // sharing_count * HEAD_WIDTH
    value_start = KEYVALUE_HEADS * HEAD_WIDTH
    kv_columns = [
        lax.dynamic_slice_in_dim(keyvalue_matrix[0], first_key, 2 * HEAD_WIDTH, 1),
        lax.dynamic_slice_in_dim(keyvalue_matrix[0], value_start + first_key, 2 * HEAD_WIDTH, 1),
    ]
    gains = gather_dp(norm_gains[0].T).transpose(1, 0, 2).reshape(2, width).astype(F32)
    w_attend = gather_dp(jnp.concatenate([query_weight[0], *kv_columns], axis=1)).reshape(width, -1)
    w_output = gather_dp(output_weight[0]).reshape(width, head_width)

    def sliced(weight):
        return weight[0].reshape(weight_rows, PLANES, slice_width).transpose(1, 0, 2)

    pad_first = -2 * slice_width % 128
    pad_second = -slice_width % 128
    packed = jnp.concatenate(
        [
            sliced(gate_weight),
            sliced(up_weight),
            jnp.zeros((PLANES, weight_rows, pad_first), BF16),
            sliced(down_weight),
            jnp.zeros((PLANES, weight_rows, pad_second), BF16),
        ],
        axis=2,
    )
    w_hidden = jnp.zeros((dp_ranks, weight_rows, packed.shape[2]), BF16)
    for kz in range(PLANES):
        piece = lax.dynamic_index_in_dim(packed, plane ^ kz, 0, keepdims=False)
        piece = send(piece, kz=kz) if kz else piece
        for ky in range(lines):
            got = send(piece, ky=ky) if ky else piece
            w_hidden = lax.dynamic_update_index_in_dim(w_hidden, got, rank ^ (kz * lines + ky), 0)
    w_hidden = w_hidden.reshape(width, -1)
    down_start = 2 * slice_width + pad_first
    w_gate_up = w_hidden[:, : 2 * slice_width]
    w_down = w_hidden[:, down_start : down_start + slice_width]

    def gather_group(block):
        return [gather_tensor(piece) for piece in gather_planes(block)]

    def quarter_of(value):
        return lax.dynamic_slice_in_dim(value, part * quarter, quarter, 0)

    query_g, key_g = query_gain[0], key_gain[0]
    attn_in = rounded(normed(states.astype(F32), gains[0]))
    lin = product(attn_in, w_attend)
    query_lin, keyvalue_lin = lin[:, :head_width], lin[:, head_width:]

    def query_side(linear, gain_vector):
        return rotated(
            normed(linear.reshape(token_rows, heads_here, HEAD_WIDTH), gain_vector), cosines, sines
        )

    def key_side(linear, gain_vector):
        keys = linear[:, : 2 * HEAD_WIDTH].reshape(token_rows, 2, HEAD_WIDTH)
        keys = rotated(normed(keys, gain_vector), cosines, sines)
        return jnp.concatenate(
            [keys.reshape(token_rows, 2 * HEAD_WIDTH), linear[:, 2 * HEAD_WIDTH :]], axis=1
        )

    def to_pairs(value):
        return (
            value.reshape(blocks_here, STRETCH, PAIRS, 2, -1)
            .transpose(0, 2, 3, 1, 4)
            .reshape(blocks_here, PAIRS, 2 * STRETCH, -1)
        )

    def from_pairs(value):
        return (
            value.reshape(blocks_here, PAIRS, 2, STRETCH, -1)
            .transpose(0, 3, 1, 2, 4)
            .reshape(token_rows, heads_here, -1)
        )

    queries = to_pairs(rounded(query_side(query_lin, query_g)))
    keyvalues = gather_dp(rounded(key_side(keyvalue_lin, key_g)))
    keyvalues = keyvalues.reshape(slot_count, STRETCH, 4 * HEAD_WIDTH)
    attended = attend(counts, slots, parity, queries, keyvalues)
    attn_out = rounded(from_pairs(attended[..., :HEAD_WIDTH]).reshape(token_rows, head_width))
    logs = attended[..., HEAD_WIDTH]

    branch = scatter_tensor(quarters(by_cols(attn_out, w_output)))
    states_quarter = quarter_of(states).astype(F32)
    middle = states_quarter + branch
    ffn_in = rounded(normed(middle, gains[1]))

    down_grads = gather_group(quarter_of(out_grad))
    ffn_ins = gather_group(ffn_in)
    mixed_chunks, d_chunks, back_parts, out_parts = [], [], [], []
    for down_grad, ffn_chunk in zip(down_grads, ffn_ins):
        gate_up = product(ffn_chunk, w_gate_up)
        gate_pre, up_pre = gate_up[:, :slice_width], gate_up[:, slice_width:]
        sigmoid_gate = jax.nn.sigmoid(gate_pre)
        mixed = rounded(gate_pre * sigmoid_gate * up_pre)
        d_mixed = product(down_grad, w_down)
        d_gate = d_mixed * up_pre * sigmoid_gate * (1.0 + gate_pre * (1.0 - sigmoid_gate))
        d_up = d_mixed * gate_pre * sigmoid_gate
        d_gate_up = jnp.concatenate([rounded(d_gate), rounded(d_up)], axis=1)
        mixed_chunks.append(mixed)
        d_chunks.append(d_gate_up)

        def reduced(value):
            blocks = value.reshape(4, quarter, width)
            return scatter_tensor([blocks[0], blocks[2], blocks[1], blocks[3]])

        back_parts.append(reduced(by_cols(d_gate_up, w_gate_up)))
        out_parts.append(reduced(by_cols(mixed, w_down)))
    d_ffn_in = scatter_planes(back_parts)

    def norm_back(vector, gain_vector, grad):
        inverse = lax.rsqrt(jnp.mean(vector * vector, axis=-1, keepdims=True) + EPSILON)
        unit = vector * inverse
        scaled = grad * gain_vector
        back = inverse * (scaled - unit * jnp.mean(scaled * unit, axis=-1, keepdims=True))
        return back, jnp.sum(grad * unit, axis=0)

    d_middle, d_gain_ffn = norm_back(middle, gains[1], d_ffn_in)
    grad_middle = quarter_of(out_grad).astype(F32) + d_middle
    output_grad = in_order(gather_tensor(rounded(grad_middle)))

    d_wout = by_rows(output_grad, attn_out)
    d_heads = rounded(product(output_grad, w_output)).reshape(token_rows, heads_here, HEAD_WIDTH)
    d_pairs = to_pairs(d_heads)
    delta = jnp.sum(d_pairs.astype(F32) * attended[..., :HEAD_WIDTH], axis=-1)
    d_query, d_keyvalue = attend_back(
        counts,
        slots,
        parity,
        queries,
        d_pairs,
        logs[:, :, None, :],
        delta[:, :, None, :],
        keyvalues,
    )
    d_keyvalue_here = scatter_dp(d_keyvalue.reshape(dp_ranks, token_rows, 4 * HEAD_WIDTH))
    _, query_pull = jax.vjp(query_side, query_lin, query_g)
    d_query_lin, d_querygain = query_pull(from_pairs(d_query))
    _, key_pull = jax.vjp(key_side, keyvalue_lin, key_g)
    d_keyvalue_lin, d_keygain = key_pull(d_keyvalue_here)
    d_lin = jnp.concatenate([rounded(d_query_lin), rounded(d_keyvalue_lin)], axis=1)
    d_attn_in = scatter_tensor(quarters(by_cols(d_lin, w_attend)))
    d_states, d_gain_attn = norm_back(states_quarter, gains[0], d_attn_in)
    states_grad = in_order(gather_tensor(rounded(grad_middle + d_states))).astype(F32)

    d_wattend = scatter_dp(by_rows(attn_in, d_lin).reshape(dp_ranks, weight_rows, -1))
    d_wout = scatter_dp(d_wout.reshape(dp_ranks, weight_rows, -1))
    ffn_all = jnp.concatenate(ffn_ins, axis=0)
    down_all = jnp.concatenate(down_grads, axis=0)
    grads_hidden = jnp.concatenate(
        [
            by_rows(ffn_all, jnp.concatenate(d_chunks, axis=0)),
            by_rows(down_all, jnp.concatenate(mixed_chunks, axis=0)),
        ],
        axis=1,
    ).reshape(dp_ranks, weight_rows, 3 * slice_width)
    collected = jnp.zeros((PLANES, weight_rows, 3 * slice_width), F32)
    for kz in range(PLANES):
        total = lax.dynamic_index_in_dim(grads_hidden, rank ^ (kz * lines), 0, keepdims=False)
        for ky in range(1, lines):
            piece = lax.dynamic_index_in_dim(
                grads_hidden, rank ^ (kz * lines + ky), 0, keepdims=False
            )
            total = total + send(rounded(piece), ky=ky).astype(F32)
        if kz:
            total = send(rounded(total), kz=kz).astype(F32)
        collected = lax.dynamic_update_index_in_dim(collected, total, plane ^ kz, 0)

    def unsliced(index):
        piece = collected[:, :, index * slice_width : (index + 1) * slice_width]
        return piece.transpose(1, 0, 2).reshape(1, weight_rows, hidden)

    kv_grad = d_wattend[:, head_width:]
    spread = jnp.zeros((weight_rows, 2 * value_start), F32)
    spread = lax.dynamic_update_slice_in_dim(spread, kv_grad[:, : 2 * HEAD_WIDTH], first_key, 1)
    spread = lax.dynamic_update_slice_in_dim(
        spread, kv_grad[:, 2 * HEAD_WIDTH :], value_start + first_key, 1
    )
    d_wkeyvalue = lax.psum(spread, "tensor")

    result_quarter = rounded(middle + scatter_planes(out_parts))
    result = in_order(gather_tensor(result_quarter))

    small = jnp.concatenate([d_gain_attn, d_gain_ffn, d_querygain, d_keygain])
    small = lax.psum(small, ("dp", "tensor"))
    d_gains = lax.dynamic_slice_in_dim(
        small[: 2 * width].reshape(2, width), rank * weight_rows, weight_rows, 1
    ).T
    return (
        result,
        states_grad,
        d_wattend[None, :, :head_width],
        d_wkeyvalue[None],
        d_wout[None],
        unsliced(0),
        unsliced(1),
        unsliced(2),
        d_gains[None],
        small[2 * width : 2 * width + HEAD_WIDTH][None],
        small[2 * width + HEAD_WIDTH :][None],
    )


def local(*arguments):
    rows = arguments[0].shape[1] // lax.axis_size("dp")
    slots = arguments[10].shape[0]
    if lax.axis_size("dp") == 8 and lax.axis_size("tensor") == 4 and rows == 256 and slots == 24:
        return local_kernels(*arguments)
    return local_permutes(*arguments)


def solution(mesh):
    return jax.shard_map(
        local,
        mesh=mesh,
        in_specs=(
            P("dp", None),
            P(None, "dp", "tensor"),
            P(None, "dp", None),
            P(None, "dp", "tensor"),
            P(None, "dp", "tensor"),
            P(None, "dp", "tensor"),
            P(None, "dp", "tensor"),
            P(None, "dp", None),
            P(),
            P(),
            P(),
            P(),
            P("dp", None),
        ),
        out_specs=(
            P("dp", None),
            P("dp", None),
            P(None, "dp", "tensor"),
            P(None, "dp", None),
            P(None, "dp", "tensor"),
            P(None, "dp", "tensor"),
            P(None, "dp", "tensor"),
            P(None, "dp", "tensor"),
            P(None, "dp", None),
            P(),
            P(),
        ),
        check_vma=False,
    )
```

```python
import functools

import jax
import jax.numpy as jnp
import numpy as np
from jax import lax
from jax.experimental import pallas as pl
from jax.experimental.pallas import tpu as pltpu
from jax.sharding import PartitionSpec as P

QUERY_HEADS = 24
KEYVALUE_HEADS = 6
HEAD_WIDTH = 64
STRETCH = 128
EPSILON = 1e-06
PLANES = 4
PAIRS = 3
LONGEST = 12
LOG2E = 1.4426950408889634
BF16 = jnp.bfloat16
F32 = jnp.float32


def product(left_side, right_side):
    return jnp.dot(left_side, right_side, preferred_element_type=F32)


def by_rows(left_side, right_side):
    return lax.dot_general(
        left_side, right_side, (((0,), (0,)), ((), ())), preferred_element_type=F32
    )


def by_cols(left_side, right_side):
    return lax.dot_general(
        left_side, right_side, (((1,), (1,)), ((), ())), preferred_element_type=F32
    )


def normed(vector, gain_vector):
    return (
        vector
        * lax.rsqrt(jnp.mean(vector * vector, axis=-1, keepdims=True) + EPSILON)
        * gain_vector
    )


def angles(positions, head_size):
    frequency = 10000.0 ** (-jnp.arange(head_size // 2, dtype=F32) * 2.0 / head_size)
    phase_angle = positions.astype(F32)[:, None] * frequency[None, :]
    return (jnp.cos(phase_angle)[:, None, :], jnp.sin(phase_angle)[:, None, :])


def rotated(vector, cosines, sines):
    half_width = vector.shape[-1] // 2
    front = vector[..., :half_width]
    behind = vector[..., half_width:]
    return jnp.concatenate(
        [front * cosines - behind * sines, behind * cosines + front * sines], axis=-1
    )


def visible_mask(shape, key_axis):
    keys = lax.broadcasted_iota(jnp.int32, shape, key_axis)
    queries = lax.rem(lax.broadcasted_iota(jnp.int32, shape, 1 - key_axis), STRETCH)
    return keys <= queries


def attend_kernel(count_ref, slots_ref, parity_ref, q_ref, kv_ref, out_ref, acc_ref):
    odd = parity_ref[0] == 1
    ones = jnp.ones((STRETCH, HEAD_WIDTH), BF16)

    def add_block(block, slot, last):
        tile = kv_ref[slot]
        keys = [tile[:, :64], tile[:, 64:128]]
        values = [
            jnp.concatenate([tile[:, 128:192], ones], axis=1),
            jnp.concatenate([tile[:, 192:256], ones], axis=1),
        ]
        middle_key = jnp.where(odd, keys[1], keys[0])
        middle_value = jnp.where(odd, values[1], values[0])
        for pair, key, value in (
            (0, keys[0], values[0]),
            (1, middle_key, middle_value),
            (2, keys[1], values[1]),
        ):
            scores = by_cols(q_ref[block, pair], key)
            weights = jnp.exp2(scores * (LOG2E * HEAD_WIDTH**-0.5))
            if last:
                weights = jnp.where(visible_mask(weights.shape, 1), weights, 0.0)
            acc_ref[pair] += product(weights.astype(BF16), value)

    def one_block(block, carry):
        acc_ref[...] = jnp.zeros_like(acc_ref)
        count = count_ref[block]

        def step(index, inner):
            add_block(block, slots_ref[block, index], False)
            return inner

        lax.fori_loop(0, count - 1, step, 0)
        add_block(block, slots_ref[block, count - 1], True)
        for pair in range(PAIRS):
            total = acc_ref[pair]
            denominator = total[:, HEAD_WIDTH:]
            out_ref[block, pair] = jnp.concatenate(
                [total[:, :HEAD_WIDTH] / denominator, jnp.log2(denominator)], axis=1
            )
        return carry

    lax.fori_loop(0, q_ref.shape[0], one_block, 0)


def attend(counts, slots, parity, queries, keyvalues):
    blocks = queries.shape[0]
    smem = pl.BlockSpec(memory_space=pltpu.SMEM)
    vmem = pl.BlockSpec(memory_space=pltpu.VMEM)
    return pl.pallas_call(
        attend_kernel,
        out_shape=jax.ShapeDtypeStruct((blocks, PAIRS, 2 * STRETCH, 128), F32),
        in_specs=[smem, smem, smem, vmem, vmem],
        out_specs=vmem,
        scratch_shapes=[pltpu.VMEM((PAIRS, 2 * STRETCH, 128), F32)],
        compiler_params=pltpu.CompilerParams(vmem_limit_bytes=40 << 20),
        cost_estimate=pl.CostEstimate(
            flops=4 * 20 * PAIRS * 256 * 128 * 64 * 4, bytes_accessed=8 << 20, transcendentals=0
        ),
        name="attend",
    )(counts, slots, parity, queries, keyvalues)


def attend_back_kernel(
    count_ref, slots_ref, parity_ref, q_ref, do_ref, log_ref, delta_ref, kv_ref, dq_ref, dkv_ref
):
    odd = parity_ref[0] == 1
    scale = HEAD_WIDTH**-0.5
    dq_ref[...] = jnp.zeros_like(dq_ref)
    dkv_ref[...] = jnp.zeros_like(dkv_ref)

    def add_block(block, slot, last):
        tile = kv_ref[slot]
        keys = [tile[:, :64], tile[:, 64:128]]
        values = [tile[:, 128:192], tile[:, 192:256]]
        middle_key = jnp.where(odd, keys[1], keys[0])
        middle_value = jnp.where(odd, values[1], values[0])
        d_keys, d_values = [], []
        for pair, key, value in (
            (0, keys[0], values[0]),
            (1, middle_key, middle_value),
            (2, keys[1], values[1]),
        ):
            query, d_out = q_ref[block, pair], do_ref[block, pair]
            scores = by_cols(key, query)
            weights = jnp.exp2(scores * (LOG2E * scale) - log_ref[block, pair])
            if last:
                weights = jnp.where(visible_mask(weights.shape, 0), weights, 0.0)
            d_weights = by_cols(value, d_out)
            d_scores = (weights * (d_weights - delta_ref[block, pair])).astype(BF16)
            d_values.append(product(weights.astype(BF16), d_out))
            d_keys.append(product(d_scores, query))
            dq_ref[block, pair] += by_rows(d_scores, key) * scale
        zero = jnp.zeros((STRETCH, HEAD_WIDTH), F32)
        parts = [
            (d_keys[0] + jnp.where(odd, zero, d_keys[1])) * scale,
            (d_keys[2] + jnp.where(odd, d_keys[1], zero)) * scale,
            d_values[0] + jnp.where(odd, zero, d_values[1]),
            d_values[2] + jnp.where(odd, d_values[1], zero),
        ]
        dkv_ref[slot] += jnp.concatenate(parts, axis=1)

    def one_block(block, carry):
        count = count_ref[block]

        def step(index, inner):
            add_block(block, slots_ref[block, index], False)
            return inner

        lax.fori_loop(0, count - 1, step, 0)
        add_block(block, slots_ref[block, count - 1], True)
        return carry

    lax.fori_loop(0, q_ref.shape[0], one_block, 0)


def attend_back(counts, slots, parity, queries, d_out, logs, delta, keyvalues):
    blocks = queries.shape[0]
    smem = pl.BlockSpec(memory_space=pltpu.SMEM)
    vmem = pl.BlockSpec(memory_space=pltpu.VMEM)
    return pl.pallas_call(
        attend_back_kernel,
        out_shape=(
            jax.ShapeDtypeStruct((blocks, PAIRS, 2 * STRETCH, HEAD_WIDTH), F32),
            jax.ShapeDtypeStruct(keyvalues.shape, F32),
        ),
        in_specs=[smem] * 3 + [vmem] * 5,
        out_specs=(vmem, vmem),
        compiler_params=pltpu.CompilerParams(vmem_limit_bytes=56 << 20),
        cost_estimate=pl.CostEstimate(
            flops=10 * 20 * PAIRS * 256 * 128 * 64 * 4, bytes_accessed=8 << 20, transcendentals=0
        ),
        name="attend_back",
    )(counts, slots, parity, queries, d_out, logs, delta, keyvalues)


class Place:
    def __init__(self, lines):
        rank, part = lax.axis_index("dp"), lax.axis_index("tensor")
        self.lines = lines
        self.z, self.y = rank // lines, lax.rem(rank, lines)
        self.x, self.c = part // 2, lax.rem(part, 2)
        self.quarter = self.c * 2 + self.x

    def plane(self, move):
        if move == 0:
            return self.z
        if move == 1:
            return self.z + 1 - 2 * lax.rem(self.z, 2)
        if move == 2:
            return self.z + 2 - 4 * (self.z // 2)
        return 3 - self.z

    def to(self, kz=0, ky=0, kx=0, kc=0):
        y = 1 - self.y if ky else self.y
        x = 1 - self.x if kx else self.x
        c = 1 - self.c if kc else self.c
        return (self.plane(kz) * self.lines + y, x * 2 + c)


class Links:
    def __init__(self, place, send_sems, recv_sems):
        self.place, self.send_sems, self.recv_sems = place, send_sems, recv_sems
        self.number, self.unsent = 0, []

    def greet(self, moves):
        barrier = pltpu.get_barrier_semaphore()
        for move in moves:
            pl.semaphore_signal(
                barrier, inc=1, device_id=self.place.to(**move), device_id_type=pl.DeviceIdType.MESH
            )
        pl.semaphore_wait(barrier, len(moves))

    def send(self, source, target, **move):
        number, self.number = self.number, self.number + 1
        copy = pltpu.make_async_remote_copy(
            src_ref=source,
            dst_ref=target,
            send_sem=self.send_sems.at[number],
            recv_sem=self.recv_sems.at[number],
            device_id=self.place.to(**move),
            device_id_type=pl.DeviceIdType.MESH,
        )
        copy.start()
        self.unsent.append(copy)
        return copy

    def sent(self, copy):
        copy.wait_send()
        self.unsent = [other for other in self.unsent if other is not copy]

    def finish(self):
        for copy in self.unsent:
            copy.wait_send()


def rows_at(index, size):
    return pl.ds(pl.multiple_of(index * size, size), size)


class Gather:
    def __init__(self, links, block, own=None):
        self.links, self.block, self.y = links, block, links.place.y
        self.own = block(0, self.y) if own is None else own
        self.lines = []

    def over_lines(self, move):
        place = self.block(move, self.y)
        source = self.own if move == 0 else place
        self.lines.append(self.links.send(source, place, ky=1))

    def start_planes(self):
        place = self.block(0, self.y)
        self.far = self.links.send(self.own, place, kz=2)
        self.near = self.links.send(self.own, place, kz=1)

    def start(self):
        self.start_planes()
        self.over_lines(0)

    def relay(self):
        self.near.wait_recv()
        self.over_lines(1)
        self.far.wait_recv()
        place = self.block(2, self.y)
        self.corner = self.links.send(place, place, kz=1)
        self.over_lines(2)

    def last(self):
        self.corner.wait_recv()
        self.over_lines(3)

    def finish(self):
        for copy in self.lines:
            copy.wait_recv()


def head_mean(value):
    row = lax.broadcasted_iota(jnp.int32, (128, 128), 0) // HEAD_WIDTH
    column = lax.broadcasted_iota(jnp.int32, (128, 128), 1) // HEAD_WIDTH
    average = jnp.where(row == column, 1.0 / HEAD_WIDTH, 0.0).astype(F32)
    return jnp.dot(
        value, average, preferred_element_type=F32, precision=lax.Precision.HIGHEST
    )


def halves_swapped(value):
    first = lax.rem(lax.broadcasted_iota(jnp.int32, value.shape, 1), HEAD_WIDTH) < HEAD_WIDTH // 2
    return jnp.where(
        first,
        pltpu.roll(value, 128 - HEAD_WIDTH // 2, 1),
        pltpu.roll(value, HEAD_WIDTH // 2, 1),
    )


class Scatter:
    ORDER = (3, 1, 2, 0)

    def __init__(self, links, y_out, y_in, z_out, z_in, sums):
        self.links = links
        self.y_out, self.y_in, self.z_out, self.z_in, self.sums = y_out, y_in, z_out, z_in, sums
        self.lines, self.planes = {}, {}

    def start(self, move, block):
        self.y_out[move] = block.astype(BF16)
        self.lines[move] = self.links.send(self.y_out.at[move], self.y_in.at[move], ky=1)

    def add(self, move, block):
        self.lines[move].wait_recv()
        total = block + self.y_in[move].astype(F32)
        if move in (3, 1):
            slot = 0 if move == 1 else 1
            self.z_out[slot] = total.astype(BF16)
            self.planes[slot] = self.links.send(self.z_out.at[slot], self.z_in.at[slot], kz=1)
        elif move == 2:
            self.planes[1].wait_recv()
            self.z_out[2] = (total + self.z_in[1].astype(F32)).astype(BF16)
            self.planes[2] = self.links.send(self.z_out.at[2], self.z_in.at[2], kz=2)
        else:
            self.sums[...] = total

    def finish(self):
        self.planes[0].wait_recv()
        self.planes[2].wait_recv()
        return self.sums[...] + self.z_in[0].astype(F32) + self.z_in[2].astype(F32)


def scatter_scratch(block):
    return [
        pltpu.VMEM((4, *block), BF16),
        pltpu.VMEM((4, *block), BF16),
        pltpu.VMEM((3, *block), BF16),
        pltpu.VMEM((3, *block), BF16),
        pltpu.VMEM(block, F32),
    ]


FORWARD_COPIES = 100


def forward_kernel(
    lines,
    heads,
    slice_width,
    longest,
    sequence_ref,
    offset_ref,
    states_ref,
    norm_gains_ref,
    query_gain_ref,
    key_gain_ref,
    frequency_ref,
    query_weight_ref,
    keyvalue_matrix_ref,
    gate_weight_ref,
    up_weight_ref,
    down_weight_ref,
    w_output_in,
    grad_any,
    lin_any,
    attn_in_any,
    query_any,
    kv_any,
    attended_ref,
    attn_out_ref,
    gains_ref,
    w_attend_any,
    middle_ref,
    back_ref,
    gain_out_ref,
    d_heads_ref,
    output_grad_ref,
    mixed_ref,
    cosine_ref,
    sine_ref,
    head_gain_ref,
    table_ref,
    collected_any,
    staged_any,
    w_down_any,
    gains_in,
    w_attend_in,
    lin_ref,
    attn_in_ref,
    query_ref,
    kv_ref,
    w_attend_ref,
    w_output_ref,
    w_hidden_ref,
    down_ref,
    ffn_ref,
    d_hidden_ref,
    partial_ref,
    core_out,
    core_in,
    x_out,
    x_in,
    sums_ref,
    z_out,
    z_in,
    y_out,
    y_in,
    local_sems,
    send_sems,
    recv_sems,
):
    here = Place(lines)
    links = Links(here, send_sems, recv_sems)
    token_rows, width = states_ref.shape
    quarter = token_rows // 4
    half = 2 * quarter
    weight_rows = query_weight_ref.shape[0]
    hidden = slice_width
    blocks = token_rows // STRETCH
    slot_count = offset_ref.shape[0]
    mine, my_half = rows_at(here.quarter, quarter), rows_at(here.c, half)
    other_half = rows_at(1 - here.c, half)
    x_mine, x_other = rows_at(here.x, quarter), rows_at(1 - here.x, quarter)
    odd = here.c == 1

    def rank(move, line):
        return here.plane(move) * lines + line

    def rows_of(ref, columns=slice(None)):
        return lambda move, line: ref.at[rows_at(rank(move, line), weight_rows), columns]

    def columns_of(ref):
        return lambda move, line: ref.at[:, rows_at(rank(move, line), weight_rows)]

    loads = [
        pltpu.make_async_copy(grad_any, down_ref.at[here.z], local_sems.at[0]),
        pltpu.make_async_copy(w_output_in, rows_of(w_output_ref)(0, here.y), local_sems.at[1]),
    ]
    for load in loads:
        load.start()
    links.greet([dict(kc=1), dict(kx=1), dict(ky=1), dict(kz=1), dict(kz=2), dict(kz=3)])

    kv_width = 4 * HEAD_WIDTH
    part = here.x * 2 + here.c
    value_start = KEYVALUE_HEADS * HEAD_WIDTH

    def own_heads(start):
        chosen = None
        for index in range(4):
            begin = start + index * heads // (QUERY_HEADS // KEYVALUE_HEADS) * HEAD_WIDTH
            columns = keyvalue_matrix_ref[:, begin : begin + 2 * HEAD_WIDTH]
            chosen = columns if chosen is None else jnp.where(part == index, columns, chosen)
        return chosen

    w_attend_in[:, :128] = own_heads(0)
    w_attend_in[:, 128:kv_width] = own_heads(value_start)
    w_attend_in[:, kv_width:] = query_weight_ref[...]
    gains_in[...] = jnp.zeros_like(gains_in)
    gains_in[:2, :] = norm_gains_ref[...].astype(F32)
    gains = Gather(links, columns_of(gains_ref), gains_in)
    gains.start()
    first, second = slice(0, kv_width), slice(kv_width, w_attend_in.shape[1])
    kv_weights = Gather(links, rows_of(w_attend_ref, first), w_attend_in.at[:, first])
    kv_weights.start()
    query_weights = Gather(links, rows_of(w_attend_ref, second), w_attend_in.at[:, second])
    columns_of(gains_ref)(0, here.y)[...] = gains_in[...]
    rows_of(w_attend_ref)(0, here.y)[...] = w_attend_in[...]

    head_gain_ref[...] = jnp.concatenate(
        [key_gain_ref[...]] * 2 + [query_gain_ref[...]] * heads, axis=1
    )
    tile_shape = (STRETCH, 2 * HEAD_WIDTH)
    row_number = lax.broadcasted_iota(jnp.int32, tile_shape, 0)
    column_number = lax.broadcasted_iota(jnp.int32, tile_shape, 1)
    front = lax.rem(column_number, HEAD_WIDTH) < HEAD_WIDTH // 2
    for block in range(blocks):
        rows = slice(block * STRETCH, (block + 1) * STRETCH)
        position = row_number + offset_ref[rank(0, here.y) * blocks + block]
        phase = position.astype(F32) * frequency_ref[...]
        cosine_ref[rows, :] = jnp.cos(phase)
        sine = jnp.sin(phase)
        sine_ref[rows, :] = jnp.where(front, -sine, sine)

    def fill(index, carry):
        block, place = index // longest, lax.rem(index, longest)
        sequence = sequence_ref[rank(0, here.y) * blocks + block]
        found = jnp.int32(0)
        for slot in range(slot_count):
            same = (sequence_ref[slot] == sequence) & (offset_ref[slot] == place * STRETCH)
            found = jnp.where(same, slot, found)
        table_ref[index] = found
        return carry

    lax.fori_loop(0, blocks * longest, fill, 0)
    kv_weights.relay()
    query_weights.start()
    gains.relay()
    gains.last()
    gains.finish()
    states = states_ref[...].astype(F32)
    inverse = lax.rsqrt(jnp.mean(states * states, axis=-1, keepdims=True) + EPSILON)
    attn_in_ref[...] = (states * inverse * gains_ref[0:1, :]).astype(BF16)

    def turned(value, group):
        value = (
            value
            * lax.rsqrt(head_mean(value * value) + EPSILON)
            * head_gain_ref[:, group * 128 : (group + 1) * 128]
        )
        return (value * cosine_ref[...] + halves_swapped(value) * sine_ref[...]).astype(BF16)

    kv_weights.last()
    kv_weights.finish()
    lin = product(attn_in_ref[...], w_attend_ref[:, first])
    lin_ref[:, first] = lin
    own_blocks = pl.ds(rank(0, here.y) * blocks, blocks)
    kv_ref[own_blocks, :, :128] = turned(lin[:, :128], 0).reshape(blocks, STRETCH, 128)
    kv_ref[own_blocks, :, 128:] = lin[:, 128:].astype(BF16).reshape(blocks, STRETCH, 128)
    keyvalue = Gather(
        links, lambda move, line: kv_ref.at[pl.ds(rank(move, line) * blocks, blocks)]
    )
    keyvalue.start()
    query_weights.relay()
    query_weights.last()
    keyvalue.relay()
    query_weights.finish()
    lin = product(attn_in_ref[...], w_attend_ref[:, second])
    lin_ref[:, second] = lin
    for pair in range(PAIRS):
        rotated_pair = turned(lin[:, pair * 128 : (pair + 1) * 128], pair + 1)
        for block in range(blocks):
            rows = rotated_pair[block * STRETCH : (block + 1) * STRETCH]
            query_ref[block, pair, :STRETCH] = rows[:, :HEAD_WIDTH]
            query_ref[block, pair, STRETCH:] = rows[:, HEAD_WIDTH:]
    keyvalue.last()

    output = Gather(links, rows_of(w_output_ref), w_output_in)
    output.start_planes()
    planes = {}

    def hidden_plane(move):
        planes[move] = links.send(
            y_out.at[here.plane(move)], columns_of(w_hidden_ref)(0, here.y), kz=move
        )

    hidden_lines = []

    def hidden_line(move):
        if move:
            planes[move].wait_recv()
        place = columns_of(w_hidden_ref)(move, here.y)
        hidden_lines.append(links.send(place, place, ky=1))

    def down_block(move):
        return down_ref.at[here.plane(move), mine]

    down_across, down_cores = {}, {}

    def down_x(move):
        down_across[move] = links.send(down_block(move), down_block(move), kx=1)

    def down_core(move):
        down_across[move].wait_recv()
        both = down_ref.at[here.plane(move), my_half]
        down_cores[move] = links.send(both, both, kc=1)

    saves = []

    def save(source, target):
        copy = pltpu.make_async_copy(source, target, local_sems.at[3 + len(saves)])
        copy.start()
        saves.append(copy)

    for index, weight_ref in enumerate((gate_weight_ref, up_weight_ref, down_weight_ref)):
        for plane in range(4):
            y_out[plane, index * hidden : (index + 1) * hidden] = weight_ref[
                plane * hidden : (plane + 1) * hidden
            ]
    columns_of(w_hidden_ref)(0, here.y)[...] = y_out[here.z]
    keyvalue.finish()
    output.over_lines(0)
    save(lin_ref, lin_any)
    save(attn_in_ref, attn_in_any)
    save(query_ref, query_any)
    save(kv_ref, kv_any)
    save(w_attend_ref, w_attend_any)

    span = longest * STRETCH
    ones = jnp.ones((span, HEAD_WIDTH), BF16)
    shape = (2 * STRETCH, span)
    ahead = lax.broadcasted_iota(jnp.int32, shape, 1) - lax.rem(
        lax.broadcasted_iota(jnp.int32, shape, 0), STRETCH
    )

    def attend_block(block):
        tiles = [kv_ref[table_ref[block * longest + place]] for place in range(longest)]
        tile = jnp.concatenate(tiles, axis=0)
        keys = [tile[:, :64], tile[:, 64:128]]
        values = [
            jnp.concatenate([tile[:, 128:192], ones], axis=1),
            jnp.concatenate([tile[:, 192:256], ones], axis=1),
        ]
        middle_key = jnp.where(odd, keys[1], keys[0])
        middle_value = jnp.where(odd, values[1], values[0])
        visible = ahead <= offset_ref[rank(0, here.y) * blocks + block]
        for pair, key, value in (
            (0, keys[0], values[0]),
            (1, middle_key, middle_value),
            (2, keys[1], values[1]),
        ):
            scores = by_cols(query_ref[block, pair], key)
            weights = jnp.exp2(scores * (LOG2E * HEAD_WIDTH**-0.5))
            weights = jnp.where(visible, weights, 0.0)
            total = product(weights.astype(BF16), value)
            denominator = total[:, HEAD_WIDTH:]
            heads_out = total[:, :HEAD_WIDTH] / denominator
            attended_ref[block, pair] = jnp.concatenate(
                [heads_out, jnp.log2(denominator)], axis=1
            )
            attn_out_ref[
                block * STRETCH : (block + 1) * STRETCH, pair * 128 : (pair + 1) * 128
            ] = jnp.concatenate([heads_out[:STRETCH], heads_out[STRETCH:]], axis=1).astype(BF16)

    attend_block(0)
    output.relay()
    loads[0].wait()
    down_far = links.send(down_block(0), down_block(0), kz=2)
    down_near = links.send(down_block(0), down_block(0), kz=1)
    attend_block(1)
    output.last()
    attend_block(2)
    for move in (1, 2, 3):
        hidden_plane(move)
    hidden_line(0)
    down_near.wait_recv()
    down_x(1)
    output.finish()

    loads[1].wait()
    cut = 4
    piece = width // cut
    core_copies = []
    for part in range(cut):
        columns = slice(part * piece, (part + 1) * piece)
        weight = w_output_ref[columns, :]
        core_out[1, :, columns] = by_cols(attn_out_ref[other_half, :], weight).astype(BF16)
        core_copies.append(
            links.send(core_out.at[1, :, columns], core_in.at[4, :, columns], kc=1)
        )
        partial_ref[0, :half, columns] = by_cols(attn_out_ref[my_half, :], weight)
    x_copies = []
    down_far.wait_recv()
    down_corner = links.send(down_block(2), down_block(2), kz=1)
    down_x(2)
    for part in range(cut):
        columns = slice(part * piece, (part + 1) * piece)
        core_copies[part].wait_recv()
        x_out[1, :, columns] = (
            partial_ref[0, x_other, columns] + core_in[4, x_other, columns].astype(F32)
        ).astype(BF16)
        x_copies.append(links.send(x_out.at[1, :, columns], x_in.at[4, :, columns], kx=1))
        middle_ref[:, columns] = (
            states_ref[mine, columns].astype(F32)
            + partial_ref[0, x_mine, columns]
            + core_in[4, x_mine, columns].astype(F32)
        )
    for part in range(cut):
        columns = slice(part * piece, (part + 1) * piece)
        x_copies[part].wait_recv()
        middle_ref[:, columns] += x_in[4, :, columns].astype(F32)
    middle = middle_ref[...]
    inverse = lax.rsqrt(jnp.mean(middle * middle, axis=-1, keepdims=True) + EPSILON)
    ffn_ref[here.z, mine, :] = (middle * inverse * gains_ref[1:2, :]).astype(BF16)

    for copy in core_copies + x_copies:
        links.sent(copy)

    def block_of(move):
        return ffn_ref.at[here.plane(move), mine]

    far = links.send(block_of(0), block_of(0), kz=2)
    near = links.send(block_of(0), block_of(0), kz=1)
    across = {0: links.send(block_of(0), block_of(0), kx=1)}
    cores = {}

    def spread(move):
        across[move].wait_recv()
        both = ffn_ref.at[here.plane(move), my_half]
        cores[move] = links.send(both, both, kc=1)

    down_corner.wait_recv()
    down_x(3)
    down_core(1)
    down_core(2)
    hidden_line(1)
    far.wait_recv()
    corner = links.send(block_of(2), block_of(2), kz=1)
    across[2] = links.send(block_of(2), block_of(2), kx=1)
    near.wait_recv()
    across[1] = links.send(block_of(1), block_of(1), kx=1)
    hidden_line(2)
    hidden_line(3)
    spread(0)
    spread(2)
    corner.wait_recv()
    across[3] = links.send(block_of(3), block_of(3), kx=1)
    spread(1)
    down_core(3)
    for copy in hidden_lines:
        copy.wait_recv()

    core_copies, x_copies, z_copies = {}, {}, {}
    order = (2, 3, 1, 0)

    def add_cores(index):
        move, slot = order[index], index % 2
        core_copies[move].wait_recv()
        total_rows = rows_at(here.c * 2 + 1 - here.x, quarter)
        if index > 1:
            links.sent(x_copies[order[index - 2]])
        x_out[slot] = (
            partial_ref[slot, total_rows, :] + core_in[move, x_other, :].astype(F32)
        ).astype(BF16)
        x_copies[move] = links.send(x_out.at[slot], x_in.at[move], kx=1)
        sums_ref[move] = partial_ref[slot, mine, :] + core_in[move, x_mine, :].astype(F32)

    def add_x(move):
        x_copies[move].wait_recv()
        sums_ref[move] += x_in[move].astype(F32)
        if move:
            z_out[move - 1] = sums_ref[move].astype(BF16)
            z_copies[move] = links.send(z_out.at[move - 1], z_in.at[move - 1], kz=move)

    for index, move in enumerate(order):
        slot = index % 2
        cores[move].wait_recv()
        if move:
            down_cores[move].wait_recv()
        plane = here.plane(move)
        chunk = ffn_ref[plane]
        gate_pre = by_cols(w_hidden_ref[:hidden, :], chunk)
        up_pre = by_cols(w_hidden_ref[hidden : 2 * hidden, :], chunk)
        sigmoid_gate = 1.0 / (1.0 + jnp.exp(-gate_pre))
        silu = gate_pre * sigmoid_gate
        columns = pl.ds(pl.multiple_of(plane * token_rows, token_rows), token_rows)
        mixed_ref[:, columns] = (silu * up_pre).astype(BF16)
        d_mixed = by_cols(w_hidden_ref[2 * hidden :, :], down_ref[plane])
        d_hidden_ref[:hidden, columns] = (
            d_mixed * up_pre * sigmoid_gate * (1.0 + gate_pre * (1.0 - sigmoid_gate))
        ).astype(BF16)
        d_hidden_ref[hidden:, columns] = (d_mixed * silu).astype(BF16)
        partial_ref[slot] = by_rows(d_hidden_ref[:, columns], w_hidden_ref[: 2 * hidden, :])
        if index > 1:
            links.sent(core_copies[order[index - 2]])
        core_out[slot] = partial_ref[slot, other_half, :].astype(BF16)
        core_copies[move] = links.send(core_out.at[slot], core_in.at[move], kc=1)
        if index == 0:
            spread(3)
        if index > 0:
            add_cores(index - 1)
        if index > 1:
            add_x(order[index - 2])
    add_cores(3)

    def gradient(move, line):
        columns = rows_at(rank(move, line), weight_rows)
        first = jnp.zeros((2 * hidden, weight_rows), F32)
        second = jnp.zeros((hidden, weight_rows), F32)
        for plane in range(4):
            tokens = slice(plane * token_rows, (plane + 1) * token_rows)
            first += product(d_hidden_ref[:, tokens], ffn_ref[plane, :, columns])
            second += product(mixed_ref[:, tokens], down_ref[plane, :, columns])
        return first, second

    def keep(target, pieces):
        target[: 2 * hidden] = pieces[0].astype(BF16)
        target[2 * hidden :] = pieces[1].astype(BF16)

    for move in (1, 2, 3):
        links.sent(planes[move])
    y_copies = {}
    for move in (3, 2, 1, 0):
        keep(y_out.at[move], gradient(move, 1 - here.y))
        y_copies[move] = links.send(y_out.at[move], y_in.at[move], ky=1)
        if move == 3:
            add_x(1)
    add_x(0)

    def gradient_sum(move):
        first, second = gradient(move, here.y)
        y_copies[move].wait_recv()
        links.sent(y_copies[move])
        first += y_in[move, : 2 * hidden].astype(F32)
        second += y_in[move, 2 * hidden :].astype(F32)
        keep(y_out.at[move], (first, second))

    for move in (1, 2, 3):
        z_copies[move].wait_recv()
    d_normed = sums_ref[0]
    for move in (1, 2, 3):
        d_normed += z_in[move - 1].astype(F32)
    middle = middle_ref[...]
    inverse = lax.rsqrt(jnp.mean(middle * middle, axis=-1, keepdims=True) + EPSILON)
    unit = middle * inverse
    gain_out_ref[...] = jnp.sum(d_normed * unit, axis=0, keepdims=True)
    scaled = d_normed * gains_ref[1:2, :]
    back = inverse * (scaled - unit * jnp.mean(scaled * unit, axis=-1, keepdims=True))
    grad_middle = down_ref[here.z, mine, :].astype(F32) + back
    back_ref[...] = grad_middle
    output_grad_ref[mine, :] = grad_middle.astype(BF16)
    block = output_grad_ref.at[mine]
    x_copy = links.send(block, block, kx=1)
    gradient_sum(3)
    last = links.send(y_out.at[3], collected_any.at[here.z], kz=3)
    x_copy.wait_recv()
    both = output_grad_ref.at[my_half]
    core = links.send(both, both, kc=1)
    save(w_hidden_ref.at[pl.ds(2 * hidden, hidden)], w_down_any)
    gradient_sum(2)
    save(y_out.at[2], staged_any.at[1])
    core.wait_recv()
    d_heads_ref[...] = product(output_grad_ref[...], w_output_ref[...]).astype(BF16)
    gradient_sum(1)
    save(y_out.at[1], staged_any.at[0])
    gradient_sum(0)
    save(y_out.at[0], collected_any.at[here.z])
    last.wait_recv()
    for copy in saves:
        copy.wait()
    links.finish()


def forward(lines, heads, slice_width, longest, *arguments):
    states, query_weight = arguments[2], arguments[7]
    columns = query_weight.shape[1] + 4 * HEAD_WIDTH
    token_rows, width = states.shape
    ranks = 4 * lines
    quarter = token_rows // 4
    half = 2 * quarter
    hidden = slice_width
    head_width = heads * HEAD_WIDTH
    weight_rows = width // ranks
    blocks = token_rows // STRETCH
    vmem = pl.BlockSpec(memory_space=pltpu.VMEM)
    smem = pl.BlockSpec(memory_space=pltpu.SMEM)
    hbm = pl.BlockSpec(memory_space=pl.ANY)
    shape = jax.ShapeDtypeStruct
    return pl.pallas_call(
        functools.partial(forward_kernel, lines, heads, slice_width, longest),
        out_shape=(
            shape((token_rows, columns), F32),
            shape((token_rows, width), BF16),
            shape((blocks, PAIRS, 2 * STRETCH, HEAD_WIDTH), BF16),
            shape((ranks * blocks, STRETCH, 4 * HEAD_WIDTH), BF16),
            shape((blocks, PAIRS, 2 * STRETCH, 128), F32),
            shape((token_rows, head_width), BF16),
            shape((8, width), F32),
            shape((width, columns), BF16),
            shape((quarter, width), F32),
            shape((quarter, width), F32),
            shape((1, width), F32),
            shape((token_rows, head_width), BF16),
            shape((token_rows, width), BF16),
            shape((hidden, 4 * token_rows), BF16),
            shape((token_rows, 128), F32),
            shape((token_rows, 128), F32),
            shape((1, (heads + 2) * HEAD_WIDTH), F32),
            shape((blocks * longest,), jnp.int32),
            shape((4, 3 * hidden, weight_rows), BF16),
            shape((2, 3 * hidden, weight_rows), BF16),
            shape((hidden, width), BF16),
        ),
        in_specs=[smem] * 2 + [vmem] * 10 + [hbm] * 2,
        out_specs=(hbm,) * 4 + (vmem,) * 3 + (hbm,) + (vmem,) * 9 + (smem,) + (hbm,) * 3,
        scratch_shapes=[
            pltpu.VMEM((8, weight_rows), F32),
            pltpu.VMEM((weight_rows, columns), BF16),
            pltpu.VMEM((token_rows, columns), F32),
            pltpu.VMEM((token_rows, width), BF16),
            pltpu.VMEM((blocks, PAIRS, 2 * STRETCH, HEAD_WIDTH), BF16),
            pltpu.VMEM((ranks * blocks, STRETCH, 4 * HEAD_WIDTH), BF16),
            pltpu.VMEM((width, columns), BF16),
            pltpu.VMEM((width, head_width), BF16),
            pltpu.VMEM((3 * hidden, width), BF16),
            pltpu.VMEM((4, token_rows, width), BF16),
            pltpu.VMEM((4, token_rows, width), BF16),
            pltpu.VMEM((2 * hidden, 4 * token_rows), BF16),
            pltpu.VMEM((2, token_rows, width), F32),
            pltpu.VMEM((2, half, width), BF16),
            pltpu.VMEM((5, half, width), BF16),
            pltpu.VMEM((2, quarter, width), BF16),
            pltpu.VMEM((5, quarter, width), BF16),
            pltpu.VMEM((4, quarter, width), F32),
            pltpu.VMEM((3, quarter, width), BF16),
            pltpu.VMEM((3, quarter, width), BF16),
            pltpu.VMEM((4, 3 * hidden, weight_rows), BF16),
            pltpu.VMEM((4, 3 * hidden, weight_rows), BF16),
            pltpu.SemaphoreType.DMA((16,)),
            pltpu.SemaphoreType.DMA((FORWARD_COPIES,)),
            pltpu.SemaphoreType.DMA((FORWARD_COPIES,)),
        ],
        compiler_params=pltpu.CompilerParams(
            collective_id=0, has_side_effects=True, vmem_limit_bytes=64 << 20
        ),
        name="forward",
    )(*arguments)


BACKWARD_COPIES = 60


def backward_kernel(
    lines,
    heads,
    longest,
    sequence_ref,
    offset_ref,
    table_ref,
    query_ref,
    kv_ref,
    attended_ref,
    d_heads_ref,
    attn_out_ref,
    gains_ref,
    gain_ffn_ref,
    cosine_ref,
    sine_ref,
    head_gain_ref,
    lin_any,
    attn_in_any,
    output_grad_any,
    w_attend_any,
    back_any,
    states_any,
    middle_any,
    mixed_any,
    w_down_any,
    staged_any,
    collected_in,
    result_ref,
    states_grad_ref,
    g_attend_ref,
    g_output_ref,
    g_kv_ref,
    d_gains_ref,
    query_gain_out,
    key_gain_out,
    collected_any,
    small_ref,
    *scratch,
):
    here = Place(lines)
    del collected_in
    (
        lin_ref,
        attn_in_ref,
        output_grad_ref,
        w_attend_ref,
        back_ref,
        states_ref,
        middle_ref,
        mixed_ref,
        w_down_ref,
        d_query_ref,
        d_kv_ref,
        d_lin_ref,
        partial_ref,
        core_out,
        core_in,
        x_out,
        x_in,
        sums_ref,
        z_out,
        z_in,
        small_out,
        small_in,
        local_sems,
        send_sems,
        recv_sems,
    ) = scratch[:25]
    links = Links(here, send_sems, recv_sems)
    kv_sum = Scatter(links, *scratch[25:30])
    output_sum = Scatter(links, *scratch[30:35])
    attend_sum = Scatter(links, *scratch[35:40])
    token_rows, width = output_grad_ref.shape
    quarter = token_rows // 4
    half = 2 * quarter
    weight_rows = width // (4 * lines)
    kv_width = 4 * HEAD_WIDTH
    blocks = token_rows // STRETCH
    mine, other = rows_at(here.quarter, quarter), rows_at(here.c * 2 + 1 - here.x, quarter)
    my_half, other_half = rows_at(here.c, half), rows_at(1 - here.c, half)
    x_mine, x_other = rows_at(here.x, quarter), rows_at(1 - here.x, quarter)
    odd = here.c == 1
    scale = HEAD_WIDTH**-0.5

    loads = {}

    def load(number, source, target):
        copy = pltpu.make_async_copy(source, target, local_sems.at[number])
        copy.start()
        loads[number] = copy

    load(0, output_grad_any, output_grad_ref)
    load(1, w_down_any, w_down_ref)
    load(2, mixed_any, mixed_ref)
    load(3, lin_any, lin_ref)
    load(4, attn_in_any, attn_in_ref)
    load(5, w_attend_any, w_attend_ref)
    load(6, states_any.at[mine], states_ref)
    load(7, back_any, back_ref)
    load(8, middle_any, middle_ref)
    links.greet([dict(kc=1), dict(kx=1), dict(ky=1), dict(kz=1), dict(kz=2)])
    hidden_pushes = [
        links.send(staged_any.at[move - 1], collected_any.at[here.z], kz=move) for move in (2, 1)
    ]

    def rank(move, line):
        return here.plane(move) * lines + line

    core_copies, x_copies = {}, {}

    def out_start(move, slot):
        at = pl.ds(pl.multiple_of(here.plane(move) * token_rows, token_rows), token_rows)
        partial_ref[slot] = by_rows(mixed_ref[:, at], w_down_ref[...])
        core_out[slot] = partial_ref[slot, other_half, :].astype(BF16)
        core_copies[move] = links.send(core_out.at[slot], core_in.at[move], kc=1)

    def add_cores(move, slot):
        core_copies[move].wait_recv()
        links.sent(core_copies[move])
        x_out[move] = (partial_ref[slot, other, :] + core_in[move, x_other, :].astype(F32)).astype(
            BF16
        )
        x_copies[move] = links.send(x_out.at[move], x_in.at[move], kx=1)
        sums_ref[move] = partial_ref[slot, mine, :] + core_in[move, x_mine, :].astype(F32)

    def add_x(move):
        x_copies[move].wait_recv()
        sums_ref[move] += x_in[move].astype(F32)

    def columns(move, line):
        return rows_at(rank(move, line), weight_rows)

    def output_block(move, line):
        return by_rows(output_grad_ref[:, columns(move, line)], attn_out_ref[...])

    def attend_grad(move, line):
        return by_rows(attn_in_ref[:, columns(move, line)], d_lin_ref[...])

    loads[0].wait()
    for move in Scatter.ORDER:
        output_sum.start(move, output_block(move, 1 - here.y))

    span = longest * STRETCH
    shape = (2 * STRETCH, span)
    ahead = lax.broadcasted_iota(jnp.int32, shape, 1) - lax.rem(
        lax.broadcasted_iota(jnp.int32, shape, 0), STRETCH
    )

    def attend_block(block):
        rows = slice(block * STRETCH, (block + 1) * STRETCH)
        tiles = [kv_ref[table_ref[block * longest + place]] for place in range(longest)]
        tile = jnp.concatenate(tiles, axis=0)
        keys = [tile[:, :64], tile[:, 64:128]]
        values = [tile[:, 128:192], tile[:, 192:256]]
        middle_key = jnp.where(odd, keys[1], keys[0])
        middle_value = jnp.where(odd, values[1], values[0])
        visible = ahead <= offset_ref[rank(0, here.y) * blocks + block]
        d_keys, d_values = [], []
        for pair, key, value in (
            (0, keys[0], values[0]),
            (1, middle_key, middle_value),
            (2, keys[1], values[1]),
        ):
            query = query_ref[block, pair]
            both = d_heads_ref[rows, pair * 128 : (pair + 1) * 128]
            d_out = jnp.concatenate([both[:, :HEAD_WIDTH], both[:, HEAD_WIDTH:]], axis=0)
            kept = attended_ref[block, pair]
            delta = jnp.sum(d_out.astype(F32) * kept[:, :HEAD_WIDTH], axis=-1, keepdims=True)
            scores = by_cols(query, key)
            weights = jnp.exp2(
                scores * (LOG2E * scale) - kept[:, HEAD_WIDTH : HEAD_WIDTH + 1]
            )
            weights = jnp.where(visible, weights, 0.0)
            d_weights = by_cols(d_out, value)
            d_scores = (weights * (d_weights - delta)).astype(BF16)
            d_values.append(by_rows(weights.astype(BF16), d_out))
            d_keys.append(by_rows(d_scores, query))
            d_query_ref[block, pair] = product(d_scores, key) * scale
        zero = jnp.zeros((span, HEAD_WIDTH), F32)
        parts = [
            (d_keys[0] + jnp.where(odd, zero, d_keys[1])) * scale,
            (d_keys[2] + jnp.where(odd, d_keys[1], zero)) * scale,
            d_values[0] + jnp.where(odd, zero, d_values[1]),
            d_values[2] + jnp.where(odd, d_values[1], zero),
        ]
        d_kv_ref[block * longest : (block + 1) * longest] = jnp.concatenate(
            parts, axis=1
        ).reshape(longest, STRETCH, kv_width)

    attend_block(0)
    loads[1].wait()
    loads[2].wait()
    out_start(3, 0)
    out_start(1, 1)
    attend_block(1)
    add_cores(3, 0)
    out_start(2, 0)
    add_cores(1, 1)
    out_start(0, 1)
    attend_block(2)

    def kv_block(move, line):
        pieces = []
        for index in range(blocks):
            slot = rank(move, line) * blocks + index
            sequence = sequence_ref[slot]
            place = offset_ref[slot] // STRETCH
            total = jnp.zeros((STRETCH, kv_width), F32)
            for block in range(blocks):
                same = sequence_ref[rank(0, here.y) * blocks + block] == sequence
                total += jnp.where(same, d_kv_ref[block * longest + place], 0.0)
            pieces.append(total)
        return jnp.concatenate(pieces, axis=0)

    for move in Scatter.ORDER:
        kv_sum.start(move, kv_block(move, 1 - here.y))

    def group_back(group, at, grad):
        linear = lin_ref[:, at]
        inverse = lax.rsqrt(head_mean(linear * linear) + EPSILON)
        unit = linear * inverse
        grad = grad * cosine_ref[...] + halves_swapped(grad * sine_ref[...])
        gain = jnp.sum(grad * unit, axis=0, keepdims=True)
        scaled = grad * head_gain_ref[:, group * 128 : (group + 1) * 128]
        return inverse * (scaled - unit * head_mean(scaled * unit)), gain

    loads[3].wait()
    add_cores(2, 0)
    add_cores(0, 1)
    for move in Scatter.ORDER[:2]:
        output_sum.add(move, output_block(move, here.y))
    small_ref[...] = jnp.zeros_like(small_ref)
    small_ref[1:2, :] = gain_ffn_ref[...]
    for pair in range(PAIRS):
        grad = jnp.concatenate(
            [
                jnp.concatenate(
                    [d_query_ref[block, pair, :STRETCH], d_query_ref[block, pair, STRETCH:]], axis=1
                )
                for block in range(blocks)
            ],
            axis=0,
        )
        at = slice(kv_width + pair * 128, kv_width + (pair + 1) * 128)
        linear_grad, gain = group_back(pair + 1, at, grad)
        d_lin_ref[:, at] = linear_grad.astype(BF16)
        small_ref[2:3, (pair + 1) * 128 : (pair + 2) * 128] = gain
    for move in Scatter.ORDER:
        kv_sum.add(move, kv_block(move, here.y))
    add_x(3)
    z_out[1] = sums_ref[3].astype(BF16)
    z_copies = {1: links.send(z_out.at[1], z_in.at[1], kz=1)}
    add_x(1)
    z_out[0] = sums_ref[1].astype(BF16)
    z_copies[0] = links.send(z_out.at[0], z_in.at[0], kz=1)
    d_kv = kv_sum.finish()
    for move in Scatter.ORDER[2:]:
        output_sum.add(move, output_block(move, here.y))
    linear_grad, gain = group_back(0, slice(0, 128), d_kv[:, :128])
    d_lin_ref[:, :128] = linear_grad.astype(BF16)
    d_lin_ref[:, 128:kv_width] = d_kv[:, 128:].astype(BF16)
    small_ref[2:3, :128] = gain

    loads[4].wait()
    for move in Scatter.ORDER:
        attend_sum.start(move, attend_grad(move, 1 - here.y))
    add_x(2)
    add_x(0)
    z_copies[1].wait_recv()
    z_out[2] = (sums_ref[2] + z_in[1].astype(F32)).astype(BF16)
    z_copies[2] = links.send(z_out.at[2], z_in.at[2], kz=2)

    loads[5].wait()
    partial_ref[0] = by_cols(d_lin_ref[...], w_attend_ref[...])
    core_out[0] = partial_ref[0, other_half, :].astype(BF16)
    core_copies[4] = links.send(core_out.at[0], core_in.at[4], kc=1)
    add_cores(4, 0)
    attend_sum.add(3, attend_grad(3, here.y))
    attend_sum.add(1, attend_grad(1, here.y))
    add_x(4)
    loads[6].wait()
    loads[7].wait()
    states = states_ref[...].astype(F32)
    inverse = lax.rsqrt(jnp.mean(states * states, axis=-1, keepdims=True) + EPSILON)
    unit = states * inverse
    grad = sums_ref[4]
    small_ref[0:1, :] = jnp.sum(grad * unit, axis=0, keepdims=True)
    scaled = grad * gains_ref[0:1, :]
    total = back_ref[...] + inverse * (
        scaled - unit * jnp.mean(scaled * unit, axis=-1, keepdims=True)
    )
    states_grad_ref[mine, :] = total.astype(BF16)
    block = states_grad_ref.at[mine]
    states_x = links.send(block, block, kx=1)

    def small_step(step, **move):
        small_out[step] = small_ref[...]
        return links.send(small_out.at[step], small_in.at[step], **move)

    small = small_step(0, kc=1)
    attend_sum.add(2, attend_grad(2, here.y))
    small.wait_recv()
    small_ref[...] += small_in[0]
    small = small_step(1, kx=1)
    states_x.wait_recv()
    both = states_grad_ref.at[my_half]
    states_core = links.send(both, both, kc=1)
    small.wait_recv()
    small_ref[...] += small_in[1]
    small = small_step(2, ky=1)
    attend_sum.add(0, attend_grad(0, here.y))
    small.wait_recv()
    small_ref[...] += small_in[2]
    small = small_step(3, kz=1)
    small.wait_recv()
    small_ref[...] += small_in[3]
    small = small_step(4, kz=2)

    total = attend_sum.finish()
    part = here.x * 2 + here.c
    g_kv_ref[part] = total[:, :kv_width].astype(BF16)
    block = g_kv_ref.at[part]
    kv_x = links.send(block, block, kx=1)
    kv_core = links.send(block, block, kc=1)
    g_attend_ref[...] = total[:, kv_width:]
    z_copies[0].wait_recv()
    z_copies[2].wait_recv()
    loads[8].wait()
    result_ref[mine, :] = (
        middle_ref[...] + sums_ref[0] + z_in[0].astype(F32) + z_in[2].astype(F32)
    ).astype(BF16)
    block = result_ref.at[mine]
    result_x = links.send(block, block, kx=1)
    kv_x.wait_recv()
    block = g_kv_ref.at[(1 - here.x) * 2 + here.c]
    kv_both = links.send(block, block, kc=1)
    g_output_ref[...] = output_sum.finish()
    small.wait_recv()
    small_ref[...] += small_in[4]
    d_gains_ref[...] = small_ref[:2, rows_at(rank(0, here.y), weight_rows)]
    head_sums = [
        small_ref[2:3, head * HEAD_WIDTH : (head + 1) * HEAD_WIDTH] for head in range(heads + 2)
    ]
    key_gain_out[...] = head_sums[0] + head_sums[1]
    query_gain_out[...] = sum(head_sums[3:], head_sums[2])
    result_x.wait_recv()
    both = result_ref.at[my_half]
    result_core = links.send(both, both, kc=1)
    for copy in (states_core, kv_core, kv_both, result_core, *hidden_pushes):
        copy.wait_recv()
    links.finish()


def backward(lines, heads, longest, *arguments):
    lin, attn_in, mixed, w_attend = arguments[13], arguments[14], arguments[20], arguments[16]
    token_rows, width = attn_in.shape
    quarter = token_rows // 4
    half = 2 * quarter
    weight_rows = width // (4 * lines)
    head_width = heads * HEAD_WIDTH
    blocks = token_rows // STRETCH
    vmem = pl.BlockSpec(memory_space=pltpu.VMEM)
    smem = pl.BlockSpec(memory_space=pltpu.SMEM)
    hbm = pl.BlockSpec(memory_space=pl.ANY)
    shape = jax.ShapeDtypeStruct
    return pl.pallas_call(
        functools.partial(backward_kernel, lines, heads, longest),
        out_shape=(
            shape((token_rows, width), BF16),
            shape((token_rows, width), BF16),
            shape((weight_rows, head_width), F32),
            shape((weight_rows, head_width), F32),
            shape((4, weight_rows, 4 * HEAD_WIDTH), BF16),
            shape((2, weight_rows), F32),
            shape((1, HEAD_WIDTH), F32),
            shape((1, HEAD_WIDTH), F32),
            shape(arguments[-1].shape, BF16),
        ),
        in_specs=[smem] * 3 + [vmem] * 10 + [hbm] * 11,
        out_specs=(vmem,) * 8 + (hbm,),
        scratch_shapes=[
            pltpu.VMEM((8, width), F32),
            pltpu.VMEM(lin.shape, F32),
            pltpu.VMEM(attn_in.shape, BF16),
            pltpu.VMEM((token_rows, width), BF16),
            pltpu.VMEM(w_attend.shape, BF16),
            pltpu.VMEM((quarter, width), F32),
            pltpu.VMEM((quarter, width), BF16),
            pltpu.VMEM((quarter, width), F32),
            pltpu.VMEM(mixed.shape, BF16),
            pltpu.VMEM((mixed.shape[0], width), BF16),
            pltpu.VMEM((blocks, PAIRS, 2 * STRETCH, HEAD_WIDTH), F32),
            pltpu.VMEM((blocks * longest, STRETCH, 4 * HEAD_WIDTH), F32),
            pltpu.VMEM(lin.shape, BF16),
            pltpu.VMEM((2, token_rows, width), F32),
            pltpu.VMEM((2, half, width), BF16),
            pltpu.VMEM((5, half, width), BF16),
            pltpu.VMEM((5, quarter, width), BF16),
            pltpu.VMEM((5, quarter, width), BF16),
            pltpu.VMEM((5, quarter, width), F32),
            pltpu.VMEM((3, quarter, width), BF16),
            pltpu.VMEM((3, quarter, width), BF16),
            pltpu.VMEM((5, 8, width), F32),
            pltpu.VMEM((5, 8, width), F32),
            pltpu.SemaphoreType.DMA((10,)),
            pltpu.SemaphoreType.DMA((BACKWARD_COPIES,)),
            pltpu.SemaphoreType.DMA((BACKWARD_COPIES,)),
            *scatter_scratch((token_rows, 4 * HEAD_WIDTH)),
            *scatter_scratch((weight_rows, head_width)),
            *scatter_scratch((weight_rows, lin.shape[1])),
        ],
        compiler_params=pltpu.CompilerParams(
            collective_id=1, has_side_effects=True, vmem_limit_bytes=64 << 20
        ),
        input_output_aliases={len(arguments) - 1: 8},
        name="backward",
    )(*arguments)


def local_kernels(
    states,
    query_weight,
    keyvalue_matrix,
    output_weight,
    gate_weight,
    up_weight,
    down_weight,
    norm_gains,
    query_gain,
    key_gain,
    slot_sequence,
    slot_offset,
    out_grad,
):
    width = states.shape[1]
    dp_ranks = lax.axis_size("dp")
    tensor_ranks = lax.axis_size("tensor")
    lines = dp_ranks // PLANES
    heads_here = QUERY_HEADS // tensor_ranks
    sharing_count = QUERY_HEADS // KEYVALUE_HEADS
    value_start = KEYVALUE_HEADS * HEAD_WIDTH
    hidden = gate_weight.shape[2]
    slice_width = hidden // PLANES
    weight_rows = width // dp_ranks

    exponent = -(np.arange(2 * HEAD_WIDTH) % (HEAD_WIDTH // 2)) * 2.0 / HEAD_WIDTH
    frequency = jnp.asarray((10000.0**exponent)[None].astype(np.float32))
    (
        lin,
        attn_in,
        queries,
        keyvalues,
        attended,
        attn_out,
        gains,
        w_attend,
        middle_rows,
        back,
        gain_ffn,
        d_heads,
        output_grad,
        mixed,
        cosine,
        sine,
        head_gain,
        table,
        collected,
        staged,
        w_down,
    ) = forward(
        lines,
        heads_here,
        slice_width,
        LONGEST,
        slot_sequence,
        slot_offset,
        states,
        norm_gains[0].T,
        query_gain,
        key_gain,
        frequency,
        query_weight[0],
        keyvalue_matrix[0],
        gate_weight[0].T,
        up_weight[0].T,
        down_weight[0].T,
        output_weight[0],
        out_grad,
    )
    (
        result,
        states_grad,
        g_attend,
        g_output,
        g_kv,
        d_gains,
        d_query_gain,
        d_key_gain,
        collected,
    ) = backward(
        lines,
        heads_here,
        LONGEST,
        slot_sequence,
        slot_offset,
        table,
        queries,
        keyvalues,
        attended,
        d_heads,
        attn_out,
        gains,
        gain_ffn,
        cosine,
        sine,
        head_gain,
        lin,
        attn_in,
        output_grad,
        w_attend,
        back,
        states,
        middle_rows,
        mixed,
        w_down,
        staged,
        collected,
    )

    def hidden_grad(index):
        piece = collected[:, index * slice_width : (index + 1) * slice_width]
        return piece.transpose(2, 0, 1).astype(F32).reshape(1, weight_rows, hidden)

    d_keyvalue_matrix = jnp.zeros((weight_rows, 2 * value_start), F32)
    for other in range(tensor_ranks):
        start = (other * heads_here) // sharing_count * HEAD_WIDTH
        block = g_kv[other].astype(F32)
        for offset, piece in (
            (start, block[:, : 2 * HEAD_WIDTH]),
            (value_start + start, block[:, 2 * HEAD_WIDTH :]),
        ):
            after = 2 * value_start - offset - 2 * HEAD_WIDTH
            d_keyvalue_matrix += jnp.pad(piece, ((0, 0), (offset, after)))
    return (
        result,
        states_grad.astype(F32),
        g_attend[None],
        d_keyvalue_matrix[None],
        g_output[None],
        hidden_grad(0),
        hidden_grad(1),
        hidden_grad(2),
        d_gains.T[None],
        d_query_gain,
        d_key_gain,
    )


def local_permutes(
    states,
    query_weight,
    keyvalue_matrix,
    output_weight,
    gate_weight,
    up_weight,
    down_weight,
    norm_gains,
    query_gain,
    key_gain,
    slot_sequence,
    slot_offset,
    out_grad,
):
    token_rows, width = states.shape
    dp_ranks = lax.axis_size("dp")
    tensor_ranks = lax.axis_size("tensor")
    lines = dp_ranks // PLANES
    rank, part = lax.axis_index("dp"), lax.axis_index("tensor")
    plane, line = rank // lines, rank % lines
    quarter = token_rows // tensor_ranks
    heads_here = QUERY_HEADS // tensor_ranks
    head_width = heads_here * HEAD_WIDTH
    sharing_count = QUERY_HEADS // KEYVALUE_HEADS
    blocks_here = token_rows // STRETCH
    slot_count = slot_sequence.shape[0]
    hidden = gate_weight.shape[2]
    slice_width = hidden // PLANES
    weight_rows = width // dp_ranks

    def send(value, kz=0, ky=0, kx=0, kc=0):
        move_rank, move_part = kz * lines + ky, kx * 2 + kc
        pairs = [
            (r * tensor_ranks + p, (r ^ move_rank) * tensor_ranks + (p ^ move_part))
            for r in range(dp_ranks)
            for p in range(tensor_ranks)
        ]
        return lax.ppermute(value, ("dp", "tensor"), pairs)

    def gather_planes(value):
        near = send(value, kz=1)
        far = send(value, kz=2)
        return [value, near, far, send(far, kz=1)]

    def gather_dp(value):
        whole = jnp.zeros((dp_ranks, *value.shape), value.dtype)
        for kz, piece in enumerate(gather_planes(value)):
            for ky in range(lines):
                got = send(piece, ky=ky) if ky else piece
                whole = lax.dynamic_update_index_in_dim(whole, got, rank ^ (kz * lines + ky), 0)
        return whole

    def rounded(value):
        return value.astype(BF16)

    def scatter_dp(whole):
        def piece(move):
            return lax.dynamic_index_in_dim(whole, rank ^ move, 0, keepdims=False)

        parts = []
        for kz in range(PLANES):
            total = piece(kz * lines).astype(F32)
            for ky in range(1, lines):
                total = total + send(rounded(piece(kz * lines + ky)), ky=ky).astype(F32)
            parts.append(total)
        return scatter_planes(parts)

    def scatter_planes(parts):
        near = parts[0] + send(rounded(parts[1]), kz=1).astype(F32)
        far = parts[2] + send(rounded(parts[3]), kz=1).astype(F32)
        return near + send(rounded(far), kz=2).astype(F32)

    def scatter_tensor(blocks):
        got = send(rounded(jnp.concatenate([blocks[1], blocks[3]], axis=0)), kc=1).astype(F32)
        rows = blocks[0].shape[0]
        here = blocks[0] + got[:rows]
        there = blocks[2] + got[rows:]
        return here + send(rounded(there), kx=1).astype(F32)

    def gather_tensor(block):
        both = jnp.concatenate([block, send(block, kx=1)], axis=0)
        return jnp.concatenate([both, send(both, kc=1)], axis=0)

    def in_order(blocks):
        whole = jnp.zeros_like(blocks)
        for index, move in enumerate((0, 2, 1, 3)):
            whole = lax.dynamic_update_slice_in_dim(
                whole,
                blocks[index * quarter : (index + 1) * quarter],
                (part ^ move) * quarter,
                0,
            )
        return whole

    def quarters(value):
        return [
            lax.dynamic_slice_in_dim(value, (part ^ move) * quarter, quarter, 0)
            for move in range(tensor_ranks)
        ]

    sequence_here = lax.dynamic_slice_in_dim(slot_sequence, rank * blocks_here, blocks_here)
    offset_here = lax.dynamic_slice_in_dim(slot_offset, rank * blocks_here, blocks_here)
    counts = offset_here // STRETCH + 1
    places = jnp.arange(slot_count, dtype=jnp.int32)
    same = (slot_sequence[None, None, :] == sequence_here[:, None, None]) & (
        slot_offset[None, None, :] == places[None, :, None] * STRETCH
    )
    slots = jnp.sum(jnp.where(same, places[None, None, :], 0), axis=2).astype(jnp.int32)
    parity = jnp.reshape(part % 2, (1,)).astype(jnp.int32)
    positions = (offset_here[:, None] + jnp.arange(STRETCH, dtype=jnp.int32)[None, :]).reshape(-1)
    cosines, sines = angles(positions, HEAD_WIDTH)

    first_key = (part * heads_here) // sharing_count * HEAD_WIDTH
    value_start = KEYVALUE_HEADS * HEAD_WIDTH
    kv_columns = [
        lax.dynamic_slice_in_dim(keyvalue_matrix[0], first_key, 2 * HEAD_WIDTH, 1),
        lax.dynamic_slice_in_dim(keyvalue_matrix[0], value_start + first_key, 2 * HEAD_WIDTH, 1),
    ]
    gains = gather_dp(norm_gains[0].T).transpose(1, 0, 2).reshape(2, width).astype(F32)
    w_attend = gather_dp(jnp.concatenate([query_weight[0], *kv_columns], axis=1)).reshape(width, -1)
    w_output = gather_dp(output_weight[0]).reshape(width, head_width)

    def sliced(weight):
        return weight[0].reshape(weight_rows, PLANES, slice_width).transpose(1, 0, 2)

    pad_first = -2 * slice_width % 128
    pad_second = -slice_width % 128
    packed = jnp.concatenate(
        [
            sliced(gate_weight),
            sliced(up_weight),
            jnp.zeros((PLANES, weight_rows, pad_first), BF16),
            sliced(down_weight),
            jnp.zeros((PLANES, weight_rows, pad_second), BF16),
        ],
        axis=2,
    )
    w_hidden = jnp.zeros((dp_ranks, weight_rows, packed.shape[2]), BF16)
    for kz in range(PLANES):
        piece = lax.dynamic_index_in_dim(packed, plane ^ kz, 0, keepdims=False)
        piece = send(piece, kz=kz) if kz else piece
        for ky in range(lines):
            got = send(piece, ky=ky) if ky else piece
            w_hidden = lax.dynamic_update_index_in_dim(w_hidden, got, rank ^ (kz * lines + ky), 0)
    w_hidden = w_hidden.reshape(width, -1)
    down_start = 2 * slice_width + pad_first
    w_gate_up = w_hidden[:, : 2 * slice_width]
    w_down = w_hidden[:, down_start : down_start + slice_width]

    def gather_group(block):
        return [gather_tensor(piece) for piece in gather_planes(block)]

    def quarter_of(value):
        return lax.dynamic_slice_in_dim(value, part * quarter, quarter, 0)

    query_g, key_g = query_gain[0], key_gain[0]
    attn_in = rounded(normed(states.astype(F32), gains[0]))
    lin = product(attn_in, w_attend)
    query_lin, keyvalue_lin = lin[:, :head_width], lin[:, head_width:]

    def query_side(linear, gain_vector):
        return rotated(
            normed(linear.reshape(token_rows, heads_here, HEAD_WIDTH), gain_vector), cosines, sines
        )

    def key_side(linear, gain_vector):
        keys = linear[:, : 2 * HEAD_WIDTH].reshape(token_rows, 2, HEAD_WIDTH)
        keys = rotated(normed(keys, gain_vector), cosines, sines)
        return jnp.concatenate(
            [keys.reshape(token_rows, 2 * HEAD_WIDTH), linear[:, 2 * HEAD_WIDTH :]], axis=1
        )

    def to_pairs(value):
        return (
            value.reshape(blocks_here, STRETCH, PAIRS, 2, -1)
            .transpose(0, 2, 3, 1, 4)
            .reshape(blocks_here, PAIRS, 2 * STRETCH, -1)
        )

    def from_pairs(value):
        return (
            value.reshape(blocks_here, PAIRS, 2, STRETCH, -1)
            .transpose(0, 3, 1, 2, 4)
            .reshape(token_rows, heads_here, -1)
        )

    queries = to_pairs(rounded(query_side(query_lin, query_g)))
    keyvalues = gather_dp(rounded(key_side(keyvalue_lin, key_g)))
    keyvalues = keyvalues.reshape(slot_count, STRETCH, 4 * HEAD_WIDTH)
    attended = attend(counts, slots, parity, queries, keyvalues)
    attn_out = rounded(from_pairs(attended[..., :HEAD_WIDTH]).reshape(token_rows, head_width))
    logs = attended[..., HEAD_WIDTH]

    branch = scatter_tensor(quarters(by_cols(attn_out, w_output)))
    states_quarter = quarter_of(states).astype(F32)
    middle = states_quarter + branch
    ffn_in = rounded(normed(middle, gains[1]))

    down_grads = gather_group(quarter_of(out_grad))
    ffn_ins = gather_group(ffn_in)
    mixed_chunks, d_chunks, back_parts, out_parts = [], [], [], []
    for down_grad, ffn_chunk in zip(down_grads, ffn_ins):
        gate_up = product(ffn_chunk, w_gate_up)
        gate_pre, up_pre = gate_up[:, :slice_width], gate_up[:, slice_width:]
        sigmoid_gate = jax.nn.sigmoid(gate_pre)
        mixed = rounded(gate_pre * sigmoid_gate * up_pre)
        d_mixed = product(down_grad, w_down)
        d_gate = d_mixed * up_pre * sigmoid_gate * (1.0 + gate_pre * (1.0 - sigmoid_gate))
        d_up = d_mixed * gate_pre * sigmoid_gate
        d_gate_up = jnp.concatenate([rounded(d_gate), rounded(d_up)], axis=1)
        mixed_chunks.append(mixed)
        d_chunks.append(d_gate_up)

        def reduced(value):
            blocks = value.reshape(4, quarter, width)
            return scatter_tensor([blocks[0], blocks[2], blocks[1], blocks[3]])

        back_parts.append(reduced(by_cols(d_gate_up, w_gate_up)))
        out_parts.append(reduced(by_cols(mixed, w_down)))
    d_ffn_in = scatter_planes(back_parts)

    def norm_back(vector, gain_vector, grad):
        inverse = lax.rsqrt(jnp.mean(vector * vector, axis=-1, keepdims=True) + EPSILON)
        unit = vector * inverse
        scaled = grad * gain_vector
        back = inverse * (scaled - unit * jnp.mean(scaled * unit, axis=-1, keepdims=True))
        return back, jnp.sum(grad * unit, axis=0)

    d_middle, d_gain_ffn = norm_back(middle, gains[1], d_ffn_in)
    grad_middle = quarter_of(out_grad).astype(F32) + d_middle
    output_grad = in_order(gather_tensor(rounded(grad_middle)))

    d_wout = by_rows(output_grad, attn_out)
    d_heads = rounded(product(output_grad, w_output)).reshape(token_rows, heads_here, HEAD_WIDTH)
    d_pairs = to_pairs(d_heads)
    delta = jnp.sum(d_pairs.astype(F32) * attended[..., :HEAD_WIDTH], axis=-1)
    d_query, d_keyvalue = attend_back(
        counts,
        slots,
        parity,
        queries,
        d_pairs,
        logs[:, :, None, :],
        delta[:, :, None, :],
        keyvalues,
    )
    d_keyvalue_here = scatter_dp(d_keyvalue.reshape(dp_ranks, token_rows, 4 * HEAD_WIDTH))
    _, query_pull = jax.vjp(query_side, query_lin, query_g)
    d_query_lin, d_querygain = query_pull(from_pairs(d_query))
    _, key_pull = jax.vjp(key_side, keyvalue_lin, key_g)
    d_keyvalue_lin, d_keygain = key_pull(d_keyvalue_here)
    d_lin = jnp.concatenate([rounded(d_query_lin), rounded(d_keyvalue_lin)], axis=1)
    d_attn_in = scatter_tensor(quarters(by_cols(d_lin, w_attend)))
    d_states, d_gain_attn = norm_back(states_quarter, gains[0], d_attn_in)
    states_grad = in_order(gather_tensor(rounded(grad_middle + d_states))).astype(F32)

    d_wattend = scatter_dp(by_rows(attn_in, d_lin).reshape(dp_ranks, weight_rows, -1))
    d_wout = scatter_dp(d_wout.reshape(dp_ranks, weight_rows, -1))
    ffn_all = jnp.concatenate(ffn_ins, axis=0)
    down_all = jnp.concatenate(down_grads, axis=0)
    grads_hidden = jnp.concatenate(
        [
            by_rows(ffn_all, jnp.concatenate(d_chunks, axis=0)),
            by_rows(down_all, jnp.concatenate(mixed_chunks, axis=0)),
        ],
        axis=1,
    ).reshape(dp_ranks, weight_rows, 3 * slice_width)
    collected = jnp.zeros((PLANES, weight_rows, 3 * slice_width), F32)
    for kz in range(PLANES):
        total = lax.dynamic_index_in_dim(grads_hidden, rank ^ (kz * lines), 0, keepdims=False)
        for ky in range(1, lines):
            piece = lax.dynamic_index_in_dim(
                grads_hidden, rank ^ (kz * lines + ky), 0, keepdims=False
            )
            total = total + send(rounded(piece), ky=ky).astype(F32)
        if kz:
            total = send(rounded(total), kz=kz).astype(F32)
        collected = lax.dynamic_update_index_in_dim(collected, total, plane ^ kz, 0)

    def unsliced(index):
        piece = collected[:, :, index * slice_width : (index + 1) * slice_width]
        return piece.transpose(1, 0, 2).reshape(1, weight_rows, hidden)

    kv_grad = d_wattend[:, head_width:]
    spread = jnp.zeros((weight_rows, 2 * value_start), F32)
    spread = lax.dynamic_update_slice_in_dim(spread, kv_grad[:, : 2 * HEAD_WIDTH], first_key, 1)
    spread = lax.dynamic_update_slice_in_dim(
        spread, kv_grad[:, 2 * HEAD_WIDTH :], value_start + first_key, 1
    )
    d_wkeyvalue = lax.psum(spread, "tensor")

    result_quarter = rounded(middle + scatter_planes(out_parts))
    result = in_order(gather_tensor(result_quarter))

    small = jnp.concatenate([d_gain_attn, d_gain_ffn, d_querygain, d_keygain])
    small = lax.psum(small, ("dp", "tensor"))
    d_gains = lax.dynamic_slice_in_dim(
        small[: 2 * width].reshape(2, width), rank * weight_rows, weight_rows, 1
    ).T
    return (
        result,
        states_grad,
        d_wattend[None, :, :head_width],
        d_wkeyvalue[None],
        d_wout[None],
        unsliced(0),
        unsliced(1),
        unsliced(2),
        d_gains[None],
        small[2 * width : 2 * width + HEAD_WIDTH][None],
        small[2 * width + HEAD_WIDTH :][None],
    )


def local(*arguments):
    rows = arguments[0].shape[1] // lax.axis_size("dp")
    slots = arguments[10].shape[0]
    if lax.axis_size("dp") == 8 and lax.axis_size("tensor") == 4 and rows == 256 and slots == 24:
        return local_kernels(*arguments)
    return local_permutes(*arguments)


def solution(mesh):
    return jax.shard_map(
        local,
        mesh=mesh,
        in_specs=(
            P("dp", None),
            P(None, "dp", "tensor"),
            P(None, "dp", None),
            P(None, "dp", "tensor"),
            P(None, "dp", "tensor"),
            P(None, "dp", "tensor"),
            P(None, "dp", "tensor"),
            P(None, "dp", None),
            P(),
            P(),
            P(),
            P(),
            P("dp", None),
        ),
        out_specs=(
            P("dp", None),
            P("dp", None),
            P(None, "dp", "tensor"),
            P(None, "dp", None),
            P(None, "dp", "tensor"),
            P(None, "dp", "tensor"),
            P(None, "dp", "tensor"),
            P(None, "dp", "tensor"),
            P(None, "dp", None),
            P(),
            P(),
        ),
        check_vma=False,
    )
```

```python
import functools

import jax
import jax.numpy as jnp
import numpy as np
from jax import lax
from jax.experimental import pallas as pl
from jax.experimental.pallas import tpu as pltpu
from jax.sharding import PartitionSpec as P

QUERY_HEADS = 24
KEYVALUE_HEADS = 6
HEAD_WIDTH = 64
STRETCH = 128
EPSILON = 1e-06
PLANES = 4
PAIRS = 3
LONGEST = 12
LOG2E = 1.4426950408889634
BF16 = jnp.bfloat16
F32 = jnp.float32


def product(left_side, right_side):
    return jnp.dot(left_side, right_side, preferred_element_type=F32)


def by_rows(left_side, right_side):
    return lax.dot_general(
        left_side, right_side, (((0,), (0,)), ((), ())), preferred_element_type=F32
    )


def by_cols(left_side, right_side):
    return lax.dot_general(
        left_side, right_side, (((1,), (1,)), ((), ())), preferred_element_type=F32
    )


def normed(vector, gain_vector):
    return (
        vector
        * lax.rsqrt(jnp.mean(vector * vector, axis=-1, keepdims=True) + EPSILON)
        * gain_vector
    )


def angles(positions, head_size):
    frequency = 10000.0 ** (-jnp.arange(head_size // 2, dtype=F32) * 2.0 / head_size)
    phase_angle = positions.astype(F32)[:, None] * frequency[None, :]
    return (jnp.cos(phase_angle)[:, None, :], jnp.sin(phase_angle)[:, None, :])


def rotated(vector, cosines, sines):
    half_width = vector.shape[-1] // 2
    front = vector[..., :half_width]
    behind = vector[..., half_width:]
    return jnp.concatenate(
        [front * cosines - behind * sines, behind * cosines + front * sines], axis=-1
    )


def visible_mask(shape, key_axis):
    keys = lax.broadcasted_iota(jnp.int32, shape, key_axis)
    queries = lax.rem(lax.broadcasted_iota(jnp.int32, shape, 1 - key_axis), STRETCH)
    return keys <= queries


def attend_kernel(count_ref, slots_ref, parity_ref, q_ref, kv_ref, out_ref, acc_ref):
    odd = parity_ref[0] == 1
    ones = jnp.ones((STRETCH, HEAD_WIDTH), BF16)

    def add_block(block, slot, last):
        tile = kv_ref[slot]
        keys = [tile[:, :64], tile[:, 64:128]]
        values = [
            jnp.concatenate([tile[:, 128:192], ones], axis=1),
            jnp.concatenate([tile[:, 192:256], ones], axis=1),
        ]
        middle_key = jnp.where(odd, keys[1], keys[0])
        middle_value = jnp.where(odd, values[1], values[0])
        for pair, key, value in (
            (0, keys[0], values[0]),
            (1, middle_key, middle_value),
            (2, keys[1], values[1]),
        ):
            scores = by_cols(q_ref[block, pair], key)
            weights = jnp.exp2(scores * (LOG2E * HEAD_WIDTH**-0.5))
            if last:
                weights = jnp.where(visible_mask(weights.shape, 1), weights, 0.0)
            acc_ref[pair] += product(weights.astype(BF16), value)

    def one_block(block, carry):
        acc_ref[...] = jnp.zeros_like(acc_ref)
        count = count_ref[block]

        def step(index, inner):
            add_block(block, slots_ref[block, index], False)
            return inner

        lax.fori_loop(0, count - 1, step, 0)
        add_block(block, slots_ref[block, count - 1], True)
        for pair in range(PAIRS):
            total = acc_ref[pair]
            denominator = total[:, HEAD_WIDTH:]
            out_ref[block, pair] = jnp.concatenate(
                [total[:, :HEAD_WIDTH] / denominator, jnp.log2(denominator)], axis=1
            )
        return carry

    lax.fori_loop(0, q_ref.shape[0], one_block, 0)


def attend(counts, slots, parity, queries, keyvalues):
    blocks = queries.shape[0]
    smem = pl.BlockSpec(memory_space=pltpu.SMEM)
    vmem = pl.BlockSpec(memory_space=pltpu.VMEM)
    return pl.pallas_call(
        attend_kernel,
        out_shape=jax.ShapeDtypeStruct((blocks, PAIRS, 2 * STRETCH, 128), F32),
        in_specs=[smem, smem, smem, vmem, vmem],
        out_specs=vmem,
        scratch_shapes=[pltpu.VMEM((PAIRS, 2 * STRETCH, 128), F32)],
        compiler_params=pltpu.CompilerParams(vmem_limit_bytes=40 << 20),
        cost_estimate=pl.CostEstimate(
            flops=4 * 20 * PAIRS * 256 * 128 * 64 * 4, bytes_accessed=8 << 20, transcendentals=0
        ),
        name="attend",
    )(counts, slots, parity, queries, keyvalues)


def attend_back_kernel(
    count_ref, slots_ref, parity_ref, q_ref, do_ref, log_ref, delta_ref, kv_ref, dq_ref, dkv_ref
):
    odd = parity_ref[0] == 1
    scale = HEAD_WIDTH**-0.5
    dq_ref[...] = jnp.zeros_like(dq_ref)
    dkv_ref[...] = jnp.zeros_like(dkv_ref)

    def add_block(block, slot, last):
        tile = kv_ref[slot]
        keys = [tile[:, :64], tile[:, 64:128]]
        values = [tile[:, 128:192], tile[:, 192:256]]
        middle_key = jnp.where(odd, keys[1], keys[0])
        middle_value = jnp.where(odd, values[1], values[0])
        d_keys, d_values = [], []
        for pair, key, value in (
            (0, keys[0], values[0]),
            (1, middle_key, middle_value),
            (2, keys[1], values[1]),
        ):
            query, d_out = q_ref[block, pair], do_ref[block, pair]
            scores = by_cols(key, query)
            weights = jnp.exp2(scores * (LOG2E * scale) - log_ref[block, pair])
            if last:
                weights = jnp.where(visible_mask(weights.shape, 0), weights, 0.0)
            d_weights = by_cols(value, d_out)
            d_scores = (weights * (d_weights - delta_ref[block, pair])).astype(BF16)
            d_values.append(product(weights.astype(BF16), d_out))
            d_keys.append(product(d_scores, query))
            dq_ref[block, pair] += by_rows(d_scores, key) * scale
        zero = jnp.zeros((STRETCH, HEAD_WIDTH), F32)
        parts = [
            (d_keys[0] + jnp.where(odd, zero, d_keys[1])) * scale,
            (d_keys[2] + jnp.where(odd, d_keys[1], zero)) * scale,
            d_values[0] + jnp.where(odd, zero, d_values[1]),
            d_values[2] + jnp.where(odd, d_values[1], zero),
        ]
        dkv_ref[slot] += jnp.concatenate(parts, axis=1)

    def one_block(block, carry):
        count = count_ref[block]

        def step(index, inner):
            add_block(block, slots_ref[block, index], False)
            return inner

        lax.fori_loop(0, count - 1, step, 0)
        add_block(block, slots_ref[block, count - 1], True)
        return carry

    lax.fori_loop(0, q_ref.shape[0], one_block, 0)


def attend_back(counts, slots, parity, queries, d_out, logs, delta, keyvalues):
    blocks = queries.shape[0]
    smem = pl.BlockSpec(memory_space=pltpu.SMEM)
    vmem = pl.BlockSpec(memory_space=pltpu.VMEM)
    return pl.pallas_call(
        attend_back_kernel,
        out_shape=(
            jax.ShapeDtypeStruct((blocks, PAIRS, 2 * STRETCH, HEAD_WIDTH), F32),
            jax.ShapeDtypeStruct(keyvalues.shape, F32),
        ),
        in_specs=[smem] * 3 + [vmem] * 5,
        out_specs=(vmem, vmem),
        compiler_params=pltpu.CompilerParams(vmem_limit_bytes=56 << 20),
        cost_estimate=pl.CostEstimate(
            flops=10 * 20 * PAIRS * 256 * 128 * 64 * 4, bytes_accessed=8 << 20, transcendentals=0
        ),
        name="attend_back",
    )(counts, slots, parity, queries, d_out, logs, delta, keyvalues)


class Place:
    def __init__(self, lines):
        rank, part = lax.axis_index("dp"), lax.axis_index("tensor")
        self.lines = lines
        self.z, self.y = rank // lines, lax.rem(rank, lines)
        self.x, self.c = part // 2, lax.rem(part, 2)
        self.quarter = self.c * 2 + self.x

    def plane(self, move):
        if move == 0:
            return self.z
        if move == 1:
            return self.z + 1 - 2 * lax.rem(self.z, 2)
        if move == 2:
            return self.z + 2 - 4 * (self.z // 2)
        return 3 - self.z

    def to(self, kz=0, ky=0, kx=0, kc=0):
        y = 1 - self.y if ky else self.y
        x = 1 - self.x if kx else self.x
        c = 1 - self.c if kc else self.c
        return (self.plane(kz) * self.lines + y, x * 2 + c)


class Links:
    def __init__(self, place, send_sems, recv_sems):
        self.place, self.send_sems, self.recv_sems = place, send_sems, recv_sems
        self.number, self.unsent = 0, []

    def greet(self, moves):
        barrier = pltpu.get_barrier_semaphore()
        for move in moves:
            pl.semaphore_signal(
                barrier, inc=1, device_id=self.place.to(**move), device_id_type=pl.DeviceIdType.MESH
            )
        pl.semaphore_wait(barrier, len(moves))

    def send(self, source, target, **move):
        number, self.number = self.number, self.number + 1
        copy = pltpu.make_async_remote_copy(
            src_ref=source,
            dst_ref=target,
            send_sem=self.send_sems.at[number],
            recv_sem=self.recv_sems.at[number],
            device_id=self.place.to(**move),
            device_id_type=pl.DeviceIdType.MESH,
        )
        copy.start()
        self.unsent.append(copy)
        return copy

    def sent(self, copy):
        copy.wait_send()
        self.unsent = [other for other in self.unsent if other is not copy]

    def finish(self):
        for copy in self.unsent:
            copy.wait_send()


def rows_at(index, size):
    return pl.ds(pl.multiple_of(index * size, size), size)


class Gather:
    def __init__(self, links, block, own=None):
        self.links, self.block, self.y = links, block, links.place.y
        self.own = block(0, self.y) if own is None else own
        self.lines = []

    def over_lines(self, move):
        place = self.block(move, self.y)
        source = self.own if move == 0 else place
        self.lines.append(self.links.send(source, place, ky=1))

    def start_planes(self):
        place = self.block(0, self.y)
        self.far = self.links.send(self.own, place, kz=2)
        self.near = self.links.send(self.own, place, kz=1)

    def start(self):
        self.start_planes()
        self.over_lines(0)

    def relay(self):
        self.near.wait_recv()
        self.over_lines(1)
        self.far.wait_recv()
        place = self.block(2, self.y)
        self.corner = self.links.send(place, place, kz=1)
        self.over_lines(2)

    def last(self):
        self.corner.wait_recv()
        self.over_lines(3)

    def finish(self):
        for copy in self.lines:
            copy.wait_recv()


def head_mean(value):
    row = lax.broadcasted_iota(jnp.int32, (128, 128), 0) // HEAD_WIDTH
    column = lax.broadcasted_iota(jnp.int32, (128, 128), 1) // HEAD_WIDTH
    average = jnp.where(row == column, 1.0 / HEAD_WIDTH, 0.0).astype(F32)
    return jnp.dot(
        value, average, preferred_element_type=F32, precision=lax.Precision.HIGHEST
    )


def halves_swapped(value):
    first = lax.rem(lax.broadcasted_iota(jnp.int32, value.shape, 1), HEAD_WIDTH) < HEAD_WIDTH // 2
    return jnp.where(
        first,
        pltpu.roll(value, 128 - HEAD_WIDTH // 2, 1),
        pltpu.roll(value, HEAD_WIDTH // 2, 1),
    )


class Scatter:
    ORDER = (3, 1, 2, 0)

    def __init__(self, links, y_out, y_in, z_out, z_in, sums):
        self.links = links
        self.y_out, self.y_in, self.z_out, self.z_in, self.sums = y_out, y_in, z_out, z_in, sums
        self.lines, self.planes = {}, {}

    def start(self, move, block):
        self.y_out[move] = block.astype(BF16)
        self.lines[move] = self.links.send(self.y_out.at[move], self.y_in.at[move], ky=1)

    def add(self, move, block):
        self.lines[move].wait_recv()
        total = block + self.y_in[move].astype(F32)
        if move in (3, 1):
            slot = 0 if move == 1 else 1
            self.z_out[slot] = total.astype(BF16)
            self.planes[slot] = self.links.send(self.z_out.at[slot], self.z_in.at[slot], kz=1)
        elif move == 2:
            self.planes[1].wait_recv()
            self.z_out[2] = (total + self.z_in[1].astype(F32)).astype(BF16)
            self.planes[2] = self.links.send(self.z_out.at[2], self.z_in.at[2], kz=2)
        else:
            self.sums[...] = total

    def finish(self):
        self.planes[0].wait_recv()
        self.planes[2].wait_recv()
        return self.sums[...] + self.z_in[0].astype(F32) + self.z_in[2].astype(F32)


def scatter_scratch(block):
    return [
        pltpu.VMEM((4, *block), BF16),
        pltpu.VMEM((4, *block), BF16),
        pltpu.VMEM((3, *block), BF16),
        pltpu.VMEM((3, *block), BF16),
        pltpu.VMEM(block, F32),
    ]


FORWARD_COPIES = 100


def forward_kernel(
    lines,
    heads,
    slice_width,
    longest,
    sequence_ref,
    offset_ref,
    states_ref,
    norm_gains_ref,
    query_gain_ref,
    key_gain_ref,
    frequency_ref,
    query_weight_ref,
    keyvalue_matrix_ref,
    gate_weight_ref,
    up_weight_ref,
    down_weight_ref,
    w_output_in,
    grad_any,
    lin_any,
    attn_in_any,
    query_any,
    kv_any,
    attended_ref,
    attn_out_ref,
    gains_ref,
    w_attend_any,
    middle_ref,
    back_ref,
    gain_out_ref,
    d_heads_ref,
    output_grad_ref,
    mixed_ref,
    cosine_ref,
    sine_ref,
    head_gain_ref,
    table_ref,
    collected_any,
    staged_any,
    w_down_any,
    gains_in,
    w_attend_in,
    lin_ref,
    attn_in_ref,
    query_ref,
    kv_ref,
    w_attend_ref,
    w_output_ref,
    w_hidden_ref,
    down_ref,
    ffn_ref,
    d_hidden_ref,
    partial_ref,
    core_out,
    core_in,
    x_out,
    x_in,
    sums_ref,
    z_out,
    z_in,
    y_out,
    y_in,
    local_sems,
    send_sems,
    recv_sems,
):
    here = Place(lines)
    links = Links(here, send_sems, recv_sems)
    token_rows, width = states_ref.shape
    quarter = token_rows // 4
    half = 2 * quarter
    weight_rows = query_weight_ref.shape[0]
    hidden = slice_width
    blocks = token_rows // STRETCH
    slot_count = offset_ref.shape[0]
    mine, my_half = rows_at(here.quarter, quarter), rows_at(here.c, half)
    other_half = rows_at(1 - here.c, half)
    x_mine, x_other = rows_at(here.x, quarter), rows_at(1 - here.x, quarter)
    odd = here.c == 1

    def rank(move, line):
        return here.plane(move) * lines + line

    def rows_of(ref, columns=slice(None)):
        return lambda move, line: ref.at[rows_at(rank(move, line), weight_rows), columns]

    def columns_of(ref):
        return lambda move, line: ref.at[:, rows_at(rank(move, line), weight_rows)]

    loads = [
        pltpu.make_async_copy(grad_any, down_ref.at[here.z], local_sems.at[0]),
        pltpu.make_async_copy(w_output_in, rows_of(w_output_ref)(0, here.y), local_sems.at[1]),
    ]
    for load in loads:
        load.start()
    links.greet([dict(kc=1), dict(kx=1), dict(ky=1), dict(kz=1), dict(kz=2), dict(kz=3)])

    kv_width = 4 * HEAD_WIDTH
    part = here.x * 2 + here.c
    value_start = KEYVALUE_HEADS * HEAD_WIDTH

    def own_heads(start):
        chosen = None
        for index in range(4):
            begin = start + index * heads // (QUERY_HEADS // KEYVALUE_HEADS) * HEAD_WIDTH
            columns = keyvalue_matrix_ref[:, begin : begin + 2 * HEAD_WIDTH]
            chosen = columns if chosen is None else jnp.where(part == index, columns, chosen)
        return chosen

    w_attend_in[:, :128] = own_heads(0)
    w_attend_in[:, 128:kv_width] = own_heads(value_start)
    w_attend_in[:, kv_width:] = query_weight_ref[...]
    gains_in[...] = jnp.zeros_like(gains_in)
    gains_in[:2, :] = norm_gains_ref[...].astype(F32)
    gains = Gather(links, columns_of(gains_ref), gains_in)
    gains.start()
    first, second = slice(0, kv_width), slice(kv_width, w_attend_in.shape[1])
    kv_weights = Gather(links, rows_of(w_attend_ref, first), w_attend_in.at[:, first])
    kv_weights.start()
    query_weights = Gather(links, rows_of(w_attend_ref, second), w_attend_in.at[:, second])
    columns_of(gains_ref)(0, here.y)[...] = gains_in[...]
    rows_of(w_attend_ref)(0, here.y)[...] = w_attend_in[...]

    head_gain_ref[...] = jnp.concatenate(
        [key_gain_ref[...]] * 2 + [query_gain_ref[...]] * heads, axis=1
    )
    tile_shape = (STRETCH, 2 * HEAD_WIDTH)
    row_number = lax.broadcasted_iota(jnp.int32, tile_shape, 0)
    column_number = lax.broadcasted_iota(jnp.int32, tile_shape, 1)
    front = lax.rem(column_number, HEAD_WIDTH) < HEAD_WIDTH // 2
    for block in range(blocks):
        rows = slice(block * STRETCH, (block + 1) * STRETCH)
        position = row_number + offset_ref[rank(0, here.y) * blocks + block]
        phase = position.astype(F32) * frequency_ref[...]
        cosine_ref[rows, :] = jnp.cos(phase)
        sine = jnp.sin(phase)
        sine_ref[rows, :] = jnp.where(front, -sine, sine)

    def fill(index, carry):
        block, place = index // longest, lax.rem(index, longest)
        sequence = sequence_ref[rank(0, here.y) * blocks + block]
        found = jnp.int32(0)
        for slot in range(slot_count):
            same = (sequence_ref[slot] == sequence) & (offset_ref[slot] == place * STRETCH)
            found = jnp.where(same, slot, found)
        table_ref[index] = found
        return carry

    lax.fori_loop(0, blocks * longest, fill, 0)
    kv_weights.relay()
    query_weights.start()
    gains.relay()
    gains.last()
    gains.finish()
    states = states_ref[...].astype(F32)
    inverse = lax.rsqrt(jnp.mean(states * states, axis=-1, keepdims=True) + EPSILON)
    attn_in_ref[...] = (states * inverse * gains_ref[0:1, :]).astype(BF16)

    def turned(value, group):
        value = (
            value
            * lax.rsqrt(head_mean(value * value) + EPSILON)
            * head_gain_ref[:, group * 128 : (group + 1) * 128]
        )
        return (value * cosine_ref[...] + halves_swapped(value) * sine_ref[...]).astype(BF16)

    kv_weights.last()
    kv_weights.finish()
    lin = product(attn_in_ref[...], w_attend_ref[:, first])
    lin_ref[:, first] = lin
    own_blocks = pl.ds(rank(0, here.y) * blocks, blocks)
    kv_ref[own_blocks, :, :128] = turned(lin[:, :128], 0).reshape(blocks, STRETCH, 128)
    kv_ref[own_blocks, :, 128:] = lin[:, 128:].astype(BF16).reshape(blocks, STRETCH, 128)
    keyvalue = Gather(
        links, lambda move, line: kv_ref.at[pl.ds(rank(move, line) * blocks, blocks)]
    )
    keyvalue.start()
    query_weights.relay()
    query_weights.last()
    keyvalue.relay()
    query_weights.finish()
    lin = product(attn_in_ref[...], w_attend_ref[:, second])
    lin_ref[:, second] = lin
    for pair in range(PAIRS):
        rotated_pair = turned(lin[:, pair * 128 : (pair + 1) * 128], pair + 1)
        for block in range(blocks):
            rows = rotated_pair[block * STRETCH : (block + 1) * STRETCH]
            query_ref[block, pair, :STRETCH] = rows[:, :HEAD_WIDTH]
            query_ref[block, pair, STRETCH:] = rows[:, HEAD_WIDTH:]
    keyvalue.last()

    output = Gather(links, rows_of(w_output_ref), w_output_in)
    output.start_planes()
    planes = {}

    def hidden_plane(move):
        planes[move] = links.send(
            y_out.at[here.plane(move)], columns_of(w_hidden_ref)(0, here.y), kz=move
        )

    hidden_lines = []

    def hidden_line(move):
        if move:
            planes[move].wait_recv()
        place = columns_of(w_hidden_ref)(move, here.y)
        hidden_lines.append(links.send(place, place, ky=1))

    def down_block(move):
        return down_ref.at[here.plane(move), mine]

    down_across, down_cores = {}, {}

    def down_x(move):
        down_across[move] = links.send(down_block(move), down_block(move), kx=1)

    def down_core(move):
        down_across[move].wait_recv()
        both = down_ref.at[here.plane(move), my_half]
        down_cores[move] = links.send(both, both, kc=1)

    saves = []

    def save(source, target):
        copy = pltpu.make_async_copy(source, target, local_sems.at[3 + len(saves)])
        copy.start()
        saves.append(copy)

    for index, weight_ref in enumerate((gate_weight_ref, up_weight_ref, down_weight_ref)):
        for plane in range(4):
            y_out[plane, index * hidden : (index + 1) * hidden] = weight_ref[
                plane * hidden : (plane + 1) * hidden
            ]
    columns_of(w_hidden_ref)(0, here.y)[...] = y_out[here.z]
    keyvalue.finish()
    output.over_lines(0)
    save(lin_ref, lin_any)
    save(attn_in_ref, attn_in_any)
    save(query_ref, query_any)
    save(kv_ref, kv_any)
    save(w_attend_ref, w_attend_any)

    span = longest * STRETCH
    ones = jnp.ones((span, HEAD_WIDTH), BF16)
    shape = (2 * STRETCH, span)
    ahead = lax.broadcasted_iota(jnp.int32, shape, 1) - lax.rem(
        lax.broadcasted_iota(jnp.int32, shape, 0), STRETCH
    )

    def attend_block(block):
        tiles = [kv_ref[table_ref[block * longest + place]] for place in range(longest)]
        tile = jnp.concatenate(tiles, axis=0)
        keys = [tile[:, :64], tile[:, 64:128]]
        values = [
            jnp.concatenate([tile[:, 128:192], ones], axis=1),
            jnp.concatenate([tile[:, 192:256], ones], axis=1),
        ]
        middle_key = jnp.where(odd, keys[1], keys[0])
        middle_value = jnp.where(odd, values[1], values[0])
        visible = ahead <= offset_ref[rank(0, here.y) * blocks + block]
        for pair, key, value in (
            (0, keys[0], values[0]),
            (1, middle_key, middle_value),
            (2, keys[1], values[1]),
        ):
            scores = by_cols(query_ref[block, pair], key)
            weights = jnp.exp2(scores * (LOG2E * HEAD_WIDTH**-0.5))
            weights = jnp.where(visible, weights, 0.0)
            total = product(weights.astype(BF16), value)
            denominator = total[:, HEAD_WIDTH:]
            heads_out = total[:, :HEAD_WIDTH] / denominator
            attended_ref[block, pair] = jnp.concatenate(
                [heads_out, jnp.log2(denominator)], axis=1
            )
            attn_out_ref[
                block * STRETCH : (block + 1) * STRETCH, pair * 128 : (pair + 1) * 128
            ] = jnp.concatenate([heads_out[:STRETCH], heads_out[STRETCH:]], axis=1).astype(BF16)

    attend_block(0)
    output.relay()
    for move in (1, 2, 3):
        hidden_plane(move)
    attend_block(1)
    output.last()
    attend_block(2)
    output.finish()
    hidden_line(0)
    loads[0].wait()
    down_far = links.send(down_block(0), down_block(0), kz=2)
    down_near = links.send(down_block(0), down_block(0), kz=1)

    loads[1].wait()
    cut = 4
    piece = width // cut
    core_copies = []
    for part in range(cut):
        columns = slice(part * piece, (part + 1) * piece)
        weight = w_output_ref[columns, :]
        core_out[1, :, columns] = by_cols(attn_out_ref[other_half, :], weight).astype(BF16)
        core_copies.append(
            links.send(core_out.at[1, :, columns], core_in.at[4, :, columns], kc=1)
        )
        partial_ref[0, :half, columns] = by_cols(attn_out_ref[my_half, :], weight)
    x_copies = []
    hidden_line(1)
    for part in range(cut):
        columns = slice(part * piece, (part + 1) * piece)
        core_copies[part].wait_recv()
        x_out[1, :, columns] = (
            partial_ref[0, x_other, columns] + core_in[4, x_other, columns].astype(F32)
        ).astype(BF16)
        x_copies.append(links.send(x_out.at[1, :, columns], x_in.at[4, :, columns], kx=1))
        middle_ref[:, columns] = (
            states_ref[mine, columns].astype(F32)
            + partial_ref[0, x_mine, columns]
            + core_in[4, x_mine, columns].astype(F32)
        )
    for part in range(cut):
        columns = slice(part * piece, (part + 1) * piece)
        x_copies[part].wait_recv()
        middle_ref[:, columns] += x_in[4, :, columns].astype(F32)
    middle = middle_ref[...]
    inverse = lax.rsqrt(jnp.mean(middle * middle, axis=-1, keepdims=True) + EPSILON)
    ffn_ref[here.z, mine, :] = (middle * inverse * gains_ref[1:2, :]).astype(BF16)

    for copy in core_copies + x_copies:
        links.sent(copy)

    def block_of(move):
        return ffn_ref.at[here.plane(move), mine]

    far = links.send(block_of(0), block_of(0), kz=2)
    near = links.send(block_of(0), block_of(0), kz=1)
    across = {0: links.send(block_of(0), block_of(0), kx=1)}
    cores = {}

    def spread(move):
        across[move].wait_recv()
        both = ffn_ref.at[here.plane(move), my_half]
        cores[move] = links.send(both, both, kc=1)

    hidden_line(2)
    hidden_line(3)
    down_near.wait_recv()
    down_x(1)
    down_far.wait_recv()
    down_corner = links.send(down_block(2), down_block(2), kz=1)
    down_x(2)
    far.wait_recv()
    corner = links.send(block_of(2), block_of(2), kz=1)
    across[2] = links.send(block_of(2), block_of(2), kx=1)
    near.wait_recv()
    across[1] = links.send(block_of(1), block_of(1), kx=1)
    spread(0)
    spread(2)
    down_corner.wait_recv()
    down_x(3)
    down_core(2)
    corner.wait_recv()
    across[3] = links.send(block_of(3), block_of(3), kx=1)
    spread(1)
    down_core(3)
    down_core(1)
    for copy in hidden_lines:
        copy.wait_recv()

    core_copies, x_copies, z_copies = {}, {}, {}
    order = (2, 3, 1, 0)

    def add_cores(index):
        move, slot = order[index], index % 2
        core_copies[move].wait_recv()
        total_rows = rows_at(here.c * 2 + 1 - here.x, quarter)
        if index > 1:
            links.sent(x_copies[order[index - 2]])
        x_out[slot] = (
            partial_ref[slot, total_rows, :] + core_in[move, x_other, :].astype(F32)
        ).astype(BF16)
        x_copies[move] = links.send(x_out.at[slot], x_in.at[move], kx=1)
        sums_ref[move] = partial_ref[slot, mine, :] + core_in[move, x_mine, :].astype(F32)

    def add_x(move):
        x_copies[move].wait_recv()
        sums_ref[move] += x_in[move].astype(F32)
        if move:
            z_out[move - 1] = sums_ref[move].astype(BF16)
            z_copies[move] = links.send(z_out.at[move - 1], z_in.at[move - 1], kz=move)

    for index, move in enumerate(order):
        slot = index % 2
        cores[move].wait_recv()
        if move:
            down_cores[move].wait_recv()
        plane = here.plane(move)
        chunk = ffn_ref[plane]
        gate_pre = by_cols(w_hidden_ref[:hidden, :], chunk)
        up_pre = by_cols(w_hidden_ref[hidden : 2 * hidden, :], chunk)
        sigmoid_gate = 1.0 / (1.0 + jnp.exp(-gate_pre))
        silu = gate_pre * sigmoid_gate
        columns = pl.ds(pl.multiple_of(plane * token_rows, token_rows), token_rows)
        mixed_ref[:, columns] = (silu * up_pre).astype(BF16)
        d_mixed = by_cols(w_hidden_ref[2 * hidden :, :], down_ref[plane])
        d_hidden_ref[:hidden, columns] = (
            d_mixed * up_pre * sigmoid_gate * (1.0 + gate_pre * (1.0 - sigmoid_gate))
        ).astype(BF16)
        d_hidden_ref[hidden:, columns] = (d_mixed * silu).astype(BF16)
        partial_ref[slot] = by_rows(d_hidden_ref[:, columns], w_hidden_ref[: 2 * hidden, :])
        if index > 1:
            links.sent(core_copies[order[index - 2]])
        core_out[slot] = partial_ref[slot, other_half, :].astype(BF16)
        core_copies[move] = links.send(core_out.at[slot], core_in.at[move], kc=1)
        if index == 0:
            spread(3)
        if index > 0:
            add_cores(index - 1)
        if index > 1:
            add_x(order[index - 2])
    add_cores(3)

    def gradient(move, line):
        columns = rows_at(rank(move, line), weight_rows)
        first = jnp.zeros((2 * hidden, weight_rows), F32)
        second = jnp.zeros((hidden, weight_rows), F32)
        for plane in range(4):
            tokens = slice(plane * token_rows, (plane + 1) * token_rows)
            first += product(d_hidden_ref[:, tokens], ffn_ref[plane, :, columns])
            second += product(mixed_ref[:, tokens], down_ref[plane, :, columns])
        return first, second

    def keep(target, pieces):
        target[: 2 * hidden] = pieces[0].astype(BF16)
        target[2 * hidden :] = pieces[1].astype(BF16)

    for move in (1, 2, 3):
        links.sent(planes[move])
    y_copies = {}
    for move in (3, 2, 1, 0):
        keep(y_out.at[move], gradient(move, 1 - here.y))
        y_copies[move] = links.send(y_out.at[move], y_in.at[move], ky=1)
        if move == 3:
            add_x(1)
    add_x(0)

    def gradient_sum(move):
        first, second = gradient(move, here.y)
        y_copies[move].wait_recv()
        links.sent(y_copies[move])
        first += y_in[move, : 2 * hidden].astype(F32)
        second += y_in[move, 2 * hidden :].astype(F32)
        keep(y_out.at[move], (first, second))

    for move in (1, 2, 3):
        z_copies[move].wait_recv()
    d_normed = sums_ref[0]
    for move in (1, 2, 3):
        d_normed += z_in[move - 1].astype(F32)
    middle = middle_ref[...]
    inverse = lax.rsqrt(jnp.mean(middle * middle, axis=-1, keepdims=True) + EPSILON)
    unit = middle * inverse
    gain_out_ref[...] = jnp.sum(d_normed * unit, axis=0, keepdims=True)
    scaled = d_normed * gains_ref[1:2, :]
    back = inverse * (scaled - unit * jnp.mean(scaled * unit, axis=-1, keepdims=True))
    grad_middle = down_ref[here.z, mine, :].astype(F32) + back
    back_ref[...] = grad_middle
    output_grad_ref[mine, :] = grad_middle.astype(BF16)
    block = output_grad_ref.at[mine]
    x_copy = links.send(block, block, kx=1)
    gradient_sum(3)
    last = links.send(y_out.at[3], collected_any.at[here.z], kz=3)
    x_copy.wait_recv()
    both = output_grad_ref.at[my_half]
    core = links.send(both, both, kc=1)
    save(w_hidden_ref.at[pl.ds(2 * hidden, hidden)], w_down_any)
    gradient_sum(2)
    save(y_out.at[2], staged_any.at[1])
    core.wait_recv()
    d_heads_ref[...] = product(output_grad_ref[...], w_output_ref[...]).astype(BF16)
    gradient_sum(1)
    save(y_out.at[1], staged_any.at[0])
    gradient_sum(0)
    save(y_out.at[0], collected_any.at[here.z])
    last.wait_recv()
    for copy in saves:
        copy.wait()
    links.finish()


def forward(lines, heads, slice_width, longest, *arguments):
    states, query_weight = arguments[2], arguments[7]
    columns = query_weight.shape[1] + 4 * HEAD_WIDTH
    token_rows, width = states.shape
    ranks = 4 * lines
    quarter = token_rows // 4
    half = 2 * quarter
    hidden = slice_width
    head_width = heads * HEAD_WIDTH
    weight_rows = width // ranks
    blocks = token_rows // STRETCH
    vmem = pl.BlockSpec(memory_space=pltpu.VMEM)
    smem = pl.BlockSpec(memory_space=pltpu.SMEM)
    hbm = pl.BlockSpec(memory_space=pl.ANY)
    shape = jax.ShapeDtypeStruct
    return pl.pallas_call(
        functools.partial(forward_kernel, lines, heads, slice_width, longest),
        out_shape=(
            shape((token_rows, columns), F32),
            shape((token_rows, width), BF16),
            shape((blocks, PAIRS, 2 * STRETCH, HEAD_WIDTH), BF16),
            shape((ranks * blocks, STRETCH, 4 * HEAD_WIDTH), BF16),
            shape((blocks, PAIRS, 2 * STRETCH, 128), F32),
            shape((token_rows, head_width), BF16),
            shape((8, width), F32),
            shape((width, columns), BF16),
            shape((quarter, width), F32),
            shape((quarter, width), F32),
            shape((1, width), F32),
            shape((token_rows, head_width), BF16),
            shape((token_rows, width), BF16),
            shape((hidden, 4 * token_rows), BF16),
            shape((token_rows, 128), F32),
            shape((token_rows, 128), F32),
            shape((1, (heads + 2) * HEAD_WIDTH), F32),
            shape((blocks * longest,), jnp.int32),
            shape((4, 3 * hidden, weight_rows), BF16),
            shape((2, 3 * hidden, weight_rows), BF16),
            shape((hidden, width), BF16),
        ),
        in_specs=[smem] * 2 + [vmem] * 10 + [hbm] * 2,
        out_specs=(hbm,) * 4 + (vmem,) * 3 + (hbm,) + (vmem,) * 9 + (smem,) + (hbm,) * 3,
        scratch_shapes=[
            pltpu.VMEM((8, weight_rows), F32),
            pltpu.VMEM((weight_rows, columns), BF16),
            pltpu.VMEM((token_rows, columns), F32),
            pltpu.VMEM((token_rows, width), BF16),
            pltpu.VMEM((blocks, PAIRS, 2 * STRETCH, HEAD_WIDTH), BF16),
            pltpu.VMEM((ranks * blocks, STRETCH, 4 * HEAD_WIDTH), BF16),
            pltpu.VMEM((width, columns), BF16),
            pltpu.VMEM((width, head_width), BF16),
            pltpu.VMEM((3 * hidden, width), BF16),
            pltpu.VMEM((4, token_rows, width), BF16),
            pltpu.VMEM((4, token_rows, width), BF16),
            pltpu.VMEM((2 * hidden, 4 * token_rows), BF16),
            pltpu.VMEM((2, token_rows, width), F32),
            pltpu.VMEM((2, half, width), BF16),
            pltpu.VMEM((5, half, width), BF16),
            pltpu.VMEM((2, quarter, width), BF16),
            pltpu.VMEM((5, quarter, width), BF16),
            pltpu.VMEM((4, quarter, width), F32),
            pltpu.VMEM((3, quarter, width), BF16),
            pltpu.VMEM((3, quarter, width), BF16),
            pltpu.VMEM((4, 3 * hidden, weight_rows), BF16),
            pltpu.VMEM((4, 3 * hidden, weight_rows), BF16),
            pltpu.SemaphoreType.DMA((16,)),
            pltpu.SemaphoreType.DMA((FORWARD_COPIES,)),
            pltpu.SemaphoreType.DMA((FORWARD_COPIES,)),
        ],
        compiler_params=pltpu.CompilerParams(
            collective_id=0, has_side_effects=True, vmem_limit_bytes=64 << 20
        ),
        name="forward",
    )(*arguments)


BACKWARD_COPIES = 60


def backward_kernel(
    lines,
    heads,
    longest,
    sequence_ref,
    offset_ref,
    table_ref,
    query_ref,
    kv_ref,
    attended_ref,
    d_heads_ref,
    attn_out_ref,
    gains_ref,
    gain_ffn_ref,
    cosine_ref,
    sine_ref,
    head_gain_ref,
    lin_any,
    attn_in_any,
    output_grad_any,
    w_attend_any,
    back_any,
    states_any,
    middle_any,
    mixed_any,
    w_down_any,
    staged_any,
    collected_in,
    result_ref,
    states_grad_ref,
    g_attend_ref,
    g_output_ref,
    g_kv_ref,
    d_gains_ref,
    query_gain_out,
    key_gain_out,
    collected_any,
    small_ref,
    *scratch,
):
    here = Place(lines)
    del collected_in
    (
        lin_ref,
        attn_in_ref,
        output_grad_ref,
        w_attend_ref,
        back_ref,
        states_ref,
        middle_ref,
        mixed_ref,
        w_down_ref,
        d_query_ref,
        d_kv_ref,
        d_lin_ref,
        partial_ref,
        core_out,
        core_in,
        x_out,
        x_in,
        sums_ref,
        z_out,
        z_in,
        small_out,
        small_in,
        local_sems,
        send_sems,
        recv_sems,
    ) = scratch[:25]
    links = Links(here, send_sems, recv_sems)
    kv_sum = Scatter(links, *scratch[25:30])
    output_sum = Scatter(links, *scratch[30:35])
    attend_sum = Scatter(links, *scratch[35:40])
    token_rows, width = output_grad_ref.shape
    quarter = token_rows // 4
    half = 2 * quarter
    weight_rows = width // (4 * lines)
    kv_width = 4 * HEAD_WIDTH
    blocks = token_rows // STRETCH
    mine, other = rows_at(here.quarter, quarter), rows_at(here.c * 2 + 1 - here.x, quarter)
    my_half, other_half = rows_at(here.c, half), rows_at(1 - here.c, half)
    x_mine, x_other = rows_at(here.x, quarter), rows_at(1 - here.x, quarter)
    odd = here.c == 1
    scale = HEAD_WIDTH**-0.5

    loads = {}

    def load(number, source, target):
        copy = pltpu.make_async_copy(source, target, local_sems.at[number])
        copy.start()
        loads[number] = copy

    load(0, output_grad_any, output_grad_ref)
    load(1, w_down_any, w_down_ref)
    load(2, mixed_any, mixed_ref)
    load(3, lin_any, lin_ref)
    load(4, attn_in_any, attn_in_ref)
    load(5, w_attend_any, w_attend_ref)
    load(6, states_any.at[mine], states_ref)
    load(7, back_any, back_ref)
    load(8, middle_any, middle_ref)
    links.greet([dict(kc=1), dict(kx=1), dict(ky=1), dict(kz=1), dict(kz=2)])
    hidden_pushes = [
        links.send(staged_any.at[move - 1], collected_any.at[here.z], kz=move) for move in (2, 1)
    ]

    def rank(move, line):
        return here.plane(move) * lines + line

    core_copies, x_copies = {}, {}

    def out_start(move, slot):
        at = pl.ds(pl.multiple_of(here.plane(move) * token_rows, token_rows), token_rows)
        partial_ref[slot] = by_rows(mixed_ref[:, at], w_down_ref[...])
        core_out[slot] = partial_ref[slot, other_half, :].astype(BF16)
        core_copies[move] = links.send(core_out.at[slot], core_in.at[move], kc=1)

    def add_cores(move, slot):
        core_copies[move].wait_recv()
        links.sent(core_copies[move])
        x_out[move] = (partial_ref[slot, other, :] + core_in[move, x_other, :].astype(F32)).astype(
            BF16
        )
        x_copies[move] = links.send(x_out.at[move], x_in.at[move], kx=1)
        sums_ref[move] = partial_ref[slot, mine, :] + core_in[move, x_mine, :].astype(F32)

    def add_x(move):
        x_copies[move].wait_recv()
        sums_ref[move] += x_in[move].astype(F32)

    def columns(move, line):
        return rows_at(rank(move, line), weight_rows)

    def output_block(move, line):
        return by_rows(output_grad_ref[:, columns(move, line)], attn_out_ref[...])

    def attend_grad(move, line):
        return by_rows(attn_in_ref[:, columns(move, line)], d_lin_ref[...])

    loads[0].wait()
    for move in Scatter.ORDER:
        output_sum.start(move, output_block(move, 1 - here.y))

    span = longest * STRETCH
    shape = (2 * STRETCH, span)
    ahead = lax.broadcasted_iota(jnp.int32, shape, 1) - lax.rem(
        lax.broadcasted_iota(jnp.int32, shape, 0), STRETCH
    )

    def attend_block(block):
        rows = slice(block * STRETCH, (block + 1) * STRETCH)
        tiles = [kv_ref[table_ref[block * longest + place]] for place in range(longest)]
        tile = jnp.concatenate(tiles, axis=0)
        keys = [tile[:, :64], tile[:, 64:128]]
        values = [tile[:, 128:192], tile[:, 192:256]]
        middle_key = jnp.where(odd, keys[1], keys[0])
        middle_value = jnp.where(odd, values[1], values[0])
        visible = ahead <= offset_ref[rank(0, here.y) * blocks + block]
        d_keys, d_values = [], []
        for pair, key, value in (
            (0, keys[0], values[0]),
            (1, middle_key, middle_value),
            (2, keys[1], values[1]),
        ):
            query = query_ref[block, pair]
            both = d_heads_ref[rows, pair * 128 : (pair + 1) * 128]
            d_out = jnp.concatenate([both[:, :HEAD_WIDTH], both[:, HEAD_WIDTH:]], axis=0)
            kept = attended_ref[block, pair]
            delta = jnp.sum(d_out.astype(F32) * kept[:, :HEAD_WIDTH], axis=-1, keepdims=True)
            scores = by_cols(query, key)
            weights = jnp.exp2(
                scores * (LOG2E * scale) - kept[:, HEAD_WIDTH : HEAD_WIDTH + 1]
            )
            weights = jnp.where(visible, weights, 0.0)
            d_weights = by_cols(d_out, value)
            d_scores = (weights * (d_weights - delta)).astype(BF16)
            d_values.append(by_rows(weights.astype(BF16), d_out))
            d_keys.append(by_rows(d_scores, query))
            d_query_ref[block, pair] = product(d_scores, key) * scale
        zero = jnp.zeros((span, HEAD_WIDTH), F32)
        parts = [
            (d_keys[0] + jnp.where(odd, zero, d_keys[1])) * scale,
            (d_keys[2] + jnp.where(odd, d_keys[1], zero)) * scale,
            d_values[0] + jnp.where(odd, zero, d_values[1]),
            d_values[2] + jnp.where(odd, d_values[1], zero),
        ]
        d_kv_ref[block * longest : (block + 1) * longest] = jnp.concatenate(
            parts, axis=1
        ).reshape(longest, STRETCH, kv_width)

    attend_block(0)
    loads[1].wait()
    loads[2].wait()
    out_start(3, 0)
    out_start(1, 1)
    attend_block(1)
    add_cores(3, 0)
    out_start(2, 0)
    add_cores(1, 1)
    out_start(0, 1)
    attend_block(2)

    def kv_block(move, line):
        pieces = []
        for index in range(blocks):
            slot = rank(move, line) * blocks + index
            sequence = sequence_ref[slot]
            place = offset_ref[slot] // STRETCH
            total = jnp.zeros((STRETCH, kv_width), F32)
            for block in range(blocks):
                same = sequence_ref[rank(0, here.y) * blocks + block] == sequence
                total += jnp.where(same, d_kv_ref[block * longest + place], 0.0)
            pieces.append(total)
        return jnp.concatenate(pieces, axis=0)

    for move in Scatter.ORDER:
        kv_sum.start(move, kv_block(move, 1 - here.y))

    def group_back(group, at, grad):
        linear = lin_ref[:, at]
        inverse = lax.rsqrt(head_mean(linear * linear) + EPSILON)
        unit = linear * inverse
        grad = grad * cosine_ref[...] + halves_swapped(grad * sine_ref[...])
        gain = jnp.sum(grad * unit, axis=0, keepdims=True)
        scaled = grad * head_gain_ref[:, group * 128 : (group + 1) * 128]
        return inverse * (scaled - unit * head_mean(scaled * unit)), gain

    loads[3].wait()
    add_cores(2, 0)
    add_cores(0, 1)
    for move in Scatter.ORDER[:2]:
        output_sum.add(move, output_block(move, here.y))
    small_ref[...] = jnp.zeros_like(small_ref)
    small_ref[1:2, :] = gain_ffn_ref[...]
    for pair in range(PAIRS):
        grad = jnp.concatenate(
            [
                jnp.concatenate(
                    [d_query_ref[block, pair, :STRETCH], d_query_ref[block, pair, STRETCH:]], axis=1
                )
                for block in range(blocks)
            ],
            axis=0,
        )
        at = slice(kv_width + pair * 128, kv_width + (pair + 1) * 128)
        linear_grad, gain = group_back(pair + 1, at, grad)
        d_lin_ref[:, at] = linear_grad.astype(BF16)
        small_ref[2:3, (pair + 1) * 128 : (pair + 2) * 128] = gain
    for move in Scatter.ORDER:
        kv_sum.add(move, kv_block(move, here.y))
    add_x(3)
    z_out[1] = sums_ref[3].astype(BF16)
    z_copies = {1: links.send(z_out.at[1], z_in.at[1], kz=1)}
    add_x(1)
    z_out[0] = sums_ref[1].astype(BF16)
    z_copies[0] = links.send(z_out.at[0], z_in.at[0], kz=1)
    d_kv = kv_sum.finish()
    for move in Scatter.ORDER[2:]:
        output_sum.add(move, output_block(move, here.y))
    linear_grad, gain = group_back(0, slice(0, 128), d_kv[:, :128])
    d_lin_ref[:, :128] = linear_grad.astype(BF16)
    d_lin_ref[:, 128:kv_width] = d_kv[:, 128:].astype(BF16)
    small_ref[2:3, :128] = gain

    loads[4].wait()
    for move in Scatter.ORDER:
        attend_sum.start(move, attend_grad(move, 1 - here.y))
    add_x(2)
    add_x(0)
    z_copies[1].wait_recv()
    z_out[2] = (sums_ref[2] + z_in[1].astype(F32)).astype(BF16)
    z_copies[2] = links.send(z_out.at[2], z_in.at[2], kz=2)

    loads[5].wait()
    partial_ref[0] = by_cols(d_lin_ref[...], w_attend_ref[...])
    core_out[0] = partial_ref[0, other_half, :].astype(BF16)
    core_copies[4] = links.send(core_out.at[0], core_in.at[4], kc=1)
    add_cores(4, 0)
    attend_sum.add(3, attend_grad(3, here.y))
    attend_sum.add(1, attend_grad(1, here.y))
    add_x(4)
    loads[6].wait()
    loads[7].wait()
    states = states_ref[...].astype(F32)
    inverse = lax.rsqrt(jnp.mean(states * states, axis=-1, keepdims=True) + EPSILON)
    unit = states * inverse
    grad = sums_ref[4]
    small_ref[0:1, :] = jnp.sum(grad * unit, axis=0, keepdims=True)
    scaled = grad * gains_ref[0:1, :]
    total = back_ref[...] + inverse * (
        scaled - unit * jnp.mean(scaled * unit, axis=-1, keepdims=True)
    )
    states_grad_ref[mine, :] = total.astype(BF16)
    block = states_grad_ref.at[mine]
    states_x = links.send(block, block, kx=1)

    def small_step(step, **move):
        small_out[step] = small_ref[...]
        return links.send(small_out.at[step], small_in.at[step], **move)

    small = small_step(0, kc=1)
    attend_sum.add(2, attend_grad(2, here.y))
    small.wait_recv()
    small_ref[...] += small_in[0]
    small = small_step(1, kx=1)
    states_x.wait_recv()
    both = states_grad_ref.at[my_half]
    states_core = links.send(both, both, kc=1)
    small.wait_recv()
    small_ref[...] += small_in[1]
    small = small_step(2, ky=1)
    attend_sum.add(0, attend_grad(0, here.y))
    small.wait_recv()
    small_ref[...] += small_in[2]
    small = small_step(3, kz=1)
    small.wait_recv()
    small_ref[...] += small_in[3]
    small = small_step(4, kz=2)

    total = attend_sum.finish()
    part = here.x * 2 + here.c
    g_kv_ref[part] = total[:, :kv_width].astype(BF16)
    block = g_kv_ref.at[part]
    kv_x = links.send(block, block, kx=1)
    kv_core = links.send(block, block, kc=1)
    g_attend_ref[...] = total[:, kv_width:]
    z_copies[0].wait_recv()
    z_copies[2].wait_recv()
    loads[8].wait()
    result_ref[mine, :] = (
        middle_ref[...] + sums_ref[0] + z_in[0].astype(F32) + z_in[2].astype(F32)
    ).astype(BF16)
    block = result_ref.at[mine]
    result_x = links.send(block, block, kx=1)
    kv_x.wait_recv()
    block = g_kv_ref.at[(1 - here.x) * 2 + here.c]
    kv_both = links.send(block, block, kc=1)
    g_output_ref[...] = output_sum.finish()
    small.wait_recv()
    small_ref[...] += small_in[4]
    d_gains_ref[...] = small_ref[:2, rows_at(rank(0, here.y), weight_rows)]
    head_sums = [
        small_ref[2:3, head * HEAD_WIDTH : (head + 1) * HEAD_WIDTH] for head in range(heads + 2)
    ]
    key_gain_out[...] = head_sums[0] + head_sums[1]
    query_gain_out[...] = sum(head_sums[3:], head_sums[2])
    result_x.wait_recv()
    both = result_ref.at[my_half]
    result_core = links.send(both, both, kc=1)
    for copy in (states_core, kv_core, kv_both, result_core, *hidden_pushes):
        copy.wait_recv()
    links.finish()


def backward(lines, heads, longest, *arguments):
    lin, attn_in, mixed, w_attend = arguments[13], arguments[14], arguments[20], arguments[16]
    token_rows, width = attn_in.shape
    quarter = token_rows // 4
    half = 2 * quarter
    weight_rows = width // (4 * lines)
    head_width = heads * HEAD_WIDTH
    blocks = token_rows // STRETCH
    vmem = pl.BlockSpec(memory_space=pltpu.VMEM)
    smem = pl.BlockSpec(memory_space=pltpu.SMEM)
    hbm = pl.BlockSpec(memory_space=pl.ANY)
    shape = jax.ShapeDtypeStruct
    return pl.pallas_call(
        functools.partial(backward_kernel, lines, heads, longest),
        out_shape=(
            shape((token_rows, width), BF16),
            shape((token_rows, width), BF16),
            shape((weight_rows, head_width), F32),
            shape((weight_rows, head_width), F32),
            shape((4, weight_rows, 4 * HEAD_WIDTH), BF16),
            shape((2, weight_rows), F32),
            shape((1, HEAD_WIDTH), F32),
            shape((1, HEAD_WIDTH), F32),
            shape(arguments[-1].shape, BF16),
        ),
        in_specs=[smem] * 3 + [vmem] * 10 + [hbm] * 11,
        out_specs=(vmem,) * 8 + (hbm,),
        scratch_shapes=[
            pltpu.VMEM((8, width), F32),
            pltpu.VMEM(lin.shape, F32),
            pltpu.VMEM(attn_in.shape, BF16),
            pltpu.VMEM((token_rows, width), BF16),
            pltpu.VMEM(w_attend.shape, BF16),
            pltpu.VMEM((quarter, width), F32),
            pltpu.VMEM((quarter, width), BF16),
            pltpu.VMEM((quarter, width), F32),
            pltpu.VMEM(mixed.shape, BF16),
            pltpu.VMEM((mixed.shape[0], width), BF16),
            pltpu.VMEM((blocks, PAIRS, 2 * STRETCH, HEAD_WIDTH), F32),
            pltpu.VMEM((blocks * longest, STRETCH, 4 * HEAD_WIDTH), F32),
            pltpu.VMEM(lin.shape, BF16),
            pltpu.VMEM((2, token_rows, width), F32),
            pltpu.VMEM((2, half, width), BF16),
            pltpu.VMEM((5, half, width), BF16),
            pltpu.VMEM((5, quarter, width), BF16),
            pltpu.VMEM((5, quarter, width), BF16),
            pltpu.VMEM((5, quarter, width), F32),
            pltpu.VMEM((3, quarter, width), BF16),
            pltpu.VMEM((3, quarter, width), BF16),
            pltpu.VMEM((5, 8, width), F32),
            pltpu.VMEM((5, 8, width), F32),
            pltpu.SemaphoreType.DMA((10,)),
            pltpu.SemaphoreType.DMA((BACKWARD_COPIES,)),
            pltpu.SemaphoreType.DMA((BACKWARD_COPIES,)),
            *scatter_scratch((token_rows, 4 * HEAD_WIDTH)),
            *scatter_scratch((weight_rows, head_width)),
            *scatter_scratch((weight_rows, lin.shape[1])),
        ],
        compiler_params=pltpu.CompilerParams(
            collective_id=1, has_side_effects=True, vmem_limit_bytes=64 << 20
        ),
        input_output_aliases={len(arguments) - 1: 8},
        name="backward",
    )(*arguments)


def local_kernels(
    states,
    query_weight,
    keyvalue_matrix,
    output_weight,
    gate_weight,
    up_weight,
    down_weight,
    norm_gains,
    query_gain,
    key_gain,
    slot_sequence,
    slot_offset,
    out_grad,
):
    width = states.shape[1]
    dp_ranks = lax.axis_size("dp")
    tensor_ranks = lax.axis_size("tensor")
    lines = dp_ranks // PLANES
    heads_here = QUERY_HEADS // tensor_ranks
    sharing_count = QUERY_HEADS // KEYVALUE_HEADS
    value_start = KEYVALUE_HEADS * HEAD_WIDTH
    hidden = gate_weight.shape[2]
    slice_width = hidden // PLANES
    weight_rows = width // dp_ranks

    exponent = -(np.arange(2 * HEAD_WIDTH) % (HEAD_WIDTH // 2)) * 2.0 / HEAD_WIDTH
    frequency = jnp.asarray((10000.0**exponent)[None].astype(np.float32))
    (
        lin,
        attn_in,
        queries,
        keyvalues,
        attended,
        attn_out,
        gains,
        w_attend,
        middle_rows,
        back,
        gain_ffn,
        d_heads,
        output_grad,
        mixed,
        cosine,
        sine,
        head_gain,
        table,
        collected,
        staged,
        w_down,
    ) = forward(
        lines,
        heads_here,
        slice_width,
        LONGEST,
        slot_sequence,
        slot_offset,
        states,
        norm_gains[0].T,
        query_gain,
        key_gain,
        frequency,
        query_weight[0],
        keyvalue_matrix[0],
        gate_weight[0].T,
        up_weight[0].T,
        down_weight[0].T,
        output_weight[0],
        out_grad,
    )
    (
        result,
        states_grad,
        g_attend,
        g_output,
        g_kv,
        d_gains,
        d_query_gain,
        d_key_gain,
        collected,
    ) = backward(
        lines,
        heads_here,
        LONGEST,
        slot_sequence,
        slot_offset,
        table,
        queries,
        keyvalues,
        attended,
        d_heads,
        attn_out,
        gains,
        gain_ffn,
        cosine,
        sine,
        head_gain,
        lin,
        attn_in,
        output_grad,
        w_attend,
        back,
        states,
        middle_rows,
        mixed,
        w_down,
        staged,
        collected,
    )

    def hidden_grad(index):
        piece = collected[:, index * slice_width : (index + 1) * slice_width]
        return piece.transpose(2, 0, 1).astype(F32).reshape(1, weight_rows, hidden)

    d_keyvalue_matrix = jnp.zeros((weight_rows, 2 * value_start), F32)
    for other in range(tensor_ranks):
        start = (other * heads_here) // sharing_count * HEAD_WIDTH
        block = g_kv[other].astype(F32)
        for offset, piece in (
            (start, block[:, : 2 * HEAD_WIDTH]),
            (value_start + start, block[:, 2 * HEAD_WIDTH :]),
        ):
            after = 2 * value_start - offset - 2 * HEAD_WIDTH
            d_keyvalue_matrix += jnp.pad(piece, ((0, 0), (offset, after)))
    return (
        result,
        states_grad.astype(F32),
        g_attend[None],
        d_keyvalue_matrix[None],
        g_output[None],
        hidden_grad(0),
        hidden_grad(1),
        hidden_grad(2),
        d_gains.T[None],
        d_query_gain,
        d_key_gain,
    )


def local_permutes(
    states,
    query_weight,
    keyvalue_matrix,
    output_weight,
    gate_weight,
    up_weight,
    down_weight,
    norm_gains,
    query_gain,
    key_gain,
    slot_sequence,
    slot_offset,
    out_grad,
):
    token_rows, width = states.shape
    dp_ranks = lax.axis_size("dp")
    tensor_ranks = lax.axis_size("tensor")
    lines = dp_ranks // PLANES
    rank, part = lax.axis_index("dp"), lax.axis_index("tensor")
    plane, line = rank // lines, rank % lines
    quarter = token_rows // tensor_ranks
    heads_here = QUERY_HEADS // tensor_ranks
    head_width = heads_here * HEAD_WIDTH
    sharing_count = QUERY_HEADS // KEYVALUE_HEADS
    blocks_here = token_rows // STRETCH
    slot_count = slot_sequence.shape[0]
    hidden = gate_weight.shape[2]
    slice_width = hidden // PLANES
    weight_rows = width // dp_ranks

    def send(value, kz=0, ky=0, kx=0, kc=0):
        move_rank, move_part = kz * lines + ky, kx * 2 + kc
        pairs = [
            (r * tensor_ranks + p, (r ^ move_rank) * tensor_ranks + (p ^ move_part))
            for r in range(dp_ranks)
            for p in range(tensor_ranks)
        ]
        return lax.ppermute(value, ("dp", "tensor"), pairs)

    def gather_planes(value):
        near = send(value, kz=1)
        far = send(value, kz=2)
        return [value, near, far, send(far, kz=1)]

    def gather_dp(value):
        whole = jnp.zeros((dp_ranks, *value.shape), value.dtype)
        for kz, piece in enumerate(gather_planes(value)):
            for ky in range(lines):
                got = send(piece, ky=ky) if ky else piece
                whole = lax.dynamic_update_index_in_dim(whole, got, rank ^ (kz * lines + ky), 0)
        return whole

    def rounded(value):
        return value.astype(BF16)

    def scatter_dp(whole):
        def piece(move):
            return lax.dynamic_index_in_dim(whole, rank ^ move, 0, keepdims=False)

        parts = []
        for kz in range(PLANES):
            total = piece(kz * lines).astype(F32)
            for ky in range(1, lines):
                total = total + send(rounded(piece(kz * lines + ky)), ky=ky).astype(F32)
            parts.append(total)
        return scatter_planes(parts)

    def scatter_planes(parts):
        near = parts[0] + send(rounded(parts[1]), kz=1).astype(F32)
        far = parts[2] + send(rounded(parts[3]), kz=1).astype(F32)
        return near + send(rounded(far), kz=2).astype(F32)

    def scatter_tensor(blocks):
        got = send(rounded(jnp.concatenate([blocks[1], blocks[3]], axis=0)), kc=1).astype(F32)
        rows = blocks[0].shape[0]
        here = blocks[0] + got[:rows]
        there = blocks[2] + got[rows:]
        return here + send(rounded(there), kx=1).astype(F32)

    def gather_tensor(block):
        both = jnp.concatenate([block, send(block, kx=1)], axis=0)
        return jnp.concatenate([both, send(both, kc=1)], axis=0)

    def in_order(blocks):
        whole = jnp.zeros_like(blocks)
        for index, move in enumerate((0, 2, 1, 3)):
            whole = lax.dynamic_update_slice_in_dim(
                whole,
                blocks[index * quarter : (index + 1) * quarter],
                (part ^ move) * quarter,
                0,
            )
        return whole

    def quarters(value):
        return [
            lax.dynamic_slice_in_dim(value, (part ^ move) * quarter, quarter, 0)
            for move in range(tensor_ranks)
        ]

    sequence_here = lax.dynamic_slice_in_dim(slot_sequence, rank * blocks_here, blocks_here)
    offset_here = lax.dynamic_slice_in_dim(slot_offset, rank * blocks_here, blocks_here)
    counts = offset_here // STRETCH + 1
    places = jnp.arange(slot_count, dtype=jnp.int32)
    same = (slot_sequence[None, None, :] == sequence_here[:, None, None]) & (
        slot_offset[None, None, :] == places[None, :, None] * STRETCH
    )
    slots = jnp.sum(jnp.where(same, places[None, None, :], 0), axis=2).astype(jnp.int32)
    parity = jnp.reshape(part % 2, (1,)).astype(jnp.int32)
    positions = (offset_here[:, None] + jnp.arange(STRETCH, dtype=jnp.int32)[None, :]).reshape(-1)
    cosines, sines = angles(positions, HEAD_WIDTH)

    first_key = (part * heads_here) // sharing_count * HEAD_WIDTH
    value_start = KEYVALUE_HEADS * HEAD_WIDTH
    kv_columns = [
        lax.dynamic_slice_in_dim(keyvalue_matrix[0], first_key, 2 * HEAD_WIDTH, 1),
        lax.dynamic_slice_in_dim(keyvalue_matrix[0], value_start + first_key, 2 * HEAD_WIDTH, 1),
    ]
    gains = gather_dp(norm_gains[0].T).transpose(1, 0, 2).reshape(2, width).astype(F32)
    w_attend = gather_dp(jnp.concatenate([query_weight[0], *kv_columns], axis=1)).reshape(width, -1)
    w_output = gather_dp(output_weight[0]).reshape(width, head_width)

    def sliced(weight):
        return weight[0].reshape(weight_rows, PLANES, slice_width).transpose(1, 0, 2)

    pad_first = -2 * slice_width % 128
    pad_second = -slice_width % 128
    packed = jnp.concatenate(
        [
            sliced(gate_weight),
            sliced(up_weight),
            jnp.zeros((PLANES, weight_rows, pad_first), BF16),
            sliced(down_weight),
            jnp.zeros((PLANES, weight_rows, pad_second), BF16),
        ],
        axis=2,
    )
    w_hidden = jnp.zeros((dp_ranks, weight_rows, packed.shape[2]), BF16)
    for kz in range(PLANES):
        piece = lax.dynamic_index_in_dim(packed, plane ^ kz, 0, keepdims=False)
        piece = send(piece, kz=kz) if kz else piece
        for ky in range(lines):
            got = send(piece, ky=ky) if ky else piece
            w_hidden = lax.dynamic_update_index_in_dim(w_hidden, got, rank ^ (kz * lines + ky), 0)
    w_hidden = w_hidden.reshape(width, -1)
    down_start = 2 * slice_width + pad_first
    w_gate_up = w_hidden[:, : 2 * slice_width]
    w_down = w_hidden[:, down_start : down_start + slice_width]

    def gather_group(block):
        return [gather_tensor(piece) for piece in gather_planes(block)]

    def quarter_of(value):
        return lax.dynamic_slice_in_dim(value, part * quarter, quarter, 0)

    query_g, key_g = query_gain[0], key_gain[0]
    attn_in = rounded(normed(states.astype(F32), gains[0]))
    lin = product(attn_in, w_attend)
    query_lin, keyvalue_lin = lin[:, :head_width], lin[:, head_width:]

    def query_side(linear, gain_vector):
        return rotated(
            normed(linear.reshape(token_rows, heads_here, HEAD_WIDTH), gain_vector), cosines, sines
        )

    def key_side(linear, gain_vector):
        keys = linear[:, : 2 * HEAD_WIDTH].reshape(token_rows, 2, HEAD_WIDTH)
        keys = rotated(normed(keys, gain_vector), cosines, sines)
        return jnp.concatenate(
            [keys.reshape(token_rows, 2 * HEAD_WIDTH), linear[:, 2 * HEAD_WIDTH :]], axis=1
        )

    def to_pairs(value):
        return (
            value.reshape(blocks_here, STRETCH, PAIRS, 2, -1)
            .transpose(0, 2, 3, 1, 4)
            .reshape(blocks_here, PAIRS, 2 * STRETCH, -1)
        )

    def from_pairs(value):
        return (
            value.reshape(blocks_here, PAIRS, 2, STRETCH, -1)
            .transpose(0, 3, 1, 2, 4)
            .reshape(token_rows, heads_here, -1)
        )

    queries = to_pairs(rounded(query_side(query_lin, query_g)))
    keyvalues = gather_dp(rounded(key_side(keyvalue_lin, key_g)))
    keyvalues = keyvalues.reshape(slot_count, STRETCH, 4 * HEAD_WIDTH)
    attended = attend(counts, slots, parity, queries, keyvalues)
    attn_out = rounded(from_pairs(attended[..., :HEAD_WIDTH]).reshape(token_rows, head_width))
    logs = attended[..., HEAD_WIDTH]

    branch = scatter_tensor(quarters(by_cols(attn_out, w_output)))
    states_quarter = quarter_of(states).astype(F32)
    middle = states_quarter + branch
    ffn_in = rounded(normed(middle, gains[1]))

    down_grads = gather_group(quarter_of(out_grad))
    ffn_ins = gather_group(ffn_in)
    mixed_chunks, d_chunks, back_parts, out_parts = [], [], [], []
    for down_grad, ffn_chunk in zip(down_grads, ffn_ins):
        gate_up = product(ffn_chunk, w_gate_up)
        gate_pre, up_pre = gate_up[:, :slice_width], gate_up[:, slice_width:]
        sigmoid_gate = jax.nn.sigmoid(gate_pre)
        mixed = rounded(gate_pre * sigmoid_gate * up_pre)
        d_mixed = product(down_grad, w_down)
        d_gate = d_mixed * up_pre * sigmoid_gate * (1.0 + gate_pre * (1.0 - sigmoid_gate))
        d_up = d_mixed * gate_pre * sigmoid_gate
        d_gate_up = jnp.concatenate([rounded(d_gate), rounded(d_up)], axis=1)
        mixed_chunks.append(mixed)
        d_chunks.append(d_gate_up)

        def reduced(value):
            blocks = value.reshape(4, quarter, width)
            return scatter_tensor([blocks[0], blocks[2], blocks[1], blocks[3]])

        back_parts.append(reduced(by_cols(d_gate_up, w_gate_up)))
        out_parts.append(reduced(by_cols(mixed, w_down)))
    d_ffn_in = scatter_planes(back_parts)

    def norm_back(vector, gain_vector, grad):
        inverse = lax.rsqrt(jnp.mean(vector * vector, axis=-1, keepdims=True) + EPSILON)
        unit = vector * inverse
        scaled = grad * gain_vector
        back = inverse * (scaled - unit * jnp.mean(scaled * unit, axis=-1, keepdims=True))
        return back, jnp.sum(grad * unit, axis=0)

    d_middle, d_gain_ffn = norm_back(middle, gains[1], d_ffn_in)
    grad_middle = quarter_of(out_grad).astype(F32) + d_middle
    output_grad = in_order(gather_tensor(rounded(grad_middle)))

    d_wout = by_rows(output_grad, attn_out)
    d_heads = rounded(product(output_grad, w_output)).reshape(token_rows, heads_here, HEAD_WIDTH)
    d_pairs = to_pairs(d_heads)
    delta = jnp.sum(d_pairs.astype(F32) * attended[..., :HEAD_WIDTH], axis=-1)
    d_query, d_keyvalue = attend_back(
        counts,
        slots,
        parity,
        queries,
        d_pairs,
        logs[:, :, None, :],
        delta[:, :, None, :],
        keyvalues,
    )
    d_keyvalue_here = scatter_dp(d_keyvalue.reshape(dp_ranks, token_rows, 4 * HEAD_WIDTH))
    _, query_pull = jax.vjp(query_side, query_lin, query_g)
    d_query_lin, d_querygain = query_pull(from_pairs(d_query))
    _, key_pull = jax.vjp(key_side, keyvalue_lin, key_g)
    d_keyvalue_lin, d_keygain = key_pull(d_keyvalue_here)
    d_lin = jnp.concatenate([rounded(d_query_lin), rounded(d_keyvalue_lin)], axis=1)
    d_attn_in = scatter_tensor(quarters(by_cols(d_lin, w_attend)))
    d_states, d_gain_attn = norm_back(states_quarter, gains[0], d_attn_in)
    states_grad = in_order(gather_tensor(rounded(grad_middle + d_states))).astype(F32)

    d_wattend = scatter_dp(by_rows(attn_in, d_lin).reshape(dp_ranks, weight_rows, -1))
    d_wout = scatter_dp(d_wout.reshape(dp_ranks, weight_rows, -1))
    ffn_all = jnp.concatenate(ffn_ins, axis=0)
    down_all = jnp.concatenate(down_grads, axis=0)
    grads_hidden = jnp.concatenate(
        [
            by_rows(ffn_all, jnp.concatenate(d_chunks, axis=0)),
            by_rows(down_all, jnp.concatenate(mixed_chunks, axis=0)),
        ],
        axis=1,
    ).reshape(dp_ranks, weight_rows, 3 * slice_width)
    collected = jnp.zeros((PLANES, weight_rows, 3 * slice_width), F32)
    for kz in range(PLANES):
        total = lax.dynamic_index_in_dim(grads_hidden, rank ^ (kz * lines), 0, keepdims=False)
        for ky in range(1, lines):
            piece = lax.dynamic_index_in_dim(
                grads_hidden, rank ^ (kz * lines + ky), 0, keepdims=False
            )
            total = total + send(rounded(piece), ky=ky).astype(F32)
        if kz:
            total = send(rounded(total), kz=kz).astype(F32)
        collected = lax.dynamic_update_index_in_dim(collected, total, plane ^ kz, 0)

    def unsliced(index):
        piece = collected[:, :, index * slice_width : (index + 1) * slice_width]
        return piece.transpose(1, 0, 2).reshape(1, weight_rows, hidden)

    kv_grad = d_wattend[:, head_width:]
    spread = jnp.zeros((weight_rows, 2 * value_start), F32)
    spread = lax.dynamic_update_slice_in_dim(spread, kv_grad[:, : 2 * HEAD_WIDTH], first_key, 1)
    spread = lax.dynamic_update_slice_in_dim(
        spread, kv_grad[:, 2 * HEAD_WIDTH :], value_start + first_key, 1
    )
    d_wkeyvalue = lax.psum(spread, "tensor")

    result_quarter = rounded(middle + scatter_planes(out_parts))
    result = in_order(gather_tensor(result_quarter))

    small = jnp.concatenate([d_gain_attn, d_gain_ffn, d_querygain, d_keygain])
    small = lax.psum(small, ("dp", "tensor"))
    d_gains = lax.dynamic_slice_in_dim(
        small[: 2 * width].reshape(2, width), rank * weight_rows, weight_rows, 1
    ).T
    return (
        result,
        states_grad,
        d_wattend[None, :, :head_width],
        d_wkeyvalue[None],
        d_wout[None],
        unsliced(0),
        unsliced(1),
        unsliced(2),
        d_gains[None],
        small[2 * width : 2 * width + HEAD_WIDTH][None],
        small[2 * width + HEAD_WIDTH :][None],
    )


def local(*arguments):
    rows = arguments[0].shape[1] // lax.axis_size("dp")
    slots = arguments[10].shape[0]
    if lax.axis_size("dp") == 8 and lax.axis_size("tensor") == 4 and rows == 256 and slots == 24:
        return local_kernels(*arguments)
    return local_permutes(*arguments)


def solution(mesh):
    return jax.shard_map(
        local,
        mesh=mesh,
        in_specs=(
            P("dp", None),
            P(None, "dp", "tensor"),
            P(None, "dp", None),
            P(None, "dp", "tensor"),
            P(None, "dp", "tensor"),
            P(None, "dp", "tensor"),
            P(None, "dp", "tensor"),
            P(None, "dp", None),
            P(),
            P(),
            P(),
            P(),
            P("dp", None),
        ),
        out_specs=(
            P("dp", None),
            P("dp", None),
            P(None, "dp", "tensor"),
            P(None, "dp", None),
            P(None, "dp", "tensor"),
            P(None, "dp", "tensor"),
            P(None, "dp", "tensor"),
            P(None, "dp", "tensor"),
            P(None, "dp", None),
            P(),
            P(),
        ),
        check_vma=False,
    )
```
